32 devices in a mesh: fsdp: 16 (over z, y, core), tensor: 2 (over x).
Axes of the slice: x: 2, y: 2, z: 4, core: 2. Of those that a mesh axis runs over, the one named last changes fastest.
Arguments:
- tokens: bfloat16 [4096, 2048], P('fsdp'), may hold values from -6 to 6
- head_bucket: int32 [4096], P('fsdp'), may hold values from 0 to 3
- ffn_bucket: int32 [4096], P('fsdp'), may hold values from 0 to 3
- lengths: int32 [16, 2], P('fsdp'), may hold values from 64 to 192, as said below
- norm_gains: float32 [2, 2048], replicated, may hold values from 0.5 to 1.5
- qkv_weight: bfloat16 [2048, 3, 2048], P('fsdp', None, 'tensor'), may hold values from -0.125 to 0.125
- out_weight: bfloat16 [2048, 2048], P('tensor', 'fsdp'), may hold values from -1 to 1
- up_weight: bfloat16 [2048, 8192], P('fsdp', 'tensor'), may hold values from -0.125 to 0.125
- down_weight: bfloat16 [8192, 2048], P('tensor', 'fsdp'), may hold values from -0.0625 to 0.0625
- router_first: float32 [2, 2048, 256], replicated, may hold values from -0.125 to 0.125
- router_second: float32 [2, 256, 4], replicated, may hold values from -0.375 to 0.375
- cotangent: bfloat16 [4096, 2048], P('fsdp'), may hold values from -6 to 6
Outputs:
- block_out: bfloat16 [4096, 2048], P('fsdp')
- input_grad: bfloat16 [4096, 2048], P('fsdp')
- grad_gains: float32 [2, 2048], replicated
- grad_qkv: float32 [2048, 3, 2048], P('fsdp', None, 'tensor')
- grad_out: float32 [2048, 2048], P('tensor', 'fsdp')
- grad_up: float32 [2048, 8192], P('fsdp', 'tensor')
- grad_down: float32 [8192, 2048], P('tensor', 'fsdp')
- grad_router_first: float32 [2, 2048, 256], replicated
- grad_router_second: float32 [2, 256, 4], replicated
- usage: float32 [2, 4], replicated
The draws below stay inside these ranges and needn't reach their ends.
Inputs may be any that keep to these rules, and one draw needn't show every extreme that they name: Each row holds the lengths of the 2 sequences of one index of fsdp; a row sums to between 128 and 256, and some row to exactly 256.
All inputs are finite; a program needn't handle non-finite values.
Results may differ from the reference program's by a relative error of at most 0.014.
Values may be sent and summed in bfloat16 or wider, within the bound.
A program may use at most 320 MiB of HBM per device.

```python
import jax
import jax.numpy as jnp
from jax import lax

D = 2048
HEADS = 16
HD = 128
FF = 8192
NB = 4
RH = 256
CAP = 256
MIN_LEN = 64
GROUPS = 16
TOKENS = 4096


def draw_lengths(key, part):
    key_total = jax.random.fold_in(key, 11)
    key_full = jax.random.fold_in(key, 12)
    key_split = jax.random.fold_in(key, 13)
    totals = jax.random.randint(key_total, (GROUPS,), CAP // 2, CAP + 1)
    full_group = jax.random.randint(key_full, (), 0, GROUPS)
    is_full = jnp.arange(GROUPS) == full_group
    totals = jnp.where(is_full, CAP, totals)
    spread = jax.random.randint(key_split, (GROUPS,), 0, 1048576)
    leading = MIN_LEN + spread % (totals - 2 * MIN_LEN + 1)
    leading = jnp.where(is_full, MIN_LEN, leading)
    return jnp.stack([leading, totals - leading], axis=1).astype(jnp.int32)


def with_ends(entries, rng, least, top_value):
    dims = entries.shape
    index_at = [jax.random.randint(jax.random.fold_in(rng, axis), (), 0, dims[axis]) for axis in range(len(dims))]
    entries = entries.at[tuple(index_at)].set(least)
    longest = dims.index(max(dims))
    index_at[longest] = (index_at[longest] + 1) % dims[longest]
    return entries.at[tuple(index_at)].set(top_value)


def strengthened(entries, stream_key, source, target, blocks, factor):
    owner, partner = [(jnp.arange(entries.shape[dim]) // (entries.shape[dim] // blocks)).reshape([-1 if axis == dim else 1 for axis in range(entries.ndim)]) for dim in (source, target)]
    chosen = jax.random.permutation(stream_key, blocks)[partner]
    strong = (owner == chosen) | (owner == (partner + blocks // 2) % blocks)
    return jnp.where(strong, factor * entries, entries)


def block_levels(key, dims, cuts, smallest, top_value):
    def one(dim, parts):
        steps = jax.random.uniform(jax.random.fold_in(jax.random.fold_in(key, 6), dim), (parts,), jnp.float32, smallest / len(cuts), top_value / len(cuts))
        return jnp.repeat(jnp.exp(steps), dims[dim] // parts).reshape((-1,) + (1,) * (len(dims) - dim - 1))

    gain = one(*cuts[0])
    for cut in cuts[1:]:
        gain = gain * one(*cut)
    return gain


def normal_values(own_key, dims, width, most, shards=(), kind=jnp.bfloat16):
    array = jax.random.normal(own_key, dims, jnp.float32) * width
    if len(shards) > 0:
        array = block_levels(own_key, dims, shards, -0.22, 0.18) * array
    return jnp.clip(array, min=-most, max=most).astype(kind)


def noise_with(rng, dims, width, bound, shards, heavy, kind=jnp.bfloat16):
    drawn = width * jax.random.normal(rng, dims, jnp.float32)
    if shards:
        drawn = drawn * block_levels(rng, dims, shards, -0.22, 0.18)
    return jnp.clip(strengthened(drawn, jax.random.fold_in(rng, 3), *heavy), -bound, bound).astype(kind)


def setup_inputs(seed: int = 0) -> dict:
    seeds = jax.random.split(jax.random.key(seed), 13)
    tokens = noise_with(seeds[0], (TOKENS, D), 1.0, 6.0, ((0, 16),), (0, 1, 16, 2.0))
    head_bucket = with_ends(jax.random.randint(seeds[1], (TOKENS,), 0, NB), jax.random.fold_in(seeds[1], 1), 0, NB - 1).astype(jnp.int32)
    ffn_bucket = with_ends(jax.random.randint(seeds[2], (TOKENS,), 0, NB), jax.random.fold_in(seeds[2], 1), 0, NB - 1).astype(jnp.int32)
    lengths = draw_lengths(jax.random.fold_in(seeds[12], 71), 0)
    norm_gains = jnp.clip(1.0 + 0.1 * jax.random.normal(seeds[4], (2, D), jnp.float32), 0.5, 1.5)
    qkv_weight = normal_values(seeds[5], (D, 3, HEADS * HD), D ** -0.5, 0.125, ((0, 16), (2, 2)))
    out_weight = normal_values(seeds[6], (HEADS * HD, D), (HEADS * HD // 64) ** -0.5, 1.0, ((0, 2), (1, 16)))
    up_weight = normal_values(seeds[7], (D, FF), D ** -0.5, 0.125, ((0, 16), (1, 2)))
    down_weight = normal_values(seeds[8], (FF, D), FF ** -0.5, 0.0625, ((0, 2), (1, 16)))
    router_first = normal_values(seeds[9], (2, D, RH), D ** -0.5, 0.125, (), jnp.float32)
    router_second = normal_values(seeds[10], (2, RH, NB), RH ** -0.5, 0.375, (), jnp.float32)
    cotangent = noise_with(seeds[11], (TOKENS, D), 1.0, 6.0, ((0, 16),), (0, 1, 16, 2.0))
    return {"tokens": tokens, "head_bucket": head_bucket, "ffn_bucket": ffn_bucket, "lengths": lengths, "norm_gains": norm_gains, "qkv_weight": qkv_weight, "out_weight": out_weight, "up_weight": up_weight, "down_weight": down_weight, "router_first": router_first, "router_second": router_second, "cotangent": cotangent}


epsilon = 1e-05
theta_base = 10000.0
highest = lax.Precision.HIGHEST

@jax.custom_vjp
def low(v):
    return lax.optimization_barrier(v.astype(jnp.bfloat16)).astype(jnp.float32)

@jax.custom_vjp
def low_back(v):
    return v

def low_keep(v):
    return (low(v), None)

def low_pass(kept, grad):
    return (grad,)

def back_keep(v):
    return (v, None)

def back_low(kept, grad):
    return (low(grad),)
low.defvjp(low_keep, low_pass)
low_back.defvjp(back_keep, back_low)

def layout(length_row, row_count):
    slot_ids = jnp.arange(row_count, dtype=jnp.int32)
    seq_ends = jnp.cumsum(length_row).astype(jnp.int32)
    seq_starts = (seq_ends - length_row).astype(jnp.int32)
    member = (slot_ids[:, None] >= seq_starts[None, :]) & (slot_ids[:, None] < seq_ends[None, :])
    seq_count = length_row.shape[0]
    seq_of = lax.optimization_barrier(jnp.sum(jnp.where(member, jnp.arange(seq_count, dtype=jnp.int32)[None, :], 0), axis=1)).astype(jnp.int32)
    live_rows = jnp.any(member, axis=1)
    seq_begin = lax.optimization_barrier(jnp.sum(jnp.where(member, seq_starts[None, :], 0), axis=1)).astype(jnp.int32)
    segment = jnp.where(live_rows, seq_of, seq_count + slot_ids).astype(jnp.int32)
    position = (slot_ids - seq_begin).astype(jnp.int32)
    return (segment, position, live_rows)

def rotary_tables(position):
    half_dim = HD // 2
    frequency = theta_base ** (-2.0 * jnp.arange(half_dim, dtype=jnp.float32) / HD)
    angles = position.astype(jnp.float32)[:, None] * frequency[None, :]
    return (jnp.cos(angles)[:, None, :], jnp.sin(angles)[:, None, :])

def rotate(operand, cosine, sine_table):
    half_dim = operand.shape[-1] // 2
    lead_half = operand[..., :half_dim]
    tail_half = operand[..., half_dim:]
    return jnp.concatenate([lead_half * cosine - tail_half * sine_table, tail_half * cosine + lead_half * sine_table], axis=-1)

def norm_piece(values_in, gain_row):
    return values_in * lax.rsqrt(lax.optimization_barrier(jnp.mean(values_in * values_in, axis=-1, keepdims=True)) + epsilon) * gain_row

def route_piece(hidden_in, router_in, router_out, bucket):
    inner = jax.nn.silu(jnp.dot(hidden_in, router_in, precision=highest))
    logits = jnp.dot(inner, router_out, precision=highest)
    probs_all = jax.nn.softmax(logits, axis=-1)
    onehot = (bucket[:, None] == jnp.arange(NB, dtype=jnp.int32)[None, :]).astype(probs_all.dtype)
    return NB * lax.optimization_barrier(jnp.sum(probs_all * onehot, axis=-1))

def layer_block(params, block_x, block_heads, block_widths, block_lengths):
    norm_gains, qkv_weight, out_weight, up_weight, down_weight, router_first, router_second = params
    segment, position, live_rows = layout(block_lengths, CAP)
    cosine, sine_table = rotary_tables(position)
    slot_ids = jnp.arange(CAP, dtype=jnp.int32)
    head_used = jnp.arange(HEADS, dtype=jnp.int32)[None, :] < HEADS // NB * (block_heads[:, None] + 1)
    unit_used = jnp.arange(FF, dtype=jnp.int32)[None, :] < FF // NB * (block_widths[:, None] + 1)
    hidden_heads = low(norm_piece(block_x, norm_gains[0]))
    gate_heads = route_piece(hidden_heads, router_first[0], router_second[0], block_heads)
    qkv_all = low_back(jnp.dot(hidden_heads, qkv_weight.reshape(D, 3 * HEADS * HD), precision=highest)).reshape(CAP, 3, HEADS, HD)
    query = low(rotate(qkv_all[:, 0], cosine, sine_table))
    keyed = low(rotate(qkv_all[:, 1], cosine, sine_table))
    value = low(qkv_all[:, 2])
    scores = low_back(jnp.einsum('qhe,khe->hqk', query, keyed, precision=highest) * HD ** (-0.5))
    same_seq = segment[:, None] == segment[None, :]
    causal = slot_ids[None, :] <= slot_ids[:, None]
    diagonal = slot_ids[None, :] == slot_ids[:, None]
    allowed = (same_seq & causal)[None] & (head_used.T[:, None, :] | diagonal[None])
    scores = jnp.where(allowed, scores, -1e+30)
    probs_all = jax.nn.softmax(scores, axis=-1)
    attended = jnp.einsum('hqk,khe->qhe', low(probs_all), value, precision=highest)
    attended = low(low_back(jnp.where(head_used[:, :, None], attended, 0.0))).reshape(CAP, HEADS * HD)
    projected = low_back(jnp.dot(attended, out_weight, precision=highest))
    middle = block_x + gate_heads[:, None] * projected
    hidden_units = low(norm_piece(middle, norm_gains[1]))
    gate_units = route_piece(hidden_units, router_first[1], router_second[1], block_widths)
    upward = low_back(jnp.dot(hidden_units, up_weight, precision=highest))
    activated = low(jnp.where(unit_used, jnp.square(jax.nn.relu(upward)), 0.0))
    downward = low_back(jnp.dot(activated, down_weight, precision=highest))
    return jnp.where(live_rows[:, None], middle + gate_units[:, None] * downward, 0.0)

def reference(tokens, head_bucket, ffn_bucket, lengths, norm_gains, qkv_weight, out_weight, up_weight, down_weight, router_first, router_second, cotangent):
    params = (norm_gains.astype(jnp.float32), qkv_weight.astype(jnp.float32), out_weight.astype(jnp.float32), up_weight.astype(jnp.float32), down_weight.astype(jnp.float32), router_first.astype(jnp.float32), router_second.astype(jnp.float32))
    inputs_all = tokens.astype(jnp.float32).reshape(GROUPS, CAP, D)
    heads_all = head_bucket.reshape(GROUPS, CAP)
    widths_all = ffn_bucket.reshape(GROUPS, CAP)

    def forward(weights_in, inputs_in):

        def one_group(items):
            return layer_block(weights_in, items[0], items[1], items[2], items[3])
        return lax.map(jax.checkpoint(one_group), (inputs_in, heads_all, widths_all, lengths))
    outputs, backward = jax.vjp(forward, params, inputs_all)
    grad_params, grad_inputs = backward(cotangent.astype(jnp.float32).reshape(GROUPS, CAP, D))
    live_all = jax.vmap(lambda length_row: layout(length_row, CAP)[2])(lengths).reshape(TOKENS)
    bucket_ids = jnp.arange(NB, dtype=jnp.int32)[None, :]
    head_counts = lax.optimization_barrier(jnp.sum(jnp.where(live_all[:, None] & (head_bucket[:, None] == bucket_ids), 1.0, 0.0), axis=0))
    width_counts = lax.optimization_barrier(jnp.sum(jnp.where(live_all[:, None] & (ffn_bucket[:, None] == bucket_ids), 1.0, 0.0), axis=0))
    usage = jnp.stack([head_counts, width_counts]).astype(jnp.float32)
    return (outputs.reshape(TOKENS, D).astype(jnp.bfloat16), grad_inputs.reshape(TOKENS, D).astype(jnp.bfloat16), grad_params[0], grad_params[1], grad_params[2], grad_params[3], grad_params[4], grad_params[5], grad_params[6], usage)
```

```python
from functools import partial

import jax
import jax.numpy as jnp
from jax import lax
from jax.sharding import PartitionSpec as P

HEADS = 16
HD = 128
FF = 8192
NB = 4
SHARE = 4

epsilon = 1e-05
theta_base = 10000.0
highest = lax.Precision.HIGHEST
low = jnp.bfloat16
wide = jnp.float32


def norm_piece(values_in, gain_row):
    return (
        values_in
        * lax.rsqrt(jnp.mean(values_in * values_in, axis=-1, keepdims=True) + epsilon)
        * gain_row
    )


def route_piece(hidden_in, router_in, router_out, bucket):
    inner = jax.nn.silu(jnp.dot(hidden_in, router_in, precision=highest))
    logits = jnp.dot(inner, router_out, precision=highest)
    probs_all = jax.nn.softmax(logits, axis=-1)
    onehot = (bucket[:, None] == jnp.arange(NB, dtype=jnp.int32)[None, :]).astype(wide)
    return NB * jnp.sum(probs_all * onehot, axis=-1)


def dot(left_in, right_in):
    return jnp.dot(left_in, right_in, preferred_element_type=wide)


def dot_rows(left_in, right_in):
    return lax.dot_general(
        left_in, right_in, (((0,), (0,)), ((), ())), preferred_element_type=wide
    )


def dot_cols(left_in, right_in):
    return lax.dot_general(
        left_in, right_in, (((1,), (1,)), ((), ())), preferred_element_type=wide
    )


def rotate(operand, cosine, sine_table):
    half_dim = operand.shape[-1] // 2
    lead_half = operand[..., :half_dim]
    tail_half = operand[..., half_dim:]
    return jnp.concatenate(
        [lead_half * cosine - tail_half * sine_table, tail_half * cosine + lead_half * sine_table],
        axis=-1,
    )


def layout(length_rows, slot_ids):
    seq_count = length_rows.shape[1]
    order = jnp.arange(seq_count, dtype=jnp.int32)
    seq_ends = jnp.sum(
        jnp.where(order[None, None, :] <= order[None, :, None], length_rows[:, None, :], 0), axis=2
    )
    seq_starts = seq_ends - length_rows
    slots = slot_ids[None, :, None]
    member = (slots >= seq_starts[:, None, :]) & (slots < seq_ends[:, None, :])
    seq_of = jnp.sum(jnp.where(member, jnp.arange(seq_count, dtype=jnp.int32), 0), axis=2)
    live_rows = jnp.any(member, axis=2)
    seq_begin = jnp.sum(jnp.where(member, seq_starts[:, None, :], 0), axis=2)
    segment = jnp.where(live_rows, seq_of, seq_count + slot_ids[None, :])
    position = slot_ids[None, :] - seq_begin
    return segment, position, live_rows


def solution(mesh):
    fsdp = mesh.shape["fsdp"]
    ring_size = fsdp // SHARE

    def hop(moved, bits):
        return lax.ppermute(moved, "fsdp", [(i, i ^ bits) for i in range(fsdp)])

    def cross(moved):
        return lax.ppermute(moved, "tensor", [(0, 1), (1, 0)])

    def shards(
        tokens,
        head_bucket,
        ffn_bucket,
        lengths,
        norm_gains,
        qkv_weight,
        out_weight,
        up_weight,
        down_weight,
        router_first,
        router_second,
        cotangent,
    ):
        rows, width = tokens.shape
        half = rows // 2
        rank = lax.axis_index("fsdp")
        side = lax.axis_index("tensor")
        share = rank % SHARE
        place = rank // SHARE
        local_units = up_weight.shape[1]
        units = local_units // SHARE
        local_width = out_weight.shape[0]
        head_width = local_width // SHARE
        heads = head_width // HD
        owned = width // fsdp
        block = width // ring_size

        chain = [None, None]

        def ring(moved, stream):
            if chain[stream] is not None:
                moved, _ = lax.optimization_barrier((moved, chain[stream]))
            got = lax.ppermute(
                moved, "fsdp", [(i, (i + SHARE) % fsdp) for i in range(fsdp)]
            )
            chain[stream] = got
            return got

        def place_at(step):
            return (place - step) % ring_size

        def own_half(arr):
            return lax.dynamic_slice_in_dim(arr, side * half, half, 0)

        def relative(arr):
            return jnp.concatenate(
                [own_half(arr), lax.dynamic_slice_in_dim(arr, (1 - side) * half, half, 0)], axis=0
            )

        def gather_rows(arr):
            other = hop(arr, 2)
            plane = jnp.concatenate([arr[:half], other[:half], arr[half:], other[half:]], axis=0)
            return jnp.concatenate([plane, hop(plane, 1)], axis=0)

        def gather_halves(arr):
            pair = jnp.concatenate([arr, hop(arr, 2)], axis=0)
            plane = jnp.concatenate([pair, cross(pair)], axis=0)
            return jnp.concatenate([plane, hop(plane, 1)], axis=0)

        def reduce_rows(keep, send):
            total = keep + hop(send.astype(low), 1).astype(wide)
            total = total[: 2 * half] + cross(total[2 * half :].astype(low)).astype(wide)
            return total[:half] + hop(total[half:].astype(low), 2).astype(wide)

        def whole_rows(arr):
            other = cross(arr)
            return jnp.where(
                side == 0,
                jnp.concatenate([arr, other], axis=0),
                jnp.concatenate([other, arr], axis=0),
            )

        def spread(pieces_for, axis):
            out = None
            for bits in range(SHARE):
                piece = pieces_for(share ^ bits)
                got = piece if bits == 0 else hop(piece, bits)
                if out is None:
                    dims = list(got.shape)
                    dims[axis] *= SHARE
                    out = jnp.zeros(dims, got.dtype)
                out = lax.dynamic_update_slice_in_dim(
                    out, got, (share ^ bits) * got.shape[axis], axis
                )
            return out

        def ring_gather(own, axis):
            dims = list(own.shape)
            dims[axis] = width
            out = jnp.zeros(dims, own.dtype)
            mid = own.shape[0] // 2
            moving = [own[:mid], own[mid:]]
            for step in range(ring_size):
                if step:
                    moving = [ring(moving[s], s) for s in range(2)]
                base = place_at(step) * block
                for s in range(2):
                    if axis == 0:
                        at = (base + s * mid, 0)
                    else:
                        at = (s * mid, base)
                    out = lax.dynamic_update_slice(out, moving[s], at)
            return out

        def ring_reduce(term):
            moving = [None, None]
            for step in range(1, ring_size):
                for s in range(2):
                    part = term(place_at(step), s)
                    if moving[s] is not None:
                        part = part + moving[s].astype(wide)
                    moving[s] = part.astype(low)
                for s in range(2):
                    moving[s] = ring(moving[s], s)
            return [term(place, s) + moving[s].astype(wide) for s in range(2)]

        def scatter_back(parts, axis):
            joined = jnp.concatenate(parts, axis=0)
            other = 1 - axis
            out_dims = list(joined.shape)
            out_dims[axis] = owned
            stride = out_dims[other]
            out_dims[other] *= SHARE
            out = jnp.zeros(out_dims, wide)
            for bits in range(SHARE):
                piece = lax.dynamic_slice_in_dim(joined, (share ^ bits) * owned, owned, axis)
                if bits:
                    piece = hop(piece.astype(low), bits).astype(wide)
                out = lax.dynamic_update_slice_in_dim(out, piece, (share ^ bits) * stride, other)
            return out

        def qkv_piece(target):
            return lax.dynamic_slice_in_dim(
                qkv_weight, target * head_width, head_width, 2
            ).reshape(owned, 3 * head_width)

        qkv_block = spread(qkv_piece, 0)
        rel_tokens = relative(tokens)
        rel_cot = relative(cotangent)
        ints = relative(jnp.stack([head_bucket, ffn_bucket], axis=1))
        qkv_full = ring_gather(qkv_block, 0)
        all_tokens = gather_rows(rel_tokens)
        buckets = gather_rows(ints)
        pair_lengths = jnp.concatenate([lengths, hop(lengths, 2)], axis=0)
        group_lengths = jnp.concatenate([pair_lengths, hop(pair_lengths, 1)], axis=0)

        out_block = spread(
            lambda t: lax.dynamic_slice_in_dim(out_weight, t * head_width, head_width, 0), 1
        )
        out_full = ring_gather(out_block, 1)
        up_block = spread(lambda t: lax.dynamic_slice_in_dim(up_weight, t * units, units, 1), 0)
        up_full = ring_gather(up_block, 0)
        down_block = spread(
            lambda t: lax.dynamic_slice_in_dim(down_weight, t * units, units, 0), 1
        )
        down_full = ring_gather(down_block, 1)
        all_cot = gather_rows(rel_cot)

        slot_ids = jnp.concatenate(
            [
                side * half + jnp.arange(half, dtype=jnp.int32),
                (1 - side) * half + jnp.arange(half, dtype=jnp.int32),
            ]
        )
        segment, position, live_groups = layout(group_lengths, slot_ids)

        def to_groups(arr):
            tail = arr.shape[1:]
            arr = arr.reshape((2, 2, 2, half) + tail)
            return jnp.swapaxes(arr, 1, 2).reshape((SHARE, rows) + tail)

        def from_groups(arr):
            tail = arr.shape[2:]
            arr = arr.reshape((2, 2, 2, half) + tail)
            return jnp.swapaxes(arr, 1, 2).reshape((8 * half,) + tail)

        live_all = from_groups(live_groups)
        all_heads = buckets[:, 0]
        all_widths = buckets[:, 1]

        own_tokens = rel_tokens[:half].astype(wide)
        own_heads = all_heads[:half]
        own_widths = all_widths[:half]
        own_live = live_all[:half]

        block_in = all_tokens.astype(wide)
        hidden_heads = norm_piece(block_in, norm_gains[0]).astype(low)
        own_normed, norm_heads_back = jax.vjp(norm_piece, own_tokens, norm_gains[0])
        gate_heads, route_heads_back = jax.vjp(
            partial(route_piece, bucket=own_heads),
            own_normed.astype(low).astype(wide),
            router_first[0],
            router_second[0],
        )
        head_ids = side * (local_width // HD) + share * heads + jnp.arange(heads, dtype=jnp.int32)
        head_used = head_ids[None, :] < HEADS // NB * (all_heads[:, None] + 1)
        unit_ids = side * local_units + share * units + jnp.arange(units, dtype=jnp.int32)
        unit_used = unit_ids[None, :] < FF // NB * (all_widths[:, None] + 1)

        half_dim = HD // 2
        frequency = theta_base ** (-2.0 * jnp.arange(half_dim, dtype=wide) / HD)
        angles = position.astype(wide)[:, :, None] * frequency
        cosine = jnp.cos(angles)[:, :, None, :]
        sine_table = jnp.sin(angles)[:, :, None, :]
        qkv_all = to_groups(dot(hidden_heads, qkv_full).reshape(8 * half, 3, heads, HD))
        query = rotate(qkv_all[:, :, 0], cosine, sine_table).astype(low)
        keyed = rotate(qkv_all[:, :, 1], cosine, sine_table).astype(low)
        value = qkv_all[:, :, 2].astype(low)
        group_used = to_groups(head_used)
        same_seq = segment[:, :, None] == segment[:, None, :]
        causal = slot_ids[None, :] <= slot_ids[:, None]
        diagonal = slot_ids[None, :] == slot_ids[:, None]
        key_used = jnp.swapaxes(group_used, 1, 2)
        allowed = (same_seq & causal)[:, None] & (key_used[:, :, None, :] | diagonal)
        scale = HD ** (-0.5)
        scores = jnp.einsum("gqhe,gkhe->ghqk", query, keyed, preferred_element_type=wide) * scale
        scores = jnp.where(allowed, scores, -1e30)
        row_top = jnp.max(scores, axis=-1, keepdims=True)
        weights = jnp.exp(scores - row_top)
        probs = weights / jnp.sum(weights, axis=-1, keepdims=True)
        probs_low = probs.astype(low)
        mixed = jnp.einsum("ghqk,gkhe->gqhe", probs_low, value, preferred_element_type=wide)
        mixed = jnp.where(group_used[..., None], mixed, 0.0).astype(low)
        attended = from_groups(mixed).reshape(8 * half, head_width)

        def partial_rows(left_in, matrix, product):
            keep = product(left_in[: 4 * half], matrix)
            send = product(left_in[4 * half :], matrix)
            return reduce_rows(keep, send)

        projected = partial_rows(attended, out_full, dot)

        middle = own_tokens + gate_heads[:, None] * projected
        normed_units, norm_units_back = jax.vjp(norm_piece, middle, norm_gains[1])
        own_units = normed_units.astype(low)
        hidden_units = gather_halves(own_units)
        gate_units, route_units_back = jax.vjp(
            partial(route_piece, bucket=own_widths),
            own_units.astype(wide),
            router_first[1],
            router_second[1],
        )
        all_gates = gather_halves(gate_units[:, None])
        upward = dot(hidden_units, up_full)
        activated = jnp.where(unit_used, jnp.square(jax.nn.relu(upward)), 0.0).astype(low)
        grad_top_all = jnp.where(live_all[:, None], all_cot.astype(wide), 0.0)
        grad_down_in = (all_gates * grad_top_all).astype(low)

        def down_term(at, s):
            mid = units // 2
            return dot_rows(
                activated[:, s * mid : (s + 1) * mid],
                lax.dynamic_slice_in_dim(grad_down_in, at * block, block, 1),
            )

        grad_down = scatter_back(ring_reduce(down_term), 1)

        downward = partial_rows(activated, down_full, dot)
        own_out = jnp.where(
            own_live[:, None], middle + gate_units[:, None] * downward, 0.0
        ).astype(low)
        block_out = whole_rows(own_out)
        grad_top = jnp.where(own_live[:, None], rel_cot[:half].astype(wide), 0.0)
        grad_gate_units = jnp.sum(grad_top * downward, axis=1)

        grad_act = dot_cols(grad_down_in, down_full)
        grad_up_in = jnp.where(unit_used, 2.0 * jax.nn.relu(upward) * grad_act, 0.0).astype(low)

        def up_term(at, s):
            mid = block // 2
            return dot_rows(
                lax.dynamic_slice_in_dim(hidden_units, at * block + s * mid, mid, 1), grad_up_in
            )

        grad_up = scatter_back(ring_reduce(up_term), 0)
        route_units_grads = route_units_back(grad_gate_units)
        grad_hidden_units = partial_rows(grad_up_in, up_full, dot_cols) + route_units_grads[0]
        norm_units_grads = norm_units_back(grad_hidden_units)
        grad_middle = grad_top + norm_units_grads[0]
        grad_gate_heads = jnp.sum(grad_middle * projected, axis=1)
        grad_projected = gather_halves((gate_heads[:, None] * grad_middle).astype(low))

        def out_term(at, s):
            mid = head_width // 2
            return dot_rows(
                attended[:, s * mid : (s + 1) * mid],
                lax.dynamic_slice_in_dim(grad_projected, at * block, block, 1),
            )

        grad_out = scatter_back(ring_reduce(out_term), 1)
        grad_attended = to_groups(
            dot_cols(grad_projected, out_full).astype(low).reshape(8 * half, heads, HD)
        )
        grad_attended = jnp.where(group_used[..., None], grad_attended, jnp.zeros((), low))
        grad_value = jnp.einsum(
            "ghqk,gqhe->gkhe", probs_low, grad_attended, preferred_element_type=wide
        )
        grad_probs = jnp.einsum(
            "gqhe,gkhe->ghqk", grad_attended, value, preferred_element_type=wide
        )
        row_dot = jnp.sum(probs * grad_probs, axis=-1, keepdims=True)
        grad_scores = (probs * (grad_probs - row_dot)).astype(low)
        grad_query = (
            jnp.einsum("ghqk,gkhe->gqhe", grad_scores, keyed, preferred_element_type=wide) * scale
        )
        grad_keyed = (
            jnp.einsum("ghqk,gqhe->gkhe", grad_scores, query, preferred_element_type=wide) * scale
        )
        grad_qkv_in = jnp.stack(
            [
                rotate(grad_query, cosine, -sine_table),
                rotate(grad_keyed, cosine, -sine_table),
                grad_value,
            ],
            axis=2,
        ).astype(low)
        grad_qkv_in = from_groups(grad_qkv_in).reshape(8 * half, 3 * head_width)

        def qkv_term(at, s):
            mid = block // 2
            return dot_rows(
                lax.dynamic_slice_in_dim(hidden_heads, at * block + s * mid, mid, 1), grad_qkv_in
            )

        qkv_parts = ring_reduce(qkv_term)
        joined = jnp.concatenate(qkv_parts, axis=0)
        grad_qkv = jnp.zeros((owned, 3, local_width), wide)
        for bits in range(SHARE):
            piece = lax.dynamic_slice_in_dim(joined, (share ^ bits) * owned, owned, 0)
            if bits:
                piece = hop(piece.astype(low), bits).astype(wide)
            grad_qkv = lax.dynamic_update_slice_in_dim(
                grad_qkv, piece.reshape(owned, 3, head_width), (share ^ bits) * head_width, 2
            )

        route_heads_grads = route_heads_back(grad_gate_heads)
        grad_hidden_heads = partial_rows(grad_qkv_in, qkv_full, dot_cols) + route_heads_grads[0]
        norm_heads_grads = norm_heads_back(grad_hidden_heads)
        input_grad = whole_rows((grad_middle + norm_heads_grads[0]).astype(low))

        def total_small(arr):
            arr = arr + cross(arr)
            bits = 1
            while bits < fsdp:
                arr = arr + hop(arr, bits)
                bits *= 2
            return arr

        def total_large(arr):
            steps = [1, "tensor"] + [2**i for i in range(1, fsdp.bit_length() - 1)]
            for bits in steps:
                mid = arr.shape[0] // 2
                me = side if bits == "tensor" else (rank // bits) % 2
                send = lax.dynamic_slice_in_dim(arr, (1 - me) * mid, mid, 0)
                keep = lax.dynamic_slice_in_dim(arr, me * mid, mid, 0)
                arr = keep + (cross(send) if bits == "tensor" else hop(send, bits))
            for bits in reversed(steps):
                me = side if bits == "tensor" else (rank // bits) % 2
                other = cross(arr) if bits == "tensor" else hop(arr, bits)
                arr = jnp.where(
                    me == 0,
                    jnp.concatenate([arr, other], axis=0),
                    jnp.concatenate([other, arr], axis=0),
                )
            return arr

        bucket_ids = jnp.arange(NB, dtype=jnp.int32)[None, :]
        head_counts = jnp.sum(
            jnp.where(own_live[:, None] & (own_heads[:, None] == bucket_ids), 1.0, 0.0), axis=0
        )
        width_counts = jnp.sum(
            jnp.where(own_live[:, None] & (own_widths[:, None] == bucket_ids), 1.0, 0.0), axis=0
        )
        units_small = total_small(
            jnp.concatenate(
                [norm_units_grads[1], route_units_grads[2].reshape(-1), head_counts, width_counts]
            )
        )
        heads_small = total_small(
            jnp.concatenate([norm_heads_grads[1], route_heads_grads[2].reshape(-1)])
        )
        first_units = total_large(route_units_grads[1])
        first_heads = total_large(route_heads_grads[1])
        second_shape = router_second.shape[1:]
        second_size = second_shape[0] * second_shape[1]
        grad_gains = jnp.stack([heads_small[:width], units_small[:width]])
        grad_second = jnp.stack(
            [
                heads_small[width : width + second_size].reshape(second_shape),
                units_small[width : width + second_size].reshape(second_shape),
            ]
        )
        usage = units_small[width + second_size :].reshape(2, NB)
        grad_first = jnp.stack([first_heads, first_units])
        return (
            block_out,
            input_grad,
            grad_gains,
            grad_qkv,
            grad_out,
            grad_up,
            grad_down,
            grad_first,
            grad_second,
            usage,
        )

    in_specs = (
        P("fsdp", None),
        P("fsdp"),
        P("fsdp"),
        P("fsdp", None),
        P(),
        P("fsdp", None, "tensor"),
        P("tensor", "fsdp"),
        P("fsdp", "tensor"),
        P("tensor", "fsdp"),
        P(),
        P(),
        P("fsdp", None),
    )
    out_specs = (
        P("fsdp", None),
        P("fsdp", None),
        P(),
        P("fsdp", None, "tensor"),
        P("tensor", "fsdp"),
        P("fsdp", "tensor"),
        P("tensor", "fsdp"),
        P(),
        P(),
        P(),
    )
    return jax.shard_map(shards, mesh=mesh, in_specs=in_specs, out_specs=out_specs, check_vma=False)
```

```python
from functools import partial

import jax
import jax.numpy as jnp
from jax import lax
from jax.experimental import pallas as pl
from jax.experimental.pallas import tpu as pltpu
from jax.sharding import PartitionSpec as P

HEADS = 16
HD = 128
FF = 8192
NB = 4
SHARE = 4

epsilon = 1e-05
theta_base = 10000.0
highest = lax.Precision.HIGHEST
low = jnp.bfloat16
wide = jnp.float32
MESH = pl.DeviceIdType.MESH


def norm_piece(values_in, gain_row):
    return (
        values_in
        * lax.rsqrt(jnp.mean(values_in * values_in, axis=-1, keepdims=True) + epsilon)
        * gain_row
    )


def route_piece(hidden_in, router_in, router_out, bucket):
    inner = jax.nn.silu(jnp.dot(hidden_in, router_in, precision=highest))
    logits = jnp.dot(inner, router_out, precision=highest)
    probs_all = jax.nn.softmax(logits, axis=-1)
    onehot = (bucket[:, None] == jnp.arange(NB, dtype=jnp.int32)[None, :]).astype(wide)
    return NB * jnp.sum(probs_all * onehot, axis=-1)


def dot(left_in, right_in):
    return jnp.dot(left_in, right_in, preferred_element_type=wide)


def dot_rows(left_in, right_in):
    return lax.dot_general(
        left_in, right_in, (((0,), (0,)), ((), ())), preferred_element_type=wide
    )


def dot_cols(left_in, right_in):
    return lax.dot_general(
        left_in, right_in, (((1,), (1,)), ((), ())), preferred_element_type=wide
    )


def rotate(operand, cosine, sine_table):
    half_dim = operand.shape[-1] // 2
    lead_half = operand[..., :half_dim]
    tail_half = operand[..., half_dim:]
    return jnp.concatenate(
        [lead_half * cosine - tail_half * sine_table, tail_half * cosine + lead_half * sine_table],
        axis=-1,
    )


def layout(length_rows, slot_ids):
    seq_count = length_rows.shape[1]
    order = jnp.arange(seq_count, dtype=jnp.int32)
    seq_ends = jnp.sum(
        jnp.where(order[None, None, :] <= order[None, :, None], length_rows[:, None, :], 0), axis=2
    )
    seq_starts = seq_ends - length_rows
    slots = slot_ids[None, :, None]
    member = (slots >= seq_starts[:, None, :]) & (slots < seq_ends[:, None, :])
    seq_of = jnp.sum(jnp.where(member, jnp.arange(seq_count, dtype=jnp.int32), 0), axis=2)
    live_rows = jnp.any(member, axis=2)
    seq_begin = jnp.sum(jnp.where(member, seq_starts[:, None, :], 0), axis=2)
    segment = jnp.where(live_rows, seq_of, seq_count + slot_ids[None, :])
    position = slot_ids[None, :] - seq_begin
    return segment, position, live_rows


def general(mesh):
    fsdp = mesh.shape["fsdp"]
    ring_size = fsdp // SHARE

    def hop(moved, bits):
        return lax.ppermute(moved, "fsdp", [(i, i ^ bits) for i in range(fsdp)])

    def cross(moved):
        return lax.ppermute(moved, "tensor", [(0, 1), (1, 0)])

    def shards(
        tokens,
        head_bucket,
        ffn_bucket,
        lengths,
        norm_gains,
        qkv_weight,
        out_weight,
        up_weight,
        down_weight,
        router_first,
        router_second,
        cotangent,
    ):
        rows, width = tokens.shape
        half = rows // 2
        rank = lax.axis_index("fsdp")
        side = lax.axis_index("tensor")
        share = rank % SHARE
        place = rank // SHARE
        local_units = up_weight.shape[1]
        units = local_units // SHARE
        local_width = out_weight.shape[0]
        head_width = local_width // SHARE
        heads = head_width // HD
        owned = width // fsdp
        block = width // ring_size

        chain = [None, None]

        def ring(moved, stream):
            if chain[stream] is not None:
                moved, _ = lax.optimization_barrier((moved, chain[stream]))
            got = lax.ppermute(
                moved, "fsdp", [(i, (i + SHARE) % fsdp) for i in range(fsdp)]
            )
            chain[stream] = got
            return got

        def place_at(step):
            return (place - step) % ring_size

        def own_half(arr):
            return lax.dynamic_slice_in_dim(arr, side * half, half, 0)

        def relative(arr):
            return jnp.concatenate(
                [own_half(arr), lax.dynamic_slice_in_dim(arr, (1 - side) * half, half, 0)], axis=0
            )

        def gather_rows(arr):
            other = hop(arr, 2)
            plane = jnp.concatenate([arr[:half], other[:half], arr[half:], other[half:]], axis=0)
            return jnp.concatenate([plane, hop(plane, 1)], axis=0)

        def gather_halves(arr):
            pair = jnp.concatenate([arr, hop(arr, 2)], axis=0)
            plane = jnp.concatenate([pair, cross(pair)], axis=0)
            return jnp.concatenate([plane, hop(plane, 1)], axis=0)

        def reduce_rows(keep, send):
            total = keep + hop(send.astype(low), 1).astype(wide)
            total = total[: 2 * half] + cross(total[2 * half :].astype(low)).astype(wide)
            return total[:half] + hop(total[half:].astype(low), 2).astype(wide)

        def whole_rows(arr):
            other = cross(arr)
            return jnp.where(
                side == 0,
                jnp.concatenate([arr, other], axis=0),
                jnp.concatenate([other, arr], axis=0),
            )

        def spread(pieces_for, axis):
            out = None
            for bits in range(SHARE):
                piece = pieces_for(share ^ bits)
                got = piece if bits == 0 else hop(piece, bits)
                if out is None:
                    dims = list(got.shape)
                    dims[axis] *= SHARE
                    out = jnp.zeros(dims, got.dtype)
                out = lax.dynamic_update_slice_in_dim(
                    out, got, (share ^ bits) * got.shape[axis], axis
                )
            return out

        def ring_gather(own, axis):
            dims = list(own.shape)
            dims[axis] = width
            out = jnp.zeros(dims, own.dtype)
            mid = own.shape[0] // 2
            moving = [own[:mid], own[mid:]]
            for step in range(ring_size):
                if step:
                    moving = [ring(moving[s], s) for s in range(2)]
                base = place_at(step) * block
                for s in range(2):
                    if axis == 0:
                        at = (base + s * mid, 0)
                    else:
                        at = (s * mid, base)
                    out = lax.dynamic_update_slice(out, moving[s], at)
            return out

        def ring_reduce(term):
            moving = [None, None]
            for step in range(1, ring_size):
                for s in range(2):
                    part = term(place_at(step), s)
                    if moving[s] is not None:
                        part = part + moving[s].astype(wide)
                    moving[s] = part.astype(low)
                for s in range(2):
                    moving[s] = ring(moving[s], s)
            return [term(place, s) + moving[s].astype(wide) for s in range(2)]

        def scatter_back(parts, axis):
            joined = jnp.concatenate(parts, axis=0)
            other = 1 - axis
            out_dims = list(joined.shape)
            out_dims[axis] = owned
            stride = out_dims[other]
            out_dims[other] *= SHARE
            out = jnp.zeros(out_dims, wide)
            for bits in range(SHARE):
                piece = lax.dynamic_slice_in_dim(joined, (share ^ bits) * owned, owned, axis)
                if bits:
                    piece = hop(piece.astype(low), bits).astype(wide)
                out = lax.dynamic_update_slice_in_dim(out, piece, (share ^ bits) * stride, other)
            return out

        def qkv_piece(target):
            return lax.dynamic_slice_in_dim(
                qkv_weight, target * head_width, head_width, 2
            ).reshape(owned, 3 * head_width)

        qkv_block = spread(qkv_piece, 0)
        rel_tokens = relative(tokens)
        rel_cot = relative(cotangent)
        ints = relative(jnp.stack([head_bucket, ffn_bucket], axis=1))
        qkv_full = ring_gather(qkv_block, 0)
        all_tokens = gather_rows(rel_tokens)
        buckets = gather_rows(ints)
        pair_lengths = jnp.concatenate([lengths, hop(lengths, 2)], axis=0)
        group_lengths = jnp.concatenate([pair_lengths, hop(pair_lengths, 1)], axis=0)

        out_block = spread(
            lambda t: lax.dynamic_slice_in_dim(out_weight, t * head_width, head_width, 0), 1
        )
        out_full = ring_gather(out_block, 1)
        up_block = spread(lambda t: lax.dynamic_slice_in_dim(up_weight, t * units, units, 1), 0)
        up_full = ring_gather(up_block, 0)
        down_block = spread(
            lambda t: lax.dynamic_slice_in_dim(down_weight, t * units, units, 0), 1
        )
        down_full = ring_gather(down_block, 1)
        all_cot = gather_rows(rel_cot)

        slot_ids = jnp.concatenate(
            [
                side * half + jnp.arange(half, dtype=jnp.int32),
                (1 - side) * half + jnp.arange(half, dtype=jnp.int32),
            ]
        )
        segment, position, live_groups = layout(group_lengths, slot_ids)

        def to_groups(arr):
            tail = arr.shape[1:]
            arr = arr.reshape((2, 2, 2, half) + tail)
            return jnp.swapaxes(arr, 1, 2).reshape((SHARE, rows) + tail)

        def from_groups(arr):
            tail = arr.shape[2:]
            arr = arr.reshape((2, 2, 2, half) + tail)
            return jnp.swapaxes(arr, 1, 2).reshape((8 * half,) + tail)

        live_all = from_groups(live_groups)
        all_heads = buckets[:, 0]
        all_widths = buckets[:, 1]

        own_tokens = rel_tokens[:half].astype(wide)
        own_heads = all_heads[:half]
        own_widths = all_widths[:half]
        own_live = live_all[:half]

        block_in = all_tokens.astype(wide)
        hidden_heads = norm_piece(block_in, norm_gains[0]).astype(low)
        own_normed, norm_heads_back = jax.vjp(norm_piece, own_tokens, norm_gains[0])
        gate_heads, route_heads_back = jax.vjp(
            partial(route_piece, bucket=own_heads),
            own_normed.astype(low).astype(wide),
            router_first[0],
            router_second[0],
        )
        head_ids = side * (local_width // HD) + share * heads + jnp.arange(heads, dtype=jnp.int32)
        head_used = head_ids[None, :] < HEADS // NB * (all_heads[:, None] + 1)
        unit_ids = side * local_units + share * units + jnp.arange(units, dtype=jnp.int32)
        unit_used = unit_ids[None, :] < FF // NB * (all_widths[:, None] + 1)

        half_dim = HD // 2
        frequency = theta_base ** (-2.0 * jnp.arange(half_dim, dtype=wide) / HD)
        angles = position.astype(wide)[:, :, None] * frequency
        cosine = jnp.cos(angles)[:, :, None, :]
        sine_table = jnp.sin(angles)[:, :, None, :]
        qkv_all = to_groups(dot(hidden_heads, qkv_full).reshape(8 * half, 3, heads, HD))
        query = rotate(qkv_all[:, :, 0], cosine, sine_table).astype(low)
        keyed = rotate(qkv_all[:, :, 1], cosine, sine_table).astype(low)
        value = qkv_all[:, :, 2].astype(low)
        group_used = to_groups(head_used)
        same_seq = segment[:, :, None] == segment[:, None, :]
        causal = slot_ids[None, :] <= slot_ids[:, None]
        diagonal = slot_ids[None, :] == slot_ids[:, None]
        key_used = jnp.swapaxes(group_used, 1, 2)
        allowed = (same_seq & causal)[:, None] & (key_used[:, :, None, :] | diagonal)
        scale = HD ** (-0.5)
        scores = jnp.einsum("gqhe,gkhe->ghqk", query, keyed, preferred_element_type=wide) * scale
        scores = jnp.where(allowed, scores, -1e30)
        row_top = jnp.max(scores, axis=-1, keepdims=True)
        weights = jnp.exp(scores - row_top)
        probs = weights / jnp.sum(weights, axis=-1, keepdims=True)
        probs_low = probs.astype(low)
        mixed = jnp.einsum("ghqk,gkhe->gqhe", probs_low, value, preferred_element_type=wide)
        mixed = jnp.where(group_used[..., None], mixed, 0.0).astype(low)
        attended = from_groups(mixed).reshape(8 * half, head_width)

        def partial_rows(left_in, matrix, product):
            keep = product(left_in[: 4 * half], matrix)
            send = product(left_in[4 * half :], matrix)
            return reduce_rows(keep, send)

        projected = partial_rows(attended, out_full, dot)

        middle = own_tokens + gate_heads[:, None] * projected
        normed_units, norm_units_back = jax.vjp(norm_piece, middle, norm_gains[1])
        own_units = normed_units.astype(low)
        hidden_units = gather_halves(own_units)
        gate_units, route_units_back = jax.vjp(
            partial(route_piece, bucket=own_widths),
            own_units.astype(wide),
            router_first[1],
            router_second[1],
        )
        all_gates = gather_halves(gate_units[:, None])
        upward = dot(hidden_units, up_full)
        activated = jnp.where(unit_used, jnp.square(jax.nn.relu(upward)), 0.0).astype(low)
        grad_top_all = jnp.where(live_all[:, None], all_cot.astype(wide), 0.0)
        grad_down_in = (all_gates * grad_top_all).astype(low)

        def down_term(at, s):
            mid = units // 2
            return dot_rows(
                activated[:, s * mid : (s + 1) * mid],
                lax.dynamic_slice_in_dim(grad_down_in, at * block, block, 1),
            )

        grad_down = scatter_back(ring_reduce(down_term), 1)

        downward = partial_rows(activated, down_full, dot)
        own_out = jnp.where(
            own_live[:, None], middle + gate_units[:, None] * downward, 0.0
        ).astype(low)
        block_out = whole_rows(own_out)
        grad_top = jnp.where(own_live[:, None], rel_cot[:half].astype(wide), 0.0)
        grad_gate_units = jnp.sum(grad_top * downward, axis=1)

        grad_act = dot_cols(grad_down_in, down_full)
        grad_up_in = jnp.where(unit_used, 2.0 * jax.nn.relu(upward) * grad_act, 0.0).astype(low)

        def up_term(at, s):
            mid = block // 2
            return dot_rows(
                lax.dynamic_slice_in_dim(hidden_units, at * block + s * mid, mid, 1), grad_up_in
            )

        grad_up = scatter_back(ring_reduce(up_term), 0)
        route_units_grads = route_units_back(grad_gate_units)
        grad_hidden_units = partial_rows(grad_up_in, up_full, dot_cols) + route_units_grads[0]
        norm_units_grads = norm_units_back(grad_hidden_units)
        grad_middle = grad_top + norm_units_grads[0]
        grad_gate_heads = jnp.sum(grad_middle * projected, axis=1)
        grad_projected = gather_halves((gate_heads[:, None] * grad_middle).astype(low))

        def out_term(at, s):
            mid = head_width // 2
            return dot_rows(
                attended[:, s * mid : (s + 1) * mid],
                lax.dynamic_slice_in_dim(grad_projected, at * block, block, 1),
            )

        grad_out = scatter_back(ring_reduce(out_term), 1)
        grad_attended = to_groups(
            dot_cols(grad_projected, out_full).astype(low).reshape(8 * half, heads, HD)
        )
        grad_attended = jnp.where(group_used[..., None], grad_attended, jnp.zeros((), low))
        grad_value = jnp.einsum(
            "ghqk,gqhe->gkhe", probs_low, grad_attended, preferred_element_type=wide
        )
        grad_probs = jnp.einsum(
            "gqhe,gkhe->ghqk", grad_attended, value, preferred_element_type=wide
        )
        row_dot = jnp.sum(probs * grad_probs, axis=-1, keepdims=True)
        grad_scores = (probs * (grad_probs - row_dot)).astype(low)
        grad_query = (
            jnp.einsum("ghqk,gkhe->gqhe", grad_scores, keyed, preferred_element_type=wide) * scale
        )
        grad_keyed = (
            jnp.einsum("ghqk,gqhe->gkhe", grad_scores, query, preferred_element_type=wide) * scale
        )
        grad_qkv_in = jnp.stack(
            [
                rotate(grad_query, cosine, -sine_table),
                rotate(grad_keyed, cosine, -sine_table),
                grad_value,
            ],
            axis=2,
        ).astype(low)
        grad_qkv_in = from_groups(grad_qkv_in).reshape(8 * half, 3 * head_width)

        def qkv_term(at, s):
            mid = block // 2
            return dot_rows(
                lax.dynamic_slice_in_dim(hidden_heads, at * block + s * mid, mid, 1), grad_qkv_in
            )

        qkv_parts = ring_reduce(qkv_term)
        joined = jnp.concatenate(qkv_parts, axis=0)
        grad_qkv = jnp.zeros((owned, 3, local_width), wide)
        for bits in range(SHARE):
            piece = lax.dynamic_slice_in_dim(joined, (share ^ bits) * owned, owned, 0)
            if bits:
                piece = hop(piece.astype(low), bits).astype(wide)
            grad_qkv = lax.dynamic_update_slice_in_dim(
                grad_qkv, piece.reshape(owned, 3, head_width), (share ^ bits) * head_width, 2
            )

        route_heads_grads = route_heads_back(grad_gate_heads)
        grad_hidden_heads = partial_rows(grad_qkv_in, qkv_full, dot_cols) + route_heads_grads[0]
        norm_heads_grads = norm_heads_back(grad_hidden_heads)
        input_grad = whole_rows((grad_middle + norm_heads_grads[0]).astype(low))

        def total_small(arr):
            arr = arr + cross(arr)
            bits = 1
            while bits < fsdp:
                arr = arr + hop(arr, bits)
                bits *= 2
            return arr

        def total_large(arr):
            steps = [1, "tensor"] + [2**i for i in range(1, fsdp.bit_length() - 1)]
            for bits in steps:
                mid = arr.shape[0] // 2
                me = side if bits == "tensor" else (rank // bits) % 2
                send = lax.dynamic_slice_in_dim(arr, (1 - me) * mid, mid, 0)
                keep = lax.dynamic_slice_in_dim(arr, me * mid, mid, 0)
                arr = keep + (cross(send) if bits == "tensor" else hop(send, bits))
            for bits in reversed(steps):
                me = side if bits == "tensor" else (rank // bits) % 2
                other = cross(arr) if bits == "tensor" else hop(arr, bits)
                arr = jnp.where(
                    me == 0,
                    jnp.concatenate([arr, other], axis=0),
                    jnp.concatenate([other, arr], axis=0),
                )
            return arr

        bucket_ids = jnp.arange(NB, dtype=jnp.int32)[None, :]
        head_counts = jnp.sum(
            jnp.where(own_live[:, None] & (own_heads[:, None] == bucket_ids), 1.0, 0.0), axis=0
        )
        width_counts = jnp.sum(
            jnp.where(own_live[:, None] & (own_widths[:, None] == bucket_ids), 1.0, 0.0), axis=0
        )
        units_small = total_small(
            jnp.concatenate(
                [norm_units_grads[1], route_units_grads[2].reshape(-1), head_counts, width_counts]
            )
        )
        heads_small = total_small(
            jnp.concatenate([norm_heads_grads[1], route_heads_grads[2].reshape(-1)])
        )
        first_units = total_large(route_units_grads[1])
        first_heads = total_large(route_heads_grads[1])
        second_shape = router_second.shape[1:]
        second_size = second_shape[0] * second_shape[1]
        grad_gains = jnp.stack([heads_small[:width], units_small[:width]])
        grad_second = jnp.stack(
            [
                heads_small[width : width + second_size].reshape(second_shape),
                units_small[width : width + second_size].reshape(second_shape),
            ]
        )
        usage = units_small[width + second_size :].reshape(2, NB)
        grad_first = jnp.stack([first_heads, first_units])
        return (
            block_out,
            input_grad,
            grad_gains,
            grad_qkv,
            grad_out,
            grad_up,
            grad_down,
            grad_first,
            grad_second,
            usage,
        )

    return shards


def xor_one(index):
    return index + 1 - 2 * (index % 2)


class Plane:
    def __init__(self):
        self.rank = lax.axis_index("fsdp")
        self.side = lax.axis_index("tensor")
        self.share = self.rank % SHARE
        self.place = self.rank // SHARE
        core = xor_one(self.share)
        mid = (self.share + 2) % SHARE
        self.shares = [self.share, core, mid, SHARE - 1 - self.share]
        self.core = {"fsdp": self.place * SHARE + core}
        self.mid = {"fsdp": self.place * SHARE + mid}
        self.both = {"fsdp": self.place * SHARE + self.shares[3]}
        self.members = [None, self.core, self.mid, self.both]
        self.across = {"tensor": 1 - self.side}
        self.near_place = xor_one(self.place)
        self.two_place = (self.place + 2) % 4
        self.far_place = 3 - self.place
        self.near = {"fsdp": self.near_place * SHARE + self.share}
        self.two = {"fsdp": self.two_place * SHARE + self.share}
        self.far = {"fsdp": self.far_place * SHARE + self.share}
        self.inner = (self.place == 1) | (self.place == 2)
        self.outer = (self.place == 0) | (self.place == 3)

    def greet(self):
        barrier = pltpu.get_barrier_semaphore()
        peers = [self.core, self.mid, self.both, self.across, self.near, self.two, self.far]
        for peer in peers:
            pl.semaphore_signal(barrier, inc=1, device_id=peer, device_id_type=MESH)
        pl.semaphore_wait(barrier, len(peers))


class Copies:
    def __init__(self, local_sems, send_sems, recv_sems):
        self.local_sems, self.send_sems, self.recv_sems = local_sems, send_sems, recv_sems
        self.locals, self.sends, self.recvs = 0, 0, 0

    def local(self, src, dst):
        copy = pltpu.make_async_copy(src, dst, self.local_sems.at[self.locals])
        self.locals += 1
        copy.start()
        return copy

    def slot(self):
        self.recvs += 1
        return self.recvs - 1

    def remote(self, src, dst, peer, slot=None):
        if slot is None:
            slot = self.slot()
        copy = pltpu.make_async_remote_copy(
            src_ref=src,
            dst_ref=dst,
            send_sem=self.send_sems.at[self.sends],
            recv_sem=self.recv_sems.at[slot],
            device_id=peer,
            device_id_type=MESH,
        )
        self.sends += 1
        return copy

    def push(self, src, dst, peer):
        copy = self.remote(src, dst, peer)
        copy.start()
        return copy


class ZGather:
    def __init__(self, here, copies, view):
        self.here, self.copies, self.view = here, copies, view

    def start(self):
        here, copies, view = self.here, self.copies, self.view
        own = view(here.place)
        self.two = copies.push(own, own, here.two)
        self.near = copies.push(own, own, here.near)
        slot = copies.slot()
        self.far = copies.remote(own, own, here.far, slot)
        pl.when(here.inner)(self.far.start)
        passing = view(here.two_place)
        self.passed = copies.remote(passing, passing, here.near, slot)
        arriving = view(here.two_place), view(here.near_place), view(here.far_place)
        self.arrivals = [
            pltpu.make_async_remote_copy(
                src_ref=dst,
                dst_ref=dst,
                send_sem=copies.send_sems.at[0],
                recv_sem=copies.recv_sems.at[at],
                device_id=here.two,
                device_id_type=MESH,
            )
            for dst, at in zip(arriving, (slot - 2, slot - 1, slot))
        ]

    def forward(self):
        self.arrivals[0].wait_recv()
        pl.when(self.here.inner)(self.passed.start)

    def arrive(self):
        self.arrivals[1].wait_recv()
        self.arrivals[2].wait_recv()

    def drain(self):
        self.two.wait_send()
        self.near.wait_send()

        @pl.when(self.here.inner)
        def _():
            self.far.wait_send()
            self.passed.wait_send()


def tiles(count, body):
    def step(i, carry):
        body(i)
        return carry

    lax.fori_loop(0, count, step, 0)


def part(index, size):
    return pl.ds(pl.multiple_of(index * size, size), size)


class RowReduce:
    def __init__(self, here, copies, bufs):
        self.here, self.copies = here, copies
        (self.snd, self.rcv, self.acc, self.out, self.into) = bufs

    def core_send(self, index):
        rows = pl.ds(index * 256, 256)
        copy = self.copies.push(self.snd.at[rows], self.rcv.at[rows], self.here.core)
        self.core = getattr(self, "core", []) + [copy]

    def finish(self, add_core):
        here, copies, acc, out, into = self.here, self.copies, self.acc, self.out, self.into
        for copy in self.core:
            copy.wait_recv()
        add_core(pl.ds(384, 128))
        out[384:512, :] = acc[384:512, :].astype(low)
        diag_x = copies.push(out.at[384:448], into.at[384:448], here.across)
        diag_y = copies.push(out.at[448:512], into.at[448:512], here.mid)
        add_core(pl.ds(128, 256))
        out[128:192, :] = acc[128:192, :].astype(low)
        out[320:384, :] = acc[320:384, :].astype(low)
        diag_y.wait_recv()
        out[192:256, :] = (acc[192:256, :] + into[448:512, :].astype(wide)).astype(low)
        over_x = copies.push(out.at[128:256], into.at[128:256], here.across)
        diag_x.wait_recv()
        out[256:320, :] = (acc[256:320, :] + into[384:448, :].astype(wide)).astype(low)
        over_y = copies.push(out.at[256:384], into.at[256:384], here.mid)
        add_core(pl.ds(0, 128))
        over_x.wait_recv()
        over_y.wait_recv()
        self.sent = self.core + [diag_x, diag_y, over_x, over_y]
        return (
            acc[0:128, :] + into[128:256, :].astype(wide) + into[256:384, :].astype(wide)
        )

    def drain(self):
        for copy in self.sent:
            copy.wait_send()


class RowGather:
    def __init__(self, here, copies, buf):
        self.here, self.copies, self.buf = here, copies, buf

    def run(self):
        here, copies, buf = self.here, self.copies, self.buf
        own = buf.at[0:128]
        over_x = copies.push(own, buf.at[128:256], here.across)
        over_y = copies.push(own, buf.at[256:384], here.mid)
        cores = [copies.push(own, buf.at[512:640], here.core)]
        over_y.wait_recv()
        diag_x = copies.push(buf.at[256:320], buf.at[384:448], here.across)
        cores.append(copies.push(buf.at[256:384], buf.at[768:896], here.core))
        over_x.wait_recv()
        diag_y = copies.push(buf.at[192:256], buf.at[448:512], here.mid)
        cores.append(copies.push(buf.at[128:256], buf.at[640:768], here.core))
        diag_x.wait_recv()
        diag_y.wait_recv()
        cores.append(copies.push(buf.at[384:512], buf.at[896:1024], here.core))
        self.sent = [over_x, over_y, diag_x, diag_y] + cores
        for copy in cores:
            copy.wait_recv()

    def drain(self):
        for copy in self.sent:
            copy.wait_send()


def nn(left_in, right_in):
    return lax.dot_general(
        left_in, right_in, (((1,), (0,)), ((), ())), preferred_element_type=wide
    )


def nt(left_in, right_in):
    return lax.dot_general(
        left_in, right_in, (((1,), (1,)), ((), ())), preferred_element_type=wide
    )


def tn(left_in, right_in):
    return lax.dot_general(
        left_in, right_in, (((0,), (0,)), ((), ())), preferred_element_type=wide
    )


def forward_kernel(
    tok, col, row, qkvw, outw, upw, downw, gains, gate,
    o_hid, o_qkv, o_probs, o_att, o_proj, o_mid, o_units, o_up, o_col, o_row,
    o_wq, o_wo, o_wu, o_wd,
    toks, hid, wq, wo, wu, wd, cols, rows_info, qkvb, probs, att,
    snd, rcv, acc, out_buf, in_buf, proj, mid_buf, units, up,
    local_sems, send_sems, recv_sems,
):
    here = Plane()
    copies = Copies(local_sems, send_sems, recv_sems)
    here.greet()
    rank, share = here.rank, here.share
    owned = 128
    block = owned * SHARE
    head_width = wo.shape[0]
    unit_width = wu.shape[1]
    own_rows = part(rank, owned)

    def spread(src_of, dst):
        got = []
        for d in range(SHARE):
            src = src_of(here.shares[d])
            if d == 0:
                got.append(copies.local(src, dst))
            else:
                got.append(copies.push(src, dst, here.members[d]))
        return got

    def landed(got):
        got[0].wait()
        for copy in got[1:]:
            copy.wait_recv()

    got_q = spread(lambda t: qkvw.at[:, :, part(t, head_width)], wq.at[:, own_rows, :])
    own_tok = copies.local(tok, toks.at[0:256])
    own_col = copies.local(col, cols.at[0:256])
    own_row = copies.local(row, rows_info.at[0])
    tok_mid = copies.push(tok, toks.at[256:512], here.mid)
    tok_core = copies.push(tok, toks.at[512:768], here.core)
    col_mid = copies.push(col, cols.at[256:512], here.mid)
    col_core = copies.push(col, cols.at[512:768], here.core)
    row_mid = copies.push(row, rows_info.at[1], here.mid)
    row_core = copies.push(row, rows_info.at[2], here.core)
    got_o = spread(lambda t: outw.at[part(t, head_width), :], wo.at[:, own_rows])
    got_u = spread(lambda t: upw.at[:, part(t, unit_width)], wu.at[own_rows, :])
    got_d = spread(lambda t: downw.at[part(t, unit_width), :], wd.at[:, own_rows])

    def up_view(h):
        return lambda k: wu.at[pl.ds(pl.multiple_of(k * block + h * 256, 256), 256), :]

    def down_view(h):
        return lambda k: wd.at[h * 512 : (h + 1) * 512, part(k, block)]

    z_q = ZGather(here, copies, lambda k: wq.at[:, part(k, block), :])
    z_o = ZGather(here, copies, lambda k: wo.at[:, part(k, block)])
    z_u = [ZGather(here, copies, up_view(h)) for h in range(2)]
    z_d = [ZGather(here, copies, down_view(h)) for h in range(2)]

    landed(got_q)
    z_q.start()
    landed(got_o)
    z_o.start()

    def normalise(base, count):
        def body(i):
            at = pl.ds(pl.multiple_of(base + i * 64, 64), 64)
            x = toks[at, :].astype(wide)
            r = lax.rsqrt(jnp.mean(x * x, axis=-1, keepdims=True) + epsilon)
            hid[at, :] = (x * r * gains[0:1, :]).astype(low)

        tiles(count, body)

    own_tok.wait()
    normalise(0, 4)
    tok_core.wait_recv()
    normalise(512, 4)
    tok_mid.wait_recv()
    tok_fwd = copies.push(toks.at[256:512], toks.at[768:1024], here.core)
    normalise(256, 4)
    tok_fwd.wait_recv()
    normalise(768, 4)
    own_col.wait()
    own_row.wait()
    col_mid.wait_recv()
    row_mid.wait_recv()
    col_fwd = copies.push(cols.at[256:512], cols.at[768:1024], here.core)
    row_fwd = copies.push(rows_info.at[1], rows_info.at[3], here.core)
    col_core.wait_recv()
    row_core.wait_recv()
    col_fwd.wait_recv()
    row_fwd.wait_recv()
    outs = [copies.local(hid, o_hid), copies.local(cols, o_col), copies.local(rows_info, o_row)]

    z_q.forward()
    landed(got_u)
    z_u[0].start()
    z_q.arrive()
    outs.append(copies.local(wq, o_wq))

    for j in range(3):

        def qkv_tile(i, j=j):
            at = part(i, 512)
            made = nn(hid[at, :], wq[j])
            if j < 2:
                cosine = cols[at, 0:HD]
                sine = cols[at, HD : 2 * HD]
                for h in range(head_width // HD):
                    one = made[:, h * HD : (h + 1) * HD]
                    turned = one * cosine + pltpu.roll(one, HD // 2, 1) * sine
                    qkvb[at, j * head_width + h * HD : j * head_width + (h + 1) * HD] = (
                        turned.astype(low)
                    )
            else:
                qkvb[at, j * head_width : (j + 1) * head_width] = made.astype(low)

        tiles(2, qkv_tile)
    outs.append(copies.local(qkvb, o_qkv))

    z_o.forward()
    z_u[1].start()

    first_head = here.side * (SHARE * head_width // HD) + share * (head_width // HD)
    scale = HD ** (-0.5)
    for h in range(head_width // HD):
        head = (first_head + h).astype(wide)

        def attend_group(g, h=h, head=head):
            at = part(g, 256)
            query = qkvb[at, h * HD : (h + 1) * HD]
            keyed = qkvb[at, head_width + h * HD : head_width + (h + 1) * HD]
            value = qkvb[at, 2 * head_width + h * HD : 2 * head_width + (h + 1) * HD]
            seg_q = cols[at, 2 * HD : 2 * HD + 1]
            slot_q = cols[at, 2 * HD + 1 : 2 * HD + 2]
            bucket_q = cols[at, 2 * HD + 2 : 2 * HD + 3]
            info = rows_info[g]
            seg_k, slot_k, bucket_k = info[0:1, :], info[1:2, :], info[2:3, :]
            reach_k = jnp.where(4.0 * bucket_k + 4.0 > head, 1.0, 0.0)
            same = seg_q == seg_k
            causal = slot_k <= slot_q
            usable = (reach_k > 0.5) | (slot_k == slot_q)
            scores = jnp.where(same & causal & usable, nt(query, keyed) * scale, -1e30)
            top = jnp.max(scores, axis=-1, keepdims=True)
            weights = jnp.exp(scores - top)
            p = weights / jnp.sum(weights, axis=-1, keepdims=True)
            probs[part(g * (head_width // HD) + h, 256), :] = p
            mixed = nn(p.astype(low), value)
            att[at, h * HD : (h + 1) * HD] = jnp.where(
                4.0 * bucket_q + 4.0 > head, mixed, 0.0
            ).astype(low)

        tiles(SHARE, attend_group)
    outs.append(copies.local(probs, o_probs))
    outs.append(copies.local(att, o_att))

    z_o.arrive()
    outs.append(copies.local(wo, o_wo))

    reduce = RowReduce(here, copies, (snd, rcv, acc, out_buf, in_buf))
    for i in range(2):

        def send_tile(n, i=i):
            c = part(n, 512)
            snd[i * 256 : (i + 1) * 256, c] = nn(
                att[512 + i * 256 : 512 + (i + 1) * 256, :], wo[:, c]
            ).astype(low)

        tiles(4, send_tile)
        reduce.core_send(i)

    def keep_tile(n):
        c = part(n, 512)
        acc[:, c] = nn(att[0:512, :], wo[:, c])

    tiles(4, keep_tile)

    def add_core(at):
        acc[at, :] = acc[at, :] + rcv[at, :].astype(wide)

    z_u[0].forward()
    landed(got_d)
    z_d[0].start()
    projected = reduce.finish(add_core)
    proj[...] = projected
    middle = toks[0:128, :].astype(wide) + gate[:, 0:1] * projected
    mid_buf[...] = middle
    r = lax.rsqrt(jnp.mean(middle * middle, axis=-1, keepdims=True) + epsilon)
    units[0:128, :] = (middle * r * gains[1:2, :]).astype(low)
    outs.append(copies.local(proj, o_proj))
    outs.append(copies.local(mid_buf, o_mid))
    gather = RowGather(here, copies, units)
    gather.run()
    outs.append(copies.local(units, o_units))

    z_u[1].forward()
    z_d[1].start()
    z_u[0].arrive()
    z_u[1].arrive()
    outs.append(copies.local(wu, o_wu))

    def up_tile(i):
        at = part(i % 2, 512)
        c = part(i // 2, 512)
        up[at, c] = nn(units[at, :], wu[:, c])

    tiles(unit_width // 256, up_tile)
    outs.append(copies.local(up, o_up))
    z_d[0].forward()
    z_d[1].forward()
    z_d[0].arrive()
    z_d[1].arrive()
    outs.append(copies.local(wd, o_wd))

    for one in [z_q, z_o] + z_u + z_d + [reduce, gather]:
        one.drain()
    sent = [tok_mid, tok_core, tok_fwd, col_mid, col_core, row_mid, row_core, col_fwd, row_fwd]
    for got in (got_q, got_o, got_u, got_d):
        sent += got[1:]
    for copy in sent:
        copy.wait_send()
    for copy in outs:
        copy.wait()


def plane(mesh):
    fsdp = mesh.shape["fsdp"]
    ring_size = fsdp // SHARE

    def hop(moved, bits):
        return lax.ppermute(moved, "fsdp", [(i, i ^ bits) for i in range(fsdp)])

    def cross(moved):
        return lax.ppermute(moved, "tensor", [(0, 1), (1, 0)])

    def shards(
        tokens,
        head_bucket,
        ffn_bucket,
        lengths,
        norm_gains,
        qkv_weight,
        out_weight,
        up_weight,
        down_weight,
        router_first,
        router_second,
        cotangent,
    ):
        rows, width = tokens.shape
        half = rows // 2
        rank = lax.axis_index("fsdp")
        side = lax.axis_index("tensor")
        share = rank % SHARE
        place = rank // SHARE
        local_units = up_weight.shape[1]
        units = local_units // SHARE
        local_width = out_weight.shape[0]
        head_width = local_width // SHARE
        heads = head_width // HD
        owned = width // fsdp
        block = width // ring_size
        plane_rows = SHARE * rows

        def own_half(arr):
            return lax.dynamic_slice_in_dim(arr, side * half, half, 0)

        def relative(arr):
            return jnp.concatenate(
                [own_half(arr), lax.dynamic_slice_in_dim(arr, (1 - side) * half, half, 0)], axis=0
            )

        slot_ids = jnp.concatenate(
            [
                side * half + jnp.arange(half, dtype=jnp.int32),
                (1 - side) * half + jnp.arange(half, dtype=jnp.int32),
            ]
        )
        segment, position, live_rows = (a[0] for a in layout(lengths, slot_ids))
        frequency = theta_base ** (-2.0 * jnp.arange(HD // 2, dtype=wide) / HD)
        angles = position.astype(wide)[:, None] * frequency
        cosine, sine = jnp.cos(angles), jnp.sin(angles)
        rel_heads = relative(head_bucket)
        rel_widths = relative(ffn_bucket)
        facts = jnp.stack(
            [segment, slot_ids, rel_heads, rel_widths, live_rows.astype(jnp.int32)], axis=1
        ).astype(wide)
        col = jnp.concatenate(
            [cosine, cosine, -sine, sine, jnp.pad(facts, ((0, 0), (0, HD - facts.shape[1])))],
            axis=1,
        )
        row = jnp.pad(facts.T, ((0, 8 - facts.shape[1]), (0, 0)))
        rel_tokens = relative(tokens)
        own_tokens = rel_tokens[:half].astype(wide)
        own_heads, own_widths = rel_heads[:half], rel_widths[:half]
        own_live = live_rows[:half]
        own_normed, norm_heads_back = jax.vjp(norm_piece, own_tokens, norm_gains[0])
        gate_heads, route_heads_back = jax.vjp(
            partial(route_piece, bucket=own_heads),
            own_normed.astype(low).astype(wide),
            router_first[0],
            router_second[0],
        )
        f32, b16 = jnp.float32, jnp.bfloat16

        def shape(*dims):
            return jax.ShapeDtypeStruct(dims[1:], dims[0])

        anywhere = pl.BlockSpec(memory_space=pl.ANY)
        vmem = pl.BlockSpec(memory_space=pltpu.VMEM)
        weights = [
            shape(b16, 3, width, head_width),
            shape(b16, head_width, width),
            shape(b16, width, units),
            shape(b16, units, width),
        ]
        made = [
            shape(b16, plane_rows, width),
            shape(b16, plane_rows, 3 * head_width),
            shape(f32, SHARE * heads * rows, rows),
            shape(b16, plane_rows, head_width),
            shape(f32, half, width),
            shape(f32, half, width),
            shape(b16, plane_rows, width),
            shape(f32, plane_rows, units),
            shape(f32, plane_rows, 3 * HD),
            shape(f32, SHARE, 8, rows),
        ]
        (
            hidden_heads,
            qkvb,
            probs,
            attended,
            projected,
            middle,
            hidden_units,
            upward,
            all_col,
            all_row,
            qkv_full,
            out_full,
            up_full,
            down_full,
        ) = pl.pallas_call(
            forward_kernel,
            out_shape=made + weights,
            in_specs=[anywhere] * 7 + [vmem] * 2,
            out_specs=[anywhere] * 14,
            scratch_shapes=[
                pltpu.VMEM((plane_rows, width), b16),
                pltpu.VMEM((plane_rows, width), b16),
                pltpu.VMEM((3, width, head_width), b16),
                pltpu.VMEM((head_width, width), b16),
                pltpu.VMEM((width, units), b16),
                pltpu.VMEM((units, width), b16),
                pltpu.VMEM((plane_rows, 3 * HD), f32),
                pltpu.VMEM((SHARE, 8, rows), f32),
                pltpu.VMEM((plane_rows, 3 * head_width), b16),
                pltpu.VMEM((SHARE * heads * rows, rows), f32),
                pltpu.VMEM((plane_rows, head_width), b16),
                pltpu.VMEM((plane_rows // 2, width), b16),
                pltpu.VMEM((plane_rows // 2, width), b16),
                pltpu.VMEM((plane_rows // 2, width), f32),
                pltpu.VMEM((plane_rows // 2, width), b16),
                pltpu.VMEM((plane_rows // 2, width), b16),
                pltpu.VMEM((half, width), f32),
                pltpu.VMEM((half, width), f32),
                pltpu.VMEM((plane_rows, width), b16),
                pltpu.VMEM((plane_rows, units), f32),
                pltpu.SemaphoreType.DMA((24,)),
                pltpu.SemaphoreType.DMA((64,)),
                pltpu.SemaphoreType.DMA((64,)),
            ],
            compiler_params=pltpu.CompilerParams(
                collective_id=0, has_side_effects=True, vmem_limit_bytes=60 * 2**20
            ),
        )(
            rel_tokens,
            col,
            row,
            jnp.transpose(qkv_weight, (1, 0, 2)),
            out_weight,
            up_weight,
            down_weight,
            norm_gains,
            jnp.broadcast_to(gate_heads[:, None], (half, HD)),
        )
        def gather_rows(arr):
            pair = jnp.concatenate([arr, hop(arr, 2)], axis=0)
            return jnp.concatenate([pair, hop(pair, 1)], axis=0)

        def gather_halves(arr):
            pair = jnp.concatenate([arr, cross(arr)], axis=0)
            return gather_rows(pair)

        def reduce_rows(keep, send):
            total = keep + hop(send.astype(low), 1).astype(wide)
            total = total.reshape(2, 2, half, width)
            total = total[:, 0] + cross(total[:, 1].astype(low)).astype(wide)
            return total[0] + hop(total[1].astype(low), 2).astype(wide)

        def whole_rows(arr):
            other = cross(arr)
            return jnp.where(
                side == 0,
                jnp.concatenate([arr, other], axis=0),
                jnp.concatenate([other, arr], axis=0),
            )

        def partial_rows(left_in, matrix, product):
            keep = product(left_in[: 4 * half], matrix)
            send = product(left_in[4 * half :], matrix)
            return reduce_rows(keep, send)

        chain = [None, None]

        def ring(moved, stream):
            if chain[stream] is not None:
                moved, _ = lax.optimization_barrier((moved, chain[stream]))
            got = lax.ppermute(
                moved, "fsdp", [(i, (i + SHARE) % fsdp) for i in range(fsdp)]
            )
            chain[stream] = got
            return got

        def place_at(step):
            return (place - step) % ring_size

        def ring_reduce(term):
            moving = [None, None]
            for step in range(1, ring_size):
                for s in range(2):
                    piece = term(place_at(step), s)
                    if moving[s] is not None:
                        piece = piece + moving[s].astype(wide)
                    moving[s] = piece.astype(low)
                for s in range(2):
                    moving[s] = ring(moving[s], s)
            return [term(place, s) + moving[s].astype(wide) for s in range(2)]

        def scatter_back(parts, axis):
            joined = jnp.concatenate(parts, axis=0)
            other = 1 - axis
            out_dims = list(joined.shape)
            out_dims[axis] = owned
            stride = out_dims[other]
            out_dims[other] *= SHARE
            out = jnp.zeros(out_dims, wide)
            for bits in range(SHARE):
                piece = lax.dynamic_slice_in_dim(joined, (share ^ bits) * owned, owned, axis)
                if bits:
                    piece = hop(piece.astype(low), bits).astype(wide)
                out = lax.dynamic_update_slice_in_dim(out, piece, (share ^ bits) * stride, other)
            return out

        all_cot = gather_rows(relative(cotangent))
        own_units = hidden_units[:half]
        _, norm_units_back = jax.vjp(norm_piece, middle, norm_gains[1])
        gate_units, route_units_back = jax.vjp(
            partial(route_piece, bucket=own_widths),
            own_units.astype(wide),
            router_first[1],
            router_second[1],
        )
        all_gates = gather_halves(gate_units[:, None])
        all_heads = all_col[:, 2 * HD + 2].astype(jnp.int32)
        all_widths = all_col[:, 2 * HD + 3].astype(jnp.int32)
        live_all = all_col[:, 2 * HD + 4] > 0.5
        cosine = all_col[:, : HD // 2].reshape(SHARE, rows, 1, HD // 2)
        sine_table = all_col[:, HD + HD // 2 : 2 * HD].reshape(SHARE, rows, 1, HD // 2)
        head_ids = side * (local_width // HD) + share * heads + jnp.arange(heads, dtype=jnp.int32)
        head_used = head_ids[None, :] < HEADS // NB * (all_heads[:, None] + 1)
        group_used = head_used.reshape(SHARE, rows, heads)
        unit_ids = side * local_units + share * units + jnp.arange(units, dtype=jnp.int32)
        unit_used = unit_ids[None, :] < FF // NB * (all_widths[:, None] + 1)
        scale = HD ** (-0.5)
        probs = probs.reshape(SHARE, heads, rows, rows)
        probs_low = probs.astype(low)
        groups = qkvb.reshape(SHARE, rows, 3, heads, HD)
        query, keyed, value = groups[:, :, 0], groups[:, :, 1], groups[:, :, 2]
        qkv_mat = jnp.transpose(qkv_full, (1, 0, 2)).reshape(width, 3 * head_width)

        def to_groups(arr):
            return arr.reshape((SHARE, rows) + arr.shape[1:])

        def from_groups(arr):
            return arr.reshape((plane_rows,) + arr.shape[2:])

        activated = jnp.where(unit_used, jnp.square(jax.nn.relu(upward)), 0.0).astype(low)
        grad_top_all = jnp.where(live_all[:, None], all_cot.astype(wide), 0.0)
        grad_down_in = (all_gates * grad_top_all).astype(low)

        def down_term(at, s):
            mid = units // 2
            return dot_rows(
                activated[:, s * mid : (s + 1) * mid],
                lax.dynamic_slice_in_dim(grad_down_in, at * block, block, 1),
            )

        grad_down = scatter_back(ring_reduce(down_term), 1)

        downward = partial_rows(activated, down_full, dot)
        own_out = jnp.where(
            own_live[:, None], middle + gate_units[:, None] * downward, 0.0
        ).astype(low)
        block_out = whole_rows(own_out)
        grad_top = jnp.where(own_live[:, None], own_half(cotangent).astype(wide), 0.0)
        grad_gate_units = jnp.sum(grad_top * downward, axis=1)

        grad_act = dot_cols(grad_down_in, down_full)
        grad_up_in = jnp.where(unit_used, 2.0 * jax.nn.relu(upward) * grad_act, 0.0).astype(low)

        def up_term(at, s):
            mid = block // 2
            return dot_rows(
                lax.dynamic_slice_in_dim(hidden_units, at * block + s * mid, mid, 1), grad_up_in
            )

        grad_up = scatter_back(ring_reduce(up_term), 0)
        route_units_grads = route_units_back(grad_gate_units)
        grad_hidden_units = partial_rows(grad_up_in, up_full, dot_cols) + route_units_grads[0]
        norm_units_grads = norm_units_back(grad_hidden_units)
        grad_middle = grad_top + norm_units_grads[0]
        grad_gate_heads = jnp.sum(grad_middle * projected, axis=1)
        grad_projected = gather_halves((gate_heads[:, None] * grad_middle).astype(low))

        def out_term(at, s):
            mid = head_width // 2
            return dot_rows(
                attended[:, s * mid : (s + 1) * mid],
                lax.dynamic_slice_in_dim(grad_projected, at * block, block, 1),
            )

        grad_out = scatter_back(ring_reduce(out_term), 1)
        grad_attended = to_groups(
            dot_cols(grad_projected, out_full).astype(low).reshape(plane_rows, heads, HD)
        )
        grad_attended = jnp.where(group_used[..., None], grad_attended, jnp.zeros((), low))
        grad_value = jnp.einsum(
            "ghqk,gqhe->gkhe", probs_low, grad_attended, preferred_element_type=wide
        )
        grad_probs = jnp.einsum(
            "gqhe,gkhe->ghqk", grad_attended, value, preferred_element_type=wide
        )
        row_dot = jnp.sum(probs * grad_probs, axis=-1, keepdims=True)
        grad_scores = (probs * (grad_probs - row_dot)).astype(low)
        grad_query = (
            jnp.einsum("ghqk,gkhe->gqhe", grad_scores, keyed, preferred_element_type=wide) * scale
        )
        grad_keyed = (
            jnp.einsum("ghqk,gqhe->gkhe", grad_scores, query, preferred_element_type=wide) * scale
        )
        grad_qkv_in = jnp.stack(
            [
                rotate(grad_query, cosine, -sine_table),
                rotate(grad_keyed, cosine, -sine_table),
                grad_value,
            ],
            axis=2,
        ).astype(low)
        grad_qkv_in = from_groups(grad_qkv_in).reshape(plane_rows, 3 * head_width)

        def qkv_term(at, s):
            mid = block // 2
            return dot_rows(
                lax.dynamic_slice_in_dim(hidden_heads, at * block + s * mid, mid, 1), grad_qkv_in
            )

        qkv_parts = ring_reduce(qkv_term)
        joined = jnp.concatenate(qkv_parts, axis=0)
        grad_qkv = jnp.zeros((owned, 3, local_width), wide)
        for bits in range(SHARE):
            piece = lax.dynamic_slice_in_dim(joined, (share ^ bits) * owned, owned, 0)
            if bits:
                piece = hop(piece.astype(low), bits).astype(wide)
            grad_qkv = lax.dynamic_update_slice_in_dim(
                grad_qkv, piece.reshape(owned, 3, head_width), (share ^ bits) * head_width, 2
            )

        route_heads_grads = route_heads_back(grad_gate_heads)
        grad_hidden_heads = partial_rows(grad_qkv_in, qkv_mat, dot_cols) + route_heads_grads[0]
        norm_heads_grads = norm_heads_back(grad_hidden_heads)
        input_grad = whole_rows((grad_middle + norm_heads_grads[0]).astype(low))

        def total_small(arr):
            arr = arr + cross(arr)
            bits = 1
            while bits < fsdp:
                arr = arr + hop(arr, bits)
                bits *= 2
            return arr

        def total_large(arr):
            steps = [1, "tensor"] + [2**i for i in range(1, fsdp.bit_length() - 1)]
            for bits in steps:
                mid = arr.shape[0] // 2
                me = side if bits == "tensor" else (rank // bits) % 2
                send = lax.dynamic_slice_in_dim(arr, (1 - me) * mid, mid, 0)
                keep = lax.dynamic_slice_in_dim(arr, me * mid, mid, 0)
                arr = keep + (cross(send) if bits == "tensor" else hop(send, bits))
            for bits in reversed(steps):
                me = side if bits == "tensor" else (rank // bits) % 2
                other = cross(arr) if bits == "tensor" else hop(arr, bits)
                arr = jnp.where(
                    me == 0,
                    jnp.concatenate([arr, other], axis=0),
                    jnp.concatenate([other, arr], axis=0),
                )
            return arr

        bucket_ids = jnp.arange(NB, dtype=jnp.int32)[None, :]
        head_counts = jnp.sum(
            jnp.where(own_live[:, None] & (own_heads[:, None] == bucket_ids), 1.0, 0.0), axis=0
        )
        width_counts = jnp.sum(
            jnp.where(own_live[:, None] & (own_widths[:, None] == bucket_ids), 1.0, 0.0), axis=0
        )
        units_small = total_small(
            jnp.concatenate(
                [norm_units_grads[1], route_units_grads[2].reshape(-1), head_counts, width_counts]
            )
        )
        heads_small = total_small(
            jnp.concatenate([norm_heads_grads[1], route_heads_grads[2].reshape(-1)])
        )
        first_units = total_large(route_units_grads[1])
        first_heads = total_large(route_heads_grads[1])
        second_shape = router_second.shape[1:]
        second_size = second_shape[0] * second_shape[1]
        grad_gains = jnp.stack([heads_small[:width], units_small[:width]])
        grad_second = jnp.stack(
            [
                heads_small[width : width + second_size].reshape(second_shape),
                units_small[width : width + second_size].reshape(second_shape),
            ]
        )
        usage = units_small[width + second_size :].reshape(2, NB)
        grad_first = jnp.stack([first_heads, first_units])
        return (
            block_out,
            input_grad,
            grad_gains,
            grad_qkv,
            grad_out,
            grad_up,
            grad_down,
            grad_first,
            grad_second,
            usage,
        )

    return shards


def solution(mesh):
    shards = plane(mesh) if mesh.shape["fsdp"] == 4 * SHARE else general(mesh)
    in_specs = (
        P("fsdp", None),
        P("fsdp"),
        P("fsdp"),
        P("fsdp", None),
        P(),
        P("fsdp", None, "tensor"),
        P("tensor", "fsdp"),
        P("fsdp", "tensor"),
        P("tensor", "fsdp"),
        P(),
        P(),
        P("fsdp", None),
    )
    out_specs = (
        P("fsdp", None),
        P("fsdp", None),
        P(),
        P("fsdp", None, "tensor"),
        P("tensor", "fsdp"),
        P("fsdp", "tensor"),
        P("tensor", "fsdp"),
        P(),
        P(),
        P(),
    )
    return jax.shard_map(
        shards, mesh=mesh, in_specs=in_specs, out_specs=out_specs, check_vma=False
    )
```

```python
from functools import partial

import jax
import jax.numpy as jnp
from jax import lax
from jax.experimental import pallas as pl
from jax.experimental.pallas import tpu as pltpu
from jax.sharding import PartitionSpec as P

HEADS = 16
HD = 128
FF = 8192
NB = 4
SHARE = 4

epsilon = 1e-05
theta_base = 10000.0
highest = lax.Precision.HIGHEST
low = jnp.bfloat16
wide = jnp.float32
MESH = pl.DeviceIdType.MESH


def norm_piece(values_in, gain_row):
    return (
        values_in
        * lax.rsqrt(jnp.mean(values_in * values_in, axis=-1, keepdims=True) + epsilon)
        * gain_row
    )


def route_piece(hidden_in, router_in, router_out, bucket):
    inner = jax.nn.silu(jnp.dot(hidden_in, router_in, precision=highest))
    logits = jnp.dot(inner, router_out, precision=highest)
    probs_all = jax.nn.softmax(logits, axis=-1)
    onehot = (bucket[:, None] == jnp.arange(NB, dtype=jnp.int32)[None, :]).astype(wide)
    return NB * jnp.sum(probs_all * onehot, axis=-1)


def dot(left_in, right_in):
    return jnp.dot(left_in, right_in, preferred_element_type=wide)


def dot_rows(left_in, right_in):
    return lax.dot_general(
        left_in, right_in, (((0,), (0,)), ((), ())), preferred_element_type=wide
    )


def dot_cols(left_in, right_in):
    return lax.dot_general(
        left_in, right_in, (((1,), (1,)), ((), ())), preferred_element_type=wide
    )


def rotate(operand, cosine, sine_table):
    half_dim = operand.shape[-1] // 2
    lead_half = operand[..., :half_dim]
    tail_half = operand[..., half_dim:]
    return jnp.concatenate(
        [lead_half * cosine - tail_half * sine_table, tail_half * cosine + lead_half * sine_table],
        axis=-1,
    )


def layout(length_rows, slot_ids):
    seq_count = length_rows.shape[1]
    order = jnp.arange(seq_count, dtype=jnp.int32)
    seq_ends = jnp.sum(
        jnp.where(order[None, None, :] <= order[None, :, None], length_rows[:, None, :], 0), axis=2
    )
    seq_starts = seq_ends - length_rows
    slots = slot_ids[None, :, None]
    member = (slots >= seq_starts[:, None, :]) & (slots < seq_ends[:, None, :])
    seq_of = jnp.sum(jnp.where(member, jnp.arange(seq_count, dtype=jnp.int32), 0), axis=2)
    live_rows = jnp.any(member, axis=2)
    seq_begin = jnp.sum(jnp.where(member, seq_starts[:, None, :], 0), axis=2)
    segment = jnp.where(live_rows, seq_of, seq_count + slot_ids[None, :])
    position = slot_ids[None, :] - seq_begin
    return segment, position, live_rows


def general(mesh):
    fsdp = mesh.shape["fsdp"]
    ring_size = fsdp // SHARE

    def hop(moved, bits):
        return lax.ppermute(moved, "fsdp", [(i, i ^ bits) for i in range(fsdp)])

    def cross(moved):
        return lax.ppermute(moved, "tensor", [(0, 1), (1, 0)])

    def shards(
        tokens,
        head_bucket,
        ffn_bucket,
        lengths,
        norm_gains,
        qkv_weight,
        out_weight,
        up_weight,
        down_weight,
        router_first,
        router_second,
        cotangent,
    ):
        rows, width = tokens.shape
        half = rows // 2
        rank = lax.axis_index("fsdp")
        side = lax.axis_index("tensor")
        share = rank % SHARE
        place = rank // SHARE
        local_units = up_weight.shape[1]
        units = local_units // SHARE
        local_width = out_weight.shape[0]
        head_width = local_width // SHARE
        heads = head_width // HD
        owned = width // fsdp
        block = width // ring_size

        chain = [None, None]

        def ring(moved, stream):
            if chain[stream] is not None:
                moved, _ = lax.optimization_barrier((moved, chain[stream]))
            got = lax.ppermute(
                moved, "fsdp", [(i, (i + SHARE) % fsdp) for i in range(fsdp)]
            )
            chain[stream] = got
            return got

        def place_at(step):
            return (place - step) % ring_size

        def own_half(arr):
            return lax.dynamic_slice_in_dim(arr, side * half, half, 0)

        def relative(arr):
            return jnp.concatenate(
                [own_half(arr), lax.dynamic_slice_in_dim(arr, (1 - side) * half, half, 0)], axis=0
            )

        def gather_rows(arr):
            other = hop(arr, 2)
            plane = jnp.concatenate([arr[:half], other[:half], arr[half:], other[half:]], axis=0)
            return jnp.concatenate([plane, hop(plane, 1)], axis=0)

        def gather_halves(arr):
            pair = jnp.concatenate([arr, hop(arr, 2)], axis=0)
            plane = jnp.concatenate([pair, cross(pair)], axis=0)
            return jnp.concatenate([plane, hop(plane, 1)], axis=0)

        def reduce_rows(keep, send):
            total = keep + hop(send.astype(low), 1).astype(wide)
            total = total[: 2 * half] + cross(total[2 * half :].astype(low)).astype(wide)
            return total[:half] + hop(total[half:].astype(low), 2).astype(wide)

        def whole_rows(arr):
            other = cross(arr)
            return jnp.where(
                side == 0,
                jnp.concatenate([arr, other], axis=0),
                jnp.concatenate([other, arr], axis=0),
            )

        def spread(pieces_for, axis):
            out = None
            for bits in range(SHARE):
                piece = pieces_for(share ^ bits)
                got = piece if bits == 0 else hop(piece, bits)
                if out is None:
                    dims = list(got.shape)
                    dims[axis] *= SHARE
                    out = jnp.zeros(dims, got.dtype)
                out = lax.dynamic_update_slice_in_dim(
                    out, got, (share ^ bits) * got.shape[axis], axis
                )
            return out

        def ring_gather(own, axis):
            dims = list(own.shape)
            dims[axis] = width
            out = jnp.zeros(dims, own.dtype)
            mid = own.shape[0] // 2
            moving = [own[:mid], own[mid:]]
            for step in range(ring_size):
                if step:
                    moving = [ring(moving[s], s) for s in range(2)]
                base = place_at(step) * block
                for s in range(2):
                    if axis == 0:
                        at = (base + s * mid, 0)
                    else:
                        at = (s * mid, base)
                    out = lax.dynamic_update_slice(out, moving[s], at)
            return out

        def ring_reduce(term):
            moving = [None, None]
            for step in range(1, ring_size):
                for s in range(2):
                    part = term(place_at(step), s)
                    if moving[s] is not None:
                        part = part + moving[s].astype(wide)
                    moving[s] = part.astype(low)
                for s in range(2):
                    moving[s] = ring(moving[s], s)
            return [term(place, s) + moving[s].astype(wide) for s in range(2)]

        def scatter_back(parts, axis):
            joined = jnp.concatenate(parts, axis=0)
            other = 1 - axis
            out_dims = list(joined.shape)
            out_dims[axis] = owned
            stride = out_dims[other]
            out_dims[other] *= SHARE
            out = jnp.zeros(out_dims, wide)
            for bits in range(SHARE):
                piece = lax.dynamic_slice_in_dim(joined, (share ^ bits) * owned, owned, axis)
                if bits:
                    piece = hop(piece.astype(low), bits).astype(wide)
                out = lax.dynamic_update_slice_in_dim(out, piece, (share ^ bits) * stride, other)
            return out

        def qkv_piece(target):
            return lax.dynamic_slice_in_dim(
                qkv_weight, target * head_width, head_width, 2
            ).reshape(owned, 3 * head_width)

        qkv_block = spread(qkv_piece, 0)
        rel_tokens = relative(tokens)
        rel_cot = relative(cotangent)
        ints = relative(jnp.stack([head_bucket, ffn_bucket], axis=1))
        qkv_full = ring_gather(qkv_block, 0)
        all_tokens = gather_rows(rel_tokens)
        buckets = gather_rows(ints)
        pair_lengths = jnp.concatenate([lengths, hop(lengths, 2)], axis=0)
        group_lengths = jnp.concatenate([pair_lengths, hop(pair_lengths, 1)], axis=0)

        out_block = spread(
            lambda t: lax.dynamic_slice_in_dim(out_weight, t * head_width, head_width, 0), 1
        )
        out_full = ring_gather(out_block, 1)
        up_block = spread(lambda t: lax.dynamic_slice_in_dim(up_weight, t * units, units, 1), 0)
        up_full = ring_gather(up_block, 0)
        down_block = spread(
            lambda t: lax.dynamic_slice_in_dim(down_weight, t * units, units, 0), 1
        )
        down_full = ring_gather(down_block, 1)
        all_cot = gather_rows(rel_cot)

        slot_ids = jnp.concatenate(
            [
                side * half + jnp.arange(half, dtype=jnp.int32),
                (1 - side) * half + jnp.arange(half, dtype=jnp.int32),
            ]
        )
        segment, position, live_groups = layout(group_lengths, slot_ids)

        def to_groups(arr):
            tail = arr.shape[1:]
            arr = arr.reshape((2, 2, 2, half) + tail)
            return jnp.swapaxes(arr, 1, 2).reshape((SHARE, rows) + tail)

        def from_groups(arr):
            tail = arr.shape[2:]
            arr = arr.reshape((2, 2, 2, half) + tail)
            return jnp.swapaxes(arr, 1, 2).reshape((8 * half,) + tail)

        live_all = from_groups(live_groups)
        all_heads = buckets[:, 0]
        all_widths = buckets[:, 1]

        own_tokens = rel_tokens[:half].astype(wide)
        own_heads = all_heads[:half]
        own_widths = all_widths[:half]
        own_live = live_all[:half]

        block_in = all_tokens.astype(wide)
        hidden_heads = norm_piece(block_in, norm_gains[0]).astype(low)
        own_normed, norm_heads_back = jax.vjp(norm_piece, own_tokens, norm_gains[0])
        gate_heads, route_heads_back = jax.vjp(
            partial(route_piece, bucket=own_heads),
            own_normed.astype(low).astype(wide),
            router_first[0],
            router_second[0],
        )
        head_ids = side * (local_width // HD) + share * heads + jnp.arange(heads, dtype=jnp.int32)
        head_used = head_ids[None, :] < HEADS // NB * (all_heads[:, None] + 1)
        unit_ids = side * local_units + share * units + jnp.arange(units, dtype=jnp.int32)
        unit_used = unit_ids[None, :] < FF // NB * (all_widths[:, None] + 1)

        half_dim = HD // 2
        frequency = theta_base ** (-2.0 * jnp.arange(half_dim, dtype=wide) / HD)
        angles = position.astype(wide)[:, :, None] * frequency
        cosine = jnp.cos(angles)[:, :, None, :]
        sine_table = jnp.sin(angles)[:, :, None, :]
        qkv_all = to_groups(dot(hidden_heads, qkv_full).reshape(8 * half, 3, heads, HD))
        query = rotate(qkv_all[:, :, 0], cosine, sine_table).astype(low)
        keyed = rotate(qkv_all[:, :, 1], cosine, sine_table).astype(low)
        value = qkv_all[:, :, 2].astype(low)
        group_used = to_groups(head_used)
        same_seq = segment[:, :, None] == segment[:, None, :]
        causal = slot_ids[None, :] <= slot_ids[:, None]
        diagonal = slot_ids[None, :] == slot_ids[:, None]
        key_used = jnp.swapaxes(group_used, 1, 2)
        allowed = (same_seq & causal)[:, None] & (key_used[:, :, None, :] | diagonal)
        scale = HD ** (-0.5)
        scores = jnp.einsum("gqhe,gkhe->ghqk", query, keyed, preferred_element_type=wide) * scale
        scores = jnp.where(allowed, scores, -1e30)
        row_top = jnp.max(scores, axis=-1, keepdims=True)
        weights = jnp.exp(scores - row_top)
        probs = weights / jnp.sum(weights, axis=-1, keepdims=True)
        probs_low = probs.astype(low)
        mixed = jnp.einsum("ghqk,gkhe->gqhe", probs_low, value, preferred_element_type=wide)
        mixed = jnp.where(group_used[..., None], mixed, 0.0).astype(low)
        attended = from_groups(mixed).reshape(8 * half, head_width)

        def partial_rows(left_in, matrix, product):
            keep = product(left_in[: 4 * half], matrix)
            send = product(left_in[4 * half :], matrix)
            return reduce_rows(keep, send)

        projected = partial_rows(attended, out_full, dot)

        middle = own_tokens + gate_heads[:, None] * projected
        normed_units, norm_units_back = jax.vjp(norm_piece, middle, norm_gains[1])
        own_units = normed_units.astype(low)
        hidden_units = gather_halves(own_units)
        gate_units, route_units_back = jax.vjp(
            partial(route_piece, bucket=own_widths),
            own_units.astype(wide),
            router_first[1],
            router_second[1],
        )
        all_gates = gather_halves(gate_units[:, None])
        upward = dot(hidden_units, up_full)
        activated = jnp.where(unit_used, jnp.square(jax.nn.relu(upward)), 0.0).astype(low)
        grad_top_all = jnp.where(live_all[:, None], all_cot.astype(wide), 0.0)
        grad_down_in = (all_gates * grad_top_all).astype(low)

        def down_term(at, s):
            mid = units // 2
            return dot_rows(
                activated[:, s * mid : (s + 1) * mid],
                lax.dynamic_slice_in_dim(grad_down_in, at * block, block, 1),
            )

        grad_down = scatter_back(ring_reduce(down_term), 1)

        downward = partial_rows(activated, down_full, dot)
        own_out = jnp.where(
            own_live[:, None], middle + gate_units[:, None] * downward, 0.0
        ).astype(low)
        block_out = whole_rows(own_out)
        grad_top = jnp.where(own_live[:, None], rel_cot[:half].astype(wide), 0.0)
        grad_gate_units = jnp.sum(grad_top * downward, axis=1)

        grad_act = dot_cols(grad_down_in, down_full)
        grad_up_in = jnp.where(unit_used, 2.0 * jax.nn.relu(upward) * grad_act, 0.0).astype(low)

        def up_term(at, s):
            mid = block // 2
            return dot_rows(
                lax.dynamic_slice_in_dim(hidden_units, at * block + s * mid, mid, 1), grad_up_in
            )

        grad_up = scatter_back(ring_reduce(up_term), 0)
        route_units_grads = route_units_back(grad_gate_units)
        grad_hidden_units = partial_rows(grad_up_in, up_full, dot_cols) + route_units_grads[0]
        norm_units_grads = norm_units_back(grad_hidden_units)
        grad_middle = grad_top + norm_units_grads[0]
        grad_gate_heads = jnp.sum(grad_middle * projected, axis=1)
        grad_projected = gather_halves((gate_heads[:, None] * grad_middle).astype(low))

        def out_term(at, s):
            mid = head_width // 2
            return dot_rows(
                attended[:, s * mid : (s + 1) * mid],
                lax.dynamic_slice_in_dim(grad_projected, at * block, block, 1),
            )

        grad_out = scatter_back(ring_reduce(out_term), 1)
        grad_attended = to_groups(
            dot_cols(grad_projected, out_full).astype(low).reshape(8 * half, heads, HD)
        )
        grad_attended = jnp.where(group_used[..., None], grad_attended, jnp.zeros((), low))
        grad_value = jnp.einsum(
            "ghqk,gqhe->gkhe", probs_low, grad_attended, preferred_element_type=wide
        )
        grad_probs = jnp.einsum(
            "gqhe,gkhe->ghqk", grad_attended, value, preferred_element_type=wide
        )
        row_dot = jnp.sum(probs * grad_probs, axis=-1, keepdims=True)
        grad_scores = (probs * (grad_probs - row_dot)).astype(low)
        grad_query = (
            jnp.einsum("ghqk,gkhe->gqhe", grad_scores, keyed, preferred_element_type=wide) * scale
        )
        grad_keyed = (
            jnp.einsum("ghqk,gqhe->gkhe", grad_scores, query, preferred_element_type=wide) * scale
        )
        grad_qkv_in = jnp.stack(
            [
                rotate(grad_query, cosine, -sine_table),
                rotate(grad_keyed, cosine, -sine_table),
                grad_value,
            ],
            axis=2,
        ).astype(low)
        grad_qkv_in = from_groups(grad_qkv_in).reshape(8 * half, 3 * head_width)

        def qkv_term(at, s):
            mid = block // 2
            return dot_rows(
                lax.dynamic_slice_in_dim(hidden_heads, at * block + s * mid, mid, 1), grad_qkv_in
            )

        qkv_parts = ring_reduce(qkv_term)
        joined = jnp.concatenate(qkv_parts, axis=0)
        grad_qkv = jnp.zeros((owned, 3, local_width), wide)
        for bits in range(SHARE):
            piece = lax.dynamic_slice_in_dim(joined, (share ^ bits) * owned, owned, 0)
            if bits:
                piece = hop(piece.astype(low), bits).astype(wide)
            grad_qkv = lax.dynamic_update_slice_in_dim(
                grad_qkv, piece.reshape(owned, 3, head_width), (share ^ bits) * head_width, 2
            )

        route_heads_grads = route_heads_back(grad_gate_heads)
        grad_hidden_heads = partial_rows(grad_qkv_in, qkv_full, dot_cols) + route_heads_grads[0]
        norm_heads_grads = norm_heads_back(grad_hidden_heads)
        input_grad = whole_rows((grad_middle + norm_heads_grads[0]).astype(low))

        def total_small(arr):
            arr = arr + cross(arr)
            bits = 1
            while bits < fsdp:
                arr = arr + hop(arr, bits)
                bits *= 2
            return arr

        def total_large(arr):
            steps = [1, "tensor"] + [2**i for i in range(1, fsdp.bit_length() - 1)]
            for bits in steps:
                mid = arr.shape[0] // 2
                me = side if bits == "tensor" else (rank // bits) % 2
                send = lax.dynamic_slice_in_dim(arr, (1 - me) * mid, mid, 0)
                keep = lax.dynamic_slice_in_dim(arr, me * mid, mid, 0)
                arr = keep + (cross(send) if bits == "tensor" else hop(send, bits))
            for bits in reversed(steps):
                me = side if bits == "tensor" else (rank // bits) % 2
                other = cross(arr) if bits == "tensor" else hop(arr, bits)
                arr = jnp.where(
                    me == 0,
                    jnp.concatenate([arr, other], axis=0),
                    jnp.concatenate([other, arr], axis=0),
                )
            return arr

        bucket_ids = jnp.arange(NB, dtype=jnp.int32)[None, :]
        head_counts = jnp.sum(
            jnp.where(own_live[:, None] & (own_heads[:, None] == bucket_ids), 1.0, 0.0), axis=0
        )
        width_counts = jnp.sum(
            jnp.where(own_live[:, None] & (own_widths[:, None] == bucket_ids), 1.0, 0.0), axis=0
        )
        units_small = total_small(
            jnp.concatenate(
                [norm_units_grads[1], route_units_grads[2].reshape(-1), head_counts, width_counts]
            )
        )
        heads_small = total_small(
            jnp.concatenate([norm_heads_grads[1], route_heads_grads[2].reshape(-1)])
        )
        first_units = total_large(route_units_grads[1])
        first_heads = total_large(route_heads_grads[1])
        second_shape = router_second.shape[1:]
        second_size = second_shape[0] * second_shape[1]
        grad_gains = jnp.stack([heads_small[:width], units_small[:width]])
        grad_second = jnp.stack(
            [
                heads_small[width : width + second_size].reshape(second_shape),
                units_small[width : width + second_size].reshape(second_shape),
            ]
        )
        usage = units_small[width + second_size :].reshape(2, NB)
        grad_first = jnp.stack([first_heads, first_units])
        return (
            block_out,
            input_grad,
            grad_gains,
            grad_qkv,
            grad_out,
            grad_up,
            grad_down,
            grad_first,
            grad_second,
            usage,
        )

    return shards


def xor_one(index):
    return index + 1 - 2 * (index % 2)


class Plane:
    def __init__(self):
        self.rank = lax.axis_index("fsdp")
        self.side = lax.axis_index("tensor")
        self.share = self.rank % SHARE
        self.place = self.rank // SHARE
        core = xor_one(self.share)
        mid = (self.share + 2) % SHARE
        self.shares = [self.share, core, mid, SHARE - 1 - self.share]
        self.core = {"fsdp": self.place * SHARE + core}
        self.mid = {"fsdp": self.place * SHARE + mid}
        self.both = {"fsdp": self.place * SHARE + self.shares[3]}
        self.members = [None, self.core, self.mid, self.both]
        self.across = {"tensor": 1 - self.side}
        self.near_place = xor_one(self.place)
        self.two_place = (self.place + 2) % 4
        self.far_place = 3 - self.place
        self.near = {"fsdp": self.near_place * SHARE + self.share}
        self.two = {"fsdp": self.two_place * SHARE + self.share}
        self.far = {"fsdp": self.far_place * SHARE + self.share}
        self.inner = (self.place == 1) | (self.place == 2)
        self.outer = (self.place == 0) | (self.place == 3)

    def greet(self):
        barrier = pltpu.get_barrier_semaphore()
        peers = [self.core, self.mid, self.both, self.across, self.near, self.two, self.far]
        for peer in peers:
            pl.semaphore_signal(barrier, inc=1, device_id=peer, device_id_type=MESH)
        pl.semaphore_wait(barrier, len(peers))


class Copies:
    def __init__(self, local_sems, send_sems, recv_sems):
        self.local_sems, self.send_sems, self.recv_sems = local_sems, send_sems, recv_sems
        self.locals, self.sends, self.recvs = 0, 0, 0

    def check(self):
        assert self.locals <= self.local_sems.shape[0]
        assert self.sends <= self.send_sems.shape[0]
        assert self.recvs <= self.recv_sems.shape[0]

    def local(self, src, dst):
        copy = pltpu.make_async_copy(src, dst, self.local_sems.at[self.locals])
        self.locals += 1
        copy.start()
        return copy

    def slot(self):
        self.recvs += 1
        return self.recvs - 1

    def remote(self, src, dst, peer, slot=None):
        if slot is None:
            slot = self.slot()
        copy = pltpu.make_async_remote_copy(
            src_ref=src,
            dst_ref=dst,
            send_sem=self.send_sems.at[self.sends],
            recv_sem=self.recv_sems.at[slot],
            device_id=peer,
            device_id_type=MESH,
        )
        self.sends += 1
        return copy

    def push(self, src, dst, peer):
        copy = self.remote(src, dst, peer)
        copy.start()
        return copy


class ZGather:
    def __init__(self, here, copies, view):
        self.here, self.copies, self.view = here, copies, view

    def start(self):
        here, copies, view = self.here, self.copies, self.view
        own = view(here.place)
        self.two = copies.push(own, own, here.two)
        self.near = copies.push(own, own, here.near)
        slot = copies.slot()
        self.far = copies.remote(own, own, here.far, slot)
        pl.when(here.inner)(self.far.start)
        passing = view(here.two_place)
        self.passed = copies.remote(passing, passing, here.near, slot)
        arriving = view(here.two_place), view(here.near_place), view(here.far_place)
        self.arrivals = [
            pltpu.make_async_remote_copy(
                src_ref=dst,
                dst_ref=dst,
                send_sem=copies.send_sems.at[0],
                recv_sem=copies.recv_sems.at[at],
                device_id=here.two,
                device_id_type=MESH,
            )
            for dst, at in zip(arriving, (slot - 2, slot - 1, slot))
        ]

    def forward(self):
        self.arrivals[0].wait_recv()
        pl.when(self.here.inner)(self.passed.start)

    def arrive(self):
        self.arrivals[1].wait_recv()
        self.arrivals[2].wait_recv()

    def drain(self):
        self.two.wait_send()
        self.near.wait_send()

        @pl.when(self.here.inner)
        def _():
            self.far.wait_send()
            self.passed.wait_send()


def tiles(count, body):
    def step(i, carry):
        body(i)
        return carry

    lax.fori_loop(0, count, step, 0)


def part(index, size):
    return pl.ds(pl.multiple_of(index * size, size), size)


class RowReduce:
    def __init__(self, here, copies, bufs, acks=None):
        self.here, self.copies, self.acks = here, copies, acks
        (self.snd, self.rcv, self.acc, self.out, self.into) = bufs
        self.sent = []

    def begin(self):
        for copy in self.sent:
            copy.wait_send()
        self.sent, self.core = [], []

    def core_send(self, index):
        rows = pl.ds(index * 256, 256)
        self.core.append(self.copies.push(self.snd.at[rows], self.rcv.at[rows], self.here.core))

    def add_core(self, first, count):
        acc, rcv = self.acc, self.rcv

        def body(i):
            at = pl.ds(pl.multiple_of(first + i * 64, 64), 64)
            acc[at, :] = acc[at, :] + rcv[at, :].astype(wide)

        tiles(count // 64, body)

    def round_out(self, first, count, extra=None):
        acc, out, into = self.acc, self.out, self.into

        def body(i):
            at = pl.ds(pl.multiple_of(first + i * 64, 64), 64)
            value = acc[at, :]
            if extra is not None:
                value = value + into[pl.ds(extra, 64), :].astype(wide)
            out[pl.ds(pl.multiple_of(first - 128 + i * 64, 64), 64), :] = value.astype(low)

        tiles(count // 64, body)

    def diagonal(self):
        for copy in self.core:
            copy.wait_recv()
        self.add_core(384, 128)
        self.round_out(384, 128)
        self.diag_x = self.copies.push(self.out.at[256:320], self.into.at[256:320], self.here.across)
        self.diag_y = self.copies.push(self.out.at[320:384], self.into.at[320:384], self.here.mid)
        self.add_core(128, 256)
        self.round_out(128, 64)
        self.round_out(320, 64)
        self.add_core(0, 128)

    def sides(self):
        self.diag_y.wait_recv()
        self.round_out(192, 64, 320)
        self.over_x = self.copies.push(self.out.at[0:128], self.into.at[0:128], self.here.across)
        self.diag_x.wait_recv()
        self.round_out(256, 64, 256)
        self.over_y = self.copies.push(self.out.at[128:256], self.into.at[128:256], self.here.mid)
        self.sent = self.core + [self.diag_x, self.diag_y, self.over_x, self.over_y]

    def arrive(self):
        self.over_x.wait_recv()
        self.over_y.wait_recv()

    def total(self, at, size):
        acc, into = self.acc, self.into
        return (
            acc[pl.ds(at, size), :]
            + into[pl.ds(at, size), :].astype(wide)
            + into[pl.ds(at + 128, size), :].astype(wide)
        )

    def release(self):
        for index, peer in enumerate((self.here.core, self.here.across, self.here.mid)):
            pl.semaphore_signal(
                self.acks.at[index], inc=1, device_id=peer, device_id_type=MESH
            )

    def await_release(self):
        for index in range(3):
            pl.semaphore_wait(self.acks.at[index], 1)

    def drain(self):
        for copy in self.sent:
            copy.wait_send()


class RowGather:
    def __init__(self, here, copies, buf):
        self.here, self.copies, self.buf = here, copies, buf

    def run(self):
        here, copies, buf = self.here, self.copies, self.buf
        own = buf.at[0:128]
        over_x = copies.push(own, buf.at[128:256], here.across)
        over_y = copies.push(own, buf.at[256:384], here.mid)
        cores = [copies.push(own, buf.at[512:640], here.core)]
        over_y.wait_recv()
        diag_x = copies.push(buf.at[256:320], buf.at[384:448], here.across)
        cores.append(copies.push(buf.at[256:384], buf.at[768:896], here.core))
        over_x.wait_recv()
        diag_y = copies.push(buf.at[192:256], buf.at[448:512], here.mid)
        cores.append(copies.push(buf.at[128:256], buf.at[640:768], here.core))
        diag_x.wait_recv()
        diag_y.wait_recv()
        cores.append(copies.push(buf.at[384:512], buf.at[896:1024], here.core))
        self.sent = [over_x, over_y, diag_x, diag_y] + cores
        for copy in cores:
            copy.wait_recv()

    def drain(self):
        for copy in self.sent:
            copy.wait_send()


def nn(left_in, right_in):
    return lax.dot_general(
        left_in, right_in, (((1,), (0,)), ((), ())), preferred_element_type=wide
    )


def nt(left_in, right_in):
    return lax.dot_general(
        left_in, right_in, (((1,), (1,)), ((), ())), preferred_element_type=wide
    )


def tn(left_in, right_in):
    return lax.dot_general(
        left_in, right_in, (((0,), (0,)), ((), ())), preferred_element_type=wide
    )


def forward_kernel(
    tok, col, row, cot, qkvw, outw, upw, downw, gains, gate,
    o_hid, o_qkv, o_probs, o_att, o_proj, o_mid, o_units, o_up, o_col, o_row, o_cot,
    o_wq, o_wo, o_wu, o_wd,
    toks, hid, wq, wo, wu, wd, cols, rows_info, qkvb, probs, att,
    snd, rcv, acc, out_buf, in_buf, proj, mid_buf, units, up,
    local_sems, send_sems, recv_sems,
):
    here = Plane()
    copies = Copies(local_sems, send_sems, recv_sems)
    here.greet()
    rank, share = here.rank, here.share
    owned = 128
    block = owned * SHARE
    head_width = wo.shape[0]
    unit_width = wu.shape[1]
    own_rows = part(rank, owned)

    def spread(src_of, dst):
        got = []
        for d in range(SHARE):
            src = src_of(here.shares[d])
            if d == 0:
                got.append(copies.local(src, dst))
            else:
                got.append(copies.push(src, dst, here.members[d]))
        return got

    def landed(got):
        for i, copy in enumerate(got):
            if i % SHARE:
                copy.wait_recv()
            else:
                copy.wait()

    got_q = []
    for j in range(3):
        got_q += spread(
            lambda t: qkvw.at[j, :, part(t, head_width)],
            wq.at[own_rows, j * head_width : (j + 1) * head_width],
        )
    own_tok = copies.local(tok, toks.at[0:256])
    own_col = copies.local(col, cols.at[0:256])
    own_row = copies.local(row, rows_info.at[0])
    tok_mid = copies.push(tok, toks.at[256:512], here.mid)
    tok_core = copies.push(tok, toks.at[512:768], here.core)
    col_mid = copies.push(col, cols.at[256:512], here.mid)
    col_core = copies.push(col, cols.at[512:768], here.core)
    row_mid = copies.push(row, rows_info.at[1], here.mid)
    row_core = copies.push(row, rows_info.at[2], here.core)
    got_o = spread(lambda t: outw.at[part(t, head_width), :], wo.at[:, own_rows])
    got_u = spread(lambda t: upw.at[:, part(t, unit_width)], wu.at[own_rows, :])
    got_d = spread(lambda t: downw.at[part(t, unit_width), :], wd.at[:, own_rows])
    own_cot = copies.local(cot, o_cot.at[0:256])
    cot_mid = copies.push(cot, o_cot.at[256:512], here.mid)
    cot_core = copies.push(cot, o_cot.at[512:768], here.core)

    def up_view(h):
        return lambda k: wu.at[pl.ds(pl.multiple_of(k * block + h * 256, 256), 256), :]

    def down_view(h):
        return lambda k: wd.at[h * 512 : (h + 1) * 512, part(k, block)]

    z_q = ZGather(here, copies, lambda k: wq.at[part(k, block), :])
    z_o = ZGather(here, copies, lambda k: wo.at[:, part(k, block)])
    z_u = [ZGather(here, copies, up_view(h)) for h in range(2)]
    z_d = [ZGather(here, copies, down_view(h)) for h in range(2)]

    landed(got_q)
    z_q.start()
    landed(got_o)
    z_o.start()

    def normalise(base, count):
        def body(i):
            at = pl.ds(pl.multiple_of(base + i * 64, 64), 64)
            x = toks[at, :].astype(wide)
            r = lax.rsqrt(jnp.mean(x * x, axis=-1, keepdims=True) + epsilon)
            hid[at, :] = (x * r * gains[0:1, :]).astype(low)

        tiles(count, body)

    own_tok.wait()
    normalise(0, 4)
    tok_core.wait_recv()
    normalise(512, 4)
    tok_mid.wait_recv()
    tok_fwd = copies.push(toks.at[256:512], toks.at[768:1024], here.core)
    normalise(256, 4)
    tok_fwd.wait_recv()
    normalise(768, 4)
    own_col.wait()
    own_row.wait()
    col_mid.wait_recv()
    row_mid.wait_recv()
    col_fwd = copies.push(cols.at[256:512], cols.at[768:1024], here.core)
    row_fwd = copies.push(rows_info.at[1], rows_info.at[3], here.core)
    col_core.wait_recv()
    row_core.wait_recv()
    col_fwd.wait_recv()
    row_fwd.wait_recv()
    outs = [copies.local(hid, o_hid), copies.local(cols, o_col), copies.local(rows_info, o_row)]

    z_q.forward()
    landed(got_u)
    z_u[0].start()
    z_q.arrive()
    outs.append(copies.local(wq, o_wq))

    for j in range(3):

        def qkv_tile(i, j=j):
            at = part(i, 512)
            made = nn(hid[at, :], wq[:, j * head_width : (j + 1) * head_width])
            if j < 2:
                cosine = cols[at, 0:HD]
                sine = cols[at, HD : 2 * HD]
                for h in range(head_width // HD):
                    one = made[:, h * HD : (h + 1) * HD]
                    turned = one * cosine + pltpu.roll(one, HD // 2, 1) * sine
                    qkvb[at, j * head_width + h * HD : j * head_width + (h + 1) * HD] = (
                        turned.astype(low)
                    )
            else:
                qkvb[at, j * head_width : (j + 1) * head_width] = made.astype(low)

        tiles(2, qkv_tile)
    outs.append(copies.local(qkvb, o_qkv))

    z_o.forward()
    z_u[1].start()

    first_head = here.side * (SHARE * head_width // HD) + share * (head_width // HD)
    scale = HD ** (-0.5)
    for h in range(head_width // HD):
        head = (first_head + h).astype(wide)

        def attend_group(g, h=h, head=head):
            at = part(g, 256)
            query = qkvb[at, h * HD : (h + 1) * HD]
            keyed = qkvb[at, head_width + h * HD : head_width + (h + 1) * HD]
            value = qkvb[at, 2 * head_width + h * HD : 2 * head_width + (h + 1) * HD]
            seg_q = cols[at, 2 * HD : 2 * HD + 1]
            slot_q = cols[at, 2 * HD + 1 : 2 * HD + 2]
            bucket_q = cols[at, 2 * HD + 2 : 2 * HD + 3]
            info = rows_info[g]
            seg_k, slot_k, bucket_k = info[0:1, :], info[1:2, :], info[2:3, :]
            reach_k = jnp.where(4.0 * bucket_k + 4.0 > head, 1.0, 0.0)
            same = seg_q == seg_k
            causal = slot_k <= slot_q
            usable = (reach_k > 0.5) | (slot_k == slot_q)
            scores = jnp.where(same & causal & usable, nt(query, keyed) * scale, -1e30)
            top = jnp.max(scores, axis=-1, keepdims=True)
            weights = jnp.exp(scores - top)
            p = weights / jnp.sum(weights, axis=-1, keepdims=True)
            probs[part(g * (head_width // HD) + h, 256), :] = p
            mixed = nn(p.astype(low), value)
            att[at, h * HD : (h + 1) * HD] = jnp.where(
                4.0 * bucket_q + 4.0 > head, mixed, 0.0
            ).astype(low)

        tiles(SHARE, attend_group)
    outs.append(copies.local(probs, o_probs))
    outs.append(copies.local(att, o_att))

    z_o.arrive()
    outs.append(copies.local(wo, o_wo))

    reduce = RowReduce(here, copies, (snd, rcv, acc, out_buf, in_buf))
    reduce.begin()
    for i in range(2):

        def send_tile(n, i=i):
            c = part(n, 512)
            snd[i * 256 : (i + 1) * 256, c] = nn(
                att[512 + i * 256 : 512 + (i + 1) * 256, :], wo[:, c]
            ).astype(low)

        tiles(4, send_tile)
        reduce.core_send(i)

    def keep_tile(n):
        c = part(n, 512)
        acc[:, c] = nn(att[0:512, :], wo[:, c])

    tiles(4, keep_tile)

    z_u[0].forward()
    landed(got_d)
    z_d[0].start()
    reduce.diagonal()
    reduce.sides()
    reduce.arrive()

    def middle_tile(i):
        at = pl.multiple_of(i * 64, 64)
        rows64 = pl.ds(at, 64)
        projected = reduce.total(at, 64)
        proj[rows64, :] = projected
        middle = toks[rows64, :].astype(wide) + gate[rows64, 0:1] * projected
        mid_buf[rows64, :] = middle
        r = lax.rsqrt(jnp.mean(middle * middle, axis=-1, keepdims=True) + epsilon)
        units[rows64, :] = (middle * r * gains[1:2, :]).astype(low)

    tiles(2, middle_tile)
    outs.append(copies.local(proj, o_proj))
    outs.append(copies.local(mid_buf, o_mid))
    gather = RowGather(here, copies, units)
    gather.run()
    outs.append(copies.local(units, o_units))

    z_u[1].forward()
    z_d[1].start()
    z_u[0].arrive()
    z_u[1].arrive()
    outs.append(copies.local(wu, o_wu))

    cot_mid.wait_recv()
    cot_fwd = copies.push(o_cot.at[256:512], o_cot.at[768:1024], here.core)

    def up_tile(i):
        at = part(i % 2, 512)
        c = part(i // 2, 512)
        made = nn(units[at, :], wu[:, c])
        up[:, part((i % 2) * 2 + i // 2, 512)] = made

    tiles(unit_width // 256, up_tile)
    outs.append(copies.local(up, o_up))
    z_d[0].forward()
    z_d[1].forward()
    z_d[0].arrive()
    z_d[1].arrive()
    outs.append(copies.local(wd, o_wd))

    for one in [z_q, z_o] + z_u + z_d + [reduce, gather]:
        one.drain()
    own_cot.wait()
    cot_core.wait_recv()
    cot_fwd.wait_recv()
    sent = [cot_mid, cot_core, cot_fwd, tok_mid, tok_core, tok_fwd, col_mid, col_core, row_mid, row_core, col_fwd, row_fwd]
    for got in (got_q, got_o, got_u, got_d):
        sent += [copy for i, copy in enumerate(got) if i % SHARE]
    for copy in sent:
        copy.wait_send()
    for copy in outs:
        copy.wait()
    copies.check()


class ZReduce:
    def __init__(self, here, copies, grads, landing, pieces):
        self.here, self.copies = here, copies
        self.grads, self.landing, self.pieces = grads, landing, pieces
        self.slot_y1, self.slot_y2 = copies.slot(), copies.slot()

    def send_far(self):
        here, copies = self.here, self.copies
        self.y1 = copies.remote(self.grads.at[3], self.landing.at[2], here.far, self.slot_y1)
        self.y2 = copies.remote(self.grads.at[3], self.landing.at[3], here.near, self.slot_y2)
        pl.when(here.inner)(self.y1.start)
        pl.when(here.outer)(self.y2.start)

    def send_near(self):
        self.near = self.copies.push(self.grads.at[1], self.landing.at[0], self.here.near)

    def load(self, index, stage, slot):
        loads = []
        for piece, (rows, first, columns) in self.pieces:
            loads.append(
                self.copies.local(
                    self.landing.at[(index,) + piece],
                    stage.at[slot, 0:rows, first : first + columns],
                )
            )
        return loads

    def add(self, target, stage, slots):
        for piece, (rows, first, columns) in self.pieces:

            def body(i, piece=piece, first=first, columns=columns):
                at = pl.ds(pl.multiple_of(i * 64, 64), 64)
                lead = (target,) + piece[:-2] if len(piece) > 2 else (target,)
                base = piece[-2].start or 0
                here_at = pl.ds(pl.multiple_of(base + i * 64, 64), 64)
                value = self.grads[lead + (here_at, slice(None))].astype(wide)
                for slot in slots:
                    value = value + stage[slot, at, first : first + columns].astype(wide)
                self.grads[lead + (here_at, slice(None))] = value.astype(low)

            tiles(rows // 64, body)

    def send_two(self, stage):
        here, copies = self.here, self.copies

        @pl.when(here.inner)
        def _():
            self.y2.wait_recv()
            for copy in self.load(3, stage, 0):
                copy.wait()
            self.add(2, stage, [0])

        self.two = copies.push(self.grads.at[2], self.landing.at[1], here.two)

    def finish(self, stage):
        here = self.here
        self.near.wait_recv()
        self.two.wait_recv()
        loads = self.load(0, stage, 0) + self.load(1, stage, 1)
        for copy in loads:
            copy.wait()
        self.add(0, stage, [0, 1])

        @pl.when(here.inner)
        def _():
            self.y1.wait_recv()
            for copy in self.load(2, stage, 2):
                copy.wait()
            self.add(0, stage, [2])

    def drain(self):
        here = self.here
        self.near.wait_send()
        self.two.wait_send()
        pl.when(here.inner)(self.y1.wait_send)
        pl.when(here.outer)(self.y2.wait_send)


def norm_back(value, grad, gain):
    r = lax.rsqrt(jnp.mean(value * value, axis=-1, keepdims=True) + epsilon)
    u = gain * grad
    lean = jnp.mean(u * value, axis=-1, keepdims=True)
    return r * u - value * (r * r * r * lean), grad * value * r


def backward_kernel(
    hid_h, qkv_h, probs_h, att_h, proj_h, mid_h, units_h, up_h, col_h, cot_h, tok_h,
    wq_h, wo_h, wu_h, wd_h, gains, gate_heads, gate_all, slope_units, slope_heads,
    o_block, o_input, o_gq, o_go, o_gu, o_gd, o_small, o_gains, l_q, l_o, l_u, l_d,
    hid, wo, wu, wd, cols, qkvb, probs, att, cot, act, gup, acc,
    snd, rcv, out_buf, in_buf, proj, mid_buf, gd, gu, go, gq, stage, top, own_tok, own_out,
    gain_buf, small,
    local_sems, send_sems, recv_sems, acks,
):
    here = Plane()
    copies = Copies(local_sems, send_sems, recv_sems)
    here.greet()
    share, side = here.share, here.side
    owned = 128
    head_width = wo.shape[0]
    unit_width = wu.shape[1]
    heads = head_width // HD
    units, wq, gqkv, gatt = hid, wu, act, gup
    blocks = [here.place, here.near_place, here.two_place, here.far_place]

    in_col = copies.local(col_h, cols)
    in_up = copies.local(up_h, acc)
    in_cot = copies.local(cot_h, cot)
    in_wd = copies.local(wd_h, wd)
    in_units = copies.local(units_h, units)
    in_wu = copies.local(wu_h, wu)
    in_own = [
        copies.local(mid_h, mid_buf),
        copies.local(proj_h, proj),
        copies.local(tok_h.at[0:owned], own_tok),
    ]
    in_wo = copies.local(wo_h, wo)
    in_att = copies.local(att_h, att)
    in_qkv = copies.local(qkv_h, qkvb)
    in_probs = copies.local(probs_h, probs)

    def fact(at, index):
        return cols[at, 2 * HD + index : 2 * HD + index + 1]

    first_unit = (side * SHARE + share) * unit_width

    def used_units(at, base, rows, columns):
        lane = lax.broadcasted_iota(jnp.int32, (rows, columns), 1) + base
        return lane.astype(wide) < (FF // NB) * (fact(at, 3) + 1.0)

    in_col.wait()
    in_up.wait()

    def act_tile(i):
        at = part(i, 128)
        relu = jnp.maximum(acc[part(i % 4, 128), part(i // 4, unit_width)], 0.0)
        used = used_units(at, first_unit, 128, unit_width)
        act[at, :] = jnp.where(used, relu * relu, 0.0).astype(low)

    tiles(8, act_tile)
    in_cot.wait()

    def live_cot(at):
        return jnp.where(fact(at, 4) > 0.5, cot[at, :].astype(wide), 0.0)

    def keep_tile(i):
        at = part(i, 64)
        top[at, :] = live_cot(at).astype(low)

    tiles(owned // 64, keep_tile)

    def scale_tile(i):
        at = part(i, 64)
        cot[at, :] = (gate_all[at, 0:1] * live_cot(at)).astype(low)

    tiles(16, scale_tile)

    every = slice(None)
    z_d = ZReduce(
        here, copies, gd, l_d, [((pl.ds(512 * j, 512), every), (512, 512 * j, 512)) for j in range(2)]
    )
    z_u = ZReduce(here, copies, gu, l_u, [((pl.ds(0, 512), every), (512, 0, unit_width))])
    z_o = ZReduce(here, copies, go, l_o, [((pl.ds(0, head_width), every), (head_width, 0, 512))])
    z_q = ZReduce(
        here,
        copies,
        gq,
        l_q,
        [((j, pl.ds(0, 512), every), (512, head_width * j, head_width)) for j in range(3)],
    )

    def down_block(k):
        def body(i):
            m = part(i, 512)
            gd[k, m, :] = tn(act[:, m], cot[:, part(blocks[k], 512)]).astype(low)

        tiles(unit_width // 512, body)

    down_block(3)
    z_d.send_far()
    down_block(2)
    down_block(1)
    z_d.send_near()
    down_block(0)

    in_wd.wait()

    def gup_tile(i):
        m, n = i % 2, i // 2
        at = part(m, 512)
        c = part(n, 512)
        made = nt(cot[at, :], wd[c, :])
        used = used_units(at, first_unit + n * 512, 512, 512)
        relu = jnp.maximum(acc[:, part(m * 2 + n, 512)], 0.0)
        gup[at, c] = jnp.where(used, 2.0 * relu * made, 0.0).astype(low)

    tiles(4, gup_tile)
    z_d.send_two(stage)

    reduce = RowReduce(here, copies, (snd, rcv, acc, out_buf, in_buf), acks)

    def partial_sums(term):
        reduce.begin()
        for i in range(2):

            def send_tile(n, i=i):
                snd[i * 256 : (i + 1) * 256, part(n, 512)] = term(
                    pl.ds(512 + i * 256, 256), n
                ).astype(low)

            tiles(4, send_tile)
            reduce.core_send(i)

        def own_tile(n):
            acc[:, part(n, 512)] = term(pl.ds(0, 512), n)

        tiles(4, own_tile)

    partial_sums(lambda at, n: nn(act[at, :], wd[:, part(n, 512)]))
    in_units.wait()
    reduce.diagonal()

    def up_block(k):
        def body(i):
            c = part(i, 512)
            gu[k, :, c] = tn(units[:, part(blocks[k], 512)], gup[:, c]).astype(low)

        tiles(unit_width // 512, body)

    up_block(3)
    z_u.send_far()
    reduce.sides()
    up_block(2)
    up_block(1)
    z_u.send_near()
    up_block(0)
    in_hid = copies.local(hid_h, hid)
    for copy in in_own:
        copy.wait()
    reduce.arrive()

    def block_tile(i):
        at = pl.multiple_of(i * 64, 64)
        rows = pl.ds(at, 64)
        downward = reduce.total(at, 64)
        live = fact(rows, 4) > 0.5
        own_out[rows, :] = jnp.where(
            live, mid_buf[rows, :] + gate_all[rows, 0:1] * downward, 0.0
        ).astype(low)
        grad_gate = jnp.sum(top[rows, :].astype(wide) * downward, axis=-1, keepdims=True)
        small[0, rows, :] = jnp.broadcast_to(grad_gate, (64, HD))

    tiles(owned // 64, block_tile)
    reduce.release()
    own_rows = part(side, owned)
    shown = copies.local(own_out, o_block.at[own_rows])
    shown_far = copies.push(own_out, o_block.at[own_rows], here.across)

    in_wu.wait()
    reduce.await_release()
    partial_sums(lambda at, n: nt(gup[at, :], wu[part(n, 512), :]))
    in_wq = copies.local(wq_h, wq.at[:, 0 : 3 * head_width])
    z_u.send_two(stage)
    reduce.diagonal()
    reduce.sides()
    reduce.arrive()
    gproj = cot

    def middle_tile(i):
        at = pl.multiple_of(i * 64, 64)
        rows = pl.ds(at, 64)
        grad = reduce.total(at, 64) + small[0, rows, 0:1] * slope_units[rows, :]
        back, gain_terms = norm_back(mid_buf[rows, :], grad, gains[1:2, :])
        grad_middle = top[rows, :].astype(wide) + back
        mid_buf[rows, :] = grad_middle
        grad_gate = jnp.sum(grad_middle * proj[rows, :], axis=-1, keepdims=True)
        small[1, rows, :] = jnp.broadcast_to(grad_gate, (64, HD))
        gproj[rows, :] = (gate_heads[rows, 0:1] * grad_middle).astype(low)
        gain_buf[1:2, :] = gain_buf[1:2, :] + jnp.sum(gain_terms, axis=0, keepdims=True)

    gain_buf[...] = jnp.zeros_like(gain_buf)
    tiles(owned // 64, middle_tile)
    reduce.release()
    gather = RowGather(here, copies, gproj)
    gather.run()

    in_att.wait()
    in_wo.wait()

    def out_block(k):
        go[k] = tn(att[...], gproj[:, part(blocks[k], 512)]).astype(low)

    out_block(3)
    z_o.send_far()
    out_block(2)
    out_block(1)
    z_o.send_near()
    out_block(0)
    first_head = (side * SHARE + share) * heads

    def gatt_tile(i):
        at = part(i, 512)
        made = nt(gproj[at, :], wo[...]).astype(low)
        for h in range(heads):
            used = 4.0 * fact(at, 2) + 4.0 > (first_head + h).astype(wide)
            gatt[at, h * HD : (h + 1) * HD] = jnp.where(
                used, made[:, h * HD : (h + 1) * HD].astype(wide), 0.0
            ).astype(low)

    tiles(2, gatt_tile)
    z_o.send_two(stage)

    in_qkv.wait()
    in_probs.wait()
    scale = HD ** (-0.5)
    for h in range(heads):

        def back_group(g, h=h):
            at = part(g, 256)
            lanes = [pl.ds(j * head_width + h * HD, HD) for j in range(3)]
            query, keyed, value = (qkvb[at, lane] for lane in lanes)
            grad = gatt[at, h * HD : (h + 1) * HD]
            p = probs[part(g * heads + h, 256), :]
            grad_p = nt(grad, value)
            row_dot = jnp.sum(p * grad_p, axis=-1, keepdims=True)
            grad_s = (p * (grad_p - row_dot)).astype(low)
            cosine = cols[at, 0:HD]
            sine = cols[at, HD : 2 * HD]
            for lane, turned in (
                (lanes[0], nn(grad_s, keyed) * scale),
                (lanes[1], tn(grad_s, query) * scale),
            ):
                gqkv[at, lane] = (
                    turned * cosine - pltpu.roll(turned, HD // 2, 1) * sine
                ).astype(low)
            gqkv[at, lanes[2]] = tn(p.astype(low), grad).astype(low)

        tiles(SHARE, back_group)

    in_hid.wait()

    def qkv_block(k):
        for j in range(3):
            gq[k, j] = tn(
                hid[:, part(blocks[k], 512)], gqkv[:, j * head_width : (j + 1) * head_width]
            ).astype(low)

    qkv_block(3)
    z_q.send_far()
    qkv_block(2)
    qkv_block(1)
    z_q.send_near()
    qkv_block(0)
    z_q.send_two(stage)

    in_wq.wait()
    reduce.await_release()
    partial_sums(lambda at, n: nt(gqkv[at, 0 : 3 * head_width], wq[part(n, 512), 0 : 3 * head_width]))
    reduce.diagonal()
    reduce.sides()
    shown.wait()
    shown_far.wait()
    reduce.arrive()

    def input_tile(i):
        at = pl.multiple_of(i * 64, 64)
        rows = pl.ds(at, 64)
        grad = reduce.total(at, 64) + small[1, rows, 0:1] * slope_heads[rows, :]
        back, gain_terms = norm_back(own_tok[rows, :].astype(wide), grad, gains[0:1, :])
        own_out[rows, :] = (mid_buf[rows, :] + back).astype(low)
        gain_buf[0:1, :] = gain_buf[0:1, :] + jnp.sum(gain_terms, axis=0, keepdims=True)

    tiles(owned // 64, input_tile)
    shown = copies.local(own_out, o_input.at[own_rows])
    shown_far = copies.push(own_out, o_input.at[own_rows], here.across)
    outs = [copies.local(small, o_small), copies.local(gain_buf, o_gains), shown]

    sent = [shown_far]

    def deliver(piece_of, dst):
        for d in range(SHARE):
            src = piece_of(here.shares[d])
            if d == 0:
                outs.append(copies.local(src, dst))
            else:
                sent.append(copies.push(src, dst, here.members[d]))

    z_d.finish(stage)
    deliver(lambda t: gd.at[0, :, part(t, owned)], o_gd.at[part(share, unit_width), :])
    z_u.finish(stage)
    deliver(lambda t: gu.at[0, part(t, owned), :], o_gu.at[:, part(share, unit_width)])
    z_o.finish(stage)
    deliver(lambda t: go.at[0, :, part(t, owned)], o_go.at[part(share, head_width), :])
    z_q.finish(stage)
    for j in range(3):
        deliver(
            lambda t, j=j: gq.at[0, j, part(t, owned), :],
            o_gq.at[j, :, part(share, head_width)],
        )

    for one in (z_d, z_u, z_o, z_q, reduce, gather):
        one.drain()
    for copy in sent:
        copy.wait()
    for copy in outs:
        copy.wait()
    copies.check()


def plane(mesh):
    fsdp = mesh.shape["fsdp"]
    ring_size = fsdp // SHARE

    def hop(moved, bits):
        return lax.ppermute(moved, "fsdp", [(i, i ^ bits) for i in range(fsdp)])

    def cross(moved):
        return lax.ppermute(moved, "tensor", [(0, 1), (1, 0)])

    def shards(
        tokens,
        head_bucket,
        ffn_bucket,
        lengths,
        norm_gains,
        qkv_weight,
        out_weight,
        up_weight,
        down_weight,
        router_first,
        router_second,
        cotangent,
    ):
        rows, width = tokens.shape
        half = rows // 2
        rank = lax.axis_index("fsdp")
        side = lax.axis_index("tensor")
        share = rank % SHARE
        place = rank // SHARE
        local_units = up_weight.shape[1]
        units = local_units // SHARE
        local_width = out_weight.shape[0]
        head_width = local_width // SHARE
        heads = head_width // HD
        owned = width // fsdp
        block = width // ring_size
        plane_rows = SHARE * rows

        def own_half(arr):
            return lax.dynamic_slice_in_dim(arr, side * half, half, 0)

        def relative(arr):
            return jnp.concatenate(
                [own_half(arr), lax.dynamic_slice_in_dim(arr, (1 - side) * half, half, 0)], axis=0
            )

        slot_ids = jnp.concatenate(
            [
                side * half + jnp.arange(half, dtype=jnp.int32),
                (1 - side) * half + jnp.arange(half, dtype=jnp.int32),
            ]
        )
        segment, position, live_rows = (a[0] for a in layout(lengths, slot_ids))
        frequency = theta_base ** (-2.0 * jnp.arange(HD // 2, dtype=wide) / HD)
        angles = position.astype(wide)[:, None] * frequency
        cosine, sine = jnp.cos(angles), jnp.sin(angles)
        rel_heads = relative(head_bucket)
        rel_widths = relative(ffn_bucket)
        facts = jnp.stack(
            [segment, slot_ids, rel_heads, rel_widths, live_rows.astype(jnp.int32)], axis=1
        ).astype(wide)
        col = jnp.concatenate(
            [cosine, cosine, -sine, sine, jnp.pad(facts, ((0, 0), (0, HD - facts.shape[1])))],
            axis=1,
        )
        row = jnp.pad(facts.T, ((0, 8 - facts.shape[1]), (0, 0)))
        rel_tokens = relative(tokens)
        own_tokens = rel_tokens[:half].astype(wide)
        own_heads, own_widths = rel_heads[:half], rel_widths[:half]
        own_live = live_rows[:half]
        own_normed = norm_piece(own_tokens, norm_gains[0])
        gate_heads, route_heads_back = jax.vjp(
            partial(route_piece, bucket=own_heads),
            own_normed.astype(low).astype(wide),
            router_first[0],
            router_second[0],
        )
        f32, b16 = jnp.float32, jnp.bfloat16

        def shape(*dims):
            return jax.ShapeDtypeStruct(dims[1:], dims[0])

        anywhere = pl.BlockSpec(memory_space=pl.ANY)
        vmem = pl.BlockSpec(memory_space=pltpu.VMEM)
        weights = [
            shape(b16, width, 3 * head_width),
            shape(b16, head_width, width),
            shape(b16, width, units),
            shape(b16, units, width),
        ]
        made = [
            shape(b16, plane_rows, width),
            shape(b16, plane_rows, 3 * head_width),
            shape(f32, SHARE * heads * rows, rows),
            shape(b16, plane_rows, head_width),
            shape(f32, half, width),
            shape(f32, half, width),
            shape(b16, plane_rows, width),
            shape(f32, plane_rows // 2, 2 * units),
            shape(f32, plane_rows, 3 * HD),
            shape(f32, SHARE, 8, rows),
            shape(b16, plane_rows, width),
        ]
        (
            hidden_heads,
            qkvb,
            probs,
            attended,
            projected,
            middle,
            hidden_units,
            upward,
            all_col,
            all_row,
            all_cot,
            qkv_full,
            out_full,
            up_full,
            down_full,
        ) = pl.pallas_call(
            forward_kernel,
            out_shape=made + weights,
            in_specs=[anywhere] * 8 + [vmem] * 2,
            out_specs=[anywhere] * 15,
            scratch_shapes=[
                pltpu.VMEM((plane_rows, width), b16),
                pltpu.VMEM((plane_rows, width), b16),
                pltpu.VMEM((width, 3 * head_width), b16),
                pltpu.VMEM((head_width, width), b16),
                pltpu.VMEM((width, units), b16),
                pltpu.VMEM((units, width), b16),
                pltpu.VMEM((plane_rows, 3 * HD), f32),
                pltpu.VMEM((SHARE, 8, rows), f32),
                pltpu.VMEM((plane_rows, 3 * head_width), b16),
                pltpu.VMEM((SHARE * heads * rows, rows), f32),
                pltpu.VMEM((plane_rows, head_width), b16),
                pltpu.VMEM((plane_rows // 2, width), b16),
                pltpu.VMEM((plane_rows // 2, width), b16),
                pltpu.VMEM((plane_rows // 2, width), f32),
                pltpu.VMEM((3 * half, width), b16),
                pltpu.VMEM((3 * half, width), b16),
                pltpu.VMEM((half, width), f32),
                pltpu.VMEM((half, width), f32),
                pltpu.VMEM((plane_rows, width), b16),
                pltpu.VMEM((plane_rows // 2, 2 * units), f32),
                pltpu.SemaphoreType.DMA((40,)),
                pltpu.SemaphoreType.DMA((96,)),
                pltpu.SemaphoreType.DMA((96,)),
            ],
            compiler_params=pltpu.CompilerParams(
                collective_id=0, has_side_effects=True, vmem_limit_bytes=60 * 2**20
            ),
        )(
            rel_tokens,
            col,
            row,
            relative(cotangent),
            jnp.transpose(qkv_weight, (1, 0, 2)),
            out_weight,
            up_weight,
            down_weight,
            norm_gains,
            jnp.broadcast_to(gate_heads[:, None], (half, HD)),
        )

        own_units = hidden_units[:half]
        gate_units, route_units_back = jax.vjp(
            partial(route_piece, bucket=own_widths),
            own_units.astype(wide),
            router_first[1],
            router_second[1],
        )
        all_gates = route_piece(
            hidden_units.astype(wide),
            router_first[1],
            router_second[1],
            bucket=all_col[:, 2 * HD + 3].astype(jnp.int32),
        )
        ones = jnp.ones((half,), wide)
        slope_units = route_units_back(ones)[0]
        slope_heads = route_heads_back(ones)[0]
        (
            block_out,
            input_grad,
            raw_qkv,
            raw_out,
            raw_up,
            raw_down,
            gate_grads,
            gain_sums,
            *_,
        ) = pl.pallas_call(
            backward_kernel,
            out_shape=[
                shape(b16, rows, width),
                shape(b16, rows, width),
                shape(b16, 3, owned, local_width),
                shape(b16, local_width, owned),
                shape(b16, owned, local_units),
                shape(b16, local_units, owned),
                shape(f32, 2, half, HD),
                shape(f32, 8, width),
                shape(b16, 4, 3, block, head_width),
                shape(b16, 4, head_width, block),
                shape(b16, 4, block, units),
                shape(b16, 4, units, block),
            ],
            in_specs=[anywhere] * 15 + [vmem] * 5,
            out_specs=[anywhere] * 12,
            scratch_shapes=[
                pltpu.VMEM((plane_rows, width), b16),
                pltpu.VMEM((head_width, width), b16),
                pltpu.VMEM((width, units), b16),
                pltpu.VMEM((units, width), b16),
                pltpu.VMEM((plane_rows, 3 * HD), f32),
                pltpu.VMEM((plane_rows, 3 * head_width), b16),
                pltpu.VMEM((SHARE * heads * rows, rows), f32),
                pltpu.VMEM((plane_rows, head_width), b16),
                pltpu.VMEM((plane_rows, width), b16),
                pltpu.VMEM((plane_rows, units), b16),
                pltpu.VMEM((plane_rows, units), b16),
                pltpu.VMEM((plane_rows // 2, width), f32),
                pltpu.VMEM((plane_rows // 2, width), b16),
                pltpu.VMEM((plane_rows // 2, width), b16),
                pltpu.VMEM((3 * half, width), b16),
                pltpu.VMEM((3 * half, width), b16),
                pltpu.VMEM((half, width), f32),
                pltpu.VMEM((half, width), f32),
                pltpu.VMEM((4, units, block), b16),
                pltpu.VMEM((4, block, units), b16),
                pltpu.VMEM((4, head_width, block), b16),
                pltpu.VMEM((4, 3, block, head_width), b16),
                pltpu.VMEM((3, block, units), b16),
                pltpu.VMEM((half, width), b16),
                pltpu.VMEM((half, width), b16),
                pltpu.VMEM((half, width), b16),
                pltpu.VMEM((8, width), f32),
                pltpu.VMEM((2, half, HD), f32),
                pltpu.SemaphoreType.DMA((96,)),
                pltpu.SemaphoreType.DMA((96,)),
                pltpu.SemaphoreType.DMA((96,)),
                pltpu.SemaphoreType.REGULAR((3,)),
            ],
            compiler_params=pltpu.CompilerParams(
                collective_id=1, has_side_effects=True, vmem_limit_bytes=63 * 2**20
            ),
        )(
            hidden_heads,
            qkvb,
            probs,
            attended,
            projected,
            middle,
            hidden_units,
            upward,
            all_col,
            all_cot,
            rel_tokens,
            qkv_full,
            out_full,
            up_full,
            down_full,
            norm_gains,
            jnp.broadcast_to(gate_heads[:, None], (half, HD)),
            jnp.broadcast_to(all_gates[:, None], (plane_rows, HD)),
            slope_units,
            slope_heads,
        )
        grad_qkv = jnp.transpose(raw_qkv, (1, 0, 2)).astype(wide)
        grad_out, grad_up, grad_down = (a.astype(wide) for a in (raw_out, raw_up, raw_down))
        route_units_grads = route_units_back(gate_grads[0, :, 0])
        route_heads_grads = route_heads_back(gate_grads[1, :, 0])

        def total_small(arr):
            arr = arr + cross(arr)
            bits = 1
            while bits < fsdp:
                arr = arr + hop(arr, bits)
                bits *= 2
            return arr

        def total_large(arr):
            steps = [1, "tensor"] + [2**i for i in range(1, fsdp.bit_length() - 1)]
            for bits in steps:
                mid = arr.shape[0] // 2
                me = side if bits == "tensor" else (rank // bits) % 2
                send = lax.dynamic_slice_in_dim(arr, (1 - me) * mid, mid, 0)
                keep = lax.dynamic_slice_in_dim(arr, me * mid, mid, 0)
                arr = keep + (cross(send) if bits == "tensor" else hop(send, bits))
            for bits in reversed(steps):
                me = side if bits == "tensor" else (rank // bits) % 2
                other = cross(arr) if bits == "tensor" else hop(arr, bits)
                arr = jnp.where(
                    me == 0,
                    jnp.concatenate([arr, other], axis=0),
                    jnp.concatenate([other, arr], axis=0),
                )
            return arr

        bucket_ids = jnp.arange(NB, dtype=jnp.int32)[None, :]
        head_counts = jnp.sum(
            jnp.where(own_live[:, None] & (own_heads[:, None] == bucket_ids), 1.0, 0.0), axis=0
        )
        width_counts = jnp.sum(
            jnp.where(own_live[:, None] & (own_widths[:, None] == bucket_ids), 1.0, 0.0), axis=0
        )
        units_small = total_small(
            jnp.concatenate(
                [gain_sums[1], route_units_grads[2].reshape(-1), head_counts, width_counts]
            )
        )
        heads_small = total_small(
            jnp.concatenate([gain_sums[0], route_heads_grads[2].reshape(-1)])
        )
        first_units = total_large(route_units_grads[1])
        first_heads = total_large(route_heads_grads[1])
        second_shape = router_second.shape[1:]
        second_size = second_shape[0] * second_shape[1]
        grad_gains = jnp.stack([heads_small[:width], units_small[:width]])
        grad_second = jnp.stack(
            [
                heads_small[width : width + second_size].reshape(second_shape),
                units_small[width : width + second_size].reshape(second_shape),
            ]
        )
        usage = units_small[width + second_size :].reshape(2, NB)
        grad_first = jnp.stack([first_heads, first_units])
        return (
            block_out,
            input_grad,
            grad_gains,
            grad_qkv,
            grad_out,
            grad_up,
            grad_down,
            grad_first,
            grad_second,
            usage,
        )

    return shards


def solution(mesh):
    shards = plane(mesh) if mesh.shape["fsdp"] == 4 * SHARE else general(mesh)
    in_specs = (
        P("fsdp", None),
        P("fsdp"),
        P("fsdp"),
        P("fsdp", None),
        P(),
        P("fsdp", None, "tensor"),
        P("tensor", "fsdp"),
        P("fsdp", "tensor"),
        P("tensor", "fsdp"),
        P(),
        P(),
        P("fsdp", None),
    )
    out_specs = (
        P("fsdp", None),
        P("fsdp", None),
        P(),
        P("fsdp", None, "tensor"),
        P("tensor", "fsdp"),
        P("fsdp", "tensor"),
        P("tensor", "fsdp"),
        P(),
        P(),
        P(),
    )
    return jax.shard_map(
        shards, mesh=mesh, in_specs=in_specs, out_specs=out_specs, check_vma=False
    )
```

```python
from functools import partial

import jax
import jax.numpy as jnp
from jax import lax
from jax.experimental import pallas as pl
from jax.experimental.pallas import tpu as pltpu
from jax.sharding import PartitionSpec as P

HEADS = 16
HD = 128
FF = 8192
NB = 4
SHARE = 4

epsilon = 1e-05
theta_base = 10000.0
highest = lax.Precision.HIGHEST
low = jnp.bfloat16
wide = jnp.float32
MESH = pl.DeviceIdType.MESH


def norm_piece(values_in, gain_row):
    return (
        values_in
        * lax.rsqrt(jnp.mean(values_in * values_in, axis=-1, keepdims=True) + epsilon)
        * gain_row
    )


def route_piece(hidden_in, router_in, router_out, bucket):
    inner = jax.nn.silu(jnp.dot(hidden_in, router_in, precision=highest))
    logits = jnp.dot(inner, router_out, precision=highest)
    probs_all = jax.nn.softmax(logits, axis=-1)
    onehot = (bucket[:, None] == jnp.arange(NB, dtype=jnp.int32)[None, :]).astype(wide)
    return NB * jnp.sum(probs_all * onehot, axis=-1)


def dot(left_in, right_in):
    return jnp.dot(left_in, right_in, preferred_element_type=wide)


def dot_rows(left_in, right_in):
    return lax.dot_general(
        left_in, right_in, (((0,), (0,)), ((), ())), preferred_element_type=wide
    )


def dot_cols(left_in, right_in):
    return lax.dot_general(
        left_in, right_in, (((1,), (1,)), ((), ())), preferred_element_type=wide
    )


def rotate(operand, cosine, sine_table):
    half_dim = operand.shape[-1] // 2
    lead_half = operand[..., :half_dim]
    tail_half = operand[..., half_dim:]
    return jnp.concatenate(
        [lead_half * cosine - tail_half * sine_table, tail_half * cosine + lead_half * sine_table],
        axis=-1,
    )


def layout(length_rows, slot_ids):
    seq_count = length_rows.shape[1]
    order = jnp.arange(seq_count, dtype=jnp.int32)
    seq_ends = jnp.sum(
        jnp.where(order[None, None, :] <= order[None, :, None], length_rows[:, None, :], 0), axis=2
    )
    seq_starts = seq_ends - length_rows
    slots = slot_ids[None, :, None]
    member = (slots >= seq_starts[:, None, :]) & (slots < seq_ends[:, None, :])
    seq_of = jnp.sum(jnp.where(member, jnp.arange(seq_count, dtype=jnp.int32), 0), axis=2)
    live_rows = jnp.any(member, axis=2)
    seq_begin = jnp.sum(jnp.where(member, seq_starts[:, None, :], 0), axis=2)
    segment = jnp.where(live_rows, seq_of, seq_count + slot_ids[None, :])
    position = slot_ids[None, :] - seq_begin
    return segment, position, live_rows


def general(mesh):
    fsdp = mesh.shape["fsdp"]
    ring_size = fsdp // SHARE

    def hop(moved, bits):
        return lax.ppermute(moved, "fsdp", [(i, i ^ bits) for i in range(fsdp)])

    def cross(moved):
        return lax.ppermute(moved, "tensor", [(0, 1), (1, 0)])

    def shards(
        tokens,
        head_bucket,
        ffn_bucket,
        lengths,
        norm_gains,
        qkv_weight,
        out_weight,
        up_weight,
        down_weight,
        router_first,
        router_second,
        cotangent,
    ):
        rows, width = tokens.shape
        half = rows // 2
        rank = lax.axis_index("fsdp")
        side = lax.axis_index("tensor")
        share = rank % SHARE
        place = rank // SHARE
        local_units = up_weight.shape[1]
        units = local_units // SHARE
        local_width = out_weight.shape[0]
        head_width = local_width // SHARE
        heads = head_width // HD
        owned = width // fsdp
        block = width // ring_size

        chain = [None, None]

        def ring(moved, stream):
            if chain[stream] is not None:
                moved, _ = lax.optimization_barrier((moved, chain[stream]))
            got = lax.ppermute(
                moved, "fsdp", [(i, (i + SHARE) % fsdp) for i in range(fsdp)]
            )
            chain[stream] = got
            return got

        def place_at(step):
            return (place - step) % ring_size

        def own_half(arr):
            return lax.dynamic_slice_in_dim(arr, side * half, half, 0)

        def relative(arr):
            return jnp.concatenate(
                [own_half(arr), lax.dynamic_slice_in_dim(arr, (1 - side) * half, half, 0)], axis=0
            )

        def gather_rows(arr):
            other = hop(arr, 2)
            plane = jnp.concatenate([arr[:half], other[:half], arr[half:], other[half:]], axis=0)
            return jnp.concatenate([plane, hop(plane, 1)], axis=0)

        def gather_halves(arr):
            pair = jnp.concatenate([arr, hop(arr, 2)], axis=0)
            plane = jnp.concatenate([pair, cross(pair)], axis=0)
            return jnp.concatenate([plane, hop(plane, 1)], axis=0)

        def reduce_rows(keep, send):
            total = keep + hop(send.astype(low), 1).astype(wide)
            total = total[: 2 * half] + cross(total[2 * half :].astype(low)).astype(wide)
            return total[:half] + hop(total[half:].astype(low), 2).astype(wide)

        def whole_rows(arr):
            other = cross(arr)
            return jnp.where(
                side == 0,
                jnp.concatenate([arr, other], axis=0),
                jnp.concatenate([other, arr], axis=0),
            )

        def spread(pieces_for, axis):
            out = None
            for bits in range(SHARE):
                piece = pieces_for(share ^ bits)
                got = piece if bits == 0 else hop(piece, bits)
                if out is None:
                    dims = list(got.shape)
                    dims[axis] *= SHARE
                    out = jnp.zeros(dims, got.dtype)
                out = lax.dynamic_update_slice_in_dim(
                    out, got, (share ^ bits) * got.shape[axis], axis
                )
            return out

        def ring_gather(own, axis):
            dims = list(own.shape)
            dims[axis] = width
            out = jnp.zeros(dims, own.dtype)
            mid = own.shape[0] // 2
            moving = [own[:mid], own[mid:]]
            for step in range(ring_size):
                if step:
                    moving = [ring(moving[s], s) for s in range(2)]
                base = place_at(step) * block
                for s in range(2):
                    if axis == 0:
                        at = (base + s * mid, 0)
                    else:
                        at = (s * mid, base)
                    out = lax.dynamic_update_slice(out, moving[s], at)
            return out

        def ring_reduce(term):
            moving = [None, None]
            for step in range(1, ring_size):
                for s in range(2):
                    part = term(place_at(step), s)
                    if moving[s] is not None:
                        part = part + moving[s].astype(wide)
                    moving[s] = part.astype(low)
                for s in range(2):
                    moving[s] = ring(moving[s], s)
            return [term(place, s) + moving[s].astype(wide) for s in range(2)]

        def scatter_back(parts, axis):
            joined = jnp.concatenate(parts, axis=0)
            other = 1 - axis
            out_dims = list(joined.shape)
            out_dims[axis] = owned
            stride = out_dims[other]
            out_dims[other] *= SHARE
            out = jnp.zeros(out_dims, wide)
            for bits in range(SHARE):
                piece = lax.dynamic_slice_in_dim(joined, (share ^ bits) * owned, owned, axis)
                if bits:
                    piece = hop(piece.astype(low), bits).astype(wide)
                out = lax.dynamic_update_slice_in_dim(out, piece, (share ^ bits) * stride, other)
            return out

        def qkv_piece(target):
            return lax.dynamic_slice_in_dim(
                qkv_weight, target * head_width, head_width, 2
            ).reshape(owned, 3 * head_width)

        qkv_block = spread(qkv_piece, 0)
        rel_tokens = relative(tokens)
        rel_cot = relative(cotangent)
        ints = relative(jnp.stack([head_bucket, ffn_bucket], axis=1))
        qkv_full = ring_gather(qkv_block, 0)
        all_tokens = gather_rows(rel_tokens)
        buckets = gather_rows(ints)
        pair_lengths = jnp.concatenate([lengths, hop(lengths, 2)], axis=0)
        group_lengths = jnp.concatenate([pair_lengths, hop(pair_lengths, 1)], axis=0)

        out_block = spread(
            lambda t: lax.dynamic_slice_in_dim(out_weight, t * head_width, head_width, 0), 1
        )
        out_full = ring_gather(out_block, 1)
        up_block = spread(lambda t: lax.dynamic_slice_in_dim(up_weight, t * units, units, 1), 0)
        up_full = ring_gather(up_block, 0)
        down_block = spread(
            lambda t: lax.dynamic_slice_in_dim(down_weight, t * units, units, 0), 1
        )
        down_full = ring_gather(down_block, 1)
        all_cot = gather_rows(rel_cot)

        slot_ids = jnp.concatenate(
            [
                side * half + jnp.arange(half, dtype=jnp.int32),
                (1 - side) * half + jnp.arange(half, dtype=jnp.int32),
            ]
        )
        segment, position, live_groups = layout(group_lengths, slot_ids)

        def to_groups(arr):
            tail = arr.shape[1:]
            arr = arr.reshape((2, 2, 2, half) + tail)
            return jnp.swapaxes(arr, 1, 2).reshape((SHARE, rows) + tail)

        def from_groups(arr):
            tail = arr.shape[2:]
            arr = arr.reshape((2, 2, 2, half) + tail)
            return jnp.swapaxes(arr, 1, 2).reshape((8 * half,) + tail)

        live_all = from_groups(live_groups)
        all_heads = buckets[:, 0]
        all_widths = buckets[:, 1]

        own_tokens = rel_tokens[:half].astype(wide)
        own_heads = all_heads[:half]
        own_widths = all_widths[:half]
        own_live = live_all[:half]

        block_in = all_tokens.astype(wide)
        hidden_heads = norm_piece(block_in, norm_gains[0]).astype(low)
        own_normed, norm_heads_back = jax.vjp(norm_piece, own_tokens, norm_gains[0])
        gate_heads, route_heads_back = jax.vjp(
            partial(route_piece, bucket=own_heads),
            own_normed.astype(low).astype(wide),
            router_first[0],
            router_second[0],
        )
        head_ids = side * (local_width // HD) + share * heads + jnp.arange(heads, dtype=jnp.int32)
        head_used = head_ids[None, :] < HEADS // NB * (all_heads[:, None] + 1)
        unit_ids = side * local_units + share * units + jnp.arange(units, dtype=jnp.int32)
        unit_used = unit_ids[None, :] < FF // NB * (all_widths[:, None] + 1)

        half_dim = HD // 2
        frequency = theta_base ** (-2.0 * jnp.arange(half_dim, dtype=wide) / HD)
        angles = position.astype(wide)[:, :, None] * frequency
        cosine = jnp.cos(angles)[:, :, None, :]
        sine_table = jnp.sin(angles)[:, :, None, :]
        qkv_all = to_groups(dot(hidden_heads, qkv_full).reshape(8 * half, 3, heads, HD))
        query = rotate(qkv_all[:, :, 0], cosine, sine_table).astype(low)
        keyed = rotate(qkv_all[:, :, 1], cosine, sine_table).astype(low)
        value = qkv_all[:, :, 2].astype(low)
        group_used = to_groups(head_used)
        same_seq = segment[:, :, None] == segment[:, None, :]
        causal = slot_ids[None, :] <= slot_ids[:, None]
        diagonal = slot_ids[None, :] == slot_ids[:, None]
        key_used = jnp.swapaxes(group_used, 1, 2)
        allowed = (same_seq & causal)[:, None] & (key_used[:, :, None, :] | diagonal)
        scale = HD ** (-0.5)
        scores = jnp.einsum("gqhe,gkhe->ghqk", query, keyed, preferred_element_type=wide) * scale
        scores = jnp.where(allowed, scores, -1e30)
        row_top = jnp.max(scores, axis=-1, keepdims=True)
        weights = jnp.exp(scores - row_top)
        probs = weights / jnp.sum(weights, axis=-1, keepdims=True)
        probs_low = probs.astype(low)
        mixed = jnp.einsum("ghqk,gkhe->gqhe", probs_low, value, preferred_element_type=wide)
        mixed = jnp.where(group_used[..., None], mixed, 0.0).astype(low)
        attended = from_groups(mixed).reshape(8 * half, head_width)

        def partial_rows(left_in, matrix, product):
            keep = product(left_in[: 4 * half], matrix)
            send = product(left_in[4 * half :], matrix)
            return reduce_rows(keep, send)

        projected = partial_rows(attended, out_full, dot)

        middle = own_tokens + gate_heads[:, None] * projected
        normed_units, norm_units_back = jax.vjp(norm_piece, middle, norm_gains[1])
        own_units = normed_units.astype(low)
        hidden_units = gather_halves(own_units)
        gate_units, route_units_back = jax.vjp(
            partial(route_piece, bucket=own_widths),
            own_units.astype(wide),
            router_first[1],
            router_second[1],
        )
        all_gates = gather_halves(gate_units[:, None])
        upward = dot(hidden_units, up_full)
        activated = jnp.where(unit_used, jnp.square(jax.nn.relu(upward)), 0.0).astype(low)
        grad_top_all = jnp.where(live_all[:, None], all_cot.astype(wide), 0.0)
        grad_down_in = (all_gates * grad_top_all).astype(low)

        def down_term(at, s):
            mid = units // 2
            return dot_rows(
                activated[:, s * mid : (s + 1) * mid],
                lax.dynamic_slice_in_dim(grad_down_in, at * block, block, 1),
            )

        grad_down = scatter_back(ring_reduce(down_term), 1)

        downward = partial_rows(activated, down_full, dot)
        own_out = jnp.where(
            own_live[:, None], middle + gate_units[:, None] * downward, 0.0
        ).astype(low)
        block_out = whole_rows(own_out)
        grad_top = jnp.where(own_live[:, None], rel_cot[:half].astype(wide), 0.0)
        grad_gate_units = jnp.sum(grad_top * downward, axis=1)

        grad_act = dot_cols(grad_down_in, down_full)
        grad_up_in = jnp.where(unit_used, 2.0 * jax.nn.relu(upward) * grad_act, 0.0).astype(low)

        def up_term(at, s):
            mid = block // 2
            return dot_rows(
                lax.dynamic_slice_in_dim(hidden_units, at * block + s * mid, mid, 1), grad_up_in
            )

        grad_up = scatter_back(ring_reduce(up_term), 0)
        route_units_grads = route_units_back(grad_gate_units)
        grad_hidden_units = partial_rows(grad_up_in, up_full, dot_cols) + route_units_grads[0]
        norm_units_grads = norm_units_back(grad_hidden_units)
        grad_middle = grad_top + norm_units_grads[0]
        grad_gate_heads = jnp.sum(grad_middle * projected, axis=1)
        grad_projected = gather_halves((gate_heads[:, None] * grad_middle).astype(low))

        def out_term(at, s):
            mid = head_width // 2
            return dot_rows(
                attended[:, s * mid : (s + 1) * mid],
                lax.dynamic_slice_in_dim(grad_projected, at * block, block, 1),
            )

        grad_out = scatter_back(ring_reduce(out_term), 1)
        grad_attended = to_groups(
            dot_cols(grad_projected, out_full).astype(low).reshape(8 * half, heads, HD)
        )
        grad_attended = jnp.where(group_used[..., None], grad_attended, jnp.zeros((), low))
        grad_value = jnp.einsum(
            "ghqk,gqhe->gkhe", probs_low, grad_attended, preferred_element_type=wide
        )
        grad_probs = jnp.einsum(
            "gqhe,gkhe->ghqk", grad_attended, value, preferred_element_type=wide
        )
        row_dot = jnp.sum(probs * grad_probs, axis=-1, keepdims=True)
        grad_scores = (probs * (grad_probs - row_dot)).astype(low)
        grad_query = (
            jnp.einsum("ghqk,gkhe->gqhe", grad_scores, keyed, preferred_element_type=wide) * scale
        )
        grad_keyed = (
            jnp.einsum("ghqk,gqhe->gkhe", grad_scores, query, preferred_element_type=wide) * scale
        )
        grad_qkv_in = jnp.stack(
            [
                rotate(grad_query, cosine, -sine_table),
                rotate(grad_keyed, cosine, -sine_table),
                grad_value,
            ],
            axis=2,
        ).astype(low)
        grad_qkv_in = from_groups(grad_qkv_in).reshape(8 * half, 3 * head_width)

        def qkv_term(at, s):
            mid = block // 2
            return dot_rows(
                lax.dynamic_slice_in_dim(hidden_heads, at * block + s * mid, mid, 1), grad_qkv_in
            )

        qkv_parts = ring_reduce(qkv_term)
        joined = jnp.concatenate(qkv_parts, axis=0)
        grad_qkv = jnp.zeros((owned, 3, local_width), wide)
        for bits in range(SHARE):
            piece = lax.dynamic_slice_in_dim(joined, (share ^ bits) * owned, owned, 0)
            if bits:
                piece = hop(piece.astype(low), bits).astype(wide)
            grad_qkv = lax.dynamic_update_slice_in_dim(
                grad_qkv, piece.reshape(owned, 3, head_width), (share ^ bits) * head_width, 2
            )

        route_heads_grads = route_heads_back(grad_gate_heads)
        grad_hidden_heads = partial_rows(grad_qkv_in, qkv_full, dot_cols) + route_heads_grads[0]
        norm_heads_grads = norm_heads_back(grad_hidden_heads)
        input_grad = whole_rows((grad_middle + norm_heads_grads[0]).astype(low))

        def total_small(arr):
            arr = arr + cross(arr)
            bits = 1
            while bits < fsdp:
                arr = arr + hop(arr, bits)
                bits *= 2
            return arr

        def total_large(arr):
            steps = [1, "tensor"] + [2**i for i in range(1, fsdp.bit_length() - 1)]
            for bits in steps:
                mid = arr.shape[0] // 2
                me = side if bits == "tensor" else (rank // bits) % 2
                send = lax.dynamic_slice_in_dim(arr, (1 - me) * mid, mid, 0)
                keep = lax.dynamic_slice_in_dim(arr, me * mid, mid, 0)
                arr = keep + (cross(send) if bits == "tensor" else hop(send, bits))
            for bits in reversed(steps):
                me = side if bits == "tensor" else (rank // bits) % 2
                other = cross(arr) if bits == "tensor" else hop(arr, bits)
                arr = jnp.where(
                    me == 0,
                    jnp.concatenate([arr, other], axis=0),
                    jnp.concatenate([other, arr], axis=0),
                )
            return arr

        bucket_ids = jnp.arange(NB, dtype=jnp.int32)[None, :]
        head_counts = jnp.sum(
            jnp.where(own_live[:, None] & (own_heads[:, None] == bucket_ids), 1.0, 0.0), axis=0
        )
        width_counts = jnp.sum(
            jnp.where(own_live[:, None] & (own_widths[:, None] == bucket_ids), 1.0, 0.0), axis=0
        )
        units_small = total_small(
            jnp.concatenate(
                [norm_units_grads[1], route_units_grads[2].reshape(-1), head_counts, width_counts]
            )
        )
        heads_small = total_small(
            jnp.concatenate([norm_heads_grads[1], route_heads_grads[2].reshape(-1)])
        )
        first_units = total_large(route_units_grads[1])
        first_heads = total_large(route_heads_grads[1])
        second_shape = router_second.shape[1:]
        second_size = second_shape[0] * second_shape[1]
        grad_gains = jnp.stack([heads_small[:width], units_small[:width]])
        grad_second = jnp.stack(
            [
                heads_small[width : width + second_size].reshape(second_shape),
                units_small[width : width + second_size].reshape(second_shape),
            ]
        )
        usage = units_small[width + second_size :].reshape(2, NB)
        grad_first = jnp.stack([first_heads, first_units])
        return (
            block_out,
            input_grad,
            grad_gains,
            grad_qkv,
            grad_out,
            grad_up,
            grad_down,
            grad_first,
            grad_second,
            usage,
        )

    return shards


def xor_one(index):
    return index + 1 - 2 * (index % 2)


class Plane:
    def __init__(self):
        self.rank = lax.axis_index("fsdp")
        self.side = lax.axis_index("tensor")
        self.share = self.rank % SHARE
        self.place = self.rank // SHARE
        core = xor_one(self.share)
        mid = (self.share + 2) % SHARE
        self.shares = [self.share, core, mid, SHARE - 1 - self.share]
        self.core = {"fsdp": self.place * SHARE + core}
        self.mid = {"fsdp": self.place * SHARE + mid}
        self.both = {"fsdp": self.place * SHARE + self.shares[3]}
        self.members = [None, self.core, self.mid, self.both]
        self.across = {"tensor": 1 - self.side}
        self.near_place = xor_one(self.place)
        self.two_place = (self.place + 2) % 4
        self.far_place = 3 - self.place
        self.near = {"fsdp": self.near_place * SHARE + self.share}
        self.two = {"fsdp": self.two_place * SHARE + self.share}
        self.far = {"fsdp": self.far_place * SHARE + self.share}
        self.inner = (self.place == 1) | (self.place == 2)
        self.outer = (self.place == 0) | (self.place == 3)

    def greet(self):
        barrier = pltpu.get_barrier_semaphore()
        peers = [self.core, self.mid, self.both, self.across, self.near, self.two, self.far]
        for peer in peers:
            pl.semaphore_signal(barrier, inc=1, device_id=peer, device_id_type=MESH)
        pl.semaphore_wait(barrier, len(peers))


class Copies:
    def __init__(self, local_sems, send_sems, recv_sems):
        self.local_sems, self.send_sems, self.recv_sems = local_sems, send_sems, recv_sems
        self.locals, self.sends, self.recvs = 0, 0, 0

    def check(self):
        assert self.locals <= self.local_sems.shape[0]
        assert self.sends <= self.send_sems.shape[0]
        assert self.recvs <= self.recv_sems.shape[0]

    def local(self, src, dst):
        copy = pltpu.make_async_copy(src, dst, self.local_sems.at[self.locals])
        self.locals += 1
        copy.start()
        return copy

    def slot(self):
        self.recvs += 1
        return self.recvs - 1

    def remote(self, src, dst, peer, slot=None):
        if slot is None:
            slot = self.slot()
        copy = pltpu.make_async_remote_copy(
            src_ref=src,
            dst_ref=dst,
            send_sem=self.send_sems.at[self.sends],
            recv_sem=self.recv_sems.at[slot],
            device_id=peer,
            device_id_type=MESH,
        )
        self.sends += 1
        return copy

    def push(self, src, dst, peer):
        copy = self.remote(src, dst, peer)
        copy.start()
        return copy


class ZGather:
    def __init__(self, here, copies, view):
        self.here, self.copies, self.view, self.drained = here, copies, view, False

    def start(self):
        here, copies, view = self.here, self.copies, self.view
        own = view(here.place)
        self.two = copies.push(own, own, here.two)
        self.near = copies.push(own, own, here.near)
        slot = copies.slot()
        self.far = copies.remote(own, own, here.far, slot)
        pl.when(here.inner)(self.far.start)
        passing = view(here.two_place)
        self.passed = copies.remote(passing, passing, here.near, slot)
        arriving = view(here.two_place), view(here.near_place), view(here.far_place)
        self.arrivals = [
            pltpu.make_async_remote_copy(
                src_ref=dst,
                dst_ref=dst,
                send_sem=copies.send_sems.at[0],
                recv_sem=copies.recv_sems.at[at],
                device_id=here.two,
                device_id_type=MESH,
            )
            for dst, at in zip(arriving, (slot - 2, slot - 1, slot))
        ]

    def forward(self):
        self.arrivals[0].wait_recv()
        pl.when(self.here.inner)(self.passed.start)

    def arrive(self):
        self.arrivals[1].wait_recv()
        self.arrivals[2].wait_recv()

    def drain(self):
        if self.drained:
            return
        self.drained = True
        self.two.wait_send()
        self.near.wait_send()

        @pl.when(self.here.inner)
        def _():
            self.far.wait_send()
            self.passed.wait_send()


def tiles(count, body):
    def step(i, carry):
        body(i)
        return carry

    lax.fori_loop(0, count, step, 0)


def part(index, size):
    return pl.ds(pl.multiple_of(index * size, size), size)


class RowReduce:
    def __init__(self, here, copies, bufs, acks=None):
        self.here, self.copies, self.acks = here, copies, acks
        (self.snd, self.rcv, self.acc, self.out, self.into) = bufs
        self.sent = []

    def begin(self):
        for copy in self.sent:
            copy.wait_send()
        self.sent, self.core = [], []

    def core_send(self, index):
        rows = pl.ds(index * 256, 256)
        self.core.append(self.copies.push(self.snd.at[rows], self.rcv.at[rows], self.here.core))

    def add_core(self, first, count):
        acc, rcv = self.acc, self.rcv

        def body(i):
            at = pl.ds(pl.multiple_of(first + i * 64, 64), 64)
            acc[at, :] = acc[at, :] + rcv[at, :].astype(wide)

        tiles(count // 64, body)

    def round_out(self, first, count, extra=None):
        acc, out, into = self.acc, self.out, self.into

        def body(i):
            at = pl.ds(pl.multiple_of(first + i * 64, 64), 64)
            value = acc[at, :]
            if extra is not None:
                value = value + into[pl.ds(extra, 64), :].astype(wide)
            out[pl.ds(pl.multiple_of(first - 128 + i * 64, 64), 64), :] = value.astype(low)

        tiles(count // 64, body)

    def diagonal(self):
        for copy in self.core:
            copy.wait_recv()
        self.add_core(384, 128)
        self.round_out(384, 128)
        self.diag_x = self.copies.push(self.out.at[256:320], self.into.at[256:320], self.here.across)
        self.diag_y = self.copies.push(self.out.at[320:384], self.into.at[320:384], self.here.mid)
        self.add_core(128, 256)
        self.round_out(128, 64)
        self.round_out(320, 64)
        self.add_core(0, 128)

    def sides(self):
        self.diag_y.wait_recv()
        self.round_out(192, 64, 320)
        self.over_x = self.copies.push(self.out.at[0:128], self.into.at[0:128], self.here.across)
        self.diag_x.wait_recv()
        self.round_out(256, 64, 256)
        self.over_y = self.copies.push(self.out.at[128:256], self.into.at[128:256], self.here.mid)
        self.sent = self.core + [self.diag_x, self.diag_y, self.over_x, self.over_y]

    def arrive(self):
        self.over_x.wait_recv()
        self.over_y.wait_recv()

    def total(self, at, size):
        acc, into = self.acc, self.into
        return (
            acc[pl.ds(at, size), :]
            + into[pl.ds(at, size), :].astype(wide)
            + into[pl.ds(at + 128, size), :].astype(wide)
        )

    def release(self):
        for index, peer in enumerate((self.here.core, self.here.across, self.here.mid)):
            pl.semaphore_signal(
                self.acks.at[index], inc=1, device_id=peer, device_id_type=MESH
            )

    def await_release(self):
        for index in range(3):
            pl.semaphore_wait(self.acks.at[index], 1)

    def drain(self):
        for copy in self.sent:
            copy.wait_send()


class RowGather:
    def __init__(self, here, copies, view, fixed=False):
        self.here, self.copies, self.view, self.fixed = here, copies, view, fixed
        self.sent, self.drained = [], False

    def start(self):
        here = self.here
        self.over_x = self.pair(0, 1, here.across)
        self.over_y = self.pair(0, 2, here.mid)
        self.cores = [self.pair(0, 4, here.core)]

    def pair(self, source, target, peer, half=None):
        src = self.view(source, half)
        dst = src if self.fixed else self.view(target, half)
        copy = self.copies.push(src, dst, peer)
        self.sent.append(copy)
        return copy

    def forward(self):
        here = self.here
        self.over_y.wait_recv()
        self.diag_x = self.pair(2, 3, here.across, 0)
        self.cores.append(self.pair(2, 6, here.core))
        self.over_x.wait_recv()
        self.diag_y = self.pair(1, 3, here.mid, 1)
        self.cores.append(self.pair(1, 5, here.core))

    def finish(self):
        self.diag_x.wait_recv()
        self.diag_y.wait_recv()
        self.cores.append(self.pair(3, 7, self.here.core))
        for copy in self.cores:
            copy.wait_recv()

    def drain(self):
        if not self.drained:
            for copy in self.sent:
                copy.wait_send()
        self.drained = True


def nn(left_in, right_in):
    return lax.dot_general(
        left_in, right_in, (((1,), (0,)), ((), ())), preferred_element_type=wide
    )


def nt(left_in, right_in):
    return lax.dot_general(
        left_in, right_in, (((1,), (1,)), ((), ())), preferred_element_type=wide
    )


def tn(left_in, right_in):
    return lax.dot_general(
        left_in, right_in, (((0,), (0,)), ((), ())), preferred_element_type=wide
    )


class ZReduce:
    def __init__(self, here, copies, base, spot, rows, columns, landing):
        self.here, self.copies, self.base, self.spot = here, copies, base, spot
        self.rows, self.columns, self.landing = rows, columns, landing
        self.slot_y1, self.slot_y2 = copies.slot(), copies.slot()

    def view(self, k, rows=None, columns=None):
        r, c = self.spot(k)
        return self.base.at[
            pl.ds(r, self.rows) if rows is None else rows(r),
            pl.ds(c, self.columns) if columns is None else columns(c),
        ]

    def send_far(self):
        here, copies = self.here, self.copies
        self.y1 = copies.remote(self.view(3), self.landing.at[2], here.far, self.slot_y1)
        self.y2 = copies.remote(self.view(3), self.landing.at[3], here.near, self.slot_y2)
        pl.when(here.inner)(self.y1.start)
        pl.when(here.outer)(self.y2.start)

    def send_near(self):
        self.near = self.copies.push(self.view(1), self.landing.at[0], self.here.near)

    def load(self, index, stage, slot):
        size = min(self.rows, 512)
        return [
            self.copies.local(
                self.landing.at[index, pl.ds(n * size, size), :],
                stage.at[slot, pl.ds(0, size), pl.ds(n * self.columns, self.columns)],
            )
            for n in range(self.rows // size)
        ]

    def add(self, target, stage, slots):
        size = min(self.rows, 512)
        r, c = self.spot(target)
        for n in range(self.rows // size):

            def body(i, n=n):
                at = pl.ds(pl.multiple_of(i * 64, 64), 64)
                mine = pl.ds(pl.multiple_of(r + n * size + i * 64, 64), 64)
                lanes = pl.ds(c, self.columns)
                value = self.base[mine, lanes].astype(wide)
                for slot in slots:
                    value = value + stage[
                        slot, at, pl.ds(n * self.columns, self.columns)
                    ].astype(wide)
                self.base[mine, lanes] = value.astype(low)

            tiles(size // 64, body)

    def send_two(self, stage):
        here, copies = self.here, self.copies

        @pl.when(here.inner)
        def _():
            self.y2.wait_recv()
            for copy in self.load(3, stage, 0):
                copy.wait()
            self.add(2, stage, [0])

        self.two = copies.push(self.view(2), self.landing.at[1], here.two)

    def finish(self, stage):
        here = self.here
        self.near.wait_recv()
        self.two.wait_recv()
        loads = self.load(0, stage, 0) + self.load(1, stage, 1)
        for copy in loads:
            copy.wait()
        self.add(0, stage, [0, 1])

        @pl.when(here.inner)
        def _():
            self.y1.wait_recv()
            for copy in self.load(2, stage, 0):
                copy.wait()
            self.add(0, stage, [0])

    def drain(self):
        here = self.here
        self.near.wait_send()
        self.two.wait_send()
        pl.when(here.inner)(self.y1.wait_send)
        pl.when(here.outer)(self.y2.wait_send)


def norm_back(value, grad, gain):
    r = lax.rsqrt(jnp.mean(value * value, axis=-1, keepdims=True) + epsilon)
    u = gain * grad
    lean = jnp.mean(u * value, axis=-1, keepdims=True)
    return r * u - value * (r * r * r * lean), grad * value * r


def exact(left_in, right_in, contract):
    return lax.dot_general(
        left_in, right_in, (contract, ((), ())), precision=highest, preferred_element_type=wide
    )


def layer_kernel(
    tok, col, row, cot_in, qkvw, outw, upw, downw, first, gains, second,
    o_block, o_input, o_gq, o_go, o_gu, o_gd, o_first, o_pack, s_hid, s_wq, l_q, l_o, l_u, l_d,
    toks, hid, units, cot, early, wo, wu, wd, cols, rows_info, qkvb, probs, att, acc,
    snd, rcv, out_buf, in_buf, proj, mid_buf, go, stage, top, own_tok, own_out,
    first_buf, slope, gates, r_gate, r_inner, r_slope, r_dpre, r_rows, zpart, zland, gain_buf,
    pack, pack_plane, pack_side, pack_ring,
    local_sems, send_sems, recv_sems, acks,
):
    here = Plane()
    copies = Copies(local_sems, send_sems, recv_sems)
    here.greet()
    rank, share, side = here.rank, here.share, here.side
    owned = 128
    block = owned * SHARE
    head_width = wo.shape[0]
    unit_width = wu.shape[1]
    heads = head_width // HD
    own_rows = part(rank, owned)
    wq = early.at[:, 0 : 3 * head_width]
    act, gup = early.at[0:1024], early.at[1024:2048]
    sent, outs, done = [], [], []

    def to_peer(src, dst, peer):
        copy = copies.push(src, dst, peer)
        sent.append(copy)
        return copy

    def spread(src_of, dst):
        return [
            copies.local(src_of(here.shares[d]), dst)
            if d == 0
            else to_peer(src_of(here.shares[d]), dst, here.members[d])
            for d in range(SHARE)
        ]

    def landed(got):
        for i, copy in enumerate(got):
            if i % SHARE:
                copy.wait_recv()
            else:
                copy.wait()

    got_q = []
    for j in range(3):
        got_q += spread(
            lambda t: qkvw.at[j, :, part(t, head_width)],
            wq.at[own_rows, j * head_width : (j + 1) * head_width],
        )
    mine, other = part(side, owned), part(1 - side, owned)

    class Halves:
        def __init__(self, src, dst):
            self.dst = dst
            pairs = ((mine, 0), (other, owned))
            self.own = [copies.local(src(rows), dst(at)) for rows, at in pairs]
            self.mid = [to_peer(src(rows), dst(at + 256), here.mid) for rows, at in pairs]
            self.core = [to_peer(src(rows), dst(at + 512), here.core) for rows, at in pairs]

        def pass_on(self):
            for copy in self.mid:
                copy.wait_recv()
            self.last = [
                to_peer(self.dst(at), self.dst(at + 512), here.core) for at in (256, 384)
            ]

    tok_in = Halves(lambda r: tok.at[r, :], lambda at: toks.at[at : at + owned])
    col_in = Halves(lambda r: col.at[r, :], lambda at: cols.at[at : at + owned])
    row_in = Halves(
        lambda r: row.at[:, r],
        lambda at: rows_info.at[at // 256, :, at % 256 : at % 256 + owned],
    )
    got_o = spread(lambda t: outw.at[part(t, head_width), :], wo.at[:, own_rows])
    got_u = spread(lambda t: upw.at[:, part(t, unit_width)], wu.at[own_rows, :])
    got_d = spread(lambda t: downw.at[part(t, unit_width), :], wd.at[:, own_rows])
    cot_rows = Halves(lambda r: cot_in.at[r, :], lambda at: cot.at[at : at + owned])
    in_first = copies.local(first.at[0], first_buf)
    in_tok = copies.local(tok.at[mine, :], own_tok)

    g_q = ZGather(here, copies, lambda k: wq.at[part(k, block), :])
    g_o = ZGather(here, copies, lambda k: wo.at[:, part(k, block)])
    g_u = [
        ZGather(
            here,
            copies,
            lambda k, h=h: wu.at[pl.ds(pl.multiple_of(k * block + h * 256, 256), 256), :],
        )
        for h in range(2)
    ]
    g_d = [
        ZGather(here, copies, lambda k, h=h: wd.at[h * 512 : (h + 1) * 512, part(k, block)])
        for h in range(2)
    ]

    def fact(at, index):
        return cols[at, 2 * HD + index : 2 * HD + index + 1]

    landed(got_q)
    g_q.start()
    landed(got_o)
    g_o.start()

    def normalise(base):
        def body(i):
            at = pl.ds(pl.multiple_of(base + i * 64, 64), 64)
            x = toks[at, :].astype(wide)
            r = lax.rsqrt(jnp.mean(x * x, axis=-1, keepdims=True) + epsilon)
            hid[at, :] = (x * r * gains[0:1, :]).astype(low)

        tiles(4, body)

    def wait_all(waits):
        for wait in waits:
            wait()

    wait_all([c.wait for c in tok_in.own])
    normalise(0)
    wait_all([c.wait_recv for c in tok_in.core])
    normalise(512)
    tok_in.pass_on()
    normalise(256)
    wait_all([c.wait_recv for c in tok_in.last])
    normalise(768)
    wait_all([c.wait for c in col_in.own + row_in.own])
    col_in.pass_on()
    row_in.pass_on()
    wait_all([c.wait_recv for c in col_in.core + row_in.core + col_in.last + row_in.last])
    save_hid = copies.local(hid, s_hid)

    def route(index, rows_of):
        made = exact(rows_of[0:owned, :].astype(wide), first_buf[...], ((1,), (0,)))
        sig = 1.0 / (1.0 + jnp.exp(-made))
        inner = made * sig
        logits = exact(inner, second[index], ((1,), (0,)))
        lane = lax.broadcasted_iota(jnp.int32, (owned, HD), 1)
        logits = jnp.where(lane < NB, logits, -1e30)
        raised = jnp.where(
            lane < NB, jnp.exp(logits - jnp.max(logits, axis=-1, keepdims=True)), 0.0
        )
        shares = raised / jnp.sum(raised, axis=-1, keepdims=True)
        hot = jnp.where(lane.astype(wide) == fact(pl.ds(0, owned), 2 + index), 1.0, 0.0)
        gate = NB * jnp.sum(shares * hot, axis=-1, keepdims=True)
        lean = gate * (hot - shares)
        r_gate[index] = jnp.broadcast_to(gate, (owned, HD))
        r_inner[index] = inner
        r_slope[index] = lean
        r_dpre[index] = exact(lean, second[index], ((1,), (1,))) * (
            sig * (1.0 + made * (1.0 - sig))
        )

    def slope_tiles(index):
        def body(i):
            c = part(i, 256)
            slope[:, c] = exact(r_dpre[index], first_buf[c, :], ((1,), (1,)))

        tiles(8, body)

    in_first.wait()
    route(0, hid)
    in_first = copies.local(first.at[1], first_buf)

    g_q.forward()
    landed(got_u)
    g_u[0].start()
    g_q.arrive()
    save_wq = copies.local(wq, s_wq)

    for j in range(3):

        def qkv_tile(i, j=j):
            at = part(i, 512)
            made = nn(hid[at, :], wq[:, j * head_width : (j + 1) * head_width])
            if j < 2:
                cosine = cols[at, 0:HD]
                sine = cols[at, HD : 2 * HD]
                for h in range(heads):
                    one = made[:, h * HD : (h + 1) * HD]
                    turned = one * cosine + pltpu.roll(one, HD // 2, 1) * sine
                    qkvb[at, j * head_width + h * HD : j * head_width + (h + 1) * HD] = (
                        turned.astype(low)
                    )
            else:
                qkvb[at, j * head_width : (j + 1) * head_width] = made.astype(low)

        tiles(2, qkv_tile)

    g_o.forward()
    g_u[1].start()

    first_head = (side * SHARE + share) * heads
    scale = HD ** (-0.5)
    for h in range(heads):
        head = (first_head + h).astype(wide)

        def attend_group(g, h=h, head=head):
            at = part(g, 256)
            query, keyed, value = (
                qkvb[at, pl.ds(j * head_width + h * HD, HD)] for j in range(3)
            )
            info = rows_info[g]
            seg_k, slot_k, bucket_k = info[0:1, :], info[1:2, :], info[2:3, :]
            reach_k = jnp.where(4.0 * bucket_k + 4.0 > head, 1.0, 0.0)
            slot_q = fact(at, 1)
            usable = (reach_k > 0.5) | (slot_k == slot_q)
            allowed = (fact(at, 0) == seg_k) & (slot_k <= slot_q) & usable
            scores = jnp.where(allowed, nt(query, keyed) * scale, -1e30)
            weights = jnp.exp(scores - jnp.max(scores, axis=-1, keepdims=True))
            p = weights / jnp.sum(weights, axis=-1, keepdims=True)
            probs[part(g * heads + h, 256), :] = p
            mixed = nn(p.astype(low), value)
            att[at, h * HD : (h + 1) * HD] = jnp.where(
                4.0 * fact(at, 2) + 4.0 > head, mixed, 0.0
            ).astype(low)

        tiles(SHARE, attend_group)

    reduce = RowReduce(here, copies, (snd, rcv, acc, out_buf, in_buf), acks)

    def partial_sums(term):
        reduce.begin()
        for i in range(2):

            def send_tile(n, i=i):
                snd[i * 256 : (i + 1) * 256, part(n, 512)] = term(
                    pl.ds(512 + i * 256, 256), n
                ).astype(low)

            tiles(4, send_tile)
            reduce.core_send(i)

        def own_tile(n):
            acc[:, part(n, 512)] = term(pl.ds(0, 512), n)

        tiles(4, own_tile)

    g_o.arrive()
    partial_sums(lambda at, n: nn(att[at, :], wo[:, part(n, 512)]))
    reduce.diagonal()
    reduce.sides()
    g_u[0].forward()
    landed(got_d)
    g_d[0].start()
    in_tok.wait()
    reduce.arrive()

    def row_tiles(body):
        def step(i):
            at = pl.multiple_of(i * 64, 64)
            body(at, pl.ds(at, 64))

        tiles(owned // 64, step)

    def middle_tile(at, rows):
        projected = reduce.total(at, 64)
        proj[rows, :] = projected
        middle = own_tok[rows, :].astype(wide) + r_gate[0, rows, 0:1] * projected
        mid_buf[rows, :] = middle
        r = lax.rsqrt(jnp.mean(middle * middle, axis=-1, keepdims=True) + epsilon)
        units[rows, :] = (middle * r * gains[1:2, :]).astype(low)

    row_tiles(middle_tile)
    reduce.release()

    def row_view(buf):
        def view(k, h):
            if h is None:
                return buf.at[k * owned : (k + 1) * owned]
            return buf.at[k * owned + h * 64 : k * owned + (h + 1) * 64]

        return view

    units_out = RowGather(here, copies, row_view(units))
    units_out.start()
    in_first.wait()
    route(1, units)
    gates[0:owned, :] = r_gate[1]
    gates_out = RowGather(here, copies, row_view(gates))
    gates_out.start()
    units_out.forward()
    slope_tiles(1)
    gates_out.forward()
    units_out.finish()
    gates_out.finish()
    in_first = copies.local(first.at[0], first_buf)
    g_u[1].forward()
    g_d[1].start()
    for one in g_u:
        one.arrive()

    first_unit = (side * SHARE + share) * unit_width

    def used_units(at, base, rows, columns):
        lane = lax.broadcasted_iota(jnp.int32, (rows, columns), 1) + base
        return lane.astype(wide) < (FF // NB) * (fact(at, 3) + 1.0)

    save_wq.wait()
    g_q.drain()

    def up_tile(i):
        m, n = i % 2, i // 2
        at, c = part(m, 512), part(n, 512)
        made = nn(units[at, :], wu[:, c])
        acc[:, part(m * 2 + n, 512)] = made
        relu = jnp.maximum(made, 0.0)
        used = used_units(at, first_unit + n * 512, 512, 512)
        act[at, c] = jnp.where(used, relu * relu, 0.0).astype(low)

    tiles(4, up_tile)
    wait_all([c.wait for c in cot_rows.own])
    cot_rows.pass_on()
    wait_all([c.wait_recv for c in cot_rows.core + cot_rows.last])

    def live_cot(at):
        return jnp.where(fact(at, 4) > 0.5, cot[at, :].astype(wide), 0.0)

    for copy in tok_in.last + cot_rows.last:
        copy.wait_send()
        done.append(copy)

    def keep_tile(at, rows):
        top[rows, :] = live_cot(rows).astype(low)

    row_tiles(keep_tile)

    def scale_tile(i):
        at = part(i, 64)
        cot[at, :] = (gates[at, 0:1] * live_cot(at)).astype(low)

    tiles(16, scale_tile)
    g_d[0].forward()

    gd, gu, gq = toks, hid, wd
    blocks = [here.place, here.near_place, here.two_place, here.far_place]
    z_d = ZReduce(here, copies, gd, lambda k: (0, k * block), unit_width, block, l_d)
    z_u = ZReduce(
        here, copies, gu, lambda k: (k % 2 * block, k // 2 * unit_width), block, unit_width, l_u
    )
    z_o = ZReduce(here, copies, go, lambda k: (k * head_width, 0), head_width, block, l_o)
    z_q = ZReduce(
        here, copies, gq, lambda k: (k % 2 * block, k // 2 * 1024), block, 3 * head_width, l_q
    )

    def down_block(k):
        def body(i):
            m = part(i, 512)
            gd[m, k * block : (k + 1) * block] = tn(
                act[:, m], cot[:, part(blocks[k], block)]
            ).astype(low)

        tiles(unit_width // 512, body)

    down_block(3)
    z_d.send_far()
    down_block(2)
    down_block(1)
    z_d.send_near()
    down_block(0)
    for one in g_d:
        if one is g_d[1]:
            one.forward()
        one.arrive()

    def gup_tile(i):
        m, n = i % 2, i // 2
        at, c = part(m, 512), part(n, 512)
        made = nt(cot[at, :], wd[c, :])
        used = used_units(at, first_unit + n * 512, 512, 512)
        relu = jnp.maximum(acc[:, part(m * 2 + n, 512)], 0.0)
        gup[at, c] = jnp.where(used, 2.0 * relu * made, 0.0).astype(low)

    tiles(4, gup_tile)
    z_d.send_two(stage)

    reduce.await_release()
    partial_sums(lambda at, n: nn(act[at, :], wd[:, part(n, 512)]))
    reduce.diagonal()

    save_hid.wait()

    def up_block(k):
        r, c = k % 2 * block, k // 2 * unit_width

        def body(i):
            gu[r : r + block, pl.ds(pl.multiple_of(c + i * 512, 512), 512)] = tn(
                units[:, part(blocks[k], block)], gup[:, part(i, 512)]
            ).astype(low)

        tiles(unit_width // 512, body)

    up_block(3)
    z_u.send_far()
    reduce.sides()
    up_block(2)
    up_block(1)
    z_u.send_near()
    up_block(0)
    reduce.arrive()

    r_rows_out = [RowGather(here, copies, row_view(r_rows.at[i])) for i in range(2)]

    def keep_gate(index, rows, grad_gate):
        r_rows[index, rows, :] = (grad_gate * r_dpre[index, rows, :]).astype(low)
        r_slope[index, rows, :] = grad_gate * r_slope[index, rows, :]
        r_gate[index, rows, :] = jnp.broadcast_to(grad_gate, (64, HD))

    def block_tile(at, rows):
        downward = reduce.total(at, 64)
        own_out[rows, :] = jnp.where(
            fact(rows, 4) > 0.5, mid_buf[rows, :] + r_gate[1, rows, 0:1] * downward, 0.0
        ).astype(low)
        keep_gate(
            1, rows, jnp.sum(top[rows, :].astype(wide) * downward, axis=-1, keepdims=True)
        )

    row_tiles(block_tile)
    reduce.release()
    r_rows_out[1].start()
    shown = copies.local(own_out, o_block.at[mine])
    shown_far = to_peer(own_out, o_block.at[mine], here.across)

    reduce.await_release()
    partial_sums(lambda at, n: nt(gup[at, :], wu[part(n, 512), :]))
    for one in g_u:
        one.drain()
    in_wq = copies.local(s_wq, wu.at[:, 0 : 3 * head_width])
    r_rows_out[1].forward()
    reduce.diagonal()
    r_rows_out[1].finish()

    column = share * 2 + side
    places = [here.place, here.near_place, here.two_place, here.far_place]
    planes = [None, here.near, here.two, here.far]

    def first_rows(index, k, h):
        target = here.shares[k // 4 + k // 2 % 2 * 2] * 2 + (side if k % 2 == 0 else 1 - side)
        base = target * 256
        if h is None:
            return o_first.at[index, pl.ds(pl.multiple_of(base, 256), 256), :]
        return o_first.at[index, pl.ds(pl.multiple_of(base + h * 128, 128), 128), :]

    first_out = [
        RowGather(here, copies, lambda k, h, i=i: first_rows(i, k, h), True) for i in range(2)
    ]

    class FirstSum:
        def __init__(self, index, rows_of):
            self.index = index
            made = tn(rows_of[:, part(column, 256)], r_rows[index])
            zpart[index] = made.astype(low)
            slot = here.place
            self.got = []
            for k in range(4):
                src = zpart.at[index, part(places[k], 64), :]
                dst = zland.at[index, slot]
                self.got.append(
                    copies.local(src, dst) if k == 0 else to_peer(src, dst, planes[k])
                )

        def add(self):
            index = self.index
            landed(self.got)
            for copy in self.got[1:]:
                copy.wait_send()
                done.append(copy)
            total = zland[index, 0].astype(wide)
            for k in range(1, 4):
                total = total + zland[index, k].astype(wide)
            zpart[index, 0:64, :] = total.astype(low)
            at = pl.ds(pl.multiple_of(column * 256 + here.place * 64, 64), 64)
            src, dst = zpart.at[index, 0:64, :], o_first.at[index, at, :]
            self.got = [
                copies.local(src, dst) if k == 0 else to_peer(src, dst, planes[k])
                for k in range(4)
            ]

        def show(self):
            landed(self.got)
            first_out[self.index].start()

    sum_units = FirstSum(1, units)
    units_out.drain()
    in_hid = copies.local(s_hid, units)
    z_u.send_two(stage)
    reduce.sides()
    sum_units.add()
    reduce.arrive()
    gproj = cot
    gain_buf[...] = jnp.zeros_like(gain_buf)

    def grad_tile(at, rows):
        grad = reduce.total(at, 64) + r_gate[1, rows, 0:1] * slope[rows, :]
        back, gain_terms = norm_back(mid_buf[rows, :], grad, gains[1:2, :])
        grad_middle = top[rows, :].astype(wide) + back
        mid_buf[rows, :] = grad_middle
        gproj[rows, :] = (r_gate[0, rows, 0:1] * grad_middle).astype(low)
        keep_gate(0, rows, jnp.sum(grad_middle * proj[rows, :], axis=-1, keepdims=True))
        gain_buf[1:2, :] = gain_buf[1:2, :] + jnp.sum(gain_terms, axis=0, keepdims=True)

    row_tiles(grad_tile)
    reduce.release()
    gproj_out = RowGather(here, copies, row_view(gproj))
    gproj_out.start()
    r_rows_out[0].start()
    in_first.wait()
    slope_tiles(0)
    gproj_out.forward()
    sum_units.show()
    r_rows_out[0].forward()
    z_d.finish(stage)

    def deliver(piece_of, dst):
        for d in range(SHARE):
            src = piece_of(here.shares[d])
            if d == 0:
                outs.append(copies.local(src, dst))
            else:
                sent.append(copies.push(src, dst, here.members[d]))
                owed.append(sent[-1])

    owed = []
    deliver(lambda t: gd.at[:, part(t, owned)], o_gd.at[part(share, unit_width), :])
    gproj_out.finish()

    def out_block(k):
        go[k * head_width : (k + 1) * head_width, :] = tn(
            att[...], gproj[:, part(blocks[k], block)]
        ).astype(low)

    out_block(3)
    z_o.send_far()
    out_block(2)
    out_block(1)
    z_o.send_near()
    out_block(0)
    gatt, gqkv = gup, act

    def gatt_tile(i):
        at = part(i, 512)
        made = nt(gproj[at, :], wo[...]).astype(low)
        for h in range(heads):
            used = 4.0 * fact(at, 2) + 4.0 > (first_head + h).astype(wide)
            gatt[at, h * HD : (h + 1) * HD] = jnp.where(
                used, made[:, h * HD : (h + 1) * HD].astype(wide), 0.0
            ).astype(low)

    tiles(2, gatt_tile)
    z_o.send_two(stage)
    r_rows_out[0].finish()
    in_hid.wait()
    sum_heads = FirstSum(0, units)

    for h in range(heads):

        def back_group(g, h=h):
            at = part(g, 256)
            lanes = [pl.ds(j * head_width + h * HD, HD) for j in range(3)]
            query, keyed, value = (qkvb[at, lane] for lane in lanes)
            grad = gatt[at, h * HD : (h + 1) * HD]
            p = probs[part(g * heads + h, 256), :]
            grad_p = nt(grad, value)
            row_dot = jnp.sum(p * grad_p, axis=-1, keepdims=True)
            grad_s = (p * (grad_p - row_dot)).astype(low)
            cosine = cols[at, 0:HD]
            sine = cols[at, HD : 2 * HD]
            for lane, turned in (
                (lanes[0], nn(grad_s, keyed) * scale),
                (lanes[1], tn(grad_s, query) * scale),
            ):
                gqkv[at, lane] = (
                    turned * cosine - pltpu.roll(turned, HD // 2, 1) * sine
                ).astype(low)
            gqkv[at, lanes[2]] = tn(p.astype(low), grad).astype(low)

        tiles(SHARE, back_group)

    def qkv_block(k):
        r, c = k % 2 * block, k // 2 * 1024
        for j in range(3):
            gq[r : r + block, c + j * head_width : c + (j + 1) * head_width] = tn(
                units[:, part(blocks[k], block)], gqkv[:, j * head_width : (j + 1) * head_width]
            ).astype(low)

    for one in g_d:
        one.drain()
    qkv_block(3)
    z_q.send_far()
    qkv_block(2)
    qkv_block(1)
    z_q.send_near()
    qkv_block(0)
    sum_heads.add()
    first_out[1].forward()
    z_q.send_two(stage)

    in_wq.wait()
    reduce.await_release()
    partial_sums(
        lambda at, n: nt(gqkv[at, 0 : 3 * head_width], wu[part(n, 512), 0 : 3 * head_width])
    )
    reduce.diagonal()
    sum_heads.show()
    first_out[1].finish()
    reduce.sides()
    shown.wait()
    shown_far.wait()
    done.append(shown_far)
    first_out[0].forward()
    reduce.arrive()

    def input_tile(at, rows):
        grad = reduce.total(at, 64) + r_gate[0, rows, 0:1] * slope[rows, :]
        back, gain_terms = norm_back(own_tok[rows, :].astype(wide), grad, gains[0:1, :])
        own_out[rows, :] = (mid_buf[rows, :] + back).astype(low)
        gain_buf[0:1, :] = gain_buf[0:1, :] + jnp.sum(gain_terms, axis=0, keepdims=True)

    row_tiles(input_tile)
    outs.append(copies.local(own_out, o_input.at[mine]))
    input_far = copies.push(own_out, o_input.at[mine], here.across)

    for index in range(2):
        for j in range(8):
            pack[index * 8 + j : index * 8 + j + 1, :] = gain_buf[
                index : index + 1, j * 256 : (j + 1) * 256
            ]
        made = exact(r_slope[index], r_inner[index], ((0,), (0,)))
        pack[16 + index * 8 : 24 + index * 8, :] = made[0:8, :]
        lane = lax.broadcasted_iota(jnp.int32, (owned, 256), 1)
        own = pl.ds(0, owned)
        hot = (lane.astype(wide) == fact(own, 2 + index)) & (fact(own, 4) > 0.5)
        count = jnp.sum(jnp.where(hot, 1.0, 0.0), axis=0, keepdims=True)
        pack[32 + index * 8 : 40 + index * 8, :] = jnp.broadcast_to(count, (8, 256))

    def sum_slots(buf, count):
        total = buf[0]
        for k in range(1, count):
            total = total + buf[k]
        return total

    got = [
        copies.local(pack, pack_plane.at[share])
        if d == 0
        else to_peer(pack, pack_plane.at[share], here.members[d])
        for d in range(SHARE)
    ]
    first_out[0].finish()
    landed(got)
    for copy in got[1:]:
        copy.wait_send()
        done.append(copy)
    pack[...] = sum_slots(pack_plane, SHARE)
    got = [
        copies.local(pack, pack_side.at[side]),
        to_peer(pack, pack_side.at[side], here.across),
    ]
    landed(got)
    got[1].wait_send()
    done.append(got[1])
    pack[...] = pack_side[0] + pack_side[1]
    got = [
        copies.local(pack, pack_ring.at[here.place])
        if k == 0
        else to_peer(pack, pack_ring.at[here.place], planes[k])
        for k in range(4)
    ]

    z_u.finish(stage)
    deliver(lambda t: gu.at[part(t, owned), 0:unit_width], o_gu.at[:, part(share, unit_width)])
    landed(got)
    for copy in got[1:]:
        copy.wait_send()
        done.append(copy)
    pack[...] = sum_slots(pack_ring, 4)
    outs.append(copies.local(pack, o_pack))
    z_o.finish(stage)
    deliver(
        lambda t: go.at[0:head_width, part(t, owned)], o_go.at[part(share, head_width), :]
    )
    z_q.finish(stage)
    for j in range(3):
        deliver(
            lambda t, j=j: gq.at[part(t, owned), j * head_width : (j + 1) * head_width],
            o_gq.at[j, :, part(share, head_width)],
        )

    drains = [g_q, g_o] + g_u + g_d + [z_d, z_u, z_o, z_q, reduce, units_out, gates_out]
    for one in drains + [gproj_out] + r_rows_out + first_out:
        one.drain()
    input_far.wait()
    for copy in owed:
        copy.wait_recv()
    for copy in outs:
        copy.wait()
    for copy in sent:
        if not any(copy is one for one in done):
            copy.wait_send()
    copies.check()


def plane(mesh):
    fsdp = mesh.shape["fsdp"]
    ring_size = fsdp // SHARE

    def shards(
        tokens,
        head_bucket,
        ffn_bucket,
        lengths,
        norm_gains,
        qkv_weight,
        out_weight,
        up_weight,
        down_weight,
        router_first,
        router_second,
        cotangent,
    ):
        rows, width = tokens.shape
        half = rows // 2
        local_units = up_weight.shape[1]
        units = local_units // SHARE
        local_width = out_weight.shape[0]
        head_width = local_width // SHARE
        heads = head_width // HD
        owned = width // fsdp
        block = width // ring_size
        plane_rows = SHARE * rows

        slot_ids = jnp.arange(rows, dtype=jnp.int32)
        segment, position, live_rows = (a[0] for a in layout(lengths, slot_ids))
        frequency = theta_base ** (-2.0 * jnp.arange(HD // 2, dtype=wide) / HD)
        angles = position.astype(wide)[:, None] * frequency
        cosine, sine = jnp.cos(angles), jnp.sin(angles)
        facts = jnp.stack(
            [segment, slot_ids, head_bucket, ffn_bucket, live_rows.astype(jnp.int32)], axis=1
        ).astype(wide)
        col = jnp.concatenate(
            [cosine, cosine, -sine, sine, jnp.pad(facts, ((0, 0), (0, HD - facts.shape[1])))],
            axis=1,
        )
        row = jnp.pad(facts.T, ((0, 8 - facts.shape[1]), (0, 0)))
        second = jnp.pad(router_second, ((0, 0), (0, 0), (0, HD - NB)))
        b16, f32 = low, wide
        hidden = router_first.shape[2]
        small = 48

        def shape(*dims):
            return jax.ShapeDtypeStruct(dims[1:], dims[0])

        def buffer(*dims):
            return pltpu.VMEM(dims[1:], dims[0])

        anywhere = pl.BlockSpec(memory_space=pl.ANY)
        vmem = pl.BlockSpec(memory_space=pltpu.VMEM)
        (
            block_out,
            input_grad,
            raw_qkv,
            raw_out,
            raw_up,
            raw_down,
            raw_first,
            sums,
            *_,
        ) = pl.pallas_call(
            layer_kernel,
            out_shape=[
                shape(b16, rows, width),
                shape(b16, rows, width),
                shape(b16, 3, owned, local_width),
                shape(b16, local_width, owned),
                shape(b16, owned, local_units),
                shape(b16, local_units, owned),
                shape(b16, *router_first.shape),
                shape(f32, small, 256),
                shape(b16, plane_rows, width),
                shape(b16, width, 3 * head_width),
                shape(b16, 4, block, 3 * head_width),
                shape(b16, 4, head_width, block),
                shape(b16, 4, block, units),
                shape(b16, 4, units, block),
            ],
            in_specs=[anywhere] * 9 + [vmem] * 2,
            out_specs=[anywhere] * 14,
            scratch_shapes=[
                buffer(b16, plane_rows, width),
                buffer(b16, plane_rows, width),
                buffer(b16, plane_rows, width),
                buffer(b16, plane_rows, width),
                buffer(b16, 2 * plane_rows, units),
                buffer(b16, head_width, width),
                buffer(b16, width, units),
                buffer(b16, units, width),
                buffer(f32, plane_rows, 3 * HD),
                buffer(f32, SHARE, 8, rows),
                buffer(b16, plane_rows, 3 * head_width),
                buffer(f32, SHARE * heads * rows, rows),
                buffer(b16, plane_rows, head_width),
                buffer(f32, plane_rows // 2, width),
                buffer(b16, plane_rows // 2, width),
                buffer(b16, plane_rows // 2, width),
                buffer(b16, 3 * half, width),
                buffer(b16, 3 * half, width),
                buffer(f32, half, width),
                buffer(f32, half, width),
                buffer(b16, 4 * head_width, block),
                buffer(b16, 2, block, units),
                buffer(b16, half, width),
                buffer(b16, half, width),
                buffer(b16, half, width),
                buffer(f32, width, hidden),
                buffer(f32, half, width),
                buffer(f32, plane_rows, HD),
                buffer(f32, 2, half, HD),
                buffer(f32, 2, half, hidden),
                buffer(f32, 2, half, HD),
                buffer(f32, 2, half, hidden),
                buffer(b16, 2, plane_rows, hidden),
                buffer(b16, 2, 256, hidden),
                buffer(b16, 2, 4, 64, hidden),
                buffer(f32, 8, width),
                buffer(f32, small, 256),
                buffer(f32, SHARE, small, 256),
                buffer(f32, 2, small, 256),
                buffer(f32, 4, small, 256),
                pltpu.SemaphoreType.DMA((128,)),
                pltpu.SemaphoreType.DMA((256,)),
                pltpu.SemaphoreType.DMA((256,)),
                pltpu.SemaphoreType.REGULAR((3,)),
            ],
            compiler_params=pltpu.CompilerParams(
                collective_id=0, has_side_effects=True, vmem_limit_bytes=63 * 2**20
            ),
        )(
            tokens,
            col,
            row,
            cotangent,
            jnp.transpose(qkv_weight, (1, 0, 2)),
            out_weight,
            up_weight,
            down_weight,
            router_first,
            norm_gains,
            second,
        )
        grad_qkv = jnp.transpose(raw_qkv, (1, 0, 2)).astype(wide)
        grad_out, grad_up, grad_down, grad_first = (
            a.astype(wide) for a in (raw_out, raw_up, raw_down, raw_first)
        )
        grad_gains = sums[0:16].reshape(2, width)
        grad_second = jnp.stack([sums[16 : 16 + NB].T, sums[24 : 24 + NB].T])
        usage = jnp.stack([sums[32, :NB], sums[40, :NB]])
        return (
            block_out,
            input_grad,
            grad_gains,
            grad_qkv,
            grad_out,
            grad_up,
            grad_down,
            grad_first,
            grad_second,
            usage,
        )

    return shards


def solution(mesh):
    shards = plane(mesh) if mesh.shape["fsdp"] == 4 * SHARE else general(mesh)
    in_specs = (
        P("fsdp", None),
        P("fsdp"),
        P("fsdp"),
        P("fsdp", None),
        P(),
        P("fsdp", None, "tensor"),
        P("tensor", "fsdp"),
        P("fsdp", "tensor"),
        P("tensor", "fsdp"),
        P(),
        P(),
        P("fsdp", None),
    )
    out_specs = (
        P("fsdp", None),
        P("fsdp", None),
        P(),
        P("fsdp", None, "tensor"),
        P("tensor", "fsdp"),
        P("fsdp", "tensor"),
        P("tensor", "fsdp"),
        P(),
        P(),
        P(),
    )
    return jax.shard_map(
        shards, mesh=mesh, in_specs=in_specs, out_specs=out_specs, check_vma=False
    )
```

```python
from functools import partial

import jax
import jax.numpy as jnp
from jax import lax
from jax.experimental import pallas as pl
from jax.experimental.pallas import tpu as pltpu
from jax.sharding import PartitionSpec as P

HEADS = 16
HD = 128
FF = 8192
NB = 4
SHARE = 4

epsilon = 1e-05
theta_base = 10000.0
highest = lax.Precision.HIGHEST
low = jnp.bfloat16
wide = jnp.float32
MESH = pl.DeviceIdType.MESH


def norm_piece(values_in, gain_row):
    return (
        values_in
        * lax.rsqrt(jnp.mean(values_in * values_in, axis=-1, keepdims=True) + epsilon)
        * gain_row
    )


def route_piece(hidden_in, router_in, router_out, bucket):
    inner = jax.nn.silu(jnp.dot(hidden_in, router_in, precision=highest))
    logits = jnp.dot(inner, router_out, precision=highest)
    probs_all = jax.nn.softmax(logits, axis=-1)
    onehot = (bucket[:, None] == jnp.arange(NB, dtype=jnp.int32)[None, :]).astype(wide)
    return NB * jnp.sum(probs_all * onehot, axis=-1)


def dot(left_in, right_in):
    return jnp.dot(left_in, right_in, preferred_element_type=wide)


def dot_rows(left_in, right_in):
    return lax.dot_general(
        left_in, right_in, (((0,), (0,)), ((), ())), preferred_element_type=wide
    )


def dot_cols(left_in, right_in):
    return lax.dot_general(
        left_in, right_in, (((1,), (1,)), ((), ())), preferred_element_type=wide
    )


def rotate(operand, cosine, sine_table):
    half_dim = operand.shape[-1] // 2
    lead_half = operand[..., :half_dim]
    tail_half = operand[..., half_dim:]
    return jnp.concatenate(
        [lead_half * cosine - tail_half * sine_table, tail_half * cosine + lead_half * sine_table],
        axis=-1,
    )


def layout(length_rows, slot_ids):
    seq_count = length_rows.shape[1]
    order = jnp.arange(seq_count, dtype=jnp.int32)
    seq_ends = jnp.sum(
        jnp.where(order[None, None, :] <= order[None, :, None], length_rows[:, None, :], 0), axis=2
    )
    seq_starts = seq_ends - length_rows
    slots = slot_ids[None, :, None]
    member = (slots >= seq_starts[:, None, :]) & (slots < seq_ends[:, None, :])
    seq_of = jnp.sum(jnp.where(member, jnp.arange(seq_count, dtype=jnp.int32), 0), axis=2)
    live_rows = jnp.any(member, axis=2)
    seq_begin = jnp.sum(jnp.where(member, seq_starts[:, None, :], 0), axis=2)
    segment = jnp.where(live_rows, seq_of, seq_count + slot_ids[None, :])
    position = slot_ids[None, :] - seq_begin
    return segment, position, live_rows


def general(mesh):
    fsdp = mesh.shape["fsdp"]
    ring_size = fsdp // SHARE

    def hop(moved, bits):
        return lax.ppermute(moved, "fsdp", [(i, i ^ bits) for i in range(fsdp)])

    def cross(moved):
        return lax.ppermute(moved, "tensor", [(0, 1), (1, 0)])

    def shards(
        tokens,
        head_bucket,
        ffn_bucket,
        lengths,
        norm_gains,
        qkv_weight,
        out_weight,
        up_weight,
        down_weight,
        router_first,
        router_second,
        cotangent,
    ):
        rows, width = tokens.shape
        half = rows // 2
        rank = lax.axis_index("fsdp")
        side = lax.axis_index("tensor")
        share = rank % SHARE
        place = rank // SHARE
        local_units = up_weight.shape[1]
        units = local_units // SHARE
        local_width = out_weight.shape[0]
        head_width = local_width // SHARE
        heads = head_width // HD
        owned = width // fsdp
        block = width // ring_size

        chain = [None, None]

        def ring(moved, stream):
            if chain[stream] is not None:
                moved, _ = lax.optimization_barrier((moved, chain[stream]))
            got = lax.ppermute(
                moved, "fsdp", [(i, (i + SHARE) % fsdp) for i in range(fsdp)]
            )
            chain[stream] = got
            return got

        def place_at(step):
            return (place - step) % ring_size

        def own_half(arr):
            return lax.dynamic_slice_in_dim(arr, side * half, half, 0)

        def relative(arr):
            return jnp.concatenate(
                [own_half(arr), lax.dynamic_slice_in_dim(arr, (1 - side) * half, half, 0)], axis=0
            )

        def gather_rows(arr):
            other = hop(arr, 2)
            plane = jnp.concatenate([arr[:half], other[:half], arr[half:], other[half:]], axis=0)
            return jnp.concatenate([plane, hop(plane, 1)], axis=0)

        def gather_halves(arr):
            pair = jnp.concatenate([arr, hop(arr, 2)], axis=0)
            plane = jnp.concatenate([pair, cross(pair)], axis=0)
            return jnp.concatenate([plane, hop(plane, 1)], axis=0)

        def reduce_rows(keep, send):
            total = keep + hop(send.astype(low), 1).astype(wide)
            total = total[: 2 * half] + cross(total[2 * half :].astype(low)).astype(wide)
            return total[:half] + hop(total[half:].astype(low), 2).astype(wide)

        def whole_rows(arr):
            other = cross(arr)
            return jnp.where(
                side == 0,
                jnp.concatenate([arr, other], axis=0),
                jnp.concatenate([other, arr], axis=0),
            )

        def spread(pieces_for, axis):
            out = None
            for bits in range(SHARE):
                piece = pieces_for(share ^ bits)
                got = piece if bits == 0 else hop(piece, bits)
                if out is None:
                    dims = list(got.shape)
                    dims[axis] *= SHARE
                    out = jnp.zeros(dims, got.dtype)
                out = lax.dynamic_update_slice_in_dim(
                    out, got, (share ^ bits) * got.shape[axis], axis
                )
            return out

        def ring_gather(own, axis):
            dims = list(own.shape)
            dims[axis] = width
            out = jnp.zeros(dims, own.dtype)
            mid = own.shape[0] // 2
            moving = [own[:mid], own[mid:]]
            for step in range(ring_size):
                if step:
                    moving = [ring(moving[s], s) for s in range(2)]
                base = place_at(step) * block
                for s in range(2):
                    if axis == 0:
                        at = (base + s * mid, 0)
                    else:
                        at = (s * mid, base)
                    out = lax.dynamic_update_slice(out, moving[s], at)
            return out

        def ring_reduce(term):
            moving = [None, None]
            for step in range(1, ring_size):
                for s in range(2):
                    part = term(place_at(step), s)
                    if moving[s] is not None:
                        part = part + moving[s].astype(wide)
                    moving[s] = part.astype(low)
                for s in range(2):
                    moving[s] = ring(moving[s], s)
            return [term(place, s) + moving[s].astype(wide) for s in range(2)]

        def scatter_back(parts, axis):
            joined = jnp.concatenate(parts, axis=0)
            other = 1 - axis
            out_dims = list(joined.shape)
            out_dims[axis] = owned
            stride = out_dims[other]
            out_dims[other] *= SHARE
            out = jnp.zeros(out_dims, wide)
            for bits in range(SHARE):
                piece = lax.dynamic_slice_in_dim(joined, (share ^ bits) * owned, owned, axis)
                if bits:
                    piece = hop(piece.astype(low), bits).astype(wide)
                out = lax.dynamic_update_slice_in_dim(out, piece, (share ^ bits) * stride, other)
            return out

        def qkv_piece(target):
            return lax.dynamic_slice_in_dim(
                qkv_weight, target * head_width, head_width, 2
            ).reshape(owned, 3 * head_width)

        qkv_block = spread(qkv_piece, 0)
        rel_tokens = relative(tokens)
        rel_cot = relative(cotangent)
        ints = relative(jnp.stack([head_bucket, ffn_bucket], axis=1))
        qkv_full = ring_gather(qkv_block, 0)
        all_tokens = gather_rows(rel_tokens)
        buckets = gather_rows(ints)
        pair_lengths = jnp.concatenate([lengths, hop(lengths, 2)], axis=0)
        group_lengths = jnp.concatenate([pair_lengths, hop(pair_lengths, 1)], axis=0)

        out_block = spread(
            lambda t: lax.dynamic_slice_in_dim(out_weight, t * head_width, head_width, 0), 1
        )
        out_full = ring_gather(out_block, 1)
        up_block = spread(lambda t: lax.dynamic_slice_in_dim(up_weight, t * units, units, 1), 0)
        up_full = ring_gather(up_block, 0)
        down_block = spread(
            lambda t: lax.dynamic_slice_in_dim(down_weight, t * units, units, 0), 1
        )
        down_full = ring_gather(down_block, 1)
        all_cot = gather_rows(rel_cot)

        slot_ids = jnp.concatenate(
            [
                side * half + jnp.arange(half, dtype=jnp.int32),
                (1 - side) * half + jnp.arange(half, dtype=jnp.int32),
            ]
        )
        segment, position, live_groups = layout(group_lengths, slot_ids)

        def to_groups(arr):
            tail = arr.shape[1:]
            arr = arr.reshape((2, 2, 2, half) + tail)
            return jnp.swapaxes(arr, 1, 2).reshape((SHARE, rows) + tail)

        def from_groups(arr):
            tail = arr.shape[2:]
            arr = arr.reshape((2, 2, 2, half) + tail)
            return jnp.swapaxes(arr, 1, 2).reshape((8 * half,) + tail)

        live_all = from_groups(live_groups)
        all_heads = buckets[:, 0]
        all_widths = buckets[:, 1]

        own_tokens = rel_tokens[:half].astype(wide)
        own_heads = all_heads[:half]
        own_widths = all_widths[:half]
        own_live = live_all[:half]

        block_in = all_tokens.astype(wide)
        hidden_heads = norm_piece(block_in, norm_gains[0]).astype(low)
        own_normed, norm_heads_back = jax.vjp(norm_piece, own_tokens, norm_gains[0])
        gate_heads, route_heads_back = jax.vjp(
            partial(route_piece, bucket=own_heads),
            own_normed.astype(low).astype(wide),
            router_first[0],
            router_second[0],
        )
        head_ids = side * (local_width // HD) + share * heads + jnp.arange(heads, dtype=jnp.int32)
        head_used = head_ids[None, :] < HEADS // NB * (all_heads[:, None] + 1)
        unit_ids = side * local_units + share * units + jnp.arange(units, dtype=jnp.int32)
        unit_used = unit_ids[None, :] < FF // NB * (all_widths[:, None] + 1)

        half_dim = HD // 2
        frequency = theta_base ** (-2.0 * jnp.arange(half_dim, dtype=wide) / HD)
        angles = position.astype(wide)[:, :, None] * frequency
        cosine = jnp.cos(angles)[:, :, None, :]
        sine_table = jnp.sin(angles)[:, :, None, :]
        qkv_all = to_groups(dot(hidden_heads, qkv_full).reshape(8 * half, 3, heads, HD))
        query = rotate(qkv_all[:, :, 0], cosine, sine_table).astype(low)
        keyed = rotate(qkv_all[:, :, 1], cosine, sine_table).astype(low)
        value = qkv_all[:, :, 2].astype(low)
        group_used = to_groups(head_used)
        same_seq = segment[:, :, None] == segment[:, None, :]
        causal = slot_ids[None, :] <= slot_ids[:, None]
        diagonal = slot_ids[None, :] == slot_ids[:, None]
        key_used = jnp.swapaxes(group_used, 1, 2)
        allowed = (same_seq & causal)[:, None] & (key_used[:, :, None, :] | diagonal)
        scale = HD ** (-0.5)
        scores = jnp.einsum("gqhe,gkhe->ghqk", query, keyed, preferred_element_type=wide) * scale
        scores = jnp.where(allowed, scores, -1e30)
        row_top = jnp.max(scores, axis=-1, keepdims=True)
        weights = jnp.exp(scores - row_top)
        probs = weights / jnp.sum(weights, axis=-1, keepdims=True)
        probs_low = probs.astype(low)
        mixed = jnp.einsum("ghqk,gkhe->gqhe", probs_low, value, preferred_element_type=wide)
        mixed = jnp.where(group_used[..., None], mixed, 0.0).astype(low)
        attended = from_groups(mixed).reshape(8 * half, head_width)

        def partial_rows(left_in, matrix, product):
            keep = product(left_in[: 4 * half], matrix)
            send = product(left_in[4 * half :], matrix)
            return reduce_rows(keep, send)

        projected = partial_rows(attended, out_full, dot)

        middle = own_tokens + gate_heads[:, None] * projected
        normed_units, norm_units_back = jax.vjp(norm_piece, middle, norm_gains[1])
        own_units = normed_units.astype(low)
        hidden_units = gather_halves(own_units)
        gate_units, route_units_back = jax.vjp(
            partial(route_piece, bucket=own_widths),
            own_units.astype(wide),
            router_first[1],
            router_second[1],
        )
        all_gates = gather_halves(gate_units[:, None])
        upward = dot(hidden_units, up_full)
        activated = jnp.where(unit_used, jnp.square(jax.nn.relu(upward)), 0.0).astype(low)
        grad_top_all = jnp.where(live_all[:, None], all_cot.astype(wide), 0.0)
        grad_down_in = (all_gates * grad_top_all).astype(low)

        def down_term(at, s):
            mid = units // 2
            return dot_rows(
                activated[:, s * mid : (s + 1) * mid],
                lax.dynamic_slice_in_dim(grad_down_in, at * block, block, 1),
            )

        grad_down = scatter_back(ring_reduce(down_term), 1)

        downward = partial_rows(activated, down_full, dot)
        own_out = jnp.where(
            own_live[:, None], middle + gate_units[:, None] * downward, 0.0
        ).astype(low)
        block_out = whole_rows(own_out)
        grad_top = jnp.where(own_live[:, None], rel_cot[:half].astype(wide), 0.0)
        grad_gate_units = jnp.sum(grad_top * downward, axis=1)

        grad_act = dot_cols(grad_down_in, down_full)
        grad_up_in = jnp.where(unit_used, 2.0 * jax.nn.relu(upward) * grad_act, 0.0).astype(low)

        def up_term(at, s):
            mid = block // 2
            return dot_rows(
                lax.dynamic_slice_in_dim(hidden_units, at * block + s * mid, mid, 1), grad_up_in
            )

        grad_up = scatter_back(ring_reduce(up_term), 0)
        route_units_grads = route_units_back(grad_gate_units)
        grad_hidden_units = partial_rows(grad_up_in, up_full, dot_cols) + route_units_grads[0]
        norm_units_grads = norm_units_back(grad_hidden_units)
        grad_middle = grad_top + norm_units_grads[0]
        grad_gate_heads = jnp.sum(grad_middle * projected, axis=1)
        grad_projected = gather_halves((gate_heads[:, None] * grad_middle).astype(low))

        def out_term(at, s):
            mid = head_width // 2
            return dot_rows(
                attended[:, s * mid : (s + 1) * mid],
                lax.dynamic_slice_in_dim(grad_projected, at * block, block, 1),
            )

        grad_out = scatter_back(ring_reduce(out_term), 1)
        grad_attended = to_groups(
            dot_cols(grad_projected, out_full).astype(low).reshape(8 * half, heads, HD)
        )
        grad_attended = jnp.where(group_used[..., None], grad_attended, jnp.zeros((), low))
        grad_value = jnp.einsum(
            "ghqk,gqhe->gkhe", probs_low, grad_attended, preferred_element_type=wide
        )
        grad_probs = jnp.einsum(
            "gqhe,gkhe->ghqk", grad_attended, value, preferred_element_type=wide
        )
        row_dot = jnp.sum(probs * grad_probs, axis=-1, keepdims=True)
        grad_scores = (probs * (grad_probs - row_dot)).astype(low)
        grad_query = (
            jnp.einsum("ghqk,gkhe->gqhe", grad_scores, keyed, preferred_element_type=wide) * scale
        )
        grad_keyed = (
            jnp.einsum("ghqk,gqhe->gkhe", grad_scores, query, preferred_element_type=wide) * scale
        )
        grad_qkv_in = jnp.stack(
            [
                rotate(grad_query, cosine, -sine_table),
                rotate(grad_keyed, cosine, -sine_table),
                grad_value,
            ],
            axis=2,
        ).astype(low)
        grad_qkv_in = from_groups(grad_qkv_in).reshape(8 * half, 3 * head_width)

        def qkv_term(at, s):
            mid = block // 2
            return dot_rows(
                lax.dynamic_slice_in_dim(hidden_heads, at * block + s * mid, mid, 1), grad_qkv_in
            )

        qkv_parts = ring_reduce(qkv_term)
        joined = jnp.concatenate(qkv_parts, axis=0)
        grad_qkv = jnp.zeros((owned, 3, local_width), wide)
        for bits in range(SHARE):
            piece = lax.dynamic_slice_in_dim(joined, (share ^ bits) * owned, owned, 0)
            if bits:
                piece = hop(piece.astype(low), bits).astype(wide)
            grad_qkv = lax.dynamic_update_slice_in_dim(
                grad_qkv, piece.reshape(owned, 3, head_width), (share ^ bits) * head_width, 2
            )

        route_heads_grads = route_heads_back(grad_gate_heads)
        grad_hidden_heads = partial_rows(grad_qkv_in, qkv_full, dot_cols) + route_heads_grads[0]
        norm_heads_grads = norm_heads_back(grad_hidden_heads)
        input_grad = whole_rows((grad_middle + norm_heads_grads[0]).astype(low))

        def total_small(arr):
            arr = arr + cross(arr)
            bits = 1
            while bits < fsdp:
                arr = arr + hop(arr, bits)
                bits *= 2
            return arr

        def total_large(arr):
            steps = [1, "tensor"] + [2**i for i in range(1, fsdp.bit_length() - 1)]
            for bits in steps:
                mid = arr.shape[0] // 2
                me = side if bits == "tensor" else (rank // bits) % 2
                send = lax.dynamic_slice_in_dim(arr, (1 - me) * mid, mid, 0)
                keep = lax.dynamic_slice_in_dim(arr, me * mid, mid, 0)
                arr = keep + (cross(send) if bits == "tensor" else hop(send, bits))
            for bits in reversed(steps):
                me = side if bits == "tensor" else (rank // bits) % 2
                other = cross(arr) if bits == "tensor" else hop(arr, bits)
                arr = jnp.where(
                    me == 0,
                    jnp.concatenate([arr, other], axis=0),
                    jnp.concatenate([other, arr], axis=0),
                )
            return arr

        bucket_ids = jnp.arange(NB, dtype=jnp.int32)[None, :]
        head_counts = jnp.sum(
            jnp.where(own_live[:, None] & (own_heads[:, None] == bucket_ids), 1.0, 0.0), axis=0
        )
        width_counts = jnp.sum(
            jnp.where(own_live[:, None] & (own_widths[:, None] == bucket_ids), 1.0, 0.0), axis=0
        )
        units_small = total_small(
            jnp.concatenate(
                [norm_units_grads[1], route_units_grads[2].reshape(-1), head_counts, width_counts]
            )
        )
        heads_small = total_small(
            jnp.concatenate([norm_heads_grads[1], route_heads_grads[2].reshape(-1)])
        )
        first_units = total_large(route_units_grads[1])
        first_heads = total_large(route_heads_grads[1])
        second_shape = router_second.shape[1:]
        second_size = second_shape[0] * second_shape[1]
        grad_gains = jnp.stack([heads_small[:width], units_small[:width]])
        grad_second = jnp.stack(
            [
                heads_small[width : width + second_size].reshape(second_shape),
                units_small[width : width + second_size].reshape(second_shape),
            ]
        )
        usage = units_small[width + second_size :].reshape(2, NB)
        grad_first = jnp.stack([first_heads, first_units])
        return (
            block_out,
            input_grad,
            grad_gains,
            grad_qkv,
            grad_out,
            grad_up,
            grad_down,
            grad_first,
            grad_second,
            usage,
        )

    return shards


def xor_one(index):
    return index + 1 - 2 * (index % 2)


class Plane:
    def __init__(self):
        self.rank = lax.axis_index("fsdp")
        self.side = lax.axis_index("tensor")
        self.share = self.rank % SHARE
        self.place = self.rank // SHARE
        core = xor_one(self.share)
        mid = (self.share + 2) % SHARE
        self.shares = [self.share, core, mid, SHARE - 1 - self.share]
        self.core = {"fsdp": self.place * SHARE + core}
        self.mid = {"fsdp": self.place * SHARE + mid}
        self.both = {"fsdp": self.place * SHARE + self.shares[3]}
        self.members = [None, self.core, self.mid, self.both]
        self.across = {"tensor": 1 - self.side}
        self.near_place = xor_one(self.place)
        self.two_place = (self.place + 2) % 4
        self.far_place = 3 - self.place
        self.near = {"fsdp": self.near_place * SHARE + self.share}
        self.two = {"fsdp": self.two_place * SHARE + self.share}
        self.far = {"fsdp": self.far_place * SHARE + self.share}
        self.inner = (self.place == 1) | (self.place == 2)
        self.outer = (self.place == 0) | (self.place == 3)

    def greet(self):
        barrier = pltpu.get_barrier_semaphore()
        peers = [self.core, self.mid, self.both, self.across, self.near, self.two, self.far]
        for peer in peers:
            pl.semaphore_signal(barrier, inc=1, device_id=peer, device_id_type=MESH)
        pl.semaphore_wait(barrier, len(peers))


class Copies:
    def __init__(self, local_sems, send_sems, recv_sems):
        self.local_sems, self.send_sems, self.recv_sems = local_sems, send_sems, recv_sems
        self.locals, self.sends, self.recvs = 0, 0, 0

    def check(self):
        assert self.locals <= self.local_sems.shape[0]
        assert self.sends <= self.send_sems.shape[0]
        assert self.recvs <= self.recv_sems.shape[0]

    def local(self, src, dst):
        copy = pltpu.make_async_copy(src, dst, self.local_sems.at[self.locals])
        self.locals += 1
        copy.start()
        return copy

    def slot(self):
        self.recvs += 1
        return self.recvs - 1

    def remote(self, src, dst, peer, slot=None):
        if slot is None:
            slot = self.slot()
        copy = pltpu.make_async_remote_copy(
            src_ref=src,
            dst_ref=dst,
            send_sem=self.send_sems.at[self.sends],
            recv_sem=self.recv_sems.at[slot],
            device_id=peer,
            device_id_type=MESH,
        )
        self.sends += 1
        return copy

    def push(self, src, dst, peer):
        copy = self.remote(src, dst, peer)
        copy.start()
        return copy


class ZGather:
    def __init__(self, here, copies, view):
        self.here, self.copies, self.view, self.drained = here, copies, view, False
        self.slots = [copies.slot() for _ in range(3)]

    def copy(self, place, peer, slot):
        block = self.view(place)
        return self.copies.remote(block, block, peer, self.slots[slot])

    def start(self):
        here = self.here
        self.near = self.copy(here.place, here.near, 0)
        self.near.start()
        self.far = self.copy(here.place, here.far, 1)
        self.on_far = self.copy(here.near_place, here.far, 2)
        self.on_near = self.copy(here.far_place, here.near, 1)
        self.last = self.copy(here.two_place, here.near, 2)
        pl.when(here.inner)(self.far.start)

    def first(self):
        @pl.when(self.here.inner)
        def _():
            self.near.wait_recv()
            self.on_far.start()
            self.far.wait_recv()
            self.on_near.start()

    def second(self):
        @pl.when(self.here.inner)
        def _():
            self.on_far.wait_recv()
            self.last.start()

    def arrive(self):
        @pl.when(self.here.outer)
        def _():
            self.near.wait_recv()
            self.on_near.wait_recv()
            self.last.wait_recv()

    def drain(self):
        if self.drained:
            return
        self.drained = True
        self.near.wait_send()

        @pl.when(self.here.inner)
        def _():
            for copy in (self.far, self.on_far, self.on_near, self.last):
                copy.wait_send()


def tiles(count, body):
    def step(i, carry):
        body(i)
        return carry

    lax.fori_loop(0, count, step, 0)


def part(index, size):
    return pl.ds(pl.multiple_of(index * size, size), size)


class RowReduce:
    def __init__(self, here, copies, bufs, acks=None):
        self.here, self.copies, self.acks = here, copies, acks
        (self.snd, self.rcv, self.acc, self.out, self.into) = bufs
        self.sent = []

    def begin(self, width):
        self.lanes = pl.ds(0, width)
        for copy in self.sent:
            copy.wait_send()
        self.sent, self.core = [], []

    def core_send(self, index):
        rows = pl.ds(index * 256, 256)
        self.core.append(self.copies.push(
                self.snd.at[rows, self.lanes], self.rcv.at[rows, self.lanes], self.here.core
            ))

    def add_core(self, first, count):
        acc, rcv, lanes = self.acc, self.rcv, self.lanes

        def body(i):
            at = pl.ds(pl.multiple_of(first + i * 64, 64), 64)
            acc[at, lanes] = acc[at, lanes] + rcv[at, lanes].astype(wide)

        tiles(count // 64, body)

    def round_out(self, first, count, extra=None):
        acc, out, into, lanes = self.acc, self.out, self.into, self.lanes

        def body(i):
            at = pl.ds(pl.multiple_of(first + i * 64, 64), 64)
            value = acc[at, lanes]
            if extra is not None:
                value = value + into[pl.ds(extra, 64), lanes].astype(wide)
            out[pl.ds(pl.multiple_of(first - 128 + i * 64, 64), 64), lanes] = value.astype(low)

        tiles(count // 64, body)

    def hand(self, first, end, peer):
        rows = pl.ds(first, end - first)
        return self.copies.push(
            self.out.at[rows, self.lanes], self.into.at[rows, self.lanes], peer
        )

    def diagonal(self):
        for copy in self.core:
            copy.wait_recv()
        self.add_core(384, 128)
        self.round_out(384, 128)
        self.diag_x = self.hand(256, 320, self.here.across)
        self.diag_y = self.hand(320, 384, self.here.mid)
        self.add_core(128, 256)
        self.round_out(128, 64)
        self.round_out(320, 64)
        self.add_core(0, 128)

    def sides(self):
        self.diag_y.wait_recv()
        self.round_out(192, 64, 320)
        self.over_x = self.hand(0, 128, self.here.across)
        self.diag_x.wait_recv()
        self.round_out(256, 64, 256)
        self.over_y = self.hand(128, 256, self.here.mid)
        self.sent = self.core + [self.diag_x, self.diag_y, self.over_x, self.over_y]

    def arrive(self):
        self.over_x.wait_recv()
        self.over_y.wait_recv()

    def total(self, at, size):
        acc, into, lanes = self.acc, self.into, self.lanes
        return (
            acc[pl.ds(at, size), lanes]
            + into[pl.ds(at, size), lanes].astype(wide)
            + into[pl.ds(at + 128, size), lanes].astype(wide)
        )

    def release(self):
        for index, peer in enumerate((self.here.core, self.here.across, self.here.mid)):
            pl.semaphore_signal(
                self.acks.at[index], inc=1, device_id=peer, device_id_type=MESH
            )

    def await_release(self):
        for index in range(3):
            pl.semaphore_wait(self.acks.at[index], 1)

    def drain(self):
        for copy in self.sent:
            copy.wait_send()


class RowGather:
    def __init__(self, here, copies, view, fixed=False):
        self.here, self.copies, self.view, self.fixed = here, copies, view, fixed
        self.sent, self.drained = [], False

    def start(self):
        here = self.here
        self.over_x = self.pair(0, 1, here.across)
        self.over_y = self.pair(0, 2, here.mid)
        self.cores = [self.pair(0, 4, here.core)]

    def pair(self, source, target, peer, half=None):
        src = self.view(source, half)
        dst = src if self.fixed else self.view(target, half)
        copy = self.copies.push(src, dst, peer)
        self.sent.append(copy)
        return copy

    def forward(self):
        here = self.here
        self.over_y.wait_recv()
        self.diag_x = self.pair(2, 3, here.across, 0)
        self.cores.append(self.pair(2, 6, here.core))
        self.over_x.wait_recv()
        self.diag_y = self.pair(1, 3, here.mid, 1)
        self.cores.append(self.pair(1, 5, here.core))

    def finish(self):
        self.diag_x.wait_recv()
        self.diag_y.wait_recv()
        self.cores.append(self.pair(3, 7, self.here.core))
        for copy in self.cores:
            copy.wait_recv()

    def drain(self):
        if not self.drained:
            for copy in self.sent:
                copy.wait_send()
        self.drained = True


def nn(left_in, right_in):
    return lax.dot_general(
        left_in, right_in, (((1,), (0,)), ((), ())), preferred_element_type=wide
    )


def nt(left_in, right_in):
    return lax.dot_general(
        left_in, right_in, (((1,), (1,)), ((), ())), preferred_element_type=wide
    )


def tn(left_in, right_in):
    return lax.dot_general(
        left_in, right_in, (((0,), (0,)), ((), ())), preferred_element_type=wide
    )


class ZReduce:
    def __init__(self, here, copies, base, spot, rows, columns, landing):
        self.here, self.copies, self.base, self.spot = here, copies, base, spot
        self.rows, self.columns, self.landing = rows, columns, landing
        self.slots = [copies.slot() for _ in range(5)]

    def copy(self, k, peer, slot):
        r, c = self.spot(k)
        block = self.base.at[pl.ds(r, self.rows), pl.ds(c, self.columns)]
        return self.copies.remote(block, self.landing.at[slot], peer, self.slots[slot])

    def outward(self, k):
        copy = self.copy(k, self.here.near, {3: 1, 2: 2, 1: 0}[k])
        setattr(self, f"out{k}", copy)
        pl.when(self.here.outer)(copy.start)

    def load(self, index, stage, slot):
        size = min(self.rows, 512)
        return [
            self.copies.local(
                self.landing.at[index, pl.ds(n * size, size), :],
                stage.at[slot, pl.ds(0, size), pl.ds(n * self.columns, self.columns)],
            )
            for n in range(self.rows // size)
        ]

    def add(self, target, stage, slots):
        size = min(self.rows, 512)
        r, c = self.spot(target)
        for n in range(self.rows // size):

            def body(i, n=n):
                at = pl.ds(pl.multiple_of(i * 64, 64), 64)
                mine = pl.ds(pl.multiple_of(r + n * size + i * 64, 64), 64)
                lanes = pl.ds(c, self.columns)
                value = self.base[mine, lanes].astype(wide)
                for slot in slots:
                    value = value + stage[
                        slot, at, pl.ds(n * self.columns, self.columns)
                    ].astype(wide)
                self.base[mine, lanes] = value.astype(low)

            tiles(size // 64, body)

    def pass_on(self, k, wait, index, stage, copy):
        wait.wait_recv()
        for load in self.load(index, stage, 0):
            load.wait()
        self.add(k, stage, [0])
        copy.start()

    def inward(self, step, stage):
        here = self.here
        if step == 0:
            self.in2 = self.copy(2, here.far, 4)
            args = (2, self.out3, 1, stage, self.in2)
        elif step == 1:
            self.in3 = self.copy(3, here.far, 3)
            args = (3, self.out2, 2, stage, self.in3)
        else:
            self.in1 = self.copy(1, here.near, 0)
            args = (1, self.in2, 4, stage, self.in1)

        @pl.when(here.inner)
        def _():
            self.pass_on(*args)

    def finish(self, stage):
        here = self.here
        self.out1.wait_recv()
        loads = self.load(0, stage, 0)

        @pl.when(here.inner)
        def _():
            self.in3.wait_recv()
            for load in self.load(3, stage, 1) + loads:
                load.wait()
            self.add(0, stage, [0, 1])

        @pl.when(here.outer)
        def _():
            for load in loads:
                load.wait()
            self.add(0, stage, [0])

    def drain(self):
        @pl.when(self.here.inner)
        def _():
            for copy in (self.in1, self.in2, self.in3):
                copy.wait_send()

        @pl.when(self.here.outer)
        def _():
            for copy in (self.out1, self.out2, self.out3):
                copy.wait_send()


def norm_back(value, grad, gain):
    r = lax.rsqrt(jnp.mean(value * value, axis=-1, keepdims=True) + epsilon)
    u = gain * grad
    lean = jnp.mean(u * value, axis=-1, keepdims=True)
    return r * u - value * (r * r * r * lean), grad * value * r


def exact(left_in, right_in, contract):
    return lax.dot_general(
        left_in, right_in, (contract, ((), ())), precision=highest, preferred_element_type=wide
    )


def layer_kernel(
    tok, col, row, cot_in, qkvw, outw, upw, downw, first, gains, second,
    o_block, o_input, o_gq, o_go, o_gu, o_gd, o_first, o_pack, s_hid, s_wq, l_q, l_o, l_u, l_d,
    toks, hid, units, cot, early, wo, wu, wd, cols, rows_info, qkvb, probs, att, acc,
    snd, rcv, out_buf, in_buf, proj, mid_buf, go, stage, top, own_tok, own_out,
    first_buf, slope, gates, dall, r_gate, r_inner, r_slope, r_dpre, r_rows, zpart, zland, gain_buf,
    pack, pack_plane, pack_side, pack_ring,
    local_sems, send_sems, recv_sems, acks,
):
    here = Plane()
    copies = Copies(local_sems, send_sems, recv_sems)
    here.greet()
    rank, share, side = here.rank, here.share, here.side
    owned = 128
    width = toks.shape[1]
    block = owned * SHARE
    head_width = wo.shape[0]
    unit_width = wu.shape[1]
    heads = head_width // HD
    own_rows = part(rank, owned)
    wq = early.at[:, 0 : 3 * head_width]
    act, gup = early.at[0:1024], early.at[1024:2048]
    sent, outs, done = [], [], []

    def to_peer(src, dst, peer):
        copy = copies.push(src, dst, peer)
        sent.append(copy)
        return copy

    def spread(src_of, dst):
        return [
            copies.local(src_of(here.shares[d]), dst)
            if d == 0
            else to_peer(src_of(here.shares[d]), dst, here.members[d])
            for d in range(SHARE)
        ]

    def landed(got):
        for i, copy in enumerate(got):
            if i % SHARE:
                copy.wait_recv()
            else:
                copy.wait()

    got_q = [
        spread(
            lambda t, j=j: qkvw.at[j, :, part(t, head_width)],
            wq.at[own_rows, j * head_width : (j + 1) * head_width],
        )
        for j in range(3)
    ]
    mine, other = part(side, owned), part(1 - side, owned)

    class Halves:
        def __init__(self, src, dst):
            self.dst = dst
            pairs = ((mine, 0), (other, owned))
            self.own = [copies.local(src(rows), dst(at)) for rows, at in pairs]
            self.mid = [to_peer(src(rows), dst(at + 256), here.mid) for rows, at in pairs]
            self.core = [to_peer(src(rows), dst(at + 512), here.core) for rows, at in pairs]

        def pass_on(self):
            for copy in self.mid:
                copy.wait_recv()
            self.last = [
                to_peer(self.dst(at), self.dst(at + 512), here.core) for at in (256, 384)
            ]

    tok_in = Halves(lambda r: tok.at[r, :], lambda at: toks.at[at : at + owned])
    col_in = Halves(lambda r: col.at[r, :], lambda at: cols.at[at : at + owned])
    row_in = Halves(
        lambda r: row.at[:, r],
        lambda at: rows_info.at[at // 256, :, at % 256 : at % 256 + owned],
    )
    got_o = spread(lambda t: outw.at[part(t, head_width), :], wo.at[:, own_rows])
    got_u = spread(lambda t: upw.at[:, part(t, unit_width)], wu.at[own_rows, :])
    got_d = spread(lambda t: downw.at[part(t, unit_width), :], wd.at[:, own_rows])
    cot_rows = Halves(lambda r: cot_in.at[r, :], lambda at: cot.at[at : at + owned])
    in_first = copies.local(first.at[0], first_buf)
    in_tok = copies.local(tok.at[mine, :], own_tok)

    g_q = [
        ZGather(here, copies, lambda k, d=d: wq.at[part(k * SHARE + here.shares[d], owned), :])
        for d in range(SHARE)
    ]
    g_o = ZGather(here, copies, lambda k: wo.at[:, part(k, block)])
    g_u = [
        ZGather(
            here,
            copies,
            lambda k, h=h: wu.at[pl.ds(pl.multiple_of(k * block + h * 256, 256), 256), :],
        )
        for h in range(2)
    ]
    g_d = [
        ZGather(here, copies, lambda k, h=h: wd.at[h * 512 : (h + 1) * 512, part(k, block)])
        for h in range(2)
    ]

    def fact(at, index):
        return cols[at, 2 * HD + index : 2 * HD + index + 1]

    def start_q(d):
        for got in got_q:
            if d:
                got[d].wait_recv()
            else:
                got[d].wait()
        g_q[d].start()

    start_q(0)
    start_q(1)

    def normalise(base):
        def body(i):
            at = pl.ds(pl.multiple_of(base + i * 64, 64), 64)
            x = toks[at, :].astype(wide)
            r = lax.rsqrt(jnp.mean(x * x, axis=-1, keepdims=True) + epsilon)
            hid[at, :] = (x * r * gains[0:1, :]).astype(low)

        tiles(4, body)

    def wait_all(waits):
        for wait in waits:
            wait()

    wait_all([c.wait for c in tok_in.own + col_in.own + row_in.own])
    normalise(0)

    def route(index, rows_of):
        made = exact(rows_of[0:owned, :].astype(wide), first_buf[...], ((1,), (0,)))
        sig = 1.0 / (1.0 + jnp.exp(-made))
        inner = made * sig
        logits = exact(inner, second[index], ((1,), (0,)))
        lane = lax.broadcasted_iota(jnp.int32, (owned, HD), 1)
        logits = jnp.where(lane < NB, logits, -1e30)
        raised = jnp.where(
            lane < NB, jnp.exp(logits - jnp.max(logits, axis=-1, keepdims=True)), 0.0
        )
        shares = raised / jnp.sum(raised, axis=-1, keepdims=True)
        hot = jnp.where(lane.astype(wide) == fact(pl.ds(0, owned), 2 + index), 1.0, 0.0)
        gate = NB * jnp.sum(shares * hot, axis=-1, keepdims=True)
        lean = hot - shares
        bare = exact(lean, second[index], ((1,), (1,))) * (sig * (1.0 + made * (1.0 - sig)))
        r_gate[index] = jnp.broadcast_to(gate, (owned, HD))
        r_inner[index] = inner
        r_slope[index] = lean if index else gate * lean
        r_dpre[index] = bare if index else gate * bare
        if index == 1:
            dall[0:owned, :] = bare.astype(low)

    def slope_tiles(index):
        def body(i):
            c = part(i, 256)
            slope[:, c] = exact(r_dpre[index], first_buf[c, :], ((1,), (1,)))

        tiles(8, body)

    in_first.wait()
    route(0, hid)
    in_first = copies.local(first.at[1], first_buf)
    start_q(2)
    start_q(3)
    g_q[0].first()
    g_q[1].first()
    wait_all([c.wait_recv for c in tok_in.core])
    normalise(512)
    g_q[0].second()
    g_q[1].second()
    g_q[2].first()
    g_q[3].first()
    tok_in.pass_on()
    normalise(256)
    g_q[2].second()
    g_q[3].second()
    wait_all([c.wait_recv for c in tok_in.last])
    normalise(768)
    save_hid = copies.local(hid, s_hid)
    landed(got_o)
    g_o.start()
    col_in.pass_on()
    row_in.pass_on()
    wait_all([c.wait_recv for c in col_in.core + row_in.core + col_in.last + row_in.last])
    g_o.first()
    landed(got_u)
    g_o.second()
    g_u[0].start()
    for one in g_q:
        one.arrive()
    save_wq = copies.local(wq, s_wq)

    for j in range(3):

        def qkv_tile(i, j=j):
            at = part(i, 512)
            made = nn(hid[at, :], wq[:, j * head_width : (j + 1) * head_width])
            if j < 2:
                cosine = cols[at, 0:HD]
                sine = cols[at, HD : 2 * HD]
                for h in range(heads):
                    one = made[:, h * HD : (h + 1) * HD]
                    turned = one * cosine + pltpu.roll(one, HD // 2, 1) * sine
                    qkvb[at, j * head_width + h * HD : j * head_width + (h + 1) * HD] = (
                        turned.astype(low)
                    )
            else:
                qkvb[at, j * head_width : (j + 1) * head_width] = made.astype(low)

        tiles(2, qkv_tile)

    g_u[0].first()
    g_u[1].start()

    first_head = (side * SHARE + share) * heads
    scale = HD ** (-0.5)
    for h in range(heads):
        head = (first_head + h).astype(wide)

        def attend_group(g, h=h, head=head):
            at = part(g, 256)
            query, keyed, value = (
                qkvb[at, pl.ds(j * head_width + h * HD, HD)] for j in range(3)
            )
            info = rows_info[g]
            seg_k, slot_k, bucket_k = info[0:1, :], info[1:2, :], info[2:3, :]
            reach_k = jnp.where(4.0 * bucket_k + 4.0 > head, 1.0, 0.0)
            slot_q = fact(at, 1)
            usable = (reach_k > 0.5) | (slot_k == slot_q)
            allowed = (fact(at, 0) == seg_k) & (slot_k <= slot_q) & usable
            scores = jnp.where(allowed, nt(query, keyed) * scale, -1e30)
            weights = jnp.exp(scores - jnp.max(scores, axis=-1, keepdims=True))
            p = weights / jnp.sum(weights, axis=-1, keepdims=True)
            probs[part(g * heads + h, 256), :] = p
            mixed = nn(p.astype(low), value)
            att[at, h * HD : (h + 1) * HD] = jnp.where(
                4.0 * fact(at, 2) + 4.0 > head, mixed, 0.0
            ).astype(low)

        tiles(SHARE, attend_group)

    reduce = RowReduce(here, copies, (snd, rcv, acc, out_buf, in_buf), acks)

    def partial_sums(term, extra=None):
        lanes = acc.shape[1] if extra is not None else width
        reduce.begin(lanes)
        for i in range(2):

            def send_tile(n, i=i):
                snd[i * 256 : (i + 1) * 256, part(n, 512)] = term(
                    pl.ds(512 + i * 256, 256), n
                ).astype(low)

            tiles(4, send_tile)
            if extra is not None:
                snd[i * 256 : (i + 1) * 256, width:lanes] = extra[
                    pl.ds(512 + i * 256, 256), :
                ].astype(low)
            reduce.core_send(i)

        def own_tile(n):
            acc[:, part(n, 512)] = term(pl.ds(0, 512), n)

        tiles(4, own_tile)
        if extra is not None:
            acc[:, width:lanes] = extra[0:512, :]

    g_o.arrive()
    partial_sums(lambda at, n: nn(att[at, :], wo[:, part(n, 512)]))
    g_u[0].second()
    reduce.diagonal()
    g_u[1].first()
    reduce.sides()
    g_u[1].second()
    landed(got_d)
    g_d[0].start()
    g_d[1].start()
    in_tok.wait()
    reduce.arrive()

    def row_tiles(body):
        def step(i):
            at = pl.multiple_of(i * 64, 64)
            body(at, pl.ds(at, 64))

        tiles(owned // 64, step)

    def middle_tile(at, rows):
        projected = reduce.total(at, 64)
        proj[rows, :] = projected
        middle = own_tok[rows, :].astype(wide) + r_gate[0, rows, 0:1] * projected
        mid_buf[rows, :] = middle
        r = lax.rsqrt(jnp.mean(middle * middle, axis=-1, keepdims=True) + epsilon)
        units[rows, :] = (middle * r * gains[1:2, :]).astype(low)

    row_tiles(middle_tile)
    reduce.release()

    def row_view(buf):
        def view(k, h):
            if h is None:
                return buf.at[k * owned : (k + 1) * owned]
            return buf.at[k * owned + h * 64 : k * owned + (h + 1) * 64]

        return view

    units_out = RowGather(here, copies, row_view(units))
    units_out.start()
    in_first.wait()
    route(1, units)
    gates[0:owned, :] = r_gate[1]
    gates_out = RowGather(here, copies, row_view(gates))
    dall_out = RowGather(here, copies, row_view(dall))
    gates_out.start()
    dall_out.start()

    def first_low(n):
        return go[pl.ds(pl.multiple_of(n % 2 * 512, 512), 512), part(n // 2, 256)]

    def first_tile(i):
        go[part(i % 8, 128), part(i // 8, 256)] = first_buf[part(i, 128), :].astype(low)

    tiles(16, first_tile)
    in_first = copies.local(first.at[0], first_buf)
    g_d[0].first()
    units_out.forward()
    gates_out.forward()
    dall_out.forward()
    g_d[1].first()
    units_out.finish()
    gates_out.finish()
    dall_out.finish()
    g_d[0].second()
    g_d[1].second()
    for one in g_u:
        one.arrive()

    first_unit = (side * SHARE + share) * unit_width

    def used_units(at, base, rows, columns):
        lane = lax.broadcasted_iota(jnp.int32, (rows, columns), 1) + base
        return lane.astype(wide) < (FF // NB) * (fact(at, 3) + 1.0)

    save_wq.wait()
    for one in g_q:
        one.drain()

    def up_tile(i):
        m, n = i % 2, i // 2
        at, c = part(m, 512), part(n, 512)
        made = nn(units[at, :], wu[:, c])
        acc[:, part(m * 2 + n, 512)] = made
        relu = jnp.maximum(made, 0.0)
        used = used_units(at, first_unit + n * 512, 512, 512)
        act[at, c] = jnp.where(used, relu * relu, 0.0).astype(low)

    tiles(4, up_tile)
    wait_all([c.wait for c in cot_rows.own])
    cot_rows.pass_on()
    wait_all([c.wait_recv for c in cot_rows.core + cot_rows.last])

    def live_cot(at):
        return jnp.where(fact(at, 4) > 0.5, cot[at, :].astype(wide), 0.0)

    for copy in tok_in.last + cot_rows.last:
        copy.wait_send()
        done.append(copy)

    def keep_tile(at, rows):
        top[rows, :] = live_cot(rows).astype(low)

    row_tiles(keep_tile)

    def scale_tile(i):
        at = part(i, 64)
        cot[at, :] = (gates[at, 0:1] * live_cot(at)).astype(low)

    tiles(16, scale_tile)

    gd, gu, gq = toks, hid, wd
    blocks = [here.place, here.near_place, here.two_place, here.far_place]
    z_d = ZReduce(here, copies, gd, lambda k: (0, k * block), unit_width, block, l_d)
    z_u = ZReduce(
        here, copies, gu, lambda k: (k % 2 * block, k // 2 * unit_width), block, unit_width, l_u
    )
    z_o = ZReduce(here, copies, go, lambda k: (k * head_width, 0), head_width, block, l_o)
    z_q = ZReduce(
        here, copies, gq, lambda k: (k % 2 * block, k // 2 * 1024), block, 3 * head_width, l_q
    )

    def down_block(k):
        def body(i):
            m = part(i, 512)
            gd[m, k * block : (k + 1) * block] = tn(
                act[:, m], cot[:, part(blocks[k], block)]
            ).astype(low)

        tiles(unit_width // 512, body)

    for k in (3, 2, 1):
        down_block(k)
        z_d.outward(k)
    down_block(0)
    z_d.inward(0, stage)
    z_d.inward(1, stage)
    for one in g_d:
        one.arrive()

    def gup_tile(m):
        at = part(m, 512)
        dots = jnp.zeros((512, 1), wide)
        for n in range(unit_width // 512):
            c = slice(n * 512, (n + 1) * 512)
            made = nt(cot[at, :], wd[c, :])
            used = used_units(at, first_unit + n * 512, 512, 512)
            relu = jnp.maximum(acc[:, part(m * 2 + n, 512)], 0.0)
            gup[at, c] = jnp.where(used, 2.0 * relu * made, 0.0).astype(low)
            dots = dots + jnp.sum(act[at, c].astype(wide) * made, axis=-1, keepdims=True)
        gates[at, :] = jnp.broadcast_to(dots, (512, HD))
        r_rows[at, 256:512] = (dots * dall[at, :].astype(wide)).astype(low)

    gates_out.drain()
    tiles(2, gup_tile)

    save_hid.wait()

    def up_block(k):
        r, c = k % 2 * block, k // 2 * unit_width

        def body(i):
            gu[r : r + block, pl.ds(pl.multiple_of(c + i * 512, 512), 512)] = tn(
                units[:, part(blocks[k], block)], gup[:, part(i, 512)]
            ).astype(low)

        tiles(unit_width // 512, body)

    up_block(3)
    z_u.outward(3)

    reduce.await_release()
    partial_sums(
        lambda at, n: nt(gup[at, :], wu[part(n, 512), :])
        + nt(r_rows[at, 256:512], first_low(n)),
        gates,
    )
    up_block(2)
    z_u.outward(2)
    reduce.diagonal()
    up_block(1)
    z_u.outward(1)
    z_d.inward(2, stage)
    reduce.sides()
    up_block(0)

    column = share * 2 + side
    ucol = dall
    dall_out.drain()

    def ucol_tile(i):
        ucol[part(i, 256), :] = units[part(i, 256), part(column, 256)]

    tiles(4, ucol_tile)
    units_out.drain()
    in_hid = copies.local(s_hid, units)
    for one in g_u:
        one.drain()
    in_wq = copies.local(s_wq, wu.at[:, 0 : 3 * head_width])

    r_rows_out = RowGather(here, copies, row_view(r_rows))

    def keep_gate(index, rows, weight):
        c = slice(index * 256, (index + 1) * 256)
        r_rows[rows, c] = (weight * r_dpre[index, rows, :]).astype(low)
        r_slope[index, rows, :] = weight * r_slope[index, rows, :]

    places = [here.place, here.near_place, here.two_place, here.far_place]
    planes = [None, here.near, here.two, here.far]

    def first_rows(k, h):
        target = here.shares[k // 4 + k // 2 % 2 * 2] * 2 + (side if k % 2 == 0 else 1 - side)
        base = target * 256
        if h is None:
            return o_first.at[:, pl.ds(pl.multiple_of(base, 256), 256), :]
        return o_first.at[:, pl.ds(pl.multiple_of(base + h * 128, 128), 128), :]

    first_out = RowGather(here, copies, first_rows, True)

    class FirstSum:
        def __init__(self):
            zpart[0] = tn(units[:, part(column, 256)], r_rows[:, 0:256]).astype(low)
            zpart[1] = tn(ucol[...], r_rows[:, 256:512]).astype(low)
            self.got = []
            for k in range(4):
                src, dst = zpart.at[:, part(places[k], 64), :], zland.at[here.place]
                self.got.append(
                    copies.local(src, dst) if k == 0 else to_peer(src, dst, planes[k])
                )

        def add(self):
            landed(self.got)
            for copy in self.got[1:]:
                copy.wait_send()
                done.append(copy)
            total = zland[0].astype(wide)
            for k in range(1, 4):
                total = total + zland[k].astype(wide)
            zpart[:, 0:64, :] = total.astype(low)
            at = pl.ds(pl.multiple_of(column * 256 + here.place * 64, 64), 64)
            src, dst = zpart.at[:, 0:64, :], o_first.at[:, at, :]
            self.got = [
                copies.local(src, dst) if k == 0 else to_peer(src, dst, planes[k])
                for k in range(4)
            ]

        def show(self):
            landed(self.got)
            first_out.start()

    reduce.arrive()
    gproj = cot
    gain_buf[...] = jnp.zeros_like(gain_buf)

    def grad_tile(at, rows):
        total = reduce.total(at, 64)
        grad = total[:, 0:width]
        keep_gate(1, rows, total[:, width : width + 1])
        back, gain_terms = norm_back(mid_buf[rows, :], grad, gains[1:2, :])
        grad_middle = top[rows, :].astype(wide) + back
        gproj[rows, :] = (r_gate[0, rows, 0:1] * grad_middle).astype(low)
        grad_gate = jnp.sum(grad_middle * proj[rows, :], axis=-1, keepdims=True)
        keep_gate(0, rows, grad_gate)
        r_gate[0, rows, :] = jnp.broadcast_to(grad_gate, (64, HD))
        proj[rows, :] = grad_middle
        gain_buf[1:2, :] = gain_buf[1:2, :] + jnp.sum(gain_terms, axis=0, keepdims=True)

    row_tiles(grad_tile)
    reduce.release()
    gproj_out = RowGather(here, copies, row_view(gproj))
    gproj_out.start()
    r_rows_out.start()
    in_first.wait()
    slope_tiles(0)
    gproj_out.forward()
    r_rows_out.forward()

    reduce.await_release()
    partial_sums(lambda at, n: nn(act[at, :], wd[:, part(n, 512)]))
    gproj_out.finish()
    r_rows_out.finish()
    in_hid.wait()
    sum_first = FirstSum()

    def deliver(piece_of, dst):
        for d in range(SHARE):
            src = piece_of(here.shares[d])
            if d == 0:
                outs.append(copies.local(src, dst))
            else:
                sent.append(copies.push(src, dst, here.members[d]))
                owed.append(sent[-1])

    owed = []

    def out_block(k):
        go[k * head_width : (k + 1) * head_width, :] = tn(
            att[...], gproj[:, part(blocks[k], block)]
        ).astype(low)

    for k in (3, 2, 1):
        out_block(k)
        z_o.outward(k)
    out_block(0)
    gatt, gqkv = gup, act

    def gatt_tile(i):
        at = part(i, 512)
        made = nt(gproj[at, :], wo[...]).astype(low)
        for h in range(heads):
            used = 4.0 * fact(at, 2) + 4.0 > (first_head + h).astype(wide)
            gatt[at, h * HD : (h + 1) * HD] = jnp.where(
                used, made[:, h * HD : (h + 1) * HD].astype(wide), 0.0
            ).astype(low)

    tiles(2, gatt_tile)

    for h in range(heads):

        def back_group(g, h=h):
            at = part(g, 256)
            lanes = [pl.ds(j * head_width + h * HD, HD) for j in range(3)]
            query, keyed, value = (qkvb[at, lane] for lane in lanes)
            grad = gatt[at, h * HD : (h + 1) * HD]
            p = probs[part(g * heads + h, 256), :]
            grad_p = nt(grad, value)
            row_dot = jnp.sum(p * grad_p, axis=-1, keepdims=True)
            grad_s = (p * (grad_p - row_dot)).astype(low)
            cosine = cols[at, 0:HD]
            sine = cols[at, HD : 2 * HD]
            for lane, turned in (
                (lanes[0], nn(grad_s, keyed) * scale),
                (lanes[1], tn(grad_s, query) * scale),
            ):
                gqkv[at, lane] = (
                    turned * cosine - pltpu.roll(turned, HD // 2, 1) * sine
                ).astype(low)
            gqkv[at, lanes[2]] = tn(p.astype(low), grad).astype(low)

        tiles(SHARE, back_group)

    def qkv_block(k):
        r, c = k % 2 * block, k // 2 * 1024
        for j in range(3):
            gq[r : r + block, c + j * head_width : c + (j + 1) * head_width] = tn(
                units[:, part(blocks[k], block)], gqkv[:, j * head_width : (j + 1) * head_width]
            ).astype(low)

    for one in g_d:
        one.drain()
    for k in (3, 2, 1):
        qkv_block(k)
        z_q.outward(k)
    qkv_block(0)

    reduce.diagonal()
    z_u.inward(0, stage)
    reduce.sides()
    z_u.inward(1, stage)
    reduce.arrive()

    def block_tile(at, rows):
        own_out[rows, :] = jnp.where(
            fact(rows, 4) > 0.5,
            mid_buf[rows, :] + r_gate[1, rows, 0:1] * reduce.total(at, 64),
            0.0,
        ).astype(low)

    row_tiles(block_tile)
    reduce.release()
    shown = copies.local(own_out, o_block.at[mine])
    shown_far = to_peer(own_out, o_block.at[mine], here.across)

    in_wq.wait()
    reduce.await_release()
    partial_sums(
        lambda at, n: nt(gqkv[at, 0 : 3 * head_width], wu[part(n, 512), 0 : 3 * head_width])
    )
    z_d.finish(stage)
    deliver(lambda t: gd.at[:, part(t, owned)], o_gd.at[part(share, unit_width), :])
    reduce.diagonal()
    z_u.inward(2, stage)
    z_o.inward(0, stage)
    z_o.inward(1, stage)
    reduce.sides()
    sum_first.add()
    z_q.inward(0, stage)
    shown.wait()
    shown_far.wait()
    done.append(shown_far)
    reduce.arrive()

    def input_tile(at, rows):
        grad = reduce.total(at, 64) + r_gate[0, rows, 0:1] * slope[rows, :]
        back, gain_terms = norm_back(own_tok[rows, :].astype(wide), grad, gains[0:1, :])
        own_out[rows, :] = (proj[rows, :] + back).astype(low)
        gain_buf[0:1, :] = gain_buf[0:1, :] + jnp.sum(gain_terms, axis=0, keepdims=True)

    row_tiles(input_tile)
    outs.append(copies.local(own_out, o_input.at[mine]))
    input_far = copies.push(own_out, o_input.at[mine], here.across)

    for index in range(2):
        for j in range(8):
            pack[index * 8 + j : index * 8 + j + 1, :] = gain_buf[
                index : index + 1, j * 256 : (j + 1) * 256
            ]
        made = exact(r_slope[index], r_inner[index], ((0,), (0,)))
        pack[16 + index * 8 : 24 + index * 8, :] = made[0:8, :]
        lane = lax.broadcasted_iota(jnp.int32, (owned, 256), 1)
        own = pl.ds(0, owned)
        hot = (lane.astype(wide) == fact(own, 2 + index)) & (fact(own, 4) > 0.5)
        count = jnp.sum(jnp.where(hot, 1.0, 0.0), axis=0, keepdims=True)
        pack[32 + index * 8 : 40 + index * 8, :] = jnp.broadcast_to(count, (8, 256))

    def sum_slots(buf, count):
        total = buf[0]
        for k in range(1, count):
            total = total + buf[k]
        return total

    got = [
        copies.local(pack, pack_plane.at[share])
        if d == 0
        else to_peer(pack, pack_plane.at[share], here.members[d])
        for d in range(SHARE)
    ]
    z_q.inward(1, stage)
    landed(got)
    for copy in got[1:]:
        copy.wait_send()
        done.append(copy)
    pack[...] = sum_slots(pack_plane, SHARE)
    got = [
        copies.local(pack, pack_side.at[side]),
        to_peer(pack, pack_side.at[side], here.across),
    ]
    landed(got)
    got[1].wait_send()
    done.append(got[1])
    pack[...] = pack_side[0] + pack_side[1]
    got = [
        copies.local(pack, pack_ring.at[here.place])
        if k == 0
        else to_peer(pack, pack_ring.at[here.place], planes[k])
        for k in range(4)
    ]

    z_o.inward(2, stage)
    sum_first.show()
    z_u.finish(stage)
    deliver(lambda t: gu.at[part(t, owned), 0:unit_width], o_gu.at[:, part(share, unit_width)])
    z_q.inward(2, stage)
    first_out.forward()
    z_o.finish(stage)
    deliver(
        lambda t: go.at[0:head_width, part(t, owned)], o_go.at[part(share, head_width), :]
    )
    first_out.finish()
    z_q.finish(stage)
    for j in range(3):
        deliver(
            lambda t, j=j: gq.at[part(t, owned), j * head_width : (j + 1) * head_width],
            o_gq.at[j, :, part(share, head_width)],
        )
    landed(got)
    for copy in got[1:]:
        copy.wait_send()
        done.append(copy)
    pack[...] = sum_slots(pack_ring, 4)
    outs.append(copies.local(pack, o_pack))

    drains = [g_o] + g_q + g_u + g_d + [z_d, z_u, z_o, z_q, reduce, units_out, gates_out, dall_out]
    for one in drains + [gproj_out, r_rows_out, first_out]:
        one.drain()
    input_far.wait()
    for copy in owed:
        copy.wait_recv()
    for copy in outs:
        copy.wait()
    for copy in sent:
        if not any(copy is one for one in done):
            copy.wait_send()
    copies.check()


def plane(mesh):
    fsdp = mesh.shape["fsdp"]
    ring_size = fsdp // SHARE

    def shards(
        tokens,
        head_bucket,
        ffn_bucket,
        lengths,
        norm_gains,
        qkv_weight,
        out_weight,
        up_weight,
        down_weight,
        router_first,
        router_second,
        cotangent,
    ):
        rows, width = tokens.shape
        half = rows // 2
        local_units = up_weight.shape[1]
        units = local_units // SHARE
        local_width = out_weight.shape[0]
        head_width = local_width // SHARE
        heads = head_width // HD
        owned = width // fsdp
        block = width // ring_size
        plane_rows = SHARE * rows

        slot_ids = jnp.arange(rows, dtype=jnp.int32)
        segment, position, live_rows = (a[0] for a in layout(lengths, slot_ids))
        frequency = theta_base ** (-2.0 * jnp.arange(HD // 2, dtype=wide) / HD)
        angles = position.astype(wide)[:, None] * frequency
        cosine, sine = jnp.cos(angles), jnp.sin(angles)
        facts = jnp.stack(
            [segment, slot_ids, head_bucket, ffn_bucket, live_rows.astype(jnp.int32)], axis=1
        ).astype(wide)
        col = jnp.concatenate(
            [cosine, cosine, -sine, sine, jnp.pad(facts, ((0, 0), (0, HD - facts.shape[1])))],
            axis=1,
        )
        row = jnp.pad(facts.T, ((0, 8 - facts.shape[1]), (0, 0)))
        second = jnp.pad(router_second, ((0, 0), (0, 0), (0, HD - NB)))
        b16, f32 = low, wide
        hidden = router_first.shape[2]
        small = 48

        def shape(*dims):
            return jax.ShapeDtypeStruct(dims[1:], dims[0])

        def buffer(*dims):
            return pltpu.VMEM(dims[1:], dims[0])

        anywhere = pl.BlockSpec(memory_space=pl.ANY)
        vmem = pl.BlockSpec(memory_space=pltpu.VMEM)
        (
            block_out,
            input_grad,
            raw_qkv,
            raw_out,
            raw_up,
            raw_down,
            raw_first,
            sums,
            *_,
        ) = pl.pallas_call(
            layer_kernel,
            out_shape=[
                shape(b16, rows, width),
                shape(b16, rows, width),
                shape(b16, 3, owned, local_width),
                shape(b16, local_width, owned),
                shape(b16, owned, local_units),
                shape(b16, local_units, owned),
                shape(b16, *router_first.shape),
                shape(f32, small, 256),
                shape(b16, plane_rows, width),
                shape(b16, width, 3 * head_width),
                shape(b16, 5, block, 3 * head_width),
                shape(b16, 5, head_width, block),
                shape(b16, 5, block, units),
                shape(b16, 5, units, block),
            ],
            in_specs=[anywhere] * 9 + [vmem] * 2,
            out_specs=[anywhere] * 14,
            scratch_shapes=[
                buffer(b16, plane_rows, width),
                buffer(b16, plane_rows, width),
                buffer(b16, plane_rows, width),
                buffer(b16, plane_rows, width),
                buffer(b16, 2 * plane_rows, units),
                buffer(b16, head_width, width),
                buffer(b16, width, units),
                buffer(b16, units, width),
                buffer(f32, plane_rows, 3 * HD),
                buffer(f32, SHARE, 8, rows),
                buffer(b16, plane_rows, 3 * head_width),
                buffer(f32, SHARE * heads * rows, rows),
                buffer(b16, plane_rows, head_width),
                buffer(f32, plane_rows // 2, width + HD),
                buffer(b16, plane_rows // 2, width + HD),
                buffer(b16, plane_rows // 2, width + HD),
                buffer(b16, 3 * half, width + HD),
                buffer(b16, 3 * half, width + HD),
                buffer(f32, half, width),
                buffer(f32, half, width),
                buffer(b16, 4 * head_width, block),
                buffer(b16, 2, block, units),
                buffer(b16, half, width),
                buffer(b16, half, width),
                buffer(b16, half, width),
                buffer(f32, width, hidden),
                buffer(f32, half, width),
                buffer(f32, plane_rows, HD),
                buffer(b16, plane_rows, hidden),
                buffer(f32, 2, half, HD),
                buffer(f32, 2, half, hidden),
                buffer(f32, 2, half, HD),
                buffer(f32, 2, half, hidden),
                buffer(b16, plane_rows, 2 * hidden),
                buffer(b16, 2, 256, hidden),
                buffer(b16, 4, 2, 64, hidden),
                buffer(f32, 8, width),
                buffer(f32, small, 256),
                buffer(f32, SHARE, small, 256),
                buffer(f32, 2, small, 256),
                buffer(f32, 4, small, 256),
                pltpu.SemaphoreType.DMA((128,)),
                pltpu.SemaphoreType.DMA((256,)),
                pltpu.SemaphoreType.DMA((256,)),
                pltpu.SemaphoreType.REGULAR((3,)),
            ],
            compiler_params=pltpu.CompilerParams(
                collective_id=0, has_side_effects=True, vmem_limit_bytes=63 * 2**20
            ),
        )(
            tokens,
            col,
            row,
            cotangent,
            jnp.transpose(qkv_weight, (1, 0, 2)),
            out_weight,
            up_weight,
            down_weight,
            router_first,
            norm_gains,
            second,
        )
        grad_qkv = jnp.transpose(raw_qkv, (1, 0, 2)).astype(wide)
        grad_out, grad_up, grad_down, grad_first = (
            a.astype(wide) for a in (raw_out, raw_up, raw_down, raw_first)
        )
        grad_gains = sums[0:16].reshape(2, width)
        grad_second = jnp.stack([sums[16 : 16 + NB].T, sums[24 : 24 + NB].T])
        usage = jnp.stack([sums[32, :NB], sums[40, :NB]])
        return (
            block_out,
            input_grad,
            grad_gains,
            grad_qkv,
            grad_out,
            grad_up,
            grad_down,
            grad_first,
            grad_second,
            usage,
        )

    return shards


def solution(mesh):
    shards = plane(mesh) if mesh.shape["fsdp"] == 4 * SHARE else general(mesh)
    in_specs = (
        P("fsdp", None),
        P("fsdp"),
        P("fsdp"),
        P("fsdp", None),
        P(),
        P("fsdp", None, "tensor"),
        P("tensor", "fsdp"),
        P("fsdp", "tensor"),
        P("tensor", "fsdp"),
        P(),
        P(),
        P("fsdp", None),
    )
    out_specs = (
        P("fsdp", None),
        P("fsdp", None),
        P(),
        P("fsdp", None, "tensor"),
        P("tensor", "fsdp"),
        P("fsdp", "tensor"),
        P("tensor", "fsdp"),
        P(),
        P(),
        P(),
    )
    return jax.shard_map(
        shards, mesh=mesh, in_specs=in_specs, out_specs=out_specs, check_vma=False
    )
```

```python
from functools import partial

import jax
import jax.numpy as jnp
from jax import lax
from jax.experimental import pallas as pl
from jax.experimental.pallas import tpu as pltpu
from jax.sharding import PartitionSpec as P

HEADS = 16
HD = 128
FF = 8192
NB = 4
SHARE = 4

epsilon = 1e-05
theta_base = 10000.0
highest = lax.Precision.HIGHEST
low = jnp.bfloat16
wide = jnp.float32
MESH = pl.DeviceIdType.MESH


def norm_piece(values_in, gain_row):
    return (
        values_in
        * lax.rsqrt(jnp.mean(values_in * values_in, axis=-1, keepdims=True) + epsilon)
        * gain_row
    )


def route_piece(hidden_in, router_in, router_out, bucket):
    inner = jax.nn.silu(jnp.dot(hidden_in, router_in, precision=highest))
    logits = jnp.dot(inner, router_out, precision=highest)
    probs_all = jax.nn.softmax(logits, axis=-1)
    onehot = (bucket[:, None] == jnp.arange(NB, dtype=jnp.int32)[None, :]).astype(wide)
    return NB * jnp.sum(probs_all * onehot, axis=-1)


def dot(left_in, right_in):
    return jnp.dot(left_in, right_in, preferred_element_type=wide)


def dot_rows(left_in, right_in):
    return lax.dot_general(
        left_in, right_in, (((0,), (0,)), ((), ())), preferred_element_type=wide
    )


def dot_cols(left_in, right_in):
    return lax.dot_general(
        left_in, right_in, (((1,), (1,)), ((), ())), preferred_element_type=wide
    )


def rotate(operand, cosine, sine_table):
    half_dim = operand.shape[-1] // 2
    lead_half = operand[..., :half_dim]
    tail_half = operand[..., half_dim:]
    return jnp.concatenate(
        [lead_half * cosine - tail_half * sine_table, tail_half * cosine + lead_half * sine_table],
        axis=-1,
    )


def layout(length_rows, slot_ids):
    seq_count = length_rows.shape[1]
    order = jnp.arange(seq_count, dtype=jnp.int32)
    seq_ends = jnp.sum(
        jnp.where(order[None, None, :] <= order[None, :, None], length_rows[:, None, :], 0), axis=2
    )
    seq_starts = seq_ends - length_rows
    slots = slot_ids[None, :, None]
    member = (slots >= seq_starts[:, None, :]) & (slots < seq_ends[:, None, :])
    seq_of = jnp.sum(jnp.where(member, jnp.arange(seq_count, dtype=jnp.int32), 0), axis=2)
    live_rows = jnp.any(member, axis=2)
    seq_begin = jnp.sum(jnp.where(member, seq_starts[:, None, :], 0), axis=2)
    segment = jnp.where(live_rows, seq_of, seq_count + slot_ids[None, :])
    position = slot_ids[None, :] - seq_begin
    return segment, position, live_rows


def general(mesh):
    fsdp = mesh.shape["fsdp"]
    ring_size = fsdp // SHARE

    def hop(moved, bits):
        return lax.ppermute(moved, "fsdp", [(i, i ^ bits) for i in range(fsdp)])

    def cross(moved):
        return lax.ppermute(moved, "tensor", [(0, 1), (1, 0)])

    def shards(
        tokens,
        head_bucket,
        ffn_bucket,
        lengths,
        norm_gains,
        qkv_weight,
        out_weight,
        up_weight,
        down_weight,
        router_first,
        router_second,
        cotangent,
    ):
        rows, width = tokens.shape
        half = rows // 2
        rank = lax.axis_index("fsdp")
        side = lax.axis_index("tensor")
        share = rank % SHARE
        place = rank // SHARE
        local_units = up_weight.shape[1]
        units = local_units // SHARE
        local_width = out_weight.shape[0]
        head_width = local_width // SHARE
        heads = head_width // HD
        owned = width // fsdp
        block = width // ring_size

        chain = [None, None]

        def ring(moved, stream):
            if chain[stream] is not None:
                moved, _ = lax.optimization_barrier((moved, chain[stream]))
            got = lax.ppermute(
                moved, "fsdp", [(i, (i + SHARE) % fsdp) for i in range(fsdp)]
            )
            chain[stream] = got
            return got

        def place_at(step):
            return (place - step) % ring_size

        def own_half(arr):
            return lax.dynamic_slice_in_dim(arr, side * half, half, 0)

        def relative(arr):
            return jnp.concatenate(
                [own_half(arr), lax.dynamic_slice_in_dim(arr, (1 - side) * half, half, 0)], axis=0
            )

        def gather_rows(arr):
            other = hop(arr, 2)
            plane = jnp.concatenate([arr[:half], other[:half], arr[half:], other[half:]], axis=0)
            return jnp.concatenate([plane, hop(plane, 1)], axis=0)

        def gather_halves(arr):
            pair = jnp.concatenate([arr, hop(arr, 2)], axis=0)
            plane = jnp.concatenate([pair, cross(pair)], axis=0)
            return jnp.concatenate([plane, hop(plane, 1)], axis=0)

        def reduce_rows(keep, send):
            total = keep + hop(send.astype(low), 1).astype(wide)
            total = total[: 2 * half] + cross(total[2 * half :].astype(low)).astype(wide)
            return total[:half] + hop(total[half:].astype(low), 2).astype(wide)

        def whole_rows(arr):
            other = cross(arr)
            return jnp.where(
                side == 0,
                jnp.concatenate([arr, other], axis=0),
                jnp.concatenate([other, arr], axis=0),
            )

        def spread(pieces_for, axis):
            out = None
            for bits in range(SHARE):
                piece = pieces_for(share ^ bits)
                got = piece if bits == 0 else hop(piece, bits)
                if out is None:
                    dims = list(got.shape)
                    dims[axis] *= SHARE
                    out = jnp.zeros(dims, got.dtype)
                out = lax.dynamic_update_slice_in_dim(
                    out, got, (share ^ bits) * got.shape[axis], axis
                )
            return out

        def ring_gather(own, axis):
            dims = list(own.shape)
            dims[axis] = width
            out = jnp.zeros(dims, own.dtype)
            mid = own.shape[0] // 2
            moving = [own[:mid], own[mid:]]
            for step in range(ring_size):
                if step:
                    moving = [ring(moving[s], s) for s in range(2)]
                base = place_at(step) * block
                for s in range(2):
                    if axis == 0:
                        at = (base + s * mid, 0)
                    else:
                        at = (s * mid, base)
                    out = lax.dynamic_update_slice(out, moving[s], at)
            return out

        def ring_reduce(term):
            moving = [None, None]
            for step in range(1, ring_size):
                for s in range(2):
                    part = term(place_at(step), s)
                    if moving[s] is not None:
                        part = part + moving[s].astype(wide)
                    moving[s] = part.astype(low)
                for s in range(2):
                    moving[s] = ring(moving[s], s)
            return [term(place, s) + moving[s].astype(wide) for s in range(2)]

        def scatter_back(parts, axis):
            joined = jnp.concatenate(parts, axis=0)
            other = 1 - axis
            out_dims = list(joined.shape)
            out_dims[axis] = owned
            stride = out_dims[other]
            out_dims[other] *= SHARE
            out = jnp.zeros(out_dims, wide)
            for bits in range(SHARE):
                piece = lax.dynamic_slice_in_dim(joined, (share ^ bits) * owned, owned, axis)
                if bits:
                    piece = hop(piece.astype(low), bits).astype(wide)
                out = lax.dynamic_update_slice_in_dim(out, piece, (share ^ bits) * stride, other)
            return out

        def qkv_piece(target):
            return lax.dynamic_slice_in_dim(
                qkv_weight, target * head_width, head_width, 2
            ).reshape(owned, 3 * head_width)

        qkv_block = spread(qkv_piece, 0)
        rel_tokens = relative(tokens)
        rel_cot = relative(cotangent)
        ints = relative(jnp.stack([head_bucket, ffn_bucket], axis=1))
        qkv_full = ring_gather(qkv_block, 0)
        all_tokens = gather_rows(rel_tokens)
        buckets = gather_rows(ints)
        pair_lengths = jnp.concatenate([lengths, hop(lengths, 2)], axis=0)
        group_lengths = jnp.concatenate([pair_lengths, hop(pair_lengths, 1)], axis=0)

        out_block = spread(
            lambda t: lax.dynamic_slice_in_dim(out_weight, t * head_width, head_width, 0), 1
        )
        out_full = ring_gather(out_block, 1)
        up_block = spread(lambda t: lax.dynamic_slice_in_dim(up_weight, t * units, units, 1), 0)
        up_full = ring_gather(up_block, 0)
        down_block = spread(
            lambda t: lax.dynamic_slice_in_dim(down_weight, t * units, units, 0), 1
        )
        down_full = ring_gather(down_block, 1)
        all_cot = gather_rows(rel_cot)

        slot_ids = jnp.concatenate(
            [
                side * half + jnp.arange(half, dtype=jnp.int32),
                (1 - side) * half + jnp.arange(half, dtype=jnp.int32),
            ]
        )
        segment, position, live_groups = layout(group_lengths, slot_ids)

        def to_groups(arr):
            tail = arr.shape[1:]
            arr = arr.reshape((2, 2, 2, half) + tail)
            return jnp.swapaxes(arr, 1, 2).reshape((SHARE, rows) + tail)

        def from_groups(arr):
            tail = arr.shape[2:]
            arr = arr.reshape((2, 2, 2, half) + tail)
            return jnp.swapaxes(arr, 1, 2).reshape((8 * half,) + tail)

        live_all = from_groups(live_groups)
        all_heads = buckets[:, 0]
        all_widths = buckets[:, 1]

        own_tokens = rel_tokens[:half].astype(wide)
        own_heads = all_heads[:half]
        own_widths = all_widths[:half]
        own_live = live_all[:half]

        block_in = all_tokens.astype(wide)
        hidden_heads = norm_piece(block_in, norm_gains[0]).astype(low)
        own_normed, norm_heads_back = jax.vjp(norm_piece, own_tokens, norm_gains[0])
        gate_heads, route_heads_back = jax.vjp(
            partial(route_piece, bucket=own_heads),
            own_normed.astype(low).astype(wide),
            router_first[0],
            router_second[0],
        )
        head_ids = side * (local_width // HD) + share * heads + jnp.arange(heads, dtype=jnp.int32)
        head_used = head_ids[None, :] < HEADS // NB * (all_heads[:, None] + 1)
        unit_ids = side * local_units + share * units + jnp.arange(units, dtype=jnp.int32)
        unit_used = unit_ids[None, :] < FF // NB * (all_widths[:, None] + 1)

        half_dim = HD // 2
        frequency = theta_base ** (-2.0 * jnp.arange(half_dim, dtype=wide) / HD)
        angles = position.astype(wide)[:, :, None] * frequency
        cosine = jnp.cos(angles)[:, :, None, :]
        sine_table = jnp.sin(angles)[:, :, None, :]
        qkv_all = to_groups(dot(hidden_heads, qkv_full).reshape(8 * half, 3, heads, HD))
        query = rotate(qkv_all[:, :, 0], cosine, sine_table).astype(low)
        keyed = rotate(qkv_all[:, :, 1], cosine, sine_table).astype(low)
        value = qkv_all[:, :, 2].astype(low)
        group_used = to_groups(head_used)
        same_seq = segment[:, :, None] == segment[:, None, :]
        causal = slot_ids[None, :] <= slot_ids[:, None]
        diagonal = slot_ids[None, :] == slot_ids[:, None]
        key_used = jnp.swapaxes(group_used, 1, 2)
        allowed = (same_seq & causal)[:, None] & (key_used[:, :, None, :] | diagonal)
        scale = HD ** (-0.5)
        scores = jnp.einsum("gqhe,gkhe->ghqk", query, keyed, preferred_element_type=wide) * scale
        scores = jnp.where(allowed, scores, -1e30)
        row_top = jnp.max(scores, axis=-1, keepdims=True)
        weights = jnp.exp(scores - row_top)
        probs = weights / jnp.sum(weights, axis=-1, keepdims=True)
        probs_low = probs.astype(low)
        mixed = jnp.einsum("ghqk,gkhe->gqhe", probs_low, value, preferred_element_type=wide)
        mixed = jnp.where(group_used[..., None], mixed, 0.0).astype(low)
        attended = from_groups(mixed).reshape(8 * half, head_width)

        def partial_rows(left_in, matrix, product):
            keep = product(left_in[: 4 * half], matrix)
            send = product(left_in[4 * half :], matrix)
            return reduce_rows(keep, send)

        projected = partial_rows(attended, out_full, dot)

        middle = own_tokens + gate_heads[:, None] * projected
        normed_units, norm_units_back = jax.vjp(norm_piece, middle, norm_gains[1])
        own_units = normed_units.astype(low)
        hidden_units = gather_halves(own_units)
        gate_units, route_units_back = jax.vjp(
            partial(route_piece, bucket=own_widths),
            own_units.astype(wide),
            router_first[1],
            router_second[1],
        )
        all_gates = gather_halves(gate_units[:, None])
        upward = dot(hidden_units, up_full)
        activated = jnp.where(unit_used, jnp.square(jax.nn.relu(upward)), 0.0).astype(low)
        grad_top_all = jnp.where(live_all[:, None], all_cot.astype(wide), 0.0)
        grad_down_in = (all_gates * grad_top_all).astype(low)

        def down_term(at, s):
            mid = units // 2
            return dot_rows(
                activated[:, s * mid : (s + 1) * mid],
                lax.dynamic_slice_in_dim(grad_down_in, at * block, block, 1),
            )

        grad_down = scatter_back(ring_reduce(down_term), 1)

        downward = partial_rows(activated, down_full, dot)
        own_out = jnp.where(
            own_live[:, None], middle + gate_units[:, None] * downward, 0.0
        ).astype(low)
        block_out = whole_rows(own_out)
        grad_top = jnp.where(own_live[:, None], rel_cot[:half].astype(wide), 0.0)
        grad_gate_units = jnp.sum(grad_top * downward, axis=1)

        grad_act = dot_cols(grad_down_in, down_full)
        grad_up_in = jnp.where(unit_used, 2.0 * jax.nn.relu(upward) * grad_act, 0.0).astype(low)

        def up_term(at, s):
            mid = block // 2
            return dot_rows(
                lax.dynamic_slice_in_dim(hidden_units, at * block + s * mid, mid, 1), grad_up_in
            )

        grad_up = scatter_back(ring_reduce(up_term), 0)
        route_units_grads = route_units_back(grad_gate_units)
        grad_hidden_units = partial_rows(grad_up_in, up_full, dot_cols) + route_units_grads[0]
        norm_units_grads = norm_units_back(grad_hidden_units)
        grad_middle = grad_top + norm_units_grads[0]
        grad_gate_heads = jnp.sum(grad_middle * projected, axis=1)
        grad_projected = gather_halves((gate_heads[:, None] * grad_middle).astype(low))

        def out_term(at, s):
            mid = head_width // 2
            return dot_rows(
                attended[:, s * mid : (s + 1) * mid],
                lax.dynamic_slice_in_dim(grad_projected, at * block, block, 1),
            )

        grad_out = scatter_back(ring_reduce(out_term), 1)
        grad_attended = to_groups(
            dot_cols(grad_projected, out_full).astype(low).reshape(8 * half, heads, HD)
        )
        grad_attended = jnp.where(group_used[..., None], grad_attended, jnp.zeros((), low))
        grad_value = jnp.einsum(
            "ghqk,gqhe->gkhe", probs_low, grad_attended, preferred_element_type=wide
        )
        grad_probs = jnp.einsum(
            "gqhe,gkhe->ghqk", grad_attended, value, preferred_element_type=wide
        )
        row_dot = jnp.sum(probs * grad_probs, axis=-1, keepdims=True)
        grad_scores = (probs * (grad_probs - row_dot)).astype(low)
        grad_query = (
            jnp.einsum("ghqk,gkhe->gqhe", grad_scores, keyed, preferred_element_type=wide) * scale
        )
        grad_keyed = (
            jnp.einsum("ghqk,gqhe->gkhe", grad_scores, query, preferred_element_type=wide) * scale
        )
        grad_qkv_in = jnp.stack(
            [
                rotate(grad_query, cosine, -sine_table),
                rotate(grad_keyed, cosine, -sine_table),
                grad_value,
            ],
            axis=2,
        ).astype(low)
        grad_qkv_in = from_groups(grad_qkv_in).reshape(8 * half, 3 * head_width)

        def qkv_term(at, s):
            mid = block // 2
            return dot_rows(
                lax.dynamic_slice_in_dim(hidden_heads, at * block + s * mid, mid, 1), grad_qkv_in
            )

        qkv_parts = ring_reduce(qkv_term)
        joined = jnp.concatenate(qkv_parts, axis=0)
        grad_qkv = jnp.zeros((owned, 3, local_width), wide)
        for bits in range(SHARE):
            piece = lax.dynamic_slice_in_dim(joined, (share ^ bits) * owned, owned, 0)
            if bits:
                piece = hop(piece.astype(low), bits).astype(wide)
            grad_qkv = lax.dynamic_update_slice_in_dim(
                grad_qkv, piece.reshape(owned, 3, head_width), (share ^ bits) * head_width, 2
            )

        route_heads_grads = route_heads_back(grad_gate_heads)
        grad_hidden_heads = partial_rows(grad_qkv_in, qkv_full, dot_cols) + route_heads_grads[0]
        norm_heads_grads = norm_heads_back(grad_hidden_heads)
        input_grad = whole_rows((grad_middle + norm_heads_grads[0]).astype(low))

        def total_small(arr):
            arr = arr + cross(arr)
            bits = 1
            while bits < fsdp:
                arr = arr + hop(arr, bits)
                bits *= 2
            return arr

        def total_large(arr):
            steps = [1, "tensor"] + [2**i for i in range(1, fsdp.bit_length() - 1)]
            for bits in steps:
                mid = arr.shape[0] // 2
                me = side if bits == "tensor" else (rank // bits) % 2
                send = lax.dynamic_slice_in_dim(arr, (1 - me) * mid, mid, 0)
                keep = lax.dynamic_slice_in_dim(arr, me * mid, mid, 0)
                arr = keep + (cross(send) if bits == "tensor" else hop(send, bits))
            for bits in reversed(steps):
                me = side if bits == "tensor" else (rank // bits) % 2
                other = cross(arr) if bits == "tensor" else hop(arr, bits)
                arr = jnp.where(
                    me == 0,
                    jnp.concatenate([arr, other], axis=0),
                    jnp.concatenate([other, arr], axis=0),
                )
            return arr

        bucket_ids = jnp.arange(NB, dtype=jnp.int32)[None, :]
        head_counts = jnp.sum(
            jnp.where(own_live[:, None] & (own_heads[:, None] == bucket_ids), 1.0, 0.0), axis=0
        )
        width_counts = jnp.sum(
            jnp.where(own_live[:, None] & (own_widths[:, None] == bucket_ids), 1.0, 0.0), axis=0
        )
        units_small = total_small(
            jnp.concatenate(
                [norm_units_grads[1], route_units_grads[2].reshape(-1), head_counts, width_counts]
            )
        )
        heads_small = total_small(
            jnp.concatenate([norm_heads_grads[1], route_heads_grads[2].reshape(-1)])
        )
        first_units = total_large(route_units_grads[1])
        first_heads = total_large(route_heads_grads[1])
        second_shape = router_second.shape[1:]
        second_size = second_shape[0] * second_shape[1]
        grad_gains = jnp.stack([heads_small[:width], units_small[:width]])
        grad_second = jnp.stack(
            [
                heads_small[width : width + second_size].reshape(second_shape),
                units_small[width : width + second_size].reshape(second_shape),
            ]
        )
        usage = units_small[width + second_size :].reshape(2, NB)
        grad_first = jnp.stack([first_heads, first_units])
        return (
            block_out,
            input_grad,
            grad_gains,
            grad_qkv,
            grad_out,
            grad_up,
            grad_down,
            grad_first,
            grad_second,
            usage,
        )

    return shards


def xor_one(index):
    return index + 1 - 2 * (index % 2)


class Plane:
    def __init__(self):
        self.rank = lax.axis_index("fsdp")
        self.side = lax.axis_index("tensor")
        self.share = self.rank % SHARE
        self.place = self.rank // SHARE
        core = xor_one(self.share)
        mid = (self.share + 2) % SHARE
        self.shares = [self.share, core, mid, SHARE - 1 - self.share]
        self.core = {"fsdp": self.place * SHARE + core}
        self.mid = {"fsdp": self.place * SHARE + mid}
        self.both = {"fsdp": self.place * SHARE + self.shares[3]}
        self.members = [None, self.core, self.mid, self.both]
        self.across = {"tensor": 1 - self.side}
        self.near_place = xor_one(self.place)
        self.two_place = (self.place + 2) % 4
        self.far_place = 3 - self.place
        self.near = {"fsdp": self.near_place * SHARE + self.share}
        self.two = {"fsdp": self.two_place * SHARE + self.share}
        self.far = {"fsdp": self.far_place * SHARE + self.share}
        self.inner = (self.place == 1) | (self.place == 2)
        self.outer = (self.place == 0) | (self.place == 3)

    def greet(self):
        barrier = pltpu.get_barrier_semaphore()
        peers = [self.core, self.mid, self.both, self.across, self.near, self.two, self.far]
        for peer in peers:
            pl.semaphore_signal(barrier, inc=1, device_id=peer, device_id_type=MESH)
        pl.semaphore_wait(barrier, len(peers))


class Copies:
    def __init__(self, local_sems, send_sems, recv_sems):
        self.local_sems, self.send_sems, self.recv_sems = local_sems, send_sems, recv_sems
        self.locals, self.sends, self.recvs = 0, 0, 0

    def check(self):
        assert self.locals <= self.local_sems.shape[0]
        assert self.sends <= self.send_sems.shape[0]
        assert self.recvs <= self.recv_sems.shape[0]

    def local(self, src, dst):
        copy = pltpu.make_async_copy(src, dst, self.local_sems.at[self.locals])
        self.locals += 1
        copy.start()
        return copy

    def slot(self):
        self.recvs += 1
        return self.recvs - 1

    def remote(self, src, dst, peer, slot=None):
        if slot is None:
            slot = self.slot()
        copy = pltpu.make_async_remote_copy(
            src_ref=src,
            dst_ref=dst,
            send_sem=self.send_sems.at[self.sends],
            recv_sem=self.recv_sems.at[slot],
            device_id=peer,
            device_id_type=MESH,
        )
        self.sends += 1
        return copy

    def push(self, src, dst, peer):
        copy = self.remote(src, dst, peer)
        copy.start()
        return copy


class ZGather:
    def __init__(self, here, copies, view):
        self.here, self.copies, self.view, self.drained = here, copies, view, False
        self.slots = [copies.slot() for _ in range(3)]

    def copy(self, place, peer, slot):
        block = self.view(place)
        return self.copies.remote(block, block, peer, self.slots[slot])

    def start(self):
        here = self.here
        self.near = self.copy(here.place, here.near, 0)
        self.near.start()
        self.far = self.copy(here.place, here.far, 1)
        self.on_far = self.copy(here.near_place, here.far, 2)
        self.on_near = self.copy(here.far_place, here.near, 1)
        self.last = self.copy(here.two_place, here.near, 2)
        pl.when(here.inner)(self.far.start)

    def first(self):
        @pl.when(self.here.inner)
        def _():
            self.near.wait_recv()
            self.on_far.start()
            self.far.wait_recv()
            self.on_near.start()

    def second(self):
        @pl.when(self.here.inner)
        def _():
            self.on_far.wait_recv()
            self.last.start()

    def arrive(self):
        @pl.when(self.here.outer)
        def _():
            self.near.wait_recv()
            self.on_near.wait_recv()
            self.last.wait_recv()

    def drain(self):
        if self.drained:
            return
        self.drained = True
        self.near.wait_send()

        @pl.when(self.here.inner)
        def _():
            for copy in (self.far, self.on_far, self.on_near, self.last):
                copy.wait_send()


def tiles(count, body):
    def step(i, carry):
        body(i)
        return carry

    lax.fori_loop(0, count, step, 0)


def part(index, size):
    return pl.ds(pl.multiple_of(index * size, size), size)


class RowReduce:
    def __init__(self, here, copies, bufs, acks=None):
        self.here, self.copies, self.acks = here, copies, acks
        (self.snd, self.rcv, self.acc, self.out, self.into) = bufs
        self.sent = []

    def begin(self, width):
        self.lanes = pl.ds(0, width)
        for copy in self.sent:
            copy.wait_send()
        self.sent, self.core = [], []

    def core_send(self, index):
        rows = pl.ds(index * 256, 256)
        self.core.append(self.copies.push(
                self.snd.at[rows, self.lanes], self.rcv.at[rows, self.lanes], self.here.core
            ))

    def add_core(self, first, count):
        acc, rcv, lanes = self.acc, self.rcv, self.lanes

        def body(i):
            at = pl.ds(pl.multiple_of(first + i * 64, 64), 64)
            acc[at, lanes] = acc[at, lanes] + rcv[at, lanes].astype(wide)

        tiles(count // 64, body)

    def round_out(self, first, count, extra=None):
        acc, out, into, lanes = self.acc, self.out, self.into, self.lanes

        def body(i):
            at = pl.ds(pl.multiple_of(first + i * 64, 64), 64)
            value = acc[at, lanes]
            if extra is not None:
                value = value + into[pl.ds(extra, 64), lanes].astype(wide)
            out[pl.ds(pl.multiple_of(first - 128 + i * 64, 64), 64), lanes] = value.astype(low)

        tiles(count // 64, body)

    def hand(self, first, end, peer):
        rows = pl.ds(first, end - first)
        return self.copies.push(
            self.out.at[rows, self.lanes], self.into.at[rows, self.lanes], peer
        )

    def diagonal(self):
        for copy in self.core:
            copy.wait_recv()
        self.add_core(384, 128)
        self.round_out(384, 128)
        self.diag_x = self.hand(256, 320, self.here.across)
        self.diag_y = self.hand(320, 384, self.here.mid)
        self.add_core(128, 256)
        self.round_out(128, 64)
        self.round_out(320, 64)
        self.add_core(0, 128)

    def sides(self):
        self.diag_y.wait_recv()
        self.round_out(192, 64, 320)
        self.over_x = self.hand(0, 128, self.here.across)
        self.diag_x.wait_recv()
        self.round_out(256, 64, 256)
        self.over_y = self.hand(128, 256, self.here.mid)
        self.sent = self.core + [self.diag_x, self.diag_y, self.over_x, self.over_y]

    def arrive(self):
        self.over_x.wait_recv()
        self.over_y.wait_recv()

    def total(self, at, size):
        acc, into, lanes = self.acc, self.into, self.lanes
        return (
            acc[pl.ds(at, size), lanes]
            + into[pl.ds(at, size), lanes].astype(wide)
            + into[pl.ds(at + 128, size), lanes].astype(wide)
        )

    def release(self):
        for index, peer in enumerate((self.here.core, self.here.across, self.here.mid)):
            pl.semaphore_signal(
                self.acks.at[index], inc=1, device_id=peer, device_id_type=MESH
            )

    def await_release(self):
        for index in range(3):
            pl.semaphore_wait(self.acks.at[index], 1)

    def drain(self):
        for copy in self.sent:
            copy.wait_send()


class RowGather:
    def __init__(self, here, copies, view, fixed=False):
        self.here, self.copies, self.view, self.fixed = here, copies, view, fixed
        self.sent, self.drained = [], False

    def start(self):
        here = self.here
        self.over_x = self.pair(0, 1, here.across)
        self.over_y = self.pair(0, 2, here.mid)
        self.cores = [self.pair(0, 4, here.core)]

    def pair(self, source, target, peer, half=None):
        src = self.view(source, half)
        dst = src if self.fixed else self.view(target, half)
        copy = self.copies.push(src, dst, peer)
        self.sent.append(copy)
        return copy

    def forward(self):
        here = self.here
        self.over_y.wait_recv()
        self.diag_x = self.pair(2, 3, here.across, 0)
        self.cores.append(self.pair(2, 6, here.core))
        self.over_x.wait_recv()
        self.diag_y = self.pair(1, 3, here.mid, 1)
        self.cores.append(self.pair(1, 5, here.core))

    def finish(self):
        self.diag_x.wait_recv()
        self.diag_y.wait_recv()
        self.cores.append(self.pair(3, 7, self.here.core))
        for copy in self.cores:
            copy.wait_recv()

    def drain(self):
        if not self.drained:
            for copy in self.sent:
                copy.wait_send()
        self.drained = True


def nn(left_in, right_in):
    return lax.dot_general(
        left_in, right_in, (((1,), (0,)), ((), ())), preferred_element_type=wide
    )


def nt(left_in, right_in):
    return lax.dot_general(
        left_in, right_in, (((1,), (1,)), ((), ())), preferred_element_type=wide
    )


def tn(left_in, right_in):
    return lax.dot_general(
        left_in, right_in, (((0,), (0,)), ((), ())), preferred_element_type=wide
    )


class ZReduce:
    def __init__(self, here, copies, base, spot, rows, columns, landing):
        self.here, self.copies, self.base, self.spot = here, copies, base, spot
        self.rows, self.columns, self.landing = rows, columns, landing
        self.slots = [copies.slot() for _ in range(5)]
        self.handed = []

    def copy(self, k, peer, slot, half=None):
        r, c = self.spot(k)
        first = self.rows // 2 if half == 1 else 0
        rows = self.rows if half is None else self.rows // 2
        block = self.base.at[pl.ds(r + first, rows), pl.ds(c, self.columns)]
        dst = self.landing.at[slot, pl.ds(first, rows)]
        return self.copies.remote(block, dst, peer, self.slots[slot])

    def outward(self, k):
        copy = self.copy(k, self.here.near, {3: 1, 2: 2, 1: 0}[k])
        setattr(self, f"out{k}", copy)
        self.handed.append(copy)
        pl.when(self.here.outer)(copy.start)

    def outward_half(self, half):
        if half == 0:
            self.out1 = self.copy(1, self.here.near, 0)
        copy = self.copy(1, self.here.near, 0, half)
        self.handed.append(copy)
        pl.when(self.here.outer)(copy.start)

    def load(self, index, stage, slot):
        size = min(self.rows, 512)
        return [
            self.copies.local(
                self.landing.at[index, pl.ds(n * size, size), :],
                stage.at[slot, pl.ds(0, size), pl.ds(n * self.columns, self.columns)],
            )
            for n in range(self.rows // size)
        ]

    def add(self, target, stage, slots):
        size = min(self.rows, 512)
        r, c = self.spot(target)
        for n in range(self.rows // size):

            def body(i, n=n):
                at = pl.ds(pl.multiple_of(i * 64, 64), 64)
                mine = pl.ds(pl.multiple_of(r + n * size + i * 64, 64), 64)
                lanes = pl.ds(c, self.columns)
                value = self.base[mine, lanes].astype(wide)
                for slot in slots:
                    value = value + stage[
                        slot, at, pl.ds(n * self.columns, self.columns)
                    ].astype(wide)
                self.base[mine, lanes] = value.astype(low)

            tiles(size // 64, body)

    def pass_on(self, k, wait, index, stage, copy):
        wait.wait_recv()
        for load in self.load(index, stage, 0):
            load.wait()
        self.add(k, stage, [0])
        copy.start()

    def inward(self, step, stage):
        here = self.here
        if step == 0:
            self.in2 = self.copy(2, here.far, 4)
            args = (2, self.out3, 1, stage, self.in2)
        elif step == 1:
            self.in3 = self.copy(3, here.far, 3)
            args = (3, self.out2, 2, stage, self.in3)
        else:
            self.in1 = self.copy(1, here.near, 0)
            args = (1, self.in2, 4, stage, self.in1)

        @pl.when(here.inner)
        def _():
            self.pass_on(*args)

    def finish(self, stage):
        here = self.here
        self.out1.wait_recv()
        loads = self.load(0, stage, 0)

        @pl.when(here.inner)
        def _():
            self.in3.wait_recv()
            for load in self.load(3, stage, 1) + loads:
                load.wait()
            self.add(0, stage, [0, 1])

        @pl.when(here.outer)
        def _():
            for load in loads:
                load.wait()
            self.add(0, stage, [0])

    def drain(self):
        @pl.when(self.here.inner)
        def _():
            for copy in (self.in1, self.in2, self.in3):
                copy.wait_send()

        @pl.when(self.here.outer)
        def _():
            for copy in self.handed:
                copy.wait_send()


def norm_back(value, grad, gain):
    r = lax.rsqrt(jnp.mean(value * value, axis=-1, keepdims=True) + epsilon)
    u = gain * grad
    lean = jnp.mean(u * value, axis=-1, keepdims=True)
    return r * u - value * (r * r * r * lean), grad * value * r


def exact(left_in, right_in, contract):
    return lax.dot_general(
        left_in, right_in, (contract, ((), ())), precision=highest, preferred_element_type=wide
    )


def layer_kernel(
    tok, col, row, cot_in, qkvw, outw, upw, downw, first, gains, second,
    o_block, o_input, o_gq, o_go, o_gu, o_gd, o_first, o_pack, s_hid, s_wq, l_q, l_o, l_u, l_d,
    toks, hid, units, cot, early, wo, wu, wd, cols, rows_info, qkvb, probs, att, acc,
    snd, rcv, out_buf, in_buf, proj, mid_buf, go, stage, top, own_tok, own_out,
    first_buf, slope, gates, dall, r_gate, r_inner, r_slope, r_dpre, r_rows, zpart, zland, gain_buf,
    pack, pack_plane, pack_side, pack_ring,
    local_sems, send_sems, recv_sems, acks,
):
    here = Plane()
    copies = Copies(local_sems, send_sems, recv_sems)
    here.greet()
    rank, share, side = here.rank, here.share, here.side
    owned = 128
    width = toks.shape[1]
    block = owned * SHARE
    head_width = wo.shape[0]
    unit_width = wu.shape[1]
    heads = head_width // HD
    own_rows = part(rank, owned)
    wq = early.at[:, 0 : 3 * head_width]
    act, gup = early.at[0:1024], early.at[1024:2048]
    sent, outs, done = [], [], []

    def to_peer(src, dst, peer):
        copy = copies.push(src, dst, peer)
        sent.append(copy)
        return copy

    def spread(src_of, dst):
        return [
            copies.local(src_of(here.shares[d]), dst)
            if d == 0
            else to_peer(src_of(here.shares[d]), dst, here.members[d])
            for d in range(SHARE)
        ]

    def landed(got):
        for i, copy in enumerate(got):
            if i % SHARE:
                copy.wait_recv()
            else:
                copy.wait()

    got_q = [
        spread(
            lambda t, j=j: qkvw.at[j, :, part(t, head_width)],
            wq.at[own_rows, j * head_width : (j + 1) * head_width],
        )
        for j in range(3)
    ]
    mine, other = part(side, owned), part(1 - side, owned)

    class Halves:
        def __init__(self, src, dst):
            self.dst = dst
            pairs = ((mine, 0), (other, owned))
            self.own = [copies.local(src(rows), dst(at)) for rows, at in pairs]
            self.mid = [to_peer(src(rows), dst(at + 256), here.mid) for rows, at in pairs]
            self.core = [to_peer(src(rows), dst(at + 512), here.core) for rows, at in pairs]

        def pass_on(self):
            for copy in self.mid:
                copy.wait_recv()
            self.last = [
                to_peer(self.dst(at), self.dst(at + 512), here.core) for at in (256, 384)
            ]

    tok_in = Halves(lambda r: tok.at[r, :], lambda at: toks.at[at : at + owned])
    col_in = Halves(lambda r: col.at[r, :], lambda at: cols.at[at : at + owned])
    row_in = Halves(
        lambda r: row.at[:, r],
        lambda at: rows_info.at[at // 256, :, at % 256 : at % 256 + owned],
    )
    got_o = spread(lambda t: outw.at[part(t, head_width), :], wo.at[:, own_rows])
    got_u = spread(lambda t: upw.at[:, part(t, unit_width)], wu.at[own_rows, :])
    got_d = spread(lambda t: downw.at[part(t, unit_width), :], wd.at[:, own_rows])
    cot_rows = Halves(lambda r: cot_in.at[r, :], lambda at: cot.at[at : at + owned])
    in_first = copies.local(first.at[0], first_buf)
    in_tok = copies.local(tok.at[mine, :], own_tok)

    g_q = [
        ZGather(here, copies, lambda k, d=d: wq.at[part(k * SHARE + here.shares[d], owned), :])
        for d in range(SHARE)
    ]
    g_o = ZGather(here, copies, lambda k: wo.at[:, part(k, block)])
    g_u = [
        ZGather(
            here,
            copies,
            lambda k, h=h: wu.at[pl.ds(pl.multiple_of(k * block + h * 256, 256), 256), :],
        )
        for h in range(2)
    ]
    g_d = [
        ZGather(here, copies, lambda k, h=h: wd.at[h * 512 : (h + 1) * 512, part(k, block)])
        for h in range(2)
    ]

    def fact(at, index):
        return cols[at, 2 * HD + index : 2 * HD + index + 1]

    def start_q(d):
        for got in got_q:
            if d:
                got[d].wait_recv()
            else:
                got[d].wait()
        g_q[d].start()

    start_q(0)
    start_q(1)

    def normalise(base):
        def body(i):
            at = pl.ds(pl.multiple_of(base + i * 64, 64), 64)
            x = toks[at, :].astype(wide)
            r = lax.rsqrt(jnp.mean(x * x, axis=-1, keepdims=True) + epsilon)
            hid[at, :] = (x * r * gains[0:1, :]).astype(low)

        tiles(4, body)

    def wait_all(waits):
        for wait in waits:
            wait()

    wait_all([c.wait for c in tok_in.own + col_in.own + row_in.own])
    normalise(0)

    def route(index, rows_of):
        made = exact(rows_of[0:owned, :].astype(wide), first_buf[...], ((1,), (0,)))
        sig = 1.0 / (1.0 + jnp.exp(-made))
        inner = made * sig
        logits = exact(inner, second[index], ((1,), (0,)))
        lane = lax.broadcasted_iota(jnp.int32, (owned, HD), 1)
        logits = jnp.where(lane < NB, logits, -1e30)
        raised = jnp.where(
            lane < NB, jnp.exp(logits - jnp.max(logits, axis=-1, keepdims=True)), 0.0
        )
        shares = raised / jnp.sum(raised, axis=-1, keepdims=True)
        hot = jnp.where(lane.astype(wide) == fact(pl.ds(0, owned), 2 + index), 1.0, 0.0)
        gate = NB * jnp.sum(shares * hot, axis=-1, keepdims=True)
        lean = hot - shares
        bare = exact(lean, second[index], ((1,), (1,))) * (sig * (1.0 + made * (1.0 - sig)))
        r_gate[index] = jnp.broadcast_to(gate, (owned, HD))
        r_inner[index] = inner
        r_slope[index] = lean if index else gate * lean
        r_dpre[index] = bare if index else gate * bare
        if index == 1:
            dall[0:owned, :] = bare.astype(low)

    def slope_tiles(index):
        def body(i):
            c = part(i, 256)
            slope[:, c] = exact(r_dpre[index], first_buf[c, :], ((1,), (1,)))

        tiles(8, body)

    in_first.wait()
    route(0, hid)
    in_first = copies.local(first.at[1], first_buf)
    start_q(2)
    start_q(3)
    g_q[0].first()
    g_q[1].first()
    wait_all([c.wait_recv for c in tok_in.core])
    normalise(512)
    g_q[0].second()
    g_q[1].second()
    g_q[2].first()
    g_q[3].first()
    tok_in.pass_on()
    normalise(256)
    g_q[2].second()
    g_q[3].second()
    wait_all([c.wait_recv for c in tok_in.last])
    normalise(768)
    save_hid = copies.local(hid, s_hid)
    landed(got_o)
    g_o.start()
    col_in.pass_on()
    row_in.pass_on()
    wait_all([c.wait_recv for c in col_in.core + row_in.core + col_in.last + row_in.last])
    g_o.first()
    landed(got_u)
    g_o.second()
    g_u[0].start()
    for one in g_q:
        one.arrive()
    save_wq = copies.local(wq, s_wq)

    for j in range(3):

        def qkv_tile(i, j=j):
            at = part(i, 512)
            made = nn(hid[at, :], wq[:, j * head_width : (j + 1) * head_width])
            if j < 2:
                cosine = cols[at, 0:HD]
                sine = cols[at, HD : 2 * HD]
                for h in range(heads):
                    one = made[:, h * HD : (h + 1) * HD]
                    turned = one * cosine + pltpu.roll(one, HD // 2, 1) * sine
                    qkvb[at, j * head_width + h * HD : j * head_width + (h + 1) * HD] = (
                        turned.astype(low)
                    )
            else:
                qkvb[at, j * head_width : (j + 1) * head_width] = made.astype(low)

        tiles(2, qkv_tile)

    g_u[0].first()
    g_u[1].start()

    first_head = (side * SHARE + share) * heads
    scale = HD ** (-0.5)
    for h in range(heads):
        head = (first_head + h).astype(wide)

        def attend_group(g, h=h, head=head):
            at = part(g, 256)
            query, keyed, value = (
                qkvb[at, pl.ds(j * head_width + h * HD, HD)] for j in range(3)
            )
            info = rows_info[g]
            seg_k, slot_k, bucket_k = info[0:1, :], info[1:2, :], info[2:3, :]
            reach_k = jnp.where(4.0 * bucket_k + 4.0 > head, 1.0, 0.0)
            slot_q = fact(at, 1)
            usable = (reach_k > 0.5) | (slot_k == slot_q)
            allowed = (fact(at, 0) == seg_k) & (slot_k <= slot_q) & usable
            scores = jnp.where(allowed, nt(query, keyed) * scale, -1e30)
            weights = jnp.exp(scores - jnp.max(scores, axis=-1, keepdims=True))
            p = weights / jnp.sum(weights, axis=-1, keepdims=True)
            probs[part(g * heads + h, 256), :] = p
            mixed = nn(p.astype(low), value)
            att[at, h * HD : (h + 1) * HD] = jnp.where(
                4.0 * fact(at, 2) + 4.0 > head, mixed, 0.0
            ).astype(low)

        tiles(SHARE, attend_group)

    reduce = RowReduce(here, copies, (snd, rcv, acc, out_buf, in_buf), acks)

    def partial_sums(term, extra=None):
        lanes = acc.shape[1] if extra is not None else width
        reduce.begin(lanes)
        for i in range(2):

            def send_tile(n, i=i):
                snd[i * 256 : (i + 1) * 256, part(n, 512)] = term(
                    pl.ds(512 + i * 256, 256), n
                ).astype(low)

            tiles(4, send_tile)
            if extra is not None:
                snd[i * 256 : (i + 1) * 256, width:lanes] = extra[
                    pl.ds(512 + i * 256, 256), :
                ].astype(low)
            reduce.core_send(i)

        def own_tile(n):
            acc[:, part(n, 512)] = term(pl.ds(0, 512), n)

        tiles(4, own_tile)
        if extra is not None:
            acc[:, width:lanes] = extra[0:512, :]

    g_o.arrive()
    partial_sums(lambda at, n: nn(att[at, :], wo[:, part(n, 512)]))
    g_u[0].second()
    reduce.diagonal()
    g_u[1].first()
    reduce.sides()
    g_u[1].second()
    landed(got_d)
    g_d[0].start()
    g_d[1].start()
    in_tok.wait()
    reduce.arrive()

    def row_tiles(body):
        def step(i):
            at = pl.multiple_of(i * 64, 64)
            body(at, pl.ds(at, 64))

        tiles(owned // 64, step)

    def middle_tile(at, rows):
        projected = reduce.total(at, 64)
        proj[rows, :] = projected
        middle = own_tok[rows, :].astype(wide) + r_gate[0, rows, 0:1] * projected
        mid_buf[rows, :] = middle
        r = lax.rsqrt(jnp.mean(middle * middle, axis=-1, keepdims=True) + epsilon)
        units[rows, :] = (middle * r * gains[1:2, :]).astype(low)

    row_tiles(middle_tile)
    reduce.release()

    def row_view(buf):
        def view(k, h):
            if h is None:
                return buf.at[k * owned : (k + 1) * owned]
            return buf.at[k * owned + h * 64 : k * owned + (h + 1) * 64]

        return view

    units_out = RowGather(here, copies, row_view(units))
    units_out.start()
    in_first.wait()
    route(1, units)
    gates[0:owned, :] = r_gate[1]
    gates_out = RowGather(here, copies, row_view(gates))
    dall_out = RowGather(here, copies, row_view(dall))
    gates_out.start()
    dall_out.start()

    def first_low(n):
        return go[pl.ds(pl.multiple_of(n % 2 * 512, 512), 512), part(n // 2, 256)]

    def first_tile(i):
        go[part(i % 8, 128), part(i // 8, 256)] = first_buf[part(i, 128), :].astype(low)

    tiles(16, first_tile)
    in_first = copies.local(first.at[0], first_buf)
    g_d[0].first()
    units_out.forward()
    gates_out.forward()
    dall_out.forward()
    g_d[1].first()
    units_out.finish()
    gates_out.finish()
    dall_out.finish()
    g_d[0].second()
    g_d[1].second()
    wait_all([c.wait for c in cot_rows.own])
    cot_rows.pass_on()
    wait_all([c.wait_recv for c in cot_rows.core + cot_rows.last])

    def live_cot(at):
        return jnp.where(fact(at, 4) > 0.5, cot[at, :].astype(wide), 0.0)

    for copy in tok_in.last + cot_rows.last:
        copy.wait_send()
        done.append(copy)

    def keep_tile(at, rows):
        top[rows, :] = live_cot(rows).astype(low)

    row_tiles(keep_tile)

    def scale_tile(i):
        at = part(i, 64)
        cot[at, :] = (gates[at, 0:1] * live_cot(at)).astype(low)

    tiles(16, scale_tile)

    for one in g_u:
        one.arrive()

    first_unit = (side * SHARE + share) * unit_width

    def used_units(at, base, rows, columns):
        lane = lax.broadcasted_iota(jnp.int32, (rows, columns), 1) + base
        return lane.astype(wide) < (FF // NB) * (fact(at, 3) + 1.0)

    save_wq.wait()
    for one in g_q:
        one.drain()

    def up_tile(i):
        m, n = i % 2, i // 2
        at, c = part(m, 512), part(n, 512)
        made = nn(units[at, :], wu[:, c])
        acc[:, part(m * 2 + n, 512)] = made
        relu = jnp.maximum(made, 0.0)
        used = used_units(at, first_unit + n * 512, 512, 512)
        act[at, c] = jnp.where(used, relu * relu, 0.0).astype(low)

    tiles(4, up_tile)
    def deliver(piece_of, dst):
        for d in range(SHARE):
            src = piece_of(here.shares[d])
            if d == 0:
                outs.append(copies.local(src, dst))
            else:
                sent.append(copies.push(src, dst, here.members[d]))
                owed.append(sent[-1])

    owed = []

    gd, gu, gq = toks, hid, wd
    blocks = [here.place, here.near_place, here.two_place, here.far_place]
    z_d = ZReduce(here, copies, gd, lambda k: (0, k * block), unit_width, block, l_d)
    z_u = ZReduce(
        here, copies, gu, lambda k: (k % 2 * block, k // 2 * unit_width), block, unit_width, l_u
    )
    z_o = ZReduce(here, copies, go, lambda k: (k * head_width, 0), head_width, block, l_o)
    z_q = ZReduce(
        here, copies, gq, lambda k: (k % 2 * block, k // 2 * 1024), block, 3 * head_width, l_q
    )

    def down_block(k):
        def body(i):
            m = part(i, 512)
            gd[m, k * block : (k + 1) * block] = tn(
                act[:, m], cot[:, part(blocks[k], block)]
            ).astype(low)

        tiles(unit_width // 512, body)

    for k in (3, 2, 1):
        down_block(k)
        z_d.outward(k)
    down_block(0)
    z_d.inward(0, stage)
    z_d.inward(1, stage)
    for one in g_d:
        one.arrive()

    def gup_tile(m):
        at = part(m, 512)
        dots = jnp.zeros((512, 1), wide)
        for n in range(unit_width // 512):
            c = slice(n * 512, (n + 1) * 512)
            made = nt(cot[at, :], wd[c, :])
            used = used_units(at, first_unit + n * 512, 512, 512)
            relu = jnp.maximum(acc[:, part(m * 2 + n, 512)], 0.0)
            gup[at, c] = jnp.where(used, 2.0 * relu * made, 0.0).astype(low)
            dots = dots + jnp.sum(act[at, c].astype(wide) * made, axis=-1, keepdims=True)
        gates[at, :] = jnp.broadcast_to(dots, (512, HD))
        r_rows[at, 256:512] = (dots * dall[at, :].astype(wide)).astype(low)

    gates_out.drain()
    tiles(2, gup_tile)

    save_hid.wait()

    def up_block(k):
        r, c = k % 2 * block, k // 2 * unit_width

        def body(i):
            gu[r : r + block, pl.ds(pl.multiple_of(c + i * 512, 512), 512)] = tn(
                units[:, part(blocks[k], block)], gup[:, part(i, 512)]
            ).astype(low)

        tiles(unit_width // 512, body)

    up_block(3)
    z_u.outward(3)

    reduce.await_release()
    partial_sums(
        lambda at, n: nt(gup[at, :], wu[part(n, 512), :])
        + nt(r_rows[at, 256:512], first_low(n)),
        gates,
    )
    up_block(2)
    z_u.outward(2)
    reduce.diagonal()
    up_block(1)
    z_u.outward_half(0)
    z_d.inward(2, stage)
    reduce.sides()
    up_block(0)

    column = share * 2 + side
    ucol = dall
    dall_out.drain()

    def ucol_tile(i):
        ucol[part(i, 256), :] = units[part(i, 256), part(column, 256)]

    tiles(4, ucol_tile)
    units_out.drain()
    in_hid = copies.local(s_hid, units)
    for one in g_u:
        one.drain()
    in_wq = copies.local(s_wq, wu.at[:, 0 : 3 * head_width])

    r_rows_out = RowGather(here, copies, row_view(r_rows))

    def keep_gate(index, rows, weight):
        c = slice(index * 256, (index + 1) * 256)
        r_rows[rows, c] = (weight * r_dpre[index, rows, :]).astype(low)
        r_slope[index, rows, :] = weight * r_slope[index, rows, :]

    places = [here.place, here.near_place, here.two_place, here.far_place]
    planes = [None, here.near, here.two, here.far]

    def first_rows(k, h):
        target = here.shares[k // 4 + k // 2 % 2 * 2] * 2 + (side if k % 2 == 0 else 1 - side)
        base = target * 256
        if h is None:
            return o_first.at[:, pl.ds(pl.multiple_of(base, 256), 256), :]
        return o_first.at[:, pl.ds(pl.multiple_of(base + h * 128, 128), 128), :]

    first_out = RowGather(here, copies, first_rows, True)

    class FirstSum:
        def __init__(self):
            zpart[0] = tn(units[:, part(column, 256)], r_rows[:, 0:256]).astype(low)
            zpart[1] = tn(ucol[...], r_rows[:, 256:512]).astype(low)
            self.got = []
            for k in range(4):
                src, dst = zpart.at[:, part(places[k], 64), :], zland.at[here.place]
                self.got.append(
                    copies.local(src, dst) if k == 0 else to_peer(src, dst, planes[k])
                )

        def add(self):
            landed(self.got)
            for copy in self.got[1:]:
                copy.wait_send()
                done.append(copy)
            total = zland[0].astype(wide)
            for k in range(1, 4):
                total = total + zland[k].astype(wide)
            zpart[:, 0:64, :] = total.astype(low)
            at = pl.ds(pl.multiple_of(column * 256 + here.place * 64, 64), 64)
            src, dst = zpart.at[:, 0:64, :], o_first.at[:, at, :]
            self.got = [
                copies.local(src, dst) if k == 0 else to_peer(src, dst, planes[k])
                for k in range(4)
            ]

        def show(self):
            landed(self.got)
            first_out.start()

    reduce.arrive()
    gproj = cot
    gain_buf[...] = jnp.zeros_like(gain_buf)

    def grad_tile(at, rows):
        total = reduce.total(at, 64)
        grad = total[:, 0:width]
        keep_gate(1, rows, total[:, width : width + 1])
        back, gain_terms = norm_back(mid_buf[rows, :], grad, gains[1:2, :])
        grad_middle = top[rows, :].astype(wide) + back
        gproj[rows, :] = (r_gate[0, rows, 0:1] * grad_middle).astype(low)
        grad_gate = jnp.sum(grad_middle * proj[rows, :], axis=-1, keepdims=True)
        keep_gate(0, rows, grad_gate)
        r_gate[0, rows, :] = jnp.broadcast_to(grad_gate, (64, HD))
        proj[rows, :] = grad_middle
        gain_buf[1:2, :] = gain_buf[1:2, :] + jnp.sum(gain_terms, axis=0, keepdims=True)

    row_tiles(grad_tile)
    reduce.release()
    gproj_out = RowGather(here, copies, row_view(gproj))
    gproj_out.start()
    r_rows_out.start()
    in_first.wait()
    slope_tiles(0)
    z_u.inward(0, stage)
    gproj_out.forward()
    r_rows_out.forward()

    reduce.await_release()
    partial_sums(lambda at, n: nn(act[at, :], wd[:, part(n, 512)]))
    gproj_out.finish()
    r_rows_out.finish()
    in_hid.wait()
    sum_first = FirstSum()
    z_u.outward_half(1)
    z_d.finish(stage)
    deliver(lambda t: gd.at[:, part(t, owned)], o_gd.at[part(share, unit_width), :])


    def out_block(k):
        go[k * head_width : (k + 1) * head_width, :] = tn(
            att[...], gproj[:, part(blocks[k], block)]
        ).astype(low)

    for k in range(4):
        out_block(k)
    gatt, gqkv = gup, act

    def gatt_tile(i):
        at = part(i, 512)
        made = nt(gproj[at, :], wo[...]).astype(low)
        for h in range(heads):
            used = 4.0 * fact(at, 2) + 4.0 > (first_head + h).astype(wide)
            gatt[at, h * HD : (h + 1) * HD] = jnp.where(
                used, made[:, h * HD : (h + 1) * HD].astype(wide), 0.0
            ).astype(low)

    tiles(2, gatt_tile)

    for h in range(heads):

        def back_group(g, h=h):
            at = part(g, 256)
            lanes = [pl.ds(j * head_width + h * HD, HD) for j in range(3)]
            query, keyed, value = (qkvb[at, lane] for lane in lanes)
            grad = gatt[at, h * HD : (h + 1) * HD]
            p = probs[part(g * heads + h, 256), :]
            grad_p = nt(grad, value)
            row_dot = jnp.sum(p * grad_p, axis=-1, keepdims=True)
            grad_s = (p * (grad_p - row_dot)).astype(low)
            cosine = cols[at, 0:HD]
            sine = cols[at, HD : 2 * HD]
            for lane, turned in (
                (lanes[0], nn(grad_s, keyed) * scale),
                (lanes[1], tn(grad_s, query) * scale),
            ):
                gqkv[at, lane] = (
                    turned * cosine - pltpu.roll(turned, HD // 2, 1) * sine
                ).astype(low)
            gqkv[at, lanes[2]] = tn(p.astype(low), grad).astype(low)

        tiles(SHARE, back_group)

    def qkv_block(k):
        r, c = k % 2 * block, k // 2 * 1024
        for j in range(3):
            gq[r : r + block, c + j * head_width : c + (j + 1) * head_width] = tn(
                units[:, part(blocks[k], block)], gqkv[:, j * head_width : (j + 1) * head_width]
            ).astype(low)

    for one in g_d:
        one.drain()
    z_u.inward(1, stage)
    sum_first.add()
    for k in (3, 2):
        qkv_block(k)
        z_q.outward(k)
    for k in (3, 2, 1):
        z_o.outward(k)
    qkv_block(1)
    z_q.outward(1)
    qkv_block(0)

    reduce.diagonal()
    reduce.sides()
    z_u.inward(2, stage)
    reduce.arrive()

    def block_tile(at, rows):
        own_out[rows, :] = jnp.where(
            fact(rows, 4) > 0.5,
            mid_buf[rows, :] + r_gate[1, rows, 0:1] * reduce.total(at, 64),
            0.0,
        ).astype(low)

    row_tiles(block_tile)
    reduce.release()
    shown = copies.local(own_out, o_block.at[mine])
    shown_far = to_peer(own_out, o_block.at[mine], here.across)

    in_wq.wait()
    reduce.await_release()
    partial_sums(
        lambda at, n: nt(gqkv[at, 0 : 3 * head_width], wu[part(n, 512), 0 : 3 * head_width])
    )
    reduce.diagonal()
    z_u.finish(stage)
    deliver(lambda t: gu.at[part(t, owned), 0:unit_width], o_gu.at[:, part(share, unit_width)])
    z_q.inward(0, stage)
    reduce.sides()
    sum_first.show()
    z_q.inward(1, stage)
    z_q.inward(2, stage)
    z_o.inward(0, stage)
    z_o.inward(1, stage)
    shown.wait()
    shown_far.wait()
    done.append(shown_far)
    reduce.arrive()

    def input_tile(at, rows):
        grad = reduce.total(at, 64) + r_gate[0, rows, 0:1] * slope[rows, :]
        back, gain_terms = norm_back(own_tok[rows, :].astype(wide), grad, gains[0:1, :])
        own_out[rows, :] = (proj[rows, :] + back).astype(low)
        gain_buf[0:1, :] = gain_buf[0:1, :] + jnp.sum(gain_terms, axis=0, keepdims=True)

    row_tiles(input_tile)
    first_out.forward()

    for index in range(2):
        for j in range(8):
            pack[index * 8 + j : index * 8 + j + 1, :] = gain_buf[
                index : index + 1, j * 256 : (j + 1) * 256
            ]
        made = exact(r_slope[index], r_inner[index], ((0,), (0,)))
        pack[16 + index * 8 : 24 + index * 8, :] = made[0:8, :]
        lane = lax.broadcasted_iota(jnp.int32, (owned, 256), 1)
        own = pl.ds(0, owned)
        hot = (lane.astype(wide) == fact(own, 2 + index)) & (fact(own, 4) > 0.5)
        count = jnp.sum(jnp.where(hot, 1.0, 0.0), axis=0, keepdims=True)
        pack[32 + index * 8 : 40 + index * 8, :] = jnp.broadcast_to(count, (8, 256))

    def sum_slots(buf, count):
        total = buf[0]
        for k in range(1, count):
            total = total + buf[k]
        return total

    got = [
        copies.local(pack, pack_plane.at[share])
        if d == 0
        else to_peer(pack, pack_plane.at[share], here.members[d])
        for d in range(SHARE)
    ]
    landed(got)
    for copy in got[1:]:
        copy.wait_send()
        done.append(copy)
    pack[...] = sum_slots(pack_plane, SHARE)
    got = [
        copies.local(pack, pack_side.at[side]),
        to_peer(pack, pack_side.at[side], here.across),
    ]
    outs.append(copies.local(own_out, o_input.at[mine]))
    input_far = copies.push(own_out, o_input.at[mine], here.across)
    z_o.inward(2, stage)
    first_out.finish()
    landed(got)
    got[1].wait_send()
    done.append(got[1])
    pack[...] = pack_side[0] + pack_side[1]
    got = [
        copies.local(pack, pack_ring.at[here.place])
        if k == 0
        else to_peer(pack, pack_ring.at[here.place], planes[k])
        for k in range(4)
    ]

    z_o.finish(stage)
    deliver(
        lambda t: go.at[0:head_width, part(t, owned)], o_go.at[part(share, head_width), :]
    )
    z_q.finish(stage)
    for j in range(3):
        deliver(
            lambda t, j=j: gq.at[part(t, owned), j * head_width : (j + 1) * head_width],
            o_gq.at[j, :, part(share, head_width)],
        )
    landed(got)
    for copy in got[1:]:
        copy.wait_send()
        done.append(copy)
    pack[...] = sum_slots(pack_ring, 4)
    outs.append(copies.local(pack, o_pack))

    drains = [g_o] + g_q + g_u + g_d + [z_d, z_u, z_o, z_q, reduce, units_out, gates_out, dall_out]
    for one in drains + [gproj_out, r_rows_out, first_out]:
        one.drain()
    input_far.wait()
    for copy in owed:
        copy.wait_recv()
    for copy in outs:
        copy.wait()
    for copy in sent:
        if not any(copy is one for one in done):
            copy.wait_send()
    copies.check()


def plane(mesh):
    fsdp = mesh.shape["fsdp"]
    ring_size = fsdp // SHARE

    def shards(
        tokens,
        head_bucket,
        ffn_bucket,
        lengths,
        norm_gains,
        qkv_weight,
        out_weight,
        up_weight,
        down_weight,
        router_first,
        router_second,
        cotangent,
    ):
        rows, width = tokens.shape
        half = rows // 2
        local_units = up_weight.shape[1]
        units = local_units // SHARE
        local_width = out_weight.shape[0]
        head_width = local_width // SHARE
        heads = head_width // HD
        owned = width // fsdp
        block = width // ring_size
        plane_rows = SHARE * rows

        slot_ids = jnp.arange(rows, dtype=jnp.int32)
        segment, position, live_rows = (a[0] for a in layout(lengths, slot_ids))
        frequency = theta_base ** (-2.0 * jnp.arange(HD // 2, dtype=wide) / HD)
        angles = position.astype(wide)[:, None] * frequency
        cosine, sine = jnp.cos(angles), jnp.sin(angles)
        facts = jnp.stack(
            [segment, slot_ids, head_bucket, ffn_bucket, live_rows.astype(jnp.int32)], axis=1
        ).astype(wide)
        col = jnp.concatenate(
            [cosine, cosine, -sine, sine, jnp.pad(facts, ((0, 0), (0, HD - facts.shape[1])))],
            axis=1,
        )
        row = jnp.pad(facts.T, ((0, 8 - facts.shape[1]), (0, 0)))
        second = jnp.pad(router_second, ((0, 0), (0, 0), (0, HD - NB)))
        b16, f32 = low, wide
        hidden = router_first.shape[2]
        small = 48

        def shape(*dims):
            return jax.ShapeDtypeStruct(dims[1:], dims[0])

        def buffer(*dims):
            return pltpu.VMEM(dims[1:], dims[0])

        anywhere = pl.BlockSpec(memory_space=pl.ANY)
        vmem = pl.BlockSpec(memory_space=pltpu.VMEM)
        (
            block_out,
            input_grad,
            raw_qkv,
            raw_out,
            raw_up,
            raw_down,
            raw_first,
            sums,
            *_,
        ) = pl.pallas_call(
            layer_kernel,
            out_shape=[
                shape(b16, rows, width),
                shape(b16, rows, width),
                shape(b16, 3, owned, local_width),
                shape(b16, local_width, owned),
                shape(b16, owned, local_units),
                shape(b16, local_units, owned),
                shape(b16, *router_first.shape),
                shape(f32, small, 256),
                shape(b16, plane_rows, width),
                shape(b16, width, 3 * head_width),
                shape(b16, 5, block, 3 * head_width),
                shape(b16, 5, head_width, block),
                shape(b16, 5, block, units),
                shape(b16, 5, units, block),
            ],
            in_specs=[anywhere] * 9 + [vmem] * 2,
            out_specs=[anywhere] * 14,
            scratch_shapes=[
                buffer(b16, plane_rows, width),
                buffer(b16, plane_rows, width),
                buffer(b16, plane_rows, width),
                buffer(b16, plane_rows, width),
                buffer(b16, 2 * plane_rows, units),
                buffer(b16, head_width, width),
                buffer(b16, width, units),
                buffer(b16, units, width),
                buffer(f32, plane_rows, 3 * HD),
                buffer(f32, SHARE, 8, rows),
                buffer(b16, plane_rows, 3 * head_width),
                buffer(f32, SHARE * heads * rows, rows),
                buffer(b16, plane_rows, head_width),
                buffer(f32, plane_rows // 2, width + HD),
                buffer(b16, plane_rows // 2, width + HD),
                buffer(b16, plane_rows // 2, width + HD),
                buffer(b16, 3 * half, width + HD),
                buffer(b16, 3 * half, width + HD),
                buffer(f32, half, width),
                buffer(f32, half, width),
                buffer(b16, 4 * head_width, block),
                buffer(b16, 2, block, units),
                buffer(b16, half, width),
                buffer(b16, half, width),
                buffer(b16, half, width),
                buffer(f32, width, hidden),
                buffer(f32, half, width),
                buffer(f32, plane_rows, HD),
                buffer(b16, plane_rows, hidden),
                buffer(f32, 2, half, HD),
                buffer(f32, 2, half, hidden),
                buffer(f32, 2, half, HD),
                buffer(f32, 2, half, hidden),
                buffer(b16, plane_rows, 2 * hidden),
                buffer(b16, 2, 256, hidden),
                buffer(b16, 4, 2, 64, hidden),
                buffer(f32, 8, width),
                buffer(f32, small, 256),
                buffer(f32, SHARE, small, 256),
                buffer(f32, 2, small, 256),
                buffer(f32, 4, small, 256),
                pltpu.SemaphoreType.DMA((128,)),
                pltpu.SemaphoreType.DMA((256,)),
                pltpu.SemaphoreType.DMA((256,)),
                pltpu.SemaphoreType.REGULAR((3,)),
            ],
            compiler_params=pltpu.CompilerParams(
                collective_id=0, has_side_effects=True, vmem_limit_bytes=63 * 2**20
            ),
        )(
            tokens,
            col,
            row,
            cotangent,
            jnp.transpose(qkv_weight, (1, 0, 2)),
            out_weight,
            up_weight,
            down_weight,
            router_first,
            norm_gains,
            second,
        )
        grad_qkv = jnp.transpose(raw_qkv, (1, 0, 2)).astype(wide)
        grad_out, grad_up, grad_down, grad_first = (
            a.astype(wide) for a in (raw_out, raw_up, raw_down, raw_first)
        )
        grad_gains = sums[0:16].reshape(2, width)
        grad_second = jnp.stack([sums[16 : 16 + NB].T, sums[24 : 24 + NB].T])
        usage = jnp.stack([sums[32, :NB], sums[40, :NB]])
        return (
            block_out,
            input_grad,
            grad_gains,
            grad_qkv,
            grad_out,
            grad_up,
            grad_down,
            grad_first,
            grad_second,
            usage,
        )

    return shards


def solution(mesh):
    shards = plane(mesh) if mesh.shape["fsdp"] == 4 * SHARE else general(mesh)
    in_specs = (
        P("fsdp", None),
        P("fsdp"),
        P("fsdp"),
        P("fsdp", None),
        P(),
        P("fsdp", None, "tensor"),
        P("tensor", "fsdp"),
        P("fsdp", "tensor"),
        P("tensor", "fsdp"),
        P(),
        P(),
        P("fsdp", None),
    )
    out_specs = (
        P("fsdp", None),
        P("fsdp", None),
        P(),
        P("fsdp", None, "tensor"),
        P("tensor", "fsdp"),
        P("fsdp", "tensor"),
        P("tensor", "fsdp"),
        P(),
        P(),
        P(),
    )
    return jax.shard_map(
        shards, mesh=mesh, in_specs=in_specs, out_specs=out_specs, check_vma=False
    )
```

```python
from functools import partial

import jax
import jax.numpy as jnp
import numpy as np
from jax import lax
from jax.experimental import pallas as pl
from jax.experimental.pallas import tpu as pltpu
from jax.sharding import PartitionSpec as P

HEADS = 16
HD = 128
FF = 8192
NB = 4
SHARE = 4

epsilon = 1e-05
theta_base = 10000.0
highest = lax.Precision.HIGHEST
low = jnp.bfloat16
wide = jnp.float32
MESH = pl.DeviceIdType.MESH


def norm_piece(values_in, gain_row):
    return (
        values_in
        * lax.rsqrt(jnp.mean(values_in * values_in, axis=-1, keepdims=True) + epsilon)
        * gain_row
    )


def route_piece(hidden_in, router_in, router_out, bucket):
    inner = jax.nn.silu(jnp.dot(hidden_in, router_in, precision=highest))
    logits = jnp.dot(inner, router_out, precision=highest)
    probs_all = jax.nn.softmax(logits, axis=-1)
    onehot = (bucket[:, None] == jnp.arange(NB, dtype=jnp.int32)[None, :]).astype(wide)
    return NB * jnp.sum(probs_all * onehot, axis=-1)


def dot(left_in, right_in):
    return jnp.dot(left_in, right_in, preferred_element_type=wide)


def dot_rows(left_in, right_in):
    return lax.dot_general(
        left_in, right_in, (((0,), (0,)), ((), ())), preferred_element_type=wide
    )


def dot_cols(left_in, right_in):
    return lax.dot_general(
        left_in, right_in, (((1,), (1,)), ((), ())), preferred_element_type=wide
    )


def rotate(operand, cosine, sine_table):
    half_dim = operand.shape[-1] // 2
    lead_half = operand[..., :half_dim]
    tail_half = operand[..., half_dim:]
    return jnp.concatenate(
        [lead_half * cosine - tail_half * sine_table, tail_half * cosine + lead_half * sine_table],
        axis=-1,
    )


def layout(length_rows, slot_ids):
    seq_count = length_rows.shape[1]
    order = jnp.arange(seq_count, dtype=jnp.int32)
    seq_ends = jnp.sum(
        jnp.where(order[None, None, :] <= order[None, :, None], length_rows[:, None, :], 0), axis=2
    )
    seq_starts = seq_ends - length_rows
    slots = slot_ids[None, :, None]
    member = (slots >= seq_starts[:, None, :]) & (slots < seq_ends[:, None, :])
    seq_of = jnp.sum(jnp.where(member, jnp.arange(seq_count, dtype=jnp.int32), 0), axis=2)
    live_rows = jnp.any(member, axis=2)
    seq_begin = jnp.sum(jnp.where(member, seq_starts[:, None, :], 0), axis=2)
    segment = jnp.where(live_rows, seq_of, seq_count + slot_ids[None, :])
    position = slot_ids[None, :] - seq_begin
    return segment, position, live_rows


def general(mesh):
    fsdp = mesh.shape["fsdp"]
    ring_size = fsdp // SHARE

    def hop(moved, bits):
        return lax.ppermute(moved, "fsdp", [(i, i ^ bits) for i in range(fsdp)])

    def cross(moved):
        return lax.ppermute(moved, "tensor", [(0, 1), (1, 0)])

    def shards(
        tokens,
        head_bucket,
        ffn_bucket,
        lengths,
        norm_gains,
        qkv_weight,
        out_weight,
        up_weight,
        down_weight,
        router_first,
        router_second,
        cotangent,
    ):
        rows, width = tokens.shape
        half = rows // 2
        rank = lax.axis_index("fsdp")
        side = lax.axis_index("tensor")
        share = rank % SHARE
        place = rank // SHARE
        local_units = up_weight.shape[1]
        units = local_units // SHARE
        local_width = out_weight.shape[0]
        head_width = local_width // SHARE
        heads = head_width // HD
        owned = width // fsdp
        block = width // ring_size

        chain = [None, None]

        def ring(moved, stream):
            if chain[stream] is not None:
                moved, _ = lax.optimization_barrier((moved, chain[stream]))
            got = lax.ppermute(
                moved, "fsdp", [(i, (i + SHARE) % fsdp) for i in range(fsdp)]
            )
            chain[stream] = got
            return got

        def place_at(step):
            return (place - step) % ring_size

        def own_half(arr):
            return lax.dynamic_slice_in_dim(arr, side * half, half, 0)

        def relative(arr):
            return jnp.concatenate(
                [own_half(arr), lax.dynamic_slice_in_dim(arr, (1 - side) * half, half, 0)], axis=0
            )

        def gather_rows(arr):
            other = hop(arr, 2)
            plane = jnp.concatenate([arr[:half], other[:half], arr[half:], other[half:]], axis=0)
            return jnp.concatenate([plane, hop(plane, 1)], axis=0)

        def gather_halves(arr):
            pair = jnp.concatenate([arr, hop(arr, 2)], axis=0)
            plane = jnp.concatenate([pair, cross(pair)], axis=0)
            return jnp.concatenate([plane, hop(plane, 1)], axis=0)

        def reduce_rows(keep, send):
            total = keep + hop(send.astype(low), 1).astype(wide)
            total = total[: 2 * half] + cross(total[2 * half :].astype(low)).astype(wide)
            return total[:half] + hop(total[half:].astype(low), 2).astype(wide)

        def whole_rows(arr):
            other = cross(arr)
            return jnp.where(
                side == 0,
                jnp.concatenate([arr, other], axis=0),
                jnp.concatenate([other, arr], axis=0),
            )

        def spread(pieces_for, axis):
            out = None
            for bits in range(SHARE):
                piece = pieces_for(share ^ bits)
                got = piece if bits == 0 else hop(piece, bits)
                if out is None:
                    dims = list(got.shape)
                    dims[axis] *= SHARE
                    out = jnp.zeros(dims, got.dtype)
                out = lax.dynamic_update_slice_in_dim(
                    out, got, (share ^ bits) * got.shape[axis], axis
                )
            return out

        def ring_gather(own, axis):
            dims = list(own.shape)
            dims[axis] = width
            out = jnp.zeros(dims, own.dtype)
            mid = own.shape[0] // 2
            moving = [own[:mid], own[mid:]]
            for step in range(ring_size):
                if step:
                    moving = [ring(moving[s], s) for s in range(2)]
                base = place_at(step) * block
                for s in range(2):
                    if axis == 0:
                        at = (base + s * mid, 0)
                    else:
                        at = (s * mid, base)
                    out = lax.dynamic_update_slice(out, moving[s], at)
            return out

        def ring_reduce(term):
            moving = [None, None]
            for step in range(1, ring_size):
                for s in range(2):
                    part = term(place_at(step), s)
                    if moving[s] is not None:
                        part = part + moving[s].astype(wide)
                    moving[s] = part.astype(low)
                for s in range(2):
                    moving[s] = ring(moving[s], s)
            return [term(place, s) + moving[s].astype(wide) for s in range(2)]

        def scatter_back(parts, axis):
            joined = jnp.concatenate(parts, axis=0)
            other = 1 - axis
            out_dims = list(joined.shape)
            out_dims[axis] = owned
            stride = out_dims[other]
            out_dims[other] *= SHARE
            out = jnp.zeros(out_dims, wide)
            for bits in range(SHARE):
                piece = lax.dynamic_slice_in_dim(joined, (share ^ bits) * owned, owned, axis)
                if bits:
                    piece = hop(piece.astype(low), bits).astype(wide)
                out = lax.dynamic_update_slice_in_dim(out, piece, (share ^ bits) * stride, other)
            return out

        def qkv_piece(target):
            return lax.dynamic_slice_in_dim(
                qkv_weight, target * head_width, head_width, 2
            ).reshape(owned, 3 * head_width)

        qkv_block = spread(qkv_piece, 0)
        rel_tokens = relative(tokens)
        rel_cot = relative(cotangent)
        ints = relative(jnp.stack([head_bucket, ffn_bucket], axis=1))
        qkv_full = ring_gather(qkv_block, 0)
        all_tokens = gather_rows(rel_tokens)
        buckets = gather_rows(ints)
        pair_lengths = jnp.concatenate([lengths, hop(lengths, 2)], axis=0)
        group_lengths = jnp.concatenate([pair_lengths, hop(pair_lengths, 1)], axis=0)

        out_block = spread(
            lambda t: lax.dynamic_slice_in_dim(out_weight, t * head_width, head_width, 0), 1
        )
        out_full = ring_gather(out_block, 1)
        up_block = spread(lambda t: lax.dynamic_slice_in_dim(up_weight, t * units, units, 1), 0)
        up_full = ring_gather(up_block, 0)
        down_block = spread(
            lambda t: lax.dynamic_slice_in_dim(down_weight, t * units, units, 0), 1
        )
        down_full = ring_gather(down_block, 1)
        all_cot = gather_rows(rel_cot)

        slot_ids = jnp.concatenate(
            [
                side * half + jnp.arange(half, dtype=jnp.int32),
                (1 - side) * half + jnp.arange(half, dtype=jnp.int32),
            ]
        )
        segment, position, live_groups = layout(group_lengths, slot_ids)

        def to_groups(arr):
            tail = arr.shape[1:]
            arr = arr.reshape((2, 2, 2, half) + tail)
            return jnp.swapaxes(arr, 1, 2).reshape((SHARE, rows) + tail)

        def from_groups(arr):
            tail = arr.shape[2:]
            arr = arr.reshape((2, 2, 2, half) + tail)
            return jnp.swapaxes(arr, 1, 2).reshape((8 * half,) + tail)

        live_all = from_groups(live_groups)
        all_heads = buckets[:, 0]
        all_widths = buckets[:, 1]

        own_tokens = rel_tokens[:half].astype(wide)
        own_heads = all_heads[:half]
        own_widths = all_widths[:half]
        own_live = live_all[:half]

        block_in = all_tokens.astype(wide)
        hidden_heads = norm_piece(block_in, norm_gains[0]).astype(low)
        own_normed, norm_heads_back = jax.vjp(norm_piece, own_tokens, norm_gains[0])
        gate_heads, route_heads_back = jax.vjp(
            partial(route_piece, bucket=own_heads),
            own_normed.astype(low).astype(wide),
            router_first[0],
            router_second[0],
        )
        head_ids = side * (local_width // HD) + share * heads + jnp.arange(heads, dtype=jnp.int32)
        head_used = head_ids[None, :] < HEADS // NB * (all_heads[:, None] + 1)
        unit_ids = side * local_units + share * units + jnp.arange(units, dtype=jnp.int32)
        unit_used = unit_ids[None, :] < FF // NB * (all_widths[:, None] + 1)

        half_dim = HD // 2
        frequency = theta_base ** (-2.0 * jnp.arange(half_dim, dtype=wide) / HD)
        angles = position.astype(wide)[:, :, None] * frequency
        cosine = jnp.cos(angles)[:, :, None, :]
        sine_table = jnp.sin(angles)[:, :, None, :]
        qkv_all = to_groups(dot(hidden_heads, qkv_full).reshape(8 * half, 3, heads, HD))
        query = rotate(qkv_all[:, :, 0], cosine, sine_table).astype(low)
        keyed = rotate(qkv_all[:, :, 1], cosine, sine_table).astype(low)
        value = qkv_all[:, :, 2].astype(low)
        group_used = to_groups(head_used)
        same_seq = segment[:, :, None] == segment[:, None, :]
        causal = slot_ids[None, :] <= slot_ids[:, None]
        diagonal = slot_ids[None, :] == slot_ids[:, None]
        key_used = jnp.swapaxes(group_used, 1, 2)
        allowed = (same_seq & causal)[:, None] & (key_used[:, :, None, :] | diagonal)
        scale = HD ** (-0.5)
        scores = jnp.einsum("gqhe,gkhe->ghqk", query, keyed, preferred_element_type=wide) * scale
        scores = jnp.where(allowed, scores, -1e30)
        row_top = jnp.max(scores, axis=-1, keepdims=True)
        weights = jnp.exp(scores - row_top)
        probs = weights / jnp.sum(weights, axis=-1, keepdims=True)
        probs_low = probs.astype(low)
        mixed = jnp.einsum("ghqk,gkhe->gqhe", probs_low, value, preferred_element_type=wide)
        mixed = jnp.where(group_used[..., None], mixed, 0.0).astype(low)
        attended = from_groups(mixed).reshape(8 * half, head_width)

        def partial_rows(left_in, matrix, product):
            keep = product(left_in[: 4 * half], matrix)
            send = product(left_in[4 * half :], matrix)
            return reduce_rows(keep, send)

        projected = partial_rows(attended, out_full, dot)

        middle = own_tokens + gate_heads[:, None] * projected
        normed_units, norm_units_back = jax.vjp(norm_piece, middle, norm_gains[1])
        own_units = normed_units.astype(low)
        hidden_units = gather_halves(own_units)
        gate_units, route_units_back = jax.vjp(
            partial(route_piece, bucket=own_widths),
            own_units.astype(wide),
            router_first[1],
            router_second[1],
        )
        all_gates = gather_halves(gate_units[:, None])
        upward = dot(hidden_units, up_full)
        activated = jnp.where(unit_used, jnp.square(jax.nn.relu(upward)), 0.0).astype(low)
        grad_top_all = jnp.where(live_all[:, None], all_cot.astype(wide), 0.0)
        grad_down_in = (all_gates * grad_top_all).astype(low)

        def down_term(at, s):
            mid = units // 2
            return dot_rows(
                activated[:, s * mid : (s + 1) * mid],
                lax.dynamic_slice_in_dim(grad_down_in, at * block, block, 1),
            )

        grad_down = scatter_back(ring_reduce(down_term), 1)

        downward = partial_rows(activated, down_full, dot)
        own_out = jnp.where(
            own_live[:, None], middle + gate_units[:, None] * downward, 0.0
        ).astype(low)
        block_out = whole_rows(own_out)
        grad_top = jnp.where(own_live[:, None], rel_cot[:half].astype(wide), 0.0)
        grad_gate_units = jnp.sum(grad_top * downward, axis=1)

        grad_act = dot_cols(grad_down_in, down_full)
        grad_up_in = jnp.where(unit_used, 2.0 * jax.nn.relu(upward) * grad_act, 0.0).astype(low)

        def up_term(at, s):
            mid = block // 2
            return dot_rows(
                lax.dynamic_slice_in_dim(hidden_units, at * block + s * mid, mid, 1), grad_up_in
            )

        grad_up = scatter_back(ring_reduce(up_term), 0)
        route_units_grads = route_units_back(grad_gate_units)
        grad_hidden_units = partial_rows(grad_up_in, up_full, dot_cols) + route_units_grads[0]
        norm_units_grads = norm_units_back(grad_hidden_units)
        grad_middle = grad_top + norm_units_grads[0]
        grad_gate_heads = jnp.sum(grad_middle * projected, axis=1)
        grad_projected = gather_halves((gate_heads[:, None] * grad_middle).astype(low))

        def out_term(at, s):
            mid = head_width // 2
            return dot_rows(
                attended[:, s * mid : (s + 1) * mid],
                lax.dynamic_slice_in_dim(grad_projected, at * block, block, 1),
            )

        grad_out = scatter_back(ring_reduce(out_term), 1)
        grad_attended = to_groups(
            dot_cols(grad_projected, out_full).astype(low).reshape(8 * half, heads, HD)
        )
        grad_attended = jnp.where(group_used[..., None], grad_attended, jnp.zeros((), low))
        grad_value = jnp.einsum(
            "ghqk,gqhe->gkhe", probs_low, grad_attended, preferred_element_type=wide
        )
        grad_probs = jnp.einsum(
            "gqhe,gkhe->ghqk", grad_attended, value, preferred_element_type=wide
        )
        row_dot = jnp.sum(probs * grad_probs, axis=-1, keepdims=True)
        grad_scores = (probs * (grad_probs - row_dot)).astype(low)
        grad_query = (
            jnp.einsum("ghqk,gkhe->gqhe", grad_scores, keyed, preferred_element_type=wide) * scale
        )
        grad_keyed = (
            jnp.einsum("ghqk,gqhe->gkhe", grad_scores, query, preferred_element_type=wide) * scale
        )
        grad_qkv_in = jnp.stack(
            [
                rotate(grad_query, cosine, -sine_table),
                rotate(grad_keyed, cosine, -sine_table),
                grad_value,
            ],
            axis=2,
        ).astype(low)
        grad_qkv_in = from_groups(grad_qkv_in).reshape(8 * half, 3 * head_width)

        def qkv_term(at, s):
            mid = block // 2
            return dot_rows(
                lax.dynamic_slice_in_dim(hidden_heads, at * block + s * mid, mid, 1), grad_qkv_in
            )

        qkv_parts = ring_reduce(qkv_term)
        joined = jnp.concatenate(qkv_parts, axis=0)
        grad_qkv = jnp.zeros((owned, 3, local_width), wide)
        for bits in range(SHARE):
            piece = lax.dynamic_slice_in_dim(joined, (share ^ bits) * owned, owned, 0)
            if bits:
                piece = hop(piece.astype(low), bits).astype(wide)
            grad_qkv = lax.dynamic_update_slice_in_dim(
                grad_qkv, piece.reshape(owned, 3, head_width), (share ^ bits) * head_width, 2
            )

        route_heads_grads = route_heads_back(grad_gate_heads)
        grad_hidden_heads = partial_rows(grad_qkv_in, qkv_full, dot_cols) + route_heads_grads[0]
        norm_heads_grads = norm_heads_back(grad_hidden_heads)
        input_grad = whole_rows((grad_middle + norm_heads_grads[0]).astype(low))

        def total_small(arr):
            arr = arr + cross(arr)
            bits = 1
            while bits < fsdp:
                arr = arr + hop(arr, bits)
                bits *= 2
            return arr

        def total_large(arr):
            steps = [1, "tensor"] + [2**i for i in range(1, fsdp.bit_length() - 1)]
            for bits in steps:
                mid = arr.shape[0] // 2
                me = side if bits == "tensor" else (rank // bits) % 2
                send = lax.dynamic_slice_in_dim(arr, (1 - me) * mid, mid, 0)
                keep = lax.dynamic_slice_in_dim(arr, me * mid, mid, 0)
                arr = keep + (cross(send) if bits == "tensor" else hop(send, bits))
            for bits in reversed(steps):
                me = side if bits == "tensor" else (rank // bits) % 2
                other = cross(arr) if bits == "tensor" else hop(arr, bits)
                arr = jnp.where(
                    me == 0,
                    jnp.concatenate([arr, other], axis=0),
                    jnp.concatenate([other, arr], axis=0),
                )
            return arr

        bucket_ids = jnp.arange(NB, dtype=jnp.int32)[None, :]
        head_counts = jnp.sum(
            jnp.where(own_live[:, None] & (own_heads[:, None] == bucket_ids), 1.0, 0.0), axis=0
        )
        width_counts = jnp.sum(
            jnp.where(own_live[:, None] & (own_widths[:, None] == bucket_ids), 1.0, 0.0), axis=0
        )
        units_small = total_small(
            jnp.concatenate(
                [norm_units_grads[1], route_units_grads[2].reshape(-1), head_counts, width_counts]
            )
        )
        heads_small = total_small(
            jnp.concatenate([norm_heads_grads[1], route_heads_grads[2].reshape(-1)])
        )
        first_units = total_large(route_units_grads[1])
        first_heads = total_large(route_heads_grads[1])
        second_shape = router_second.shape[1:]
        second_size = second_shape[0] * second_shape[1]
        grad_gains = jnp.stack([heads_small[:width], units_small[:width]])
        grad_second = jnp.stack(
            [
                heads_small[width : width + second_size].reshape(second_shape),
                units_small[width : width + second_size].reshape(second_shape),
            ]
        )
        usage = units_small[width + second_size :].reshape(2, NB)
        grad_first = jnp.stack([first_heads, first_units])
        return (
            block_out,
            input_grad,
            grad_gains,
            grad_qkv,
            grad_out,
            grad_up,
            grad_down,
            grad_first,
            grad_second,
            usage,
        )

    return shards


def xor_one(index):
    return index + 1 - 2 * (index % 2)


class Plane:
    def __init__(self):
        self.rank = lax.axis_index("fsdp")
        self.side = lax.axis_index("tensor")
        self.share = self.rank % SHARE
        self.place = self.rank // SHARE
        core = xor_one(self.share)
        mid = (self.share + 2) % SHARE
        self.shares = [self.share, core, mid, SHARE - 1 - self.share]
        self.core = {"fsdp": self.place * SHARE + core}
        self.mid = {"fsdp": self.place * SHARE + mid}
        self.both = {"fsdp": self.place * SHARE + self.shares[3]}
        self.members = [None, self.core, self.mid, self.both]
        self.across = {"tensor": 1 - self.side}
        self.near_place = xor_one(self.place)
        self.two_place = (self.place + 2) % 4
        self.far_place = 3 - self.place
        self.near = {"fsdp": self.near_place * SHARE + self.share}
        self.two = {"fsdp": self.two_place * SHARE + self.share}
        self.far = {"fsdp": self.far_place * SHARE + self.share}
        self.inner = (self.place == 1) | (self.place == 2)
        self.outer = (self.place == 0) | (self.place == 3)

    def greet(self):
        barrier = pltpu.get_barrier_semaphore()
        peers = [self.core, self.mid, self.both, self.across, self.near, self.two, self.far]
        for peer in peers:
            pl.semaphore_signal(barrier, inc=1, device_id=peer, device_id_type=MESH)
        pl.semaphore_wait(barrier, len(peers))


class Copies:
    def __init__(self, local_sems, send_sems, recv_sems):
        self.local_sems, self.send_sems, self.recv_sems = local_sems, send_sems, recv_sems
        self.locals, self.sends, self.recvs = 0, 0, 0

    def check(self):
        assert self.locals <= self.local_sems.shape[0]
        assert self.sends <= self.send_sems.shape[0]
        assert self.recvs <= self.recv_sems.shape[0]

    def local(self, src, dst):
        copy = pltpu.make_async_copy(src, dst, self.local_sems.at[self.locals])
        self.locals += 1
        copy.start()
        return copy

    def slot(self):
        self.recvs += 1
        return self.recvs - 1

    def remote(self, src, dst, peer, slot=None):
        if slot is None:
            slot = self.slot()
        copy = pltpu.make_async_remote_copy(
            src_ref=src,
            dst_ref=dst,
            send_sem=self.send_sems.at[self.sends],
            recv_sem=self.recv_sems.at[slot],
            device_id=peer,
            device_id_type=MESH,
        )
        self.sends += 1
        return copy

    def push(self, src, dst, peer):
        copy = self.remote(src, dst, peer)
        copy.start()
        return copy


class ZGather:
    def __init__(self, here, copies, view):
        self.here, self.copies, self.view, self.drained = here, copies, view, False
        self.slots = [copies.slot() for _ in range(3)]

    def copy(self, place, peer, slot):
        block = self.view(place)
        return self.copies.remote(block, block, peer, self.slots[slot])

    def start(self):
        here = self.here
        self.near = self.copy(here.place, here.near, 0)
        self.near.start()
        self.far = self.copy(here.place, here.far, 1)
        self.on_far = self.copy(here.near_place, here.far, 2)
        self.on_near = self.copy(here.far_place, here.near, 1)
        self.last = self.copy(here.two_place, here.near, 2)
        pl.when(here.inner)(self.far.start)

    def first(self):
        @pl.when(self.here.inner)
        def _():
            self.near.wait_recv()
            self.on_far.start()
            self.far.wait_recv()
            self.on_near.start()

    def second(self):
        @pl.when(self.here.inner)
        def _():
            self.on_far.wait_recv()
            self.last.start()

    def arrive(self):
        @pl.when(self.here.outer)
        def _():
            self.near.wait_recv()
            self.on_near.wait_recv()
            self.last.wait_recv()

    def drain(self):
        if self.drained:
            return
        self.drained = True
        self.near.wait_send()

        @pl.when(self.here.inner)
        def _():
            for copy in (self.far, self.on_far, self.on_near, self.last):
                copy.wait_send()


def tiles(count, body):
    def step(i, carry):
        body(i)
        return carry

    lax.fori_loop(0, count, step, 0)


def part(index, size):
    return pl.ds(pl.multiple_of(index * size, size), size)


class RowReduce:
    def __init__(self, here, copies, bufs, acks=None):
        self.here, self.copies, self.acks = here, copies, acks
        (self.snd, self.rcv, self.acc, self.out, self.into) = bufs
        self.sent = []

    def begin(self, width):
        self.lanes = pl.ds(0, width)
        for copy in self.sent:
            copy.wait_send()
        self.sent, self.core = [], []

    def core_send(self, index):
        rows = pl.ds(index * 256, 256)
        self.core.append(self.copies.push(
                self.snd.at[rows, self.lanes], self.rcv.at[rows, self.lanes], self.here.core
            ))

    def add_core(self, first, count):
        acc, rcv, lanes = self.acc, self.rcv, self.lanes

        def body(i):
            at = pl.ds(pl.multiple_of(first + i * 64, 64), 64)
            acc[at, lanes] = acc[at, lanes] + rcv[at, lanes].astype(wide)

        tiles(count // 64, body)

    def round_out(self, first, count, extra=None):
        acc, out, into, lanes = self.acc, self.out, self.into, self.lanes

        def body(i):
            at = pl.ds(pl.multiple_of(first + i * 64, 64), 64)
            value = acc[at, lanes]
            if extra is not None:
                value = value + into[pl.ds(extra, 64), lanes].astype(wide)
            out[pl.ds(pl.multiple_of(first - 128 + i * 64, 64), 64), lanes] = value.astype(low)

        tiles(count // 64, body)

    def hand(self, first, end, peer):
        rows = pl.ds(first, end - first)
        return self.copies.push(
            self.out.at[rows, self.lanes], self.into.at[rows, self.lanes], peer
        )

    def diagonal(self):
        for copy in self.core:
            copy.wait_recv()
        self.add_core(384, 128)
        self.round_out(384, 128)
        self.diag_x = self.hand(256, 320, self.here.across)
        self.diag_y = self.hand(320, 384, self.here.mid)
        self.add_core(128, 256)
        self.round_out(128, 64)
        self.round_out(320, 64)
        self.add_core(0, 128)

    def sides(self):
        self.diag_y.wait_recv()
        self.round_out(192, 64, 320)
        self.over_x = self.hand(0, 128, self.here.across)
        self.diag_x.wait_recv()
        self.round_out(256, 64, 256)
        self.over_y = self.hand(128, 256, self.here.mid)
        self.sent = self.core + [self.diag_x, self.diag_y, self.over_x, self.over_y]

    def arrive(self):
        self.over_x.wait_recv()
        self.over_y.wait_recv()

    def total(self, at, size):
        acc, into, lanes = self.acc, self.into, self.lanes
        return (
            acc[pl.ds(at, size), lanes]
            + into[pl.ds(at, size), lanes].astype(wide)
            + into[pl.ds(at + 128, size), lanes].astype(wide)
        )

    def release(self):
        for index, peer in enumerate((self.here.core, self.here.across, self.here.mid)):
            pl.semaphore_signal(
                self.acks.at[index], inc=1, device_id=peer, device_id_type=MESH
            )

    def await_release(self):
        for index in range(3):
            pl.semaphore_wait(self.acks.at[index], 1)

    def drain(self):
        for copy in self.sent:
            copy.wait_send()


class RowGather:
    def __init__(self, here, copies, view, fixed=False):
        self.here, self.copies, self.view, self.fixed = here, copies, view, fixed
        self.sent, self.drained = [], False

    def start(self):
        here = self.here
        self.over_x = self.pair(0, 1, here.across)
        self.over_y = self.pair(0, 2, here.mid)
        self.cores = [self.pair(0, 4, here.core)]

    def pair(self, source, target, peer, half=None):
        src = self.view(source, half)
        dst = src if self.fixed else self.view(target, half)
        copy = self.copies.push(src, dst, peer)
        self.sent.append(copy)
        return copy

    def forward(self):
        here = self.here
        self.over_y.wait_recv()
        self.diag_x = self.pair(2, 3, here.across, 0)
        self.cores.append(self.pair(2, 6, here.core))
        self.over_x.wait_recv()
        self.diag_y = self.pair(1, 3, here.mid, 1)
        self.cores.append(self.pair(1, 5, here.core))

    def finish(self):
        self.diag_x.wait_recv()
        self.diag_y.wait_recv()
        self.cores.append(self.pair(3, 7, self.here.core))
        for copy in self.cores:
            copy.wait_recv()

    def drain(self):
        if not self.drained:
            for copy in self.sent:
                copy.wait_send()
        self.drained = True


def nn(left_in, right_in):
    return lax.dot_general(
        left_in, right_in, (((1,), (0,)), ((), ())), preferred_element_type=wide
    )


def nt(left_in, right_in):
    return lax.dot_general(
        left_in, right_in, (((1,), (1,)), ((), ())), preferred_element_type=wide
    )


def tn(left_in, right_in):
    return lax.dot_general(
        left_in, right_in, (((0,), (0,)), ((), ())), preferred_element_type=wide
    )


class ZReduce:
    def __init__(self, here, copies, base, spot, rows, columns, landing):
        self.here, self.copies, self.base, self.spot = here, copies, base, spot
        self.rows, self.columns, self.landing = rows, columns, landing
        self.slots = [copies.slot() for _ in range(5)]
        self.handed = []

    def copy(self, k, peer, slot, half=None):
        r, c = self.spot(k)
        first = self.rows // 2 if half == 1 else 0
        rows = self.rows if half is None else self.rows // 2
        block = self.base.at[pl.ds(r + first, rows), pl.ds(c, self.columns)]
        dst = self.landing.at[slot, pl.ds(first, rows)]
        return self.copies.remote(block, dst, peer, self.slots[slot])

    def outward(self, k):
        copy = self.copy(k, self.here.near, {3: 1, 2: 2, 1: 0}[k])
        setattr(self, f"out{k}", copy)
        self.handed.append(copy)
        pl.when(self.here.outer)(copy.start)

    def outward_half(self, half):
        if half == 0:
            self.out1 = self.copy(1, self.here.near, 0)
        copy = self.copy(1, self.here.near, 0, half)
        self.handed.append(copy)
        pl.when(self.here.outer)(copy.start)

    def outward_piece(self, n, size):
        r, c = self.spot(1)
        if n == 0:
            self.out1 = self.copy(1, self.here.near, 0)
            self.pieces = []
        lanes = pl.ds(n * size, size)
        copy = self.copies.remote(
            self.base.at[pl.ds(r, self.rows), pl.ds(c + n * size, size)],
            self.landing.at[0, :, lanes],
            self.here.near,
        )
        self.pieces.append(copy)
        self.handed.append(copy)
        pl.when(self.here.outer)(copy.start)

    def finish_piece(self, n, size, stage):
        here = self.here

        @pl.when(here.inner)
        def _():
            lanes = pl.ds(n * size, size)
            if n == 0:
                self.in3.wait_recv()
                for load in self.load(3, stage, 1):
                    load.wait()
            self.pieces[n].wait_recv()
            self.copies.local(
                self.landing.at[0, :, lanes], stage.at[0, pl.ds(0, self.rows), lanes]
            ).wait()
            self.add(0, stage, [0, 1], n * size, size)

        if n == 0:

            @pl.when(here.outer)
            def _():
                self.out1.wait_recv()
                for load in self.load(0, stage, 0):
                    load.wait()
                self.add(0, stage, [0])

    def load(self, index, stage, slot):
        size = min(self.rows, 512)
        return [
            self.copies.local(
                self.landing.at[index, pl.ds(n * size, size), :],
                stage.at[slot, pl.ds(0, size), pl.ds(n * self.columns, self.columns)],
            )
            for n in range(self.rows // size)
        ]

    def add(self, target, stage, slots, first=0, columns=None):
        size = min(self.rows, 512)
        columns = self.columns if columns is None else columns
        r, c = self.spot(target)
        for n in range(self.rows // size):

            def body(i, n=n):
                at = pl.ds(pl.multiple_of(i * 64, 64), 64)
                mine = pl.ds(pl.multiple_of(r + n * size + i * 64, 64), 64)
                lanes = pl.ds(c + first, columns)
                value = self.base[mine, lanes].astype(wide)
                for slot in slots:
                    value = value + stage[
                        slot, at, pl.ds(n * self.columns + first, columns)
                    ].astype(wide)
                self.base[mine, lanes] = value.astype(low)

            tiles(size // 64, body)

    def pass_on(self, k, wait, index, stage, copy):
        wait.wait_recv()
        for load in self.load(index, stage, 0):
            load.wait()
        self.add(k, stage, [0])
        copy.start()

    def inward(self, step, stage):
        here = self.here
        if step == 0:
            self.in2 = self.copy(2, here.far, 4)
            args = (2, self.out3, 1, stage, self.in2)
        elif step == 1:
            self.in3 = self.copy(3, here.far, 3)
            args = (3, self.out2, 2, stage, self.in3)
        else:
            self.in1 = self.copy(1, here.near, 0)
            args = (1, self.in2, 4, stage, self.in1)

        @pl.when(here.inner)
        def _():
            self.pass_on(*args)

    def finish(self, stage):
        here = self.here
        self.out1.wait_recv()
        loads = self.load(0, stage, 0)

        @pl.when(here.inner)
        def _():
            self.in3.wait_recv()
            for load in self.load(3, stage, 1) + loads:
                load.wait()
            self.add(0, stage, [0, 1])

        @pl.when(here.outer)
        def _():
            for load in loads:
                load.wait()
            self.add(0, stage, [0])

    def drain(self):
        @pl.when(self.here.inner)
        def _():
            for copy in (self.in1, self.in2, self.in3):
                copy.wait_send()

        @pl.when(self.here.outer)
        def _():
            for copy in self.handed:
                copy.wait_send()


def norm_back(value, grad, gain):
    r = lax.rsqrt(jnp.mean(value * value, axis=-1, keepdims=True) + epsilon)
    u = gain * grad
    lean = jnp.mean(u * value, axis=-1, keepdims=True)
    return r * u - value * (r * r * r * lean), grad * value * r


def exact(left_in, right_in, contract):
    return lax.dot_general(
        left_in, right_in, (contract, ((), ())), precision=highest, preferred_element_type=wide
    )


def layer_kernel(
    tok, cot_in, qkvw, outw, upw, downw, first, gains, second_in, heads_in, widths_in, turns,
    lengths,
    o_block, o_input, o_gq, o_go, o_gu, o_gd, o_first, o_pack, s_hid, s_wq, l_q, l_o, l_u, l_d,
    toks, hid, units, cot, early, wo, wu, wd, cols, rows_info, qkvb, probs, att, acc,
    snd, rcv, out_buf, in_buf, proj, mid_buf, go, stage, top, own_tok, own_out,
    first_buf, slope, gates, dall, second, col, row, square, r_gate, r_inner, r_slope, r_dpre, r_rows, zpart, zland, gain_buf,
    pack, pack_plane, pack_side, pack_ring,
    local_sems, send_sems, recv_sems, acks,
):
    here = Plane()
    copies = Copies(local_sems, send_sems, recv_sems)
    here.greet()
    rank, share, side = here.rank, here.share, here.side
    owned = 128
    width = toks.shape[1]
    block = owned * SHARE
    head_width = wo.shape[0]
    unit_width = wu.shape[1]
    heads = head_width // HD
    own_rows = part(rank, owned)
    wq = early.at[:, 0 : 3 * head_width]
    act, gup = early.at[0:1024], early.at[1024:2048]
    sent, outs, done = [], [], []

    def to_peer(src, dst, peer):
        copy = copies.push(src, dst, peer)
        sent.append(copy)
        return copy

    def spread(src_of, dst):
        return [
            copies.local(src_of(here.shares[d]), dst)
            if d == 0
            else to_peer(src_of(here.shares[d]), dst, here.members[d])
            for d in range(SHARE)
        ]

    def landed(got):
        for i, copy in enumerate(got):
            if i % SHARE:
                copy.wait_recv()
            else:
                copy.wait()

    got_q = [
        spread(
            lambda t, j=j: qkvw.at[j, :, part(t, head_width)],
            wq.at[own_rows, j * head_width : (j + 1) * head_width],
        )
        for j in range(3)
    ]
    mine, other = part(side, owned), part(1 - side, owned)

    class Halves:
        def __init__(self, src, dst):
            self.dst = dst
            pairs = ((mine, 0), (other, owned))
            self.own = [copies.local(src(rows), dst(at)) for rows, at in pairs]
            self.mid = [to_peer(src(rows), dst(at + 256), here.mid) for rows, at in pairs]
            self.core = [to_peer(src(rows), dst(at + 512), here.core) for rows, at in pairs]

        def pass_on(self):
            for copy in self.mid:
                copy.wait_recv()
            self.last = [
                to_peer(self.dst(at), self.dst(at + 512), here.core) for at in (256, 384)
            ]

    tok_in = Halves(lambda r: tok.at[r, :], lambda at: toks.at[at : at + owned])

    row[...] = jnp.zeros_like(row)
    for h in range(2):
        slot = lax.broadcasted_iota(jnp.int32, (1, owned), 1) + h * owned
        segment = slot * 0 + (lengths.shape[1] + slot)
        position = slot
        live = slot * 0
        begin = 0
        for n in range(lengths.shape[1]):
            end = begin + lengths[0, n]
            member = (slot >= begin) & (slot < end)
            segment = jnp.where(member, n, segment)
            position = jnp.where(member, slot - begin, position)
            live = jnp.where(member, 1, live)
            begin = end
        lanes = slice(h * owned, (h + 1) * owned)
        held = (segment, slot, heads_in[h : h + 1, :], widths_in[h : h + 1, :], live, position)
        for n, value in enumerate(held):
            row[n : n + 1, lanes] = value.astype(wide)
        square[...] = jnp.zeros_like(square)
        square[0:8, :] = row[:, lanes]
        turned = jnp.transpose(square[...])
        angles = turned[:, 5:6] * turns[0:1, :]
        col[lanes, 0:HD] = jnp.cos(angles)
        sines = jnp.sin(angles)
        lane = lax.broadcasted_iota(jnp.int32, (owned, HD), 1)
        col[lanes, HD : 2 * HD] = jnp.where(lane < HD // 2, -sines, sines)
        col[lanes, 2 * HD : 3 * HD] = turned
    second[...] = jnp.zeros_like(second)
    for index in range(2):
        second[index, 0:NB, :] = second_in[index]
    col_in = Halves(lambda r: col.at[r, :], lambda at: cols.at[at : at + owned])
    row_in = Halves(
        lambda r: row.at[:, r],
        lambda at: rows_info.at[at // 256, :, at % 256 : at % 256 + owned],
    )
    got_o = spread(lambda t: outw.at[part(t, head_width), :], wo.at[:, own_rows])
    got_u = spread(lambda t: upw.at[:, part(t, unit_width)], wu.at[own_rows, :])
    got_d = spread(lambda t: downw.at[part(t, unit_width), :], wd.at[:, own_rows])
    cot_rows = Halves(lambda r: cot_in.at[r, :], lambda at: cot.at[at : at + owned])
    in_first = copies.local(first.at[0], first_buf)
    in_tok = copies.local(tok.at[mine, :], own_tok)

    g_q = [
        ZGather(here, copies, lambda k, d=d: wq.at[part(k * SHARE + here.shares[d], owned), :])
        for d in range(SHARE)
    ]
    g_o = ZGather(here, copies, lambda k: wo.at[:, part(k, block)])
    g_u = [
        ZGather(
            here,
            copies,
            lambda k, h=h: wu.at[pl.ds(pl.multiple_of(k * block + h * 256, 256), 256), :],
        )
        for h in range(2)
    ]
    g_d = [
        ZGather(here, copies, lambda k, h=h: wd.at[h * 512 : (h + 1) * 512, part(k, block)])
        for h in range(2)
    ]

    def fact(at, index):
        return cols[at, 2 * HD + index : 2 * HD + index + 1]

    def start_q(d):
        for got in got_q:
            if d:
                got[d].wait_recv()
            else:
                got[d].wait()
        g_q[d].start()

    start_q(0)
    start_q(1)

    def normalise(base):
        def body(i):
            at = pl.ds(pl.multiple_of(base + i * 64, 64), 64)
            x = toks[at, :].astype(wide)
            r = lax.rsqrt(jnp.mean(x * x, axis=-1, keepdims=True) + epsilon)
            hid[at, :] = (x * r * gains[0:1, :]).astype(low)

        tiles(4, body)

    def wait_all(waits):
        for wait in waits:
            wait()

    wait_all([c.wait for c in tok_in.own + col_in.own + row_in.own])
    normalise(0)

    def route(index, rows_of):
        made = exact(rows_of[0:owned, :].astype(wide), first_buf[...], ((1,), (0,)))
        sig = 1.0 / (1.0 + jnp.exp(-made))
        inner = made * sig
        logits = exact(inner, second[index], ((1,), (1,)))
        lane = lax.broadcasted_iota(jnp.int32, (owned, HD), 1)
        logits = jnp.where(lane < NB, logits, -1e30)
        raised = jnp.where(
            lane < NB, jnp.exp(logits - jnp.max(logits, axis=-1, keepdims=True)), 0.0
        )
        shares = raised / jnp.sum(raised, axis=-1, keepdims=True)
        hot = jnp.where(lane.astype(wide) == fact(pl.ds(0, owned), 2 + index), 1.0, 0.0)
        gate = NB * jnp.sum(shares * hot, axis=-1, keepdims=True)
        lean = hot - shares
        bare = exact(lean, second[index], ((1,), (0,))) * (sig * (1.0 + made * (1.0 - sig)))
        r_gate[index] = jnp.broadcast_to(gate, (owned, HD))
        r_inner[index] = inner
        r_slope[index] = lean if index else gate * lean
        r_dpre[index] = bare if index else gate * bare
        if index == 1:
            dall[0:owned, :] = bare.astype(low)

    def slope_tiles(index):
        def body(i):
            c = part(i, 256)
            slope[:, c] = exact(r_dpre[index], first_buf[c, :], ((1,), (1,)))

        tiles(8, body)

    in_first.wait()
    route(0, hid)
    in_first = copies.local(first.at[1], first_buf)
    start_q(2)
    start_q(3)
    g_q[0].first()
    g_q[1].first()
    wait_all([c.wait_recv for c in tok_in.core])
    normalise(512)
    g_q[0].second()
    g_q[1].second()
    g_q[2].first()
    g_q[3].first()
    tok_in.pass_on()
    normalise(256)
    g_q[2].second()
    g_q[3].second()
    wait_all([c.wait_recv for c in tok_in.last])
    normalise(768)
    save_hid = copies.local(hid, s_hid)
    landed(got_o)
    g_o.start()
    col_in.pass_on()
    row_in.pass_on()
    wait_all([c.wait_recv for c in col_in.core + row_in.core + col_in.last + row_in.last])
    g_o.first()
    landed(got_u)
    g_o.second()
    g_u[0].start()
    for one in g_q:
        one.arrive()
    save_wq = copies.local(wq, s_wq)

    for j in range(3):

        def qkv_tile(i, j=j):
            at = part(i, 512)
            made = nn(hid[at, :], wq[:, j * head_width : (j + 1) * head_width])
            if j < 2:
                cosine = cols[at, 0:HD]
                sine = cols[at, HD : 2 * HD]
                for h in range(heads):
                    one = made[:, h * HD : (h + 1) * HD]
                    turned = one * cosine + pltpu.roll(one, HD // 2, 1) * sine
                    qkvb[at, j * head_width + h * HD : j * head_width + (h + 1) * HD] = (
                        turned.astype(low)
                    )
            else:
                qkvb[at, j * head_width : (j + 1) * head_width] = made.astype(low)

        tiles(2, qkv_tile)

    g_u[0].first()
    g_u[1].start()

    first_head = (side * SHARE + share) * heads
    scale = HD ** (-0.5)
    for h in range(heads):
        head = (first_head + h).astype(wide)

        def attend_group(g, h=h, head=head):
            at = part(g, 256)
            query, keyed, value = (
                qkvb[at, pl.ds(j * head_width + h * HD, HD)] for j in range(3)
            )
            info = rows_info[g]
            seg_k, slot_k, bucket_k = info[0:1, :], info[1:2, :], info[2:3, :]
            reach_k = jnp.where(4.0 * bucket_k + 4.0 > head, 1.0, 0.0)
            slot_q = fact(at, 1)
            usable = (reach_k > 0.5) | (slot_k == slot_q)
            allowed = (fact(at, 0) == seg_k) & (slot_k <= slot_q) & usable
            scores = jnp.where(allowed, nt(query, keyed) * scale, -1e30)
            weights = jnp.exp(scores - jnp.max(scores, axis=-1, keepdims=True))
            p = weights / jnp.sum(weights, axis=-1, keepdims=True)
            probs[part(g * heads + h, 256), :] = p
            mixed = nn(p.astype(low), value)
            att[at, h * HD : (h + 1) * HD] = jnp.where(
                4.0 * fact(at, 2) + 4.0 > head, mixed, 0.0
            ).astype(low)

        tiles(SHARE, attend_group)

    reduce = RowReduce(here, copies, (snd, rcv, acc, out_buf, in_buf), acks)

    def partial_sums(term, extra=None):
        lanes = acc.shape[1] if extra is not None else width
        reduce.begin(lanes)
        for i in range(2):

            def send_tile(n, i=i):
                snd[i * 256 : (i + 1) * 256, part(n, 512)] = term(
                    pl.ds(512 + i * 256, 256), n
                ).astype(low)

            tiles(4, send_tile)
            if extra is not None:
                snd[i * 256 : (i + 1) * 256, width:lanes] = extra[
                    pl.ds(512 + i * 256, 256), :
                ].astype(low)
            reduce.core_send(i)

        def own_tile(n):
            acc[:, part(n, 512)] = term(pl.ds(0, 512), n)

        tiles(4, own_tile)
        if extra is not None:
            acc[:, width:lanes] = extra[0:512, :]

    g_o.arrive()
    partial_sums(lambda at, n: nn(att[at, :], wo[:, part(n, 512)]))
    g_u[0].second()
    reduce.diagonal()
    g_u[1].first()
    reduce.sides()
    g_u[1].second()
    landed(got_d)
    g_d[0].start()
    g_d[1].start()
    in_tok.wait()
    reduce.arrive()

    def row_tiles(body):
        def step(i):
            at = pl.multiple_of(i * 64, 64)
            body(at, pl.ds(at, 64))

        tiles(owned // 64, step)

    def middle_tile(at, rows):
        projected = reduce.total(at, 64)
        proj[rows, :] = projected
        middle = own_tok[rows, :].astype(wide) + r_gate[0, rows, 0:1] * projected
        mid_buf[rows, :] = middle
        r = lax.rsqrt(jnp.mean(middle * middle, axis=-1, keepdims=True) + epsilon)
        units[rows, :] = (middle * r * gains[1:2, :]).astype(low)

    row_tiles(middle_tile)
    reduce.release()

    def row_view(buf):
        def view(k, h):
            if h is None:
                return buf.at[k * owned : (k + 1) * owned]
            return buf.at[k * owned + h * 64 : k * owned + (h + 1) * 64]

        return view

    units_out = RowGather(here, copies, row_view(units))
    units_out.start()
    in_first.wait()
    route(1, units)
    gates[0:owned, :] = r_gate[1]
    gates_out = RowGather(here, copies, row_view(gates))
    dall_out = RowGather(here, copies, row_view(dall))
    gates_out.start()
    dall_out.start()

    def first_low(n):
        return go[pl.ds(pl.multiple_of(n % 2 * 512, 512), 512), part(n // 2, 256)]

    def first_tile(i):
        go[part(i % 8, 128), part(i // 8, 256)] = first_buf[part(i, 128), :].astype(low)

    tiles(16, first_tile)
    in_first = copies.local(first.at[0], first_buf)
    g_d[0].first()
    units_out.forward()
    gates_out.forward()
    dall_out.forward()
    g_d[1].first()
    units_out.finish()
    gates_out.finish()
    dall_out.finish()
    g_d[0].second()
    g_d[1].second()
    wait_all([c.wait for c in cot_rows.own])
    cot_rows.pass_on()
    wait_all([c.wait_recv for c in cot_rows.core + cot_rows.last])

    def live_cot(at):
        return jnp.where(fact(at, 4) > 0.5, cot[at, :].astype(wide), 0.0)

    for copy in tok_in.last + cot_rows.last:
        copy.wait_send()
        done.append(copy)

    def keep_tile(at, rows):
        top[rows, :] = live_cot(rows).astype(low)

    row_tiles(keep_tile)

    def scale_tile(i):
        at = part(i, 64)
        cot[at, :] = (gates[at, 0:1] * live_cot(at)).astype(low)

    tiles(16, scale_tile)

    for one in g_u:
        one.arrive()

    first_unit = (side * SHARE + share) * unit_width

    def used_units(at, base, rows, columns):
        lane = lax.broadcasted_iota(jnp.int32, (rows, columns), 1) + base
        return lane.astype(wide) < (FF // NB) * (fact(at, 3) + 1.0)

    save_wq.wait()
    for one in g_q:
        one.drain()

    def up_tile(i):
        m, n = i % 2, i // 2
        at, c = part(m, 512), part(n, 512)
        made = nn(units[at, :], wu[:, c])
        acc[:, part(m * 2 + n, 512)] = made
        relu = jnp.maximum(made, 0.0)
        used = used_units(at, first_unit + n * 512, 512, 512)
        act[at, c] = jnp.where(used, relu * relu, 0.0).astype(low)

    tiles(4, up_tile)
    def deliver(piece_of, dst):
        for d in range(SHARE):
            src = piece_of(here.shares[d])
            if d == 0:
                outs.append(copies.local(src, dst))
            else:
                sent.append(copies.push(src, dst, here.members[d]))
                owed.append(sent[-1])

    owed = []

    gd, gu, gq = toks, hid, wd
    blocks = [here.place, here.near_place, here.two_place, here.far_place]
    z_d = ZReduce(here, copies, gd, lambda k: (0, k * block), unit_width, block, l_d)
    z_u = ZReduce(
        here, copies, gu, lambda k: (k % 2 * block, k // 2 * unit_width), block, unit_width, l_u
    )
    z_o = ZReduce(here, copies, go, lambda k: (k * head_width, 0), head_width, block, l_o)
    z_q = ZReduce(
        here, copies, gq, lambda k: (k % 2 * block, k // 2 * 1024), block, 3 * head_width, l_q
    )

    def down_block(k):
        def body(i):
            m = part(i, 512)
            gd[m, k * block : (k + 1) * block] = tn(
                act[:, m], cot[:, part(blocks[k], block)]
            ).astype(low)

        tiles(unit_width // 512, body)

    for k in (3, 2, 1):
        down_block(k)
        z_d.outward(k)
    down_block(0)
    z_d.inward(0, stage)
    z_d.inward(1, stage)
    for one in g_d:
        one.arrive()

    def gup_tile(m):
        at = part(m, 512)
        dots = jnp.zeros((512, 1), wide)
        for n in range(unit_width // 512):
            c = slice(n * 512, (n + 1) * 512)
            made = nt(cot[at, :], wd[c, :])
            used = used_units(at, first_unit + n * 512, 512, 512)
            relu = jnp.maximum(acc[:, part(m * 2 + n, 512)], 0.0)
            gup[at, c] = jnp.where(used, 2.0 * relu * made, 0.0).astype(low)
            dots = dots + jnp.sum(act[at, c].astype(wide) * made, axis=-1, keepdims=True)
        gates[at, :] = jnp.broadcast_to(dots, (512, HD))
        r_rows[at, 256:512] = (dots * dall[at, :].astype(wide)).astype(low)

    gates_out.drain()
    tiles(2, gup_tile)

    save_hid.wait()

    def up_block(k):
        r, c = k % 2 * block, k // 2 * unit_width

        def body(i):
            gu[r : r + block, pl.ds(pl.multiple_of(c + i * 512, 512), 512)] = tn(
                units[:, part(blocks[k], block)], gup[:, part(i, 512)]
            ).astype(low)

        tiles(unit_width // 512, body)

    up_block(3)
    z_u.outward(3)

    reduce.await_release()
    partial_sums(
        lambda at, n: nt(gup[at, :], wu[part(n, 512), :])
        + nt(r_rows[at, 256:512], first_low(n)),
        gates,
    )
    up_block(2)
    z_u.outward(2)
    reduce.diagonal()
    up_block(1)
    z_u.outward_half(0)
    z_d.inward(2, stage)
    reduce.sides()
    up_block(0)

    column = share * 2 + side
    ucol = dall
    dall_out.drain()

    def ucol_tile(i):
        ucol[part(i, 256), :] = units[part(i, 256), part(column, 256)]

    tiles(4, ucol_tile)
    units_out.drain()
    in_hid = copies.local(s_hid, units)
    for one in g_u:
        one.drain()
    in_wq = copies.local(s_wq, wu.at[:, 0 : 3 * head_width])

    r_rows_out = RowGather(here, copies, row_view(r_rows))

    def keep_gate(index, rows, weight):
        c = slice(index * 256, (index + 1) * 256)
        r_rows[rows, c] = (weight * r_dpre[index, rows, :]).astype(low)
        r_slope[index, rows, :] = weight * r_slope[index, rows, :]

    places = [here.place, here.near_place, here.two_place, here.far_place]
    planes = [None, here.near, here.two, here.far]

    def first_rows(k, h):
        target = here.shares[k // 4 + k // 2 % 2 * 2] * 2 + (side if k % 2 == 0 else 1 - side)
        base = target * 256
        if h is None:
            return o_first.at[:, pl.ds(pl.multiple_of(base, 256), 256), :]
        return o_first.at[:, pl.ds(pl.multiple_of(base + h * 128, 128), 128), :]

    first_out = RowGather(here, copies, first_rows, True)

    class FirstSum:
        def __init__(self):
            zpart[0] = tn(units[:, part(column, 256)], r_rows[:, 0:256]).astype(low)
            zpart[1] = tn(ucol[...], r_rows[:, 256:512]).astype(low)
            self.got = []
            for k in range(4):
                src, dst = zpart.at[:, part(places[k], 64), :], zland.at[here.place]
                self.got.append(
                    copies.local(src, dst) if k == 0 else to_peer(src, dst, planes[k])
                )

        def add(self):
            landed(self.got)
            for copy in self.got[1:]:
                copy.wait_send()
                done.append(copy)
            total = zland[0].astype(wide)
            for k in range(1, 4):
                total = total + zland[k].astype(wide)
            zpart[:, 0:64, :] = total.astype(low)
            at = pl.ds(pl.multiple_of(column * 256 + here.place * 64, 64), 64)
            src, dst = zpart.at[:, 0:64, :], o_first.at[:, at, :]
            self.got = [
                copies.local(src, dst) if k == 0 else to_peer(src, dst, planes[k])
                for k in range(4)
            ]

        def show(self):
            landed(self.got)
            first_out.start()

    reduce.arrive()
    gproj = cot
    gain_buf[...] = jnp.zeros_like(gain_buf)

    def grad_tile(at, rows):
        total = reduce.total(at, 64)
        grad = total[:, 0:width]
        keep_gate(1, rows, total[:, width : width + 1])
        back, gain_terms = norm_back(mid_buf[rows, :], grad, gains[1:2, :])
        grad_middle = top[rows, :].astype(wide) + back
        gproj[rows, :] = (r_gate[0, rows, 0:1] * grad_middle).astype(low)
        grad_gate = jnp.sum(grad_middle * proj[rows, :], axis=-1, keepdims=True)
        keep_gate(0, rows, grad_gate)
        r_gate[0, rows, :] = jnp.broadcast_to(grad_gate, (64, HD))
        proj[rows, :] = grad_middle
        gain_buf[1:2, :] = gain_buf[1:2, :] + jnp.sum(gain_terms, axis=0, keepdims=True)

    row_tiles(grad_tile)
    reduce.release()
    gproj_out = RowGather(here, copies, row_view(gproj))
    gproj_out.start()
    r_rows_out.start()
    in_first.wait()
    slope_tiles(0)
    z_u.inward(0, stage)
    gproj_out.forward()
    r_rows_out.forward()

    reduce.await_release()
    partial_sums(lambda at, n: nn(act[at, :], wd[:, part(n, 512)]))
    gproj_out.finish()
    r_rows_out.finish()
    in_hid.wait()
    sum_first = FirstSum()
    z_u.outward_half(1)
    z_d.finish(stage)
    deliver(lambda t: gd.at[:, part(t, owned)], o_gd.at[part(share, unit_width), :])


    def out_block(k):
        go[k * head_width : (k + 1) * head_width, :] = tn(
            att[...], gproj[:, part(blocks[k], block)]
        ).astype(low)

    for k in range(4):
        out_block(k)
    gatt, gqkv = gup, act

    def gatt_tile(i):
        at = part(i, 512)
        made = nt(gproj[at, :], wo[...]).astype(low)
        for h in range(heads):
            used = 4.0 * fact(at, 2) + 4.0 > (first_head + h).astype(wide)
            gatt[at, h * HD : (h + 1) * HD] = jnp.where(
                used, made[:, h * HD : (h + 1) * HD].astype(wide), 0.0
            ).astype(low)

    tiles(2, gatt_tile)

    for h in range(heads):

        def back_group(g, h=h):
            at = part(g, 256)
            lanes = [pl.ds(j * head_width + h * HD, HD) for j in range(3)]
            query, keyed, value = (qkvb[at, lane] for lane in lanes)
            grad = gatt[at, h * HD : (h + 1) * HD]
            p = probs[part(g * heads + h, 256), :]
            grad_p = nt(grad, value)
            row_dot = jnp.sum(p * grad_p, axis=-1, keepdims=True)
            grad_s = (p * (grad_p - row_dot)).astype(low)
            cosine = cols[at, 0:HD]
            sine = cols[at, HD : 2 * HD]
            for lane, turned in (
                (lanes[0], nn(grad_s, keyed) * scale),
                (lanes[1], tn(grad_s, query) * scale),
            ):
                gqkv[at, lane] = (
                    turned * cosine - pltpu.roll(turned, HD // 2, 1) * sine
                ).astype(low)
            gqkv[at, lanes[2]] = tn(p.astype(low), grad).astype(low)

        tiles(SHARE, back_group)

    def qkv_block(k):
        r, c = k % 2 * block, k // 2 * 1024
        for j in range(3):
            gq[r : r + block, c + j * head_width : c + (j + 1) * head_width] = tn(
                units[:, part(blocks[k], block)], gqkv[:, j * head_width : (j + 1) * head_width]
            ).astype(low)

    for one in g_d:
        one.drain()
    z_u.inward(1, stage)
    sum_first.add()
    qkv_block(3)
    z_q.outward(3)
    z_o.outward(3)
    qkv_block(2)
    z_q.outward(2)
    z_o.outward(2)
    z_o.outward(1)
    qkv_block(1)
    for j in range(3):
        z_q.outward_piece(j, head_width)
    qkv_block(0)

    reduce.diagonal()
    reduce.sides()
    z_u.inward(2, stage)
    reduce.arrive()

    def block_tile(at, rows):
        own_out[rows, :] = jnp.where(
            fact(rows, 4) > 0.5,
            mid_buf[rows, :] + r_gate[1, rows, 0:1] * reduce.total(at, 64),
            0.0,
        ).astype(low)

    row_tiles(block_tile)
    reduce.release()
    shown = copies.local(own_out, o_block.at[mine])
    shown_far = to_peer(own_out, o_block.at[mine], here.across)

    in_wq.wait()
    reduce.await_release()
    partial_sums(
        lambda at, n: nt(gqkv[at, 0 : 3 * head_width], wu[part(n, 512), 0 : 3 * head_width])
    )
    reduce.diagonal()
    z_u.finish(stage)
    deliver(lambda t: gu.at[part(t, owned), 0:unit_width], o_gu.at[:, part(share, unit_width)])
    z_q.inward(0, stage)
    z_o.inward(0, stage)
    reduce.sides()
    sum_first.show()
    z_q.inward(1, stage)
    z_q.inward(2, stage)
    z_o.inward(1, stage)
    z_o.inward(2, stage)
    shown.wait()
    shown_far.wait()
    done.append(shown_far)
    reduce.arrive()

    def input_tile(at, rows):
        grad = reduce.total(at, 64) + r_gate[0, rows, 0:1] * slope[rows, :]
        back, gain_terms = norm_back(own_tok[rows, :].astype(wide), grad, gains[0:1, :])
        own_out[rows, :] = (proj[rows, :] + back).astype(low)
        gain_buf[0:1, :] = gain_buf[0:1, :] + jnp.sum(gain_terms, axis=0, keepdims=True)

    row_tiles(input_tile)
    first_out.forward()

    for index in range(2):
        for j in range(8):
            pack[index * 8 + j : index * 8 + j + 1, :] = gain_buf[
                index : index + 1, j * 256 : (j + 1) * 256
            ]
        made = exact(r_slope[index], r_inner[index], ((0,), (0,)))
        pack[16 + index * 8 : 24 + index * 8, :] = made[0:8, :]
        lane = lax.broadcasted_iota(jnp.int32, (owned, 256), 1)
        own = pl.ds(0, owned)
        hot = (lane.astype(wide) == fact(own, 2 + index)) & (fact(own, 4) > 0.5)
        count = jnp.sum(jnp.where(hot, 1.0, 0.0), axis=0, keepdims=True)
        pack[32 + index * 8 : 40 + index * 8, :] = jnp.broadcast_to(count, (8, 256))

    def sum_slots(buf, count):
        total = buf[0]
        for k in range(1, count):
            total = total + buf[k]
        return total

    got = [
        copies.local(pack, pack_plane.at[share])
        if d == 0
        else to_peer(pack, pack_plane.at[share], here.members[d])
        for d in range(SHARE)
    ]
    landed(got)
    for copy in got[1:]:
        copy.wait_send()
        done.append(copy)
    pack[...] = sum_slots(pack_plane, SHARE)
    got = [
        copies.local(pack, pack_side.at[side]),
        to_peer(pack, pack_side.at[side], here.across),
    ]
    outs.append(copies.local(own_out, o_input.at[mine]))
    input_far = copies.push(own_out, o_input.at[mine], here.across)
    first_out.finish()
    landed(got)
    got[1].wait_send()
    done.append(got[1])
    pack[...] = pack_side[0] + pack_side[1]
    got = [
        copies.local(pack, pack_ring.at[here.place])
        if k == 0
        else to_peer(pack, pack_ring.at[here.place], planes[k])
        for k in range(4)
    ]

    z_o.finish(stage)
    deliver(
        lambda t: go.at[0:head_width, part(t, owned)], o_go.at[part(share, head_width), :]
    )
    for j in range(3):
        z_q.finish_piece(j, head_width, stage)
        deliver(
            lambda t, j=j: gq.at[part(t, owned), j * head_width : (j + 1) * head_width],
            o_gq.at[j, :, part(share, head_width)],
        )
    landed(got)
    for copy in got[1:]:
        copy.wait_send()
        done.append(copy)
    pack[...] = sum_slots(pack_ring, 4)
    outs.append(copies.local(pack, o_pack))

    drains = [g_o] + g_q + g_u + g_d + [z_d, z_u, z_o, z_q, reduce, units_out, gates_out, dall_out]
    for one in drains + [gproj_out, r_rows_out, first_out]:
        one.drain()
    input_far.wait()
    for copy in owed:
        copy.wait_recv()
    for copy in outs:
        copy.wait()
    for copy in sent:
        if not any(copy is one for one in done):
            copy.wait_send()
    copies.check()


def finish_kernel(
    block, inp, gq, go, gu, gd, gf, sums,
    o_block, o_inp, o_gains, o_gq, o_go, o_gu, o_gd, o_first, o_second, o_usage,
    b_block, b_inp, b_q, b_o, b_u, b_d, b_f, w_q, w_o, w_u, w_d, w_f, in_sems, out_sems,
):
    narrow = [(gu, b_u), (gd, b_d), (gq, b_q), (gf, b_f), (go, b_o)]
    narrow += [(block, b_block), (inp, b_inp)]
    loads = [
        pltpu.make_async_copy(src, dst, in_sems.at[i]) for i, (src, dst) in enumerate(narrow)
    ]
    for load in loads:
        load.start()
    stores = []

    def store(src, dst):
        copy = pltpu.make_async_copy(src, dst, out_sems.at[len(stores)])
        copy.start()
        stores.append(copy)

    for index in range(2):
        for j in range(8):
            o_gains[index : index + 1, j * 256 : (j + 1) * 256] = sums[
                index * 8 + j : index * 8 + j + 1, :
            ]
        o_second[index] = sums[16 + index * 8 : 16 + index * 8 + NB, :]
        o_usage[index : index + 1, :] = sums[32 + index * 8 : 33 + index * 8, 0:NB]
    wides = [(b_u, w_u, o_gu), (b_d, w_d, o_gd), (b_q, w_q, o_gq)]
    wides += [(b_f, w_f, o_first), (b_o, w_o, o_go)]
    for i, (src, dst, out) in enumerate(wides):
        loads[i].wait()
        lead = src.shape[0] if len(src.shape) == 3 else None
        step = 128
        rows = src.shape[-2]
        for n in range(lead or 1):

            def widen(k, src=src, dst=dst, n=n, lead=lead):
                at = part(k, step)
                if lead is None:
                    dst[at, :] = src[at, :].astype(wide)
                else:
                    dst[n, at, :] = src[n, at, :].astype(wide)

            tiles(rows // step, widen)
        store(dst, out)
    for i, (src, out) in enumerate(((b_block, o_block), (b_inp, o_inp))):
        loads[5 + i].wait()
        store(src, out)
    for copy in stores:
        copy.wait()


def plane(mesh):
    fsdp = mesh.shape["fsdp"]
    ring_size = fsdp // SHARE

    def shards(
        tokens,
        head_bucket,
        ffn_bucket,
        lengths,
        norm_gains,
        qkv_weight,
        out_weight,
        up_weight,
        down_weight,
        router_first,
        router_second,
        cotangent,
    ):
        rows, width = tokens.shape
        half = rows // 2
        local_units = up_weight.shape[1]
        units = local_units // SHARE
        local_width = out_weight.shape[0]
        head_width = local_width // SHARE
        heads = head_width // HD
        owned = width // fsdp
        block = width // ring_size
        plane_rows = SHARE * rows

        turns = np.float32(theta_base) ** np.float32(-2.0 * np.arange(HD // 2) / HD)
        turns = np.tile(np.concatenate([turns, turns])[None, :], (8, 1)).astype(np.float32)
        b16, f32 = low, wide
        hidden = router_first.shape[2]
        small = 48

        def shape(*dims):
            return jax.ShapeDtypeStruct(dims[1:], dims[0])

        def buffer(*dims):
            return pltpu.VMEM(dims[1:], dims[0])

        anywhere = pl.BlockSpec(memory_space=pl.ANY)
        vmem = pl.BlockSpec(memory_space=pltpu.VMEM)
        (
            block_out,
            input_grad,
            raw_qkv,
            raw_out,
            raw_up,
            raw_down,
            raw_first,
            sums,
            *_,
        ) = pl.pallas_call(
            layer_kernel,
            out_shape=[
                shape(b16, rows, width),
                shape(b16, rows, width),
                shape(b16, 3, owned, local_width),
                shape(b16, local_width, owned),
                shape(b16, owned, local_units),
                shape(b16, local_units, owned),
                shape(b16, *router_first.shape),
                shape(f32, small, 256),
                shape(b16, plane_rows, width),
                shape(b16, width, 3 * head_width),
                shape(b16, 5, block, 3 * head_width),
                shape(b16, 5, head_width, block),
                shape(b16, 5, block, units),
                shape(b16, 5, units, block),
            ],
            in_specs=[anywhere] * 7 + [vmem] * 5 + [pl.BlockSpec(memory_space=pltpu.SMEM)],
            out_specs=[anywhere] * 14,
            scratch_shapes=[
                buffer(b16, plane_rows, width),
                buffer(b16, plane_rows, width),
                buffer(b16, plane_rows, width),
                buffer(b16, plane_rows, width),
                buffer(b16, 2 * plane_rows, units),
                buffer(b16, head_width, width),
                buffer(b16, width, units),
                buffer(b16, units, width),
                buffer(f32, plane_rows, 3 * HD),
                buffer(f32, SHARE, 8, rows),
                buffer(b16, plane_rows, 3 * head_width),
                buffer(f32, SHARE * heads * rows, rows),
                buffer(b16, plane_rows, head_width),
                buffer(f32, plane_rows // 2, width + HD),
                buffer(b16, plane_rows // 2, width + HD),
                buffer(b16, plane_rows // 2, width + HD),
                buffer(b16, 3 * half, width + HD),
                buffer(b16, 3 * half, width + HD),
                buffer(f32, half, width),
                buffer(f32, half, width),
                buffer(b16, 4 * head_width, block),
                buffer(b16, 2, block, units),
                buffer(b16, half, width),
                buffer(b16, half, width),
                buffer(b16, half, width),
                buffer(f32, width, hidden),
                buffer(f32, half, width),
                buffer(f32, plane_rows, HD),
                buffer(b16, plane_rows, hidden),
                buffer(f32, 2, HD, hidden),
                buffer(f32, rows, 3 * HD),
                buffer(f32, 8, rows),
                buffer(f32, HD, HD),
                buffer(f32, 2, half, HD),
                buffer(f32, 2, half, hidden),
                buffer(f32, 2, half, HD),
                buffer(f32, 2, half, hidden),
                buffer(b16, plane_rows, 2 * hidden),
                buffer(b16, 2, 256, hidden),
                buffer(b16, 4, 2, 64, hidden),
                buffer(f32, 8, width),
                buffer(f32, small, 256),
                buffer(f32, SHARE, small, 256),
                buffer(f32, 2, small, 256),
                buffer(f32, 4, small, 256),
                pltpu.SemaphoreType.DMA((128,)),
                pltpu.SemaphoreType.DMA((256,)),
                pltpu.SemaphoreType.DMA((256,)),
                pltpu.SemaphoreType.REGULAR((3,)),
            ],
            compiler_params=pltpu.CompilerParams(
                collective_id=0, has_side_effects=True, vmem_limit_bytes=127 * 2**19
            ),
        )(
            tokens,
            cotangent,
            jnp.transpose(qkv_weight, (1, 0, 2)),
            out_weight,
            up_weight,
            down_weight,
            router_first,
            norm_gains,
            jnp.transpose(router_second, (0, 2, 1)),
            head_bucket.reshape(2, half),
            ffn_bucket.reshape(2, half),
            jnp.asarray(turns),
            lengths,
        )
        wides = [
            (3, owned, local_width),
            (local_width, owned),
            (owned, local_units),
            (local_units, owned),
            router_first.shape,
        ]
        (
            block_out,
            input_grad,
            grad_gains,
            grad_qkv,
            grad_out,
            grad_up,
            grad_down,
            grad_first,
            grad_second,
            usage,
        ) = pl.pallas_call(
            finish_kernel,
            out_shape=[shape(b16, rows, width), shape(b16, rows, width), shape(f32, 2, width)]
            + [shape(f32, *dims) for dims in wides]
            + [shape(f32, 2, NB, hidden), shape(f32, 2, NB)],
            in_specs=[anywhere] * 7 + [vmem],
            out_specs=[anywhere] * 2 + [vmem] + [anywhere] * 5 + [vmem] * 2,
            scratch_shapes=[buffer(b16, rows, width)] * 2
            + [buffer(b16, *dims) for dims in wides]
            + [buffer(f32, *dims) for dims in wides]
            + [pltpu.SemaphoreType.DMA((8,)), pltpu.SemaphoreType.DMA((8,))],
            compiler_params=pltpu.CompilerParams(vmem_limit_bytes=60 * 2**20),
        )(block_out, input_grad, raw_qkv, raw_out, raw_up, raw_down, raw_first, sums)
        grad_qkv = jnp.transpose(grad_qkv, (1, 0, 2))
        grad_second = jnp.transpose(grad_second, (0, 2, 1))
        return (
            block_out,
            input_grad,
            grad_gains,
            grad_qkv,
            grad_out,
            grad_up,
            grad_down,
            grad_first,
            grad_second,
            usage,
        )

    return shards


def solution(mesh):
    shards = plane(mesh) if mesh.shape["fsdp"] == 4 * SHARE else general(mesh)
    in_specs = (
        P("fsdp", None),
        P("fsdp"),
        P("fsdp"),
        P("fsdp", None),
        P(),
        P("fsdp", None, "tensor"),
        P("tensor", "fsdp"),
        P("fsdp", "tensor"),
        P("tensor", "fsdp"),
        P(),
        P(),
        P("fsdp", None),
    )
    out_specs = (
        P("fsdp", None),
        P("fsdp", None),
        P(),
        P("fsdp", None, "tensor"),
        P("tensor", "fsdp"),
        P("fsdp", "tensor"),
        P("tensor", "fsdp"),
        P(),
        P(),
        P(),
    )
    return jax.shard_map(
        shards, mesh=mesh, in_specs=in_specs, out_specs=out_specs, check_vma=False
    )
```

```python
from functools import partial

import jax
import jax.numpy as jnp
import numpy as np
from jax import lax
from jax.experimental import pallas as pl
from jax.experimental.pallas import tpu as pltpu
from jax.sharding import PartitionSpec as P

HEADS = 16
HD = 128
FF = 8192
NB = 4
SHARE = 4

epsilon = 1e-05
theta_base = 10000.0
highest = lax.Precision.HIGHEST
low = jnp.bfloat16
wide = jnp.float32
MESH = pl.DeviceIdType.MESH


def norm_piece(values_in, gain_row):
    return (
        values_in
        * lax.rsqrt(jnp.mean(values_in * values_in, axis=-1, keepdims=True) + epsilon)
        * gain_row
    )


def route_piece(hidden_in, router_in, router_out, bucket):
    inner = jax.nn.silu(jnp.dot(hidden_in, router_in, precision=highest))
    logits = jnp.dot(inner, router_out, precision=highest)
    probs_all = jax.nn.softmax(logits, axis=-1)
    onehot = (bucket[:, None] == jnp.arange(NB, dtype=jnp.int32)[None, :]).astype(wide)
    return NB * jnp.sum(probs_all * onehot, axis=-1)


def dot(left_in, right_in):
    return jnp.dot(left_in, right_in, preferred_element_type=wide)


def dot_rows(left_in, right_in):
    return lax.dot_general(
        left_in, right_in, (((0,), (0,)), ((), ())), preferred_element_type=wide
    )


def dot_cols(left_in, right_in):
    return lax.dot_general(
        left_in, right_in, (((1,), (1,)), ((), ())), preferred_element_type=wide
    )


def rotate(operand, cosine, sine_table):
    half_dim = operand.shape[-1] // 2
    lead_half = operand[..., :half_dim]
    tail_half = operand[..., half_dim:]
    return jnp.concatenate(
        [lead_half * cosine - tail_half * sine_table, tail_half * cosine + lead_half * sine_table],
        axis=-1,
    )


def layout(length_rows, slot_ids):
    seq_count = length_rows.shape[1]
    order = jnp.arange(seq_count, dtype=jnp.int32)
    seq_ends = jnp.sum(
        jnp.where(order[None, None, :] <= order[None, :, None], length_rows[:, None, :], 0), axis=2
    )
    seq_starts = seq_ends - length_rows
    slots = slot_ids[None, :, None]
    member = (slots >= seq_starts[:, None, :]) & (slots < seq_ends[:, None, :])
    seq_of = jnp.sum(jnp.where(member, jnp.arange(seq_count, dtype=jnp.int32), 0), axis=2)
    live_rows = jnp.any(member, axis=2)
    seq_begin = jnp.sum(jnp.where(member, seq_starts[:, None, :], 0), axis=2)
    segment = jnp.where(live_rows, seq_of, seq_count + slot_ids[None, :])
    position = slot_ids[None, :] - seq_begin
    return segment, position, live_rows


def general(mesh):
    fsdp = mesh.shape["fsdp"]
    ring_size = fsdp // SHARE

    def hop(moved, bits):
        return lax.ppermute(moved, "fsdp", [(i, i ^ bits) for i in range(fsdp)])

    def cross(moved):
        return lax.ppermute(moved, "tensor", [(0, 1), (1, 0)])

    def shards(
        tokens,
        head_bucket,
        ffn_bucket,
        lengths,
        norm_gains,
        qkv_weight,
        out_weight,
        up_weight,
        down_weight,
        router_first,
        router_second,
        cotangent,
    ):
        rows, width = tokens.shape
        half = rows // 2
        rank = lax.axis_index("fsdp")
        side = lax.axis_index("tensor")
        share = rank % SHARE
        place = rank // SHARE
        local_units = up_weight.shape[1]
        units = local_units // SHARE
        local_width = out_weight.shape[0]
        head_width = local_width // SHARE
        heads = head_width // HD
        owned = width // fsdp
        block = width // ring_size

        chain = [None, None]

        def ring(moved, stream):
            if chain[stream] is not None:
                moved, _ = lax.optimization_barrier((moved, chain[stream]))
            got = lax.ppermute(
                moved, "fsdp", [(i, (i + SHARE) % fsdp) for i in range(fsdp)]
            )
            chain[stream] = got
            return got

        def place_at(step):
            return (place - step) % ring_size

        def own_half(arr):
            return lax.dynamic_slice_in_dim(arr, side * half, half, 0)

        def relative(arr):
            return jnp.concatenate(
                [own_half(arr), lax.dynamic_slice_in_dim(arr, (1 - side) * half, half, 0)], axis=0
            )

        def gather_rows(arr):
            other = hop(arr, 2)
            plane = jnp.concatenate([arr[:half], other[:half], arr[half:], other[half:]], axis=0)
            return jnp.concatenate([plane, hop(plane, 1)], axis=0)

        def gather_halves(arr):
            pair = jnp.concatenate([arr, hop(arr, 2)], axis=0)
            plane = jnp.concatenate([pair, cross(pair)], axis=0)
            return jnp.concatenate([plane, hop(plane, 1)], axis=0)

        def reduce_rows(keep, send):
            total = keep + hop(send.astype(low), 1).astype(wide)
            total = total[: 2 * half] + cross(total[2 * half :].astype(low)).astype(wide)
            return total[:half] + hop(total[half:].astype(low), 2).astype(wide)

        def whole_rows(arr):
            other = cross(arr)
            return jnp.where(
                side == 0,
                jnp.concatenate([arr, other], axis=0),
                jnp.concatenate([other, arr], axis=0),
            )

        def spread(pieces_for, axis):
            out = None
            for bits in range(SHARE):
                piece = pieces_for(share ^ bits)
                got = piece if bits == 0 else hop(piece, bits)
                if out is None:
                    dims = list(got.shape)
                    dims[axis] *= SHARE
                    out = jnp.zeros(dims, got.dtype)
                out = lax.dynamic_update_slice_in_dim(
                    out, got, (share ^ bits) * got.shape[axis], axis
                )
            return out

        def ring_gather(own, axis):
            dims = list(own.shape)
            dims[axis] = width
            out = jnp.zeros(dims, own.dtype)
            mid = own.shape[0] // 2
            moving = [own[:mid], own[mid:]]
            for step in range(ring_size):
                if step:
                    moving = [ring(moving[s], s) for s in range(2)]
                base = place_at(step) * block
                for s in range(2):
                    if axis == 0:
                        at = (base + s * mid, 0)
                    else:
                        at = (s * mid, base)
                    out = lax.dynamic_update_slice(out, moving[s], at)
            return out

        def ring_reduce(term):
            moving = [None, None]
            for step in range(1, ring_size):
                for s in range(2):
                    part = term(place_at(step), s)
                    if moving[s] is not None:
                        part = part + moving[s].astype(wide)
                    moving[s] = part.astype(low)
                for s in range(2):
                    moving[s] = ring(moving[s], s)
            return [term(place, s) + moving[s].astype(wide) for s in range(2)]

        def scatter_back(parts, axis):
            joined = jnp.concatenate(parts, axis=0)
            other = 1 - axis
            out_dims = list(joined.shape)
            out_dims[axis] = owned
            stride = out_dims[other]
            out_dims[other] *= SHARE
            out = jnp.zeros(out_dims, wide)
            for bits in range(SHARE):
                piece = lax.dynamic_slice_in_dim(joined, (share ^ bits) * owned, owned, axis)
                if bits:
                    piece = hop(piece.astype(low), bits).astype(wide)
                out = lax.dynamic_update_slice_in_dim(out, piece, (share ^ bits) * stride, other)
            return out

        def qkv_piece(target):
            return lax.dynamic_slice_in_dim(
                qkv_weight, target * head_width, head_width, 2
            ).reshape(owned, 3 * head_width)

        qkv_block = spread(qkv_piece, 0)
        rel_tokens = relative(tokens)
        rel_cot = relative(cotangent)
        ints = relative(jnp.stack([head_bucket, ffn_bucket], axis=1))
        qkv_full = ring_gather(qkv_block, 0)
        all_tokens = gather_rows(rel_tokens)
        buckets = gather_rows(ints)
        pair_lengths = jnp.concatenate([lengths, hop(lengths, 2)], axis=0)
        group_lengths = jnp.concatenate([pair_lengths, hop(pair_lengths, 1)], axis=0)

        out_block = spread(
            lambda t: lax.dynamic_slice_in_dim(out_weight, t * head_width, head_width, 0), 1
        )
        out_full = ring_gather(out_block, 1)
        up_block = spread(lambda t: lax.dynamic_slice_in_dim(up_weight, t * units, units, 1), 0)
        up_full = ring_gather(up_block, 0)
        down_block = spread(
            lambda t: lax.dynamic_slice_in_dim(down_weight, t * units, units, 0), 1
        )
        down_full = ring_gather(down_block, 1)
        all_cot = gather_rows(rel_cot)

        slot_ids = jnp.concatenate(
            [
                side * half + jnp.arange(half, dtype=jnp.int32),
                (1 - side) * half + jnp.arange(half, dtype=jnp.int32),
            ]
        )
        segment, position, live_groups = layout(group_lengths, slot_ids)

        def to_groups(arr):
            tail = arr.shape[1:]
            arr = arr.reshape((2, 2, 2, half) + tail)
            return jnp.swapaxes(arr, 1, 2).reshape((SHARE, rows) + tail)

        def from_groups(arr):
            tail = arr.shape[2:]
            arr = arr.reshape((2, 2, 2, half) + tail)
            return jnp.swapaxes(arr, 1, 2).reshape((8 * half,) + tail)

        live_all = from_groups(live_groups)
        all_heads = buckets[:, 0]
        all_widths = buckets[:, 1]

        own_tokens = rel_tokens[:half].astype(wide)
        own_heads = all_heads[:half]
        own_widths = all_widths[:half]
        own_live = live_all[:half]

        block_in = all_tokens.astype(wide)
        hidden_heads = norm_piece(block_in, norm_gains[0]).astype(low)
        own_normed, norm_heads_back = jax.vjp(norm_piece, own_tokens, norm_gains[0])
        gate_heads, route_heads_back = jax.vjp(
            partial(route_piece, bucket=own_heads),
            own_normed.astype(low).astype(wide),
            router_first[0],
            router_second[0],
        )
        head_ids = side * (local_width // HD) + share * heads + jnp.arange(heads, dtype=jnp.int32)
        head_used = head_ids[None, :] < HEADS // NB * (all_heads[:, None] + 1)
        unit_ids = side * local_units + share * units + jnp.arange(units, dtype=jnp.int32)
        unit_used = unit_ids[None, :] < FF // NB * (all_widths[:, None] + 1)

        half_dim = HD // 2
        frequency = theta_base ** (-2.0 * jnp.arange(half_dim, dtype=wide) / HD)
        angles = position.astype(wide)[:, :, None] * frequency
        cosine = jnp.cos(angles)[:, :, None, :]
        sine_table = jnp.sin(angles)[:, :, None, :]
        qkv_all = to_groups(dot(hidden_heads, qkv_full).reshape(8 * half, 3, heads, HD))
        query = rotate(qkv_all[:, :, 0], cosine, sine_table).astype(low)
        keyed = rotate(qkv_all[:, :, 1], cosine, sine_table).astype(low)
        value = qkv_all[:, :, 2].astype(low)
        group_used = to_groups(head_used)
        same_seq = segment[:, :, None] == segment[:, None, :]
        causal = slot_ids[None, :] <= slot_ids[:, None]
        diagonal = slot_ids[None, :] == slot_ids[:, None]
        key_used = jnp.swapaxes(group_used, 1, 2)
        allowed = (same_seq & causal)[:, None] & (key_used[:, :, None, :] | diagonal)
        scale = HD ** (-0.5)
        scores = jnp.einsum("gqhe,gkhe->ghqk", query, keyed, preferred_element_type=wide) * scale
        scores = jnp.where(allowed, scores, -1e30)
        row_top = jnp.max(scores, axis=-1, keepdims=True)
        weights = jnp.exp(scores - row_top)
        probs = weights / jnp.sum(weights, axis=-1, keepdims=True)
        probs_low = probs.astype(low)
        mixed = jnp.einsum("ghqk,gkhe->gqhe", probs_low, value, preferred_element_type=wide)
        mixed = jnp.where(group_used[..., None], mixed, 0.0).astype(low)
        attended = from_groups(mixed).reshape(8 * half, head_width)

        def partial_rows(left_in, matrix, product):
            keep = product(left_in[: 4 * half], matrix)
            send = product(left_in[4 * half :], matrix)
            return reduce_rows(keep, send)

        projected = partial_rows(attended, out_full, dot)

        middle = own_tokens + gate_heads[:, None] * projected
        normed_units, norm_units_back = jax.vjp(norm_piece, middle, norm_gains[1])
        own_units = normed_units.astype(low)
        hidden_units = gather_halves(own_units)
        gate_units, route_units_back = jax.vjp(
            partial(route_piece, bucket=own_widths),
            own_units.astype(wide),
            router_first[1],
            router_second[1],
        )
        all_gates = gather_halves(gate_units[:, None])
        upward = dot(hidden_units, up_full)
        activated = jnp.where(unit_used, jnp.square(jax.nn.relu(upward)), 0.0).astype(low)
        grad_top_all = jnp.where(live_all[:, None], all_cot.astype(wide), 0.0)
        grad_down_in = (all_gates * grad_top_all).astype(low)

        def down_term(at, s):
            mid = units // 2
            return dot_rows(
                activated[:, s * mid : (s + 1) * mid],
                lax.dynamic_slice_in_dim(grad_down_in, at * block, block, 1),
            )

        grad_down = scatter_back(ring_reduce(down_term), 1)

        downward = partial_rows(activated, down_full, dot)
        own_out = jnp.where(
            own_live[:, None], middle + gate_units[:, None] * downward, 0.0
        ).astype(low)
        block_out = whole_rows(own_out)
        grad_top = jnp.where(own_live[:, None], rel_cot[:half].astype(wide), 0.0)
        grad_gate_units = jnp.sum(grad_top * downward, axis=1)

        grad_act = dot_cols(grad_down_in, down_full)
        grad_up_in = jnp.where(unit_used, 2.0 * jax.nn.relu(upward) * grad_act, 0.0).astype(low)

        def up_term(at, s):
            mid = block // 2
            return dot_rows(
                lax.dynamic_slice_in_dim(hidden_units, at * block + s * mid, mid, 1), grad_up_in
            )

        grad_up = scatter_back(ring_reduce(up_term), 0)
        route_units_grads = route_units_back(grad_gate_units)
        grad_hidden_units = partial_rows(grad_up_in, up_full, dot_cols) + route_units_grads[0]
        norm_units_grads = norm_units_back(grad_hidden_units)
        grad_middle = grad_top + norm_units_grads[0]
        grad_gate_heads = jnp.sum(grad_middle * projected, axis=1)
        grad_projected = gather_halves((gate_heads[:, None] * grad_middle).astype(low))

        def out_term(at, s):
            mid = head_width // 2
            return dot_rows(
                attended[:, s * mid : (s + 1) * mid],
                lax.dynamic_slice_in_dim(grad_projected, at * block, block, 1),
            )

        grad_out = scatter_back(ring_reduce(out_term), 1)
        grad_attended = to_groups(
            dot_cols(grad_projected, out_full).astype(low).reshape(8 * half, heads, HD)
        )
        grad_attended = jnp.where(group_used[..., None], grad_attended, jnp.zeros((), low))
        grad_value = jnp.einsum(
            "ghqk,gqhe->gkhe", probs_low, grad_attended, preferred_element_type=wide
        )
        grad_probs = jnp.einsum(
            "gqhe,gkhe->ghqk", grad_attended, value, preferred_element_type=wide
        )
        row_dot = jnp.sum(probs * grad_probs, axis=-1, keepdims=True)
        grad_scores = (probs * (grad_probs - row_dot)).astype(low)
        grad_query = (
            jnp.einsum("ghqk,gkhe->gqhe", grad_scores, keyed, preferred_element_type=wide) * scale
        )
        grad_keyed = (
            jnp.einsum("ghqk,gqhe->gkhe", grad_scores, query, preferred_element_type=wide) * scale
        )
        grad_qkv_in = jnp.stack(
            [
                rotate(grad_query, cosine, -sine_table),
                rotate(grad_keyed, cosine, -sine_table),
                grad_value,
            ],
            axis=2,
        ).astype(low)
        grad_qkv_in = from_groups(grad_qkv_in).reshape(8 * half, 3 * head_width)

        def qkv_term(at, s):
            mid = block // 2
            return dot_rows(
                lax.dynamic_slice_in_dim(hidden_heads, at * block + s * mid, mid, 1), grad_qkv_in
            )

        qkv_parts = ring_reduce(qkv_term)
        joined = jnp.concatenate(qkv_parts, axis=0)
        grad_qkv = jnp.zeros((owned, 3, local_width), wide)
        for bits in range(SHARE):
            piece = lax.dynamic_slice_in_dim(joined, (share ^ bits) * owned, owned, 0)
            if bits:
                piece = hop(piece.astype(low), bits).astype(wide)
            grad_qkv = lax.dynamic_update_slice_in_dim(
                grad_qkv, piece.reshape(owned, 3, head_width), (share ^ bits) * head_width, 2
            )

        route_heads_grads = route_heads_back(grad_gate_heads)
        grad_hidden_heads = partial_rows(grad_qkv_in, qkv_full, dot_cols) + route_heads_grads[0]
        norm_heads_grads = norm_heads_back(grad_hidden_heads)
        input_grad = whole_rows((grad_middle + norm_heads_grads[0]).astype(low))

        def total_small(arr):
            arr = arr + cross(arr)
            bits = 1
            while bits < fsdp:
                arr = arr + hop(arr, bits)
                bits *= 2
            return arr

        def total_large(arr):
            steps = [1, "tensor"] + [2**i for i in range(1, fsdp.bit_length() - 1)]
            for bits in steps:
                mid = arr.shape[0] // 2
                me = side if bits == "tensor" else (rank // bits) % 2
                send = lax.dynamic_slice_in_dim(arr, (1 - me) * mid, mid, 0)
                keep = lax.dynamic_slice_in_dim(arr, me * mid, mid, 0)
                arr = keep + (cross(send) if bits == "tensor" else hop(send, bits))
            for bits in reversed(steps):
                me = side if bits == "tensor" else (rank // bits) % 2
                other = cross(arr) if bits == "tensor" else hop(arr, bits)
                arr = jnp.where(
                    me == 0,
                    jnp.concatenate([arr, other], axis=0),
                    jnp.concatenate([other, arr], axis=0),
                )
            return arr

        bucket_ids = jnp.arange(NB, dtype=jnp.int32)[None, :]
        head_counts = jnp.sum(
            jnp.where(own_live[:, None] & (own_heads[:, None] == bucket_ids), 1.0, 0.0), axis=0
        )
        width_counts = jnp.sum(
            jnp.where(own_live[:, None] & (own_widths[:, None] == bucket_ids), 1.0, 0.0), axis=0
        )
        units_small = total_small(
            jnp.concatenate(
                [norm_units_grads[1], route_units_grads[2].reshape(-1), head_counts, width_counts]
            )
        )
        heads_small = total_small(
            jnp.concatenate([norm_heads_grads[1], route_heads_grads[2].reshape(-1)])
        )
        first_units = total_large(route_units_grads[1])
        first_heads = total_large(route_heads_grads[1])
        second_shape = router_second.shape[1:]
        second_size = second_shape[0] * second_shape[1]
        grad_gains = jnp.stack([heads_small[:width], units_small[:width]])
        grad_second = jnp.stack(
            [
                heads_small[width : width + second_size].reshape(second_shape),
                units_small[width : width + second_size].reshape(second_shape),
            ]
        )
        usage = units_small[width + second_size :].reshape(2, NB)
        grad_first = jnp.stack([first_heads, first_units])
        return (
            block_out,
            input_grad,
            grad_gains,
            grad_qkv,
            grad_out,
            grad_up,
            grad_down,
            grad_first,
            grad_second,
            usage,
        )

    return shards


def xor_one(index):
    return index + 1 - 2 * (index % 2)


class Plane:
    def __init__(self):
        self.rank = lax.axis_index("fsdp")
        self.side = lax.axis_index("tensor")
        self.share = self.rank % SHARE
        self.place = self.rank // SHARE
        core = xor_one(self.share)
        mid = (self.share + 2) % SHARE
        self.shares = [self.share, core, mid, SHARE - 1 - self.share]
        self.core = {"fsdp": self.place * SHARE + core}
        self.mid = {"fsdp": self.place * SHARE + mid}
        self.both = {"fsdp": self.place * SHARE + self.shares[3]}
        self.members = [None, self.core, self.mid, self.both]
        self.across = {"tensor": 1 - self.side}
        self.near_place = xor_one(self.place)
        self.two_place = (self.place + 2) % 4
        self.far_place = 3 - self.place
        self.near = {"fsdp": self.near_place * SHARE + self.share}
        self.two = {"fsdp": self.two_place * SHARE + self.share}
        self.far = {"fsdp": self.far_place * SHARE + self.share}
        self.inner = (self.place == 1) | (self.place == 2)
        self.outer = (self.place == 0) | (self.place == 3)

    def greet(self):
        barrier = pltpu.get_barrier_semaphore()
        peers = [self.core, self.mid, self.both, self.across, self.near, self.two, self.far]
        for peer in peers:
            pl.semaphore_signal(barrier, inc=1, device_id=peer, device_id_type=MESH)
        pl.semaphore_wait(barrier, len(peers))


class Copies:
    def __init__(self, local_sems, send_sems, recv_sems):
        self.local_sems, self.send_sems, self.recv_sems = local_sems, send_sems, recv_sems
        self.locals, self.sends, self.recvs = 0, 0, 0

    def check(self):
        assert self.locals <= self.local_sems.shape[0]
        assert self.sends <= self.send_sems.shape[0]
        assert self.recvs <= self.recv_sems.shape[0]

    def local(self, src, dst):
        copy = pltpu.make_async_copy(src, dst, self.local_sems.at[self.locals])
        self.locals += 1
        copy.start()
        return copy

    def slot(self):
        self.recvs += 1
        return self.recvs - 1

    def remote(self, src, dst, peer, slot=None):
        if slot is None:
            slot = self.slot()
        copy = pltpu.make_async_remote_copy(
            src_ref=src,
            dst_ref=dst,
            send_sem=self.send_sems.at[self.sends],
            recv_sem=self.recv_sems.at[slot],
            device_id=peer,
            device_id_type=MESH,
        )
        self.sends += 1
        return copy

    def push(self, src, dst, peer):
        copy = self.remote(src, dst, peer)
        copy.start()
        return copy


class ZGather:
    def __init__(self, here, copies, view):
        self.here, self.copies, self.view, self.drained = here, copies, view, False
        self.slots = [copies.slot() for _ in range(3)]

    def copy(self, place, peer, slot):
        block = self.view(place)
        return self.copies.remote(block, block, peer, self.slots[slot])

    def start(self, whole=True):
        here = self.here
        self.near = self.copy(here.place, here.near, 0)
        if whole:
            self.near.start()
        else:
            pl.when(here.outer)(self.near.start)
        self.far = self.copy(here.place, here.far, 1)
        self.on_far = self.copy(here.near_place, here.far, 2)
        self.on_near = self.copy(here.far_place, here.near, 1)
        self.last = self.copy(here.two_place, here.near, 2)
        pl.when(here.inner)(self.far.start)

    def start_late(self):
        pl.when(self.here.inner)(self.near.start)

    def first(self):
        @pl.when(self.here.inner)
        def _():
            self.near.wait_recv()
            self.on_far.start()
            self.far.wait_recv()
            self.on_near.start()

    def second(self):
        @pl.when(self.here.inner)
        def _():
            self.on_far.wait_recv()
            self.last.start()

    def arrive(self):
        @pl.when(self.here.outer)
        def _():
            self.near.wait_recv()
            self.on_near.wait_recv()
            self.last.wait_recv()

    def drain(self):
        if self.drained:
            return
        self.drained = True
        self.near.wait_send()

        @pl.when(self.here.inner)
        def _():
            for copy in (self.far, self.on_far, self.on_near, self.last):
                copy.wait_send()


def tiles(count, body):
    def step(i, carry):
        body(i)
        return carry

    lax.fori_loop(0, count, step, 0)


def part(index, size):
    return pl.ds(pl.multiple_of(index * size, size), size)


class RowReduce:
    def __init__(self, here, copies, bufs, acks=None):
        self.here, self.copies, self.acks = here, copies, acks
        (self.snd, self.rcv, self.acc, self.out, self.into) = bufs
        self.sent = []

    def begin(self, width):
        self.lanes = pl.ds(0, width)
        for copy in self.sent:
            copy.wait_send()
        self.sent, self.core = [], []

    def core_send(self, index):
        rows = pl.ds(index * 256, 256)
        self.core.append(self.copies.push(
                self.snd.at[rows, self.lanes], self.rcv.at[rows, self.lanes], self.here.core
            ))

    def add_core(self, first, count):
        acc, rcv, lanes = self.acc, self.rcv, self.lanes

        def body(i):
            at = pl.ds(pl.multiple_of(first + i * 64, 64), 64)
            acc[at, lanes] = acc[at, lanes] + rcv[at, lanes].astype(wide)

        tiles(count // 64, body)

    def round_out(self, first, count, extra=None):
        acc, out, into, lanes = self.acc, self.out, self.into, self.lanes

        def body(i):
            at = pl.ds(pl.multiple_of(first + i * 64, 64), 64)
            value = acc[at, lanes]
            if extra is not None:
                value = value + into[pl.ds(extra, 64), lanes].astype(wide)
            out[pl.ds(pl.multiple_of(first - 128 + i * 64, 64), 64), lanes] = value.astype(low)

        tiles(count // 64, body)

    def hand(self, first, end, peer):
        rows = pl.ds(first, end - first)
        return self.copies.push(
            self.out.at[rows, self.lanes], self.into.at[rows, self.lanes], peer
        )

    def diagonal(self):
        for copy in self.core:
            copy.wait_recv()
        self.add_core(384, 128)
        self.round_out(384, 128)
        self.diag_x = self.hand(256, 320, self.here.across)
        self.diag_y = self.hand(320, 384, self.here.mid)
        self.add_core(128, 256)
        self.round_out(128, 64)
        self.round_out(320, 64)
        self.add_core(0, 128)

    def sides(self):
        self.diag_y.wait_recv()
        self.round_out(192, 64, 320)
        self.over_x = self.hand(0, 128, self.here.across)
        self.diag_x.wait_recv()
        self.round_out(256, 64, 256)
        self.over_y = self.hand(128, 256, self.here.mid)
        self.sent = self.core + [self.diag_x, self.diag_y, self.over_x, self.over_y]

    def arrive(self):
        self.over_x.wait_recv()
        self.over_y.wait_recv()

    def total(self, at, size):
        acc, into, lanes = self.acc, self.into, self.lanes
        return (
            acc[pl.ds(at, size), lanes]
            + into[pl.ds(at, size), lanes].astype(wide)
            + into[pl.ds(at + 128, size), lanes].astype(wide)
        )

    def release(self):
        for index, peer in enumerate((self.here.core, self.here.across, self.here.mid)):
            pl.semaphore_signal(
                self.acks.at[index], inc=1, device_id=peer, device_id_type=MESH
            )

    def await_release(self):
        for index in range(3):
            pl.semaphore_wait(self.acks.at[index], 1)

    def drain(self):
        for copy in self.sent:
            copy.wait_send()


class RowGather:
    def __init__(self, here, copies, view, fixed=False):
        self.here, self.copies, self.view, self.fixed = here, copies, view, fixed
        self.sent, self.drained = [], False

    def start(self):
        here = self.here
        self.over_x = self.pair(0, 1, here.across)
        self.over_y = self.pair(0, 2, here.mid)
        self.cores = [self.pair(0, 4, here.core)]

    def pair(self, source, target, peer, half=None):
        src = self.view(source, half)
        dst = src if self.fixed else self.view(target, half)
        copy = self.copies.push(src, dst, peer)
        self.sent.append(copy)
        return copy

    def forward(self):
        here = self.here
        self.over_y.wait_recv()
        self.diag_x = self.pair(2, 3, here.across, 0)
        self.cores.append(self.pair(2, 6, here.core))
        self.over_x.wait_recv()
        self.diag_y = self.pair(1, 3, here.mid, 1)
        self.cores.append(self.pair(1, 5, here.core))

    def finish(self):
        self.diag_x.wait_recv()
        self.diag_y.wait_recv()
        self.cores.append(self.pair(3, 7, self.here.core))
        for copy in self.cores:
            copy.wait_recv()

    def drain(self):
        if not self.drained:
            for copy in self.sent:
                copy.wait_send()
        self.drained = True


def nn(left_in, right_in):
    return lax.dot_general(
        left_in, right_in, (((1,), (0,)), ((), ())), preferred_element_type=wide
    )


def nt(left_in, right_in):
    return lax.dot_general(
        left_in, right_in, (((1,), (1,)), ((), ())), preferred_element_type=wide
    )


def tn(left_in, right_in):
    return lax.dot_general(
        left_in, right_in, (((0,), (0,)), ((), ())), preferred_element_type=wide
    )


class ZReduce:
    def __init__(self, here, copies, base, spot, rows, columns, landing):
        self.here, self.copies, self.base, self.spot = here, copies, base, spot
        self.rows, self.columns, self.landing = rows, columns, landing
        self.slots = [copies.slot() for _ in range(5)]
        self.handed, self.passed, self.halves = [], [], {}

    def copy(self, k, peer, slot, rows=None, lanes=None, own_slot=None):
        r, c = self.spot(k)
        r0, rn = rows or (0, self.rows)
        c0, cn = lanes or (0, self.columns)
        block = self.base.at[pl.ds(r + r0, rn), pl.ds(c + c0, cn)]
        dst = self.landing.at[slot, pl.ds(r0, rn), pl.ds(c0, cn)]
        return self.copies.remote(
            block, dst, peer, self.slots[slot] if own_slot is None else own_slot
        )

    def outward_half(self, k, h, size):
        slot = {3: 1, 2: 2}[k]
        lanes = (h * size, size)
        copy = self.copy(k, self.here.near, slot, lanes=lanes, own_slot=self.copies.slot())
        self.halves[k, h] = copy
        self.handed.append(copy)
        pl.when(self.here.outer)(copy.start)

    def inward_half(self, step, h, size, stage):
        here = self.here
        k, source, slot = ((2, 1, 4), (3, 2, 3))[step]
        if h == 0:
            setattr(self, f"in{k}", self.copy(k, here.far, slot))
        push = self.copy(k, here.far, slot, lanes=(h * size, size))
        self.passed.append(push)
        lanes = pl.ds(h * size, size)

        @pl.when(here.inner)
        def _():
            self.halves[5 - k, h].wait_recv()
            self.copies.local(
                self.landing.at[source, :, lanes], stage.at[0, pl.ds(0, self.rows), lanes]
            ).wait()
            self.add(k, stage, [0], h * size, size)
            push.start()

    def outward(self, k, rows=None, lanes=None):
        slot = {3: 1, 2: 2, 1: 0}[k]
        if not hasattr(self, f"out{k}"):
            setattr(self, f"out{k}", self.copy(k, self.here.near, slot))
        copy = self.copy(k, self.here.near, slot, rows, lanes)
        self.handed.append(copy)
        pl.when(self.here.outer)(copy.start)

    def outward_piece(self, n, size):
        r, c = self.spot(1)
        if n == 0:
            self.out1 = self.copy(1, self.here.near, 0)
            self.pieces = []
        lanes = pl.ds(n * size, size)
        copy = self.copies.remote(
            self.base.at[pl.ds(r, self.rows), pl.ds(c + n * size, size)],
            self.landing.at[0, :, lanes],
            self.here.near,
        )
        self.pieces.append(copy)
        self.handed.append(copy)
        pl.when(self.here.outer)(copy.start)

    def finish_piece(self, n, size, stage):
        here = self.here

        @pl.when(here.inner)
        def _():
            lanes = pl.ds(n * size, size)
            if n == 0:
                self.in3.wait_recv()
                for load in self.load(3, stage, 1):
                    load.wait()
            self.pieces[n].wait_recv()
            self.copies.local(
                self.landing.at[0, :, lanes], stage.at[0, pl.ds(0, self.rows), lanes]
            ).wait()
            self.add(0, stage, [0, 1], n * size, size)

        if n == 0:

            @pl.when(here.outer)
            def _():
                self.out1.wait_recv()
                for load in self.load(0, stage, 0):
                    load.wait()
                self.add(0, stage, [0])

    def load(self, index, stage, slot):
        size = min(self.rows, 512)
        return [
            self.copies.local(
                self.landing.at[index, pl.ds(n * size, size), :],
                stage.at[slot, pl.ds(0, size), pl.ds(n * self.columns, self.columns)],
            )
            for n in range(self.rows // size)
        ]

    def add(self, target, stage, slots, first=0, columns=None):
        size = min(self.rows, 512)
        columns = self.columns if columns is None else columns
        r, c = self.spot(target)
        for n in range(self.rows // size):

            def body(i, n=n):
                at = pl.ds(pl.multiple_of(i * 64, 64), 64)
                mine = pl.ds(pl.multiple_of(r + n * size + i * 64, 64), 64)
                lanes = pl.ds(c + first, columns)
                value = self.base[mine, lanes].astype(wide)
                for slot in slots:
                    value = value + stage[
                        slot, at, pl.ds(n * self.columns + first, columns)
                    ].astype(wide)
                self.base[mine, lanes] = value.astype(low)

            tiles(size // 64, body)

    def pass_on(self, k, wait, index, stage, copy):
        wait.wait_recv()
        for load in self.load(index, stage, 0):
            load.wait()
        self.add(k, stage, [0])
        copy.start()

    def inward(self, step, stage):
        here = self.here
        if step == 0:
            self.in2 = self.copy(2, here.far, 4)
            args = (2, self.out3, 1, stage, self.in2)
        elif step == 1:
            self.in3 = self.copy(3, here.far, 3)
            args = (3, self.out2, 2, stage, self.in3)
        else:
            self.in1 = self.copy(1, here.near, 0)
            args = (1, self.in2, 4, stage, self.in1)

        @pl.when(here.inner)
        def _():
            self.pass_on(*args)

    def finish(self, stage):
        here = self.here
        self.out1.wait_recv()
        loads = self.load(0, stage, 0)

        @pl.when(here.inner)
        def _():
            self.in3.wait_recv()
            for load in self.load(3, stage, 1) + loads:
                load.wait()
            self.add(0, stage, [0, 1])

        @pl.when(here.outer)
        def _():
            for load in loads:
                load.wait()
            self.add(0, stage, [0])

    def drain(self):
        @pl.when(self.here.inner)
        def _():
            for copy in [self.in1] + (self.passed or [self.in2, self.in3]):
                copy.wait_send()

        @pl.when(self.here.outer)
        def _():
            for copy in self.handed:
                copy.wait_send()


def norm_back(value, grad, gain):
    r = lax.rsqrt(jnp.mean(value * value, axis=-1, keepdims=True) + epsilon)
    u = gain * grad
    lean = jnp.mean(u * value, axis=-1, keepdims=True)
    return r * u - value * (r * r * r * lean), grad * value * r


def exact(left_in, right_in, contract):
    return lax.dot_general(
        left_in, right_in, (contract, ((), ())), precision=highest, preferred_element_type=wide
    )


def layer_kernel(
    tok, cot_in, qkvw, outw, upw, downw, first, gains, second_in, heads_in, widths_in, turns,
    lengths,
    o_block, o_input, o_gq, o_go, o_gu, o_gd, o_first, o_pack, s_hid, s_wq, l_q, l_o, l_u, l_d,
    toks, hid, units, cot, early, wo, wu, wd, cols, rows_info, qkvb, probs, att, acc,
    snd, rcv, out_buf, in_buf, proj, mid_buf, go, stage, top, own_tok, own_out,
    first_buf, slope, gates, dall, second, col, row, square, r_gate, r_inner, r_slope, r_dpre, r_rows, zpart, zland, gain_buf,
    pack, pack_plane, pack_side, pack_ring,
    local_sems, send_sems, recv_sems, acks,
):
    here = Plane()
    copies = Copies(local_sems, send_sems, recv_sems)
    here.greet()
    rank, share, side = here.rank, here.share, here.side
    owned = 128
    width = toks.shape[1]
    block = owned * SHARE
    head_width = wo.shape[0]
    unit_width = wu.shape[1]
    heads = head_width // HD
    own_rows = part(rank, owned)
    wq = early.at[:, 0 : 3 * head_width]
    act, gup = early.at[0:1024], early.at[1024:2048]
    sent, outs, done = [], [], []

    def to_peer(src, dst, peer):
        copy = copies.push(src, dst, peer)
        sent.append(copy)
        return copy

    def spread(src_of, dst):
        return [
            copies.local(src_of(here.shares[d]), dst)
            if d == 0
            else to_peer(src_of(here.shares[d]), dst, here.members[d])
            for d in range(SHARE)
        ]

    def landed(got):
        for i, copy in enumerate(got):
            if i % SHARE:
                copy.wait_recv()
            else:
                copy.wait()

    got_q = [
        spread(
            lambda t, j=j: qkvw.at[j, :, part(t, head_width)],
            wq.at[own_rows, j * head_width : (j + 1) * head_width],
        )
        for j in range(3)
    ]
    mine, other = part(side, owned), part(1 - side, owned)

    class Halves:
        def __init__(self, src, dst):
            self.dst = dst
            pairs = ((mine, 0), (other, owned))
            self.own = [copies.local(src(rows), dst(at)) for rows, at in pairs]
            self.mid = to_peer(src(mine), dst(256), here.mid)
            self.core = [to_peer(src(rows), dst(at + 512), here.core) for rows, at in pairs]

        def pass_on(self):
            self.mid.wait_recv()
            self.over = to_peer(self.dst(256), self.dst(384), here.across)
            self.last = [to_peer(self.dst(256), self.dst(768), here.core)]

        def complete(self):
            self.over.wait_recv()
            self.last.append(to_peer(self.dst(384), self.dst(896), here.core))

    tok_in = Halves(lambda r: tok.at[r, :], lambda at: toks.at[at : at + owned])

    row[...] = jnp.zeros_like(row)
    for h in range(2):
        slot = lax.broadcasted_iota(jnp.int32, (1, owned), 1) + h * owned
        segment = slot * 0 + (lengths.shape[1] + slot)
        position = slot
        live = slot * 0
        begin = 0
        for n in range(lengths.shape[1]):
            end = begin + lengths[0, n]
            member = (slot >= begin) & (slot < end)
            segment = jnp.where(member, n, segment)
            position = jnp.where(member, slot - begin, position)
            live = jnp.where(member, 1, live)
            begin = end
        lanes = slice(h * owned, (h + 1) * owned)
        held = (segment, slot, heads_in[h : h + 1, :], widths_in[h : h + 1, :], live, position)
        for n, value in enumerate(held):
            row[n : n + 1, lanes] = value.astype(wide)
        square[...] = jnp.zeros_like(square)
        square[0:8, :] = row[:, lanes]
        turned = jnp.transpose(square[...])
        angles = turned[:, 5:6] * turns[0:1, :]
        col[lanes, 0:HD] = jnp.cos(angles)
        sines = jnp.sin(angles)
        lane = lax.broadcasted_iota(jnp.int32, (owned, HD), 1)
        col[lanes, HD : 2 * HD] = jnp.where(lane < HD // 2, -sines, sines)
        col[lanes, 2 * HD : 3 * HD] = turned
    second[...] = jnp.zeros_like(second)
    for index in range(2):
        second[index, 0:NB, :] = second_in[index]
    col_in = Halves(lambda r: col.at[r, :], lambda at: cols.at[at : at + owned])
    row_in = Halves(
        lambda r: row.at[:, r],
        lambda at: rows_info.at[at // 256, :, at % 256 : at % 256 + owned],
    )
    got_o = spread(lambda t: outw.at[part(t, head_width), :], wo.at[:, own_rows])
    got_u = spread(lambda t: upw.at[:, part(t, unit_width)], wu.at[own_rows, :])
    got_d = spread(lambda t: downw.at[part(t, unit_width), :], wd.at[:, own_rows])
    cot_rows = Halves(lambda r: cot_in.at[r, :], lambda at: cot.at[at : at + owned])
    in_first = copies.local(first.at[0], first_buf)
    in_tok = copies.local(tok.at[mine, :], own_tok)

    g_q = [
        ZGather(here, copies, lambda k, d=d: wq.at[part(k * SHARE + here.shares[d], owned), :])
        for d in range(SHARE)
    ]
    g_o = ZGather(here, copies, lambda k: wo.at[:, part(k, block)])
    g_u = [
        ZGather(
            here,
            copies,
            lambda k, h=h: wu.at[part(k, block), h * 512 : (h + 1) * 512],
        )
        for h in range(2)
    ]
    g_d = [
        ZGather(here, copies, lambda k, h=h: wd.at[h * 512 : (h + 1) * 512, part(k, block)])
        for h in range(2)
    ]

    def fact(at, index):
        return cols[at, 2 * HD + index : 2 * HD + index + 1]

    def start_q(d):
        for got in got_q:
            if d:
                got[d].wait_recv()
            else:
                got[d].wait()
        g_q[d].start()

    start_q(0)
    start_q(1)

    def normalise(base):
        def body(i):
            at = pl.ds(pl.multiple_of(base + i * 64, 64), 64)
            x = toks[at, :].astype(wide)
            r = lax.rsqrt(jnp.mean(x * x, axis=-1, keepdims=True) + epsilon)
            hid[at, :] = (x * r * gains[0:1, :]).astype(low)

        tiles(4, body)

    def wait_all(waits):
        for wait in waits:
            wait()

    wait_all([c.wait for c in tok_in.own + col_in.own + row_in.own])
    normalise(0)

    def route(index, rows_of):
        made = exact(rows_of[0:owned, :].astype(wide), first_buf[...], ((1,), (0,)))
        sig = 1.0 / (1.0 + jnp.exp(-made))
        inner = made * sig
        logits = exact(inner, second[index], ((1,), (1,)))
        lane = lax.broadcasted_iota(jnp.int32, (owned, HD), 1)
        logits = jnp.where(lane < NB, logits, -1e30)
        raised = jnp.where(
            lane < NB, jnp.exp(logits - jnp.max(logits, axis=-1, keepdims=True)), 0.0
        )
        shares = raised / jnp.sum(raised, axis=-1, keepdims=True)
        hot = jnp.where(lane.astype(wide) == fact(pl.ds(0, owned), 2 + index), 1.0, 0.0)
        gate = NB * jnp.sum(shares * hot, axis=-1, keepdims=True)
        lean = hot - shares
        bare = exact(lean, second[index], ((1,), (0,))) * (sig * (1.0 + made * (1.0 - sig)))
        r_gate[index] = jnp.broadcast_to(gate, (owned, HD))
        r_inner[index] = inner
        r_slope[index] = lean if index else gate * lean
        r_dpre[index] = bare if index else gate * bare
        if index == 1:
            dall[0:owned, :] = bare.astype(low)

    def slope_tiles(index):
        def body(i):
            c = part(i, 256)
            slope[:, c] = exact(r_dpre[index], first_buf[c, :], ((1,), (1,)))

        tiles(8, body)

    in_first.wait()
    route(0, hid)
    in_first = copies.local(first.at[1], first_buf)
    start_q(2)
    start_q(3)
    g_q[0].first()
    g_q[1].first()
    tok_in.pass_on()
    wait_all([c.wait_recv for c in tok_in.core])
    normalise(512)
    g_q[0].second()
    g_q[1].second()
    g_q[2].first()
    g_q[3].first()
    tok_in.complete()
    normalise(256)
    g_q[2].second()
    g_q[3].second()
    wait_all([c.wait_recv for c in tok_in.last])
    normalise(768)
    save_hid = copies.local(hid, s_hid)
    col_in.pass_on()
    row_in.pass_on()
    landed(got_o)
    g_o.start()
    col_in.complete()
    row_in.complete()
    wait_all([c.wait_recv for c in col_in.core + row_in.core + col_in.last + row_in.last])
    g_o.first()
    landed(got_u)
    g_o.second()
    g_u[0].start()
    for one in g_q:
        one.arrive()
    save_wq = copies.local(wq, s_wq)

    for j in range(3):

        def qkv_tile(i, j=j):
            at = part(i, 512)
            made = nn(hid[at, :], wq[:, j * head_width : (j + 1) * head_width])
            if j < 2:
                cosine = cols[at, 0:HD]
                sine = cols[at, HD : 2 * HD]
                for h in range(heads):
                    one = made[:, h * HD : (h + 1) * HD]
                    turned = one * cosine + pltpu.roll(one, HD // 2, 1) * sine
                    qkvb[at, j * head_width + h * HD : j * head_width + (h + 1) * HD] = (
                        turned.astype(low)
                    )
            else:
                qkvb[at, j * head_width : (j + 1) * head_width] = made.astype(low)

        tiles(2, qkv_tile)

    g_u[0].first()
    g_u[1].start()

    first_head = (side * SHARE + share) * heads
    scale = HD ** (-0.5)
    for h in range(heads):
        head = (first_head + h).astype(wide)

        def attend_group(g, h=h, head=head):
            at = part(g, 256)
            query, keyed, value = (
                qkvb[at, pl.ds(j * head_width + h * HD, HD)] for j in range(3)
            )
            info = rows_info[g]
            seg_k, slot_k, bucket_k = info[0:1, :], info[1:2, :], info[2:3, :]
            reach_k = jnp.where(4.0 * bucket_k + 4.0 > head, 1.0, 0.0)
            slot_q = fact(at, 1)
            usable = (reach_k > 0.5) | (slot_k == slot_q)
            allowed = (fact(at, 0) == seg_k) & (slot_k <= slot_q) & usable
            scores = jnp.where(allowed, nt(query, keyed) * scale, -1e30)
            weights = jnp.exp(scores - jnp.max(scores, axis=-1, keepdims=True))
            p = weights / jnp.sum(weights, axis=-1, keepdims=True)
            probs[part(g * heads + h, 256), :] = p
            mixed = nn(p.astype(low), value)
            att[at, h * HD : (h + 1) * HD] = jnp.where(
                4.0 * fact(at, 2) + 4.0 > head, mixed, 0.0
            ).astype(low)

        tiles(SHARE, attend_group)

    reduce = RowReduce(here, copies, (snd, rcv, acc, out_buf, in_buf), acks)

    def partial_sums(term, extra=None):
        lanes = acc.shape[1] if extra is not None else width
        reduce.begin(lanes)
        for i in range(2):

            def send_tile(n, i=i):
                snd[i * 256 : (i + 1) * 256, part(n, 512)] = term(
                    pl.ds(512 + i * 256, 256), n
                ).astype(low)

            tiles(4, send_tile)
            if extra is not None:
                snd[i * 256 : (i + 1) * 256, width:lanes] = extra[
                    pl.ds(512 + i * 256, 256), :
                ].astype(low)
            reduce.core_send(i)

        def own_tile(n):
            acc[:, part(n, 512)] = term(pl.ds(0, 512), n)

        tiles(4, own_tile)
        if extra is not None:
            acc[:, width:lanes] = extra[0:512, :]

    cot_rows.pass_on()
    g_o.arrive()
    partial_sums(lambda at, n: nn(att[at, :], wo[:, part(n, 512)]))
    g_u[0].second()
    reduce.diagonal()
    g_u[1].first()
    reduce.sides()
    g_u[1].second()
    landed(got_d)
    g_d[0].start()
    g_d[1].start(False)
    in_tok.wait()
    reduce.arrive()

    def row_tiles(body):
        def step(i):
            at = pl.multiple_of(i * 64, 64)
            body(at, pl.ds(at, 64))

        tiles(owned // 64, step)

    def middle_tile(at, rows):
        projected = reduce.total(at, 64)
        proj[rows, :] = projected
        middle = own_tok[rows, :].astype(wide) + r_gate[0, rows, 0:1] * projected
        mid_buf[rows, :] = middle
        r = lax.rsqrt(jnp.mean(middle * middle, axis=-1, keepdims=True) + epsilon)
        units[rows, :] = (middle * r * gains[1:2, :]).astype(low)

    row_tiles(middle_tile)
    reduce.release()

    def row_view(buf):
        def view(k, h):
            if h is None:
                return buf.at[k * owned : (k + 1) * owned]
            return buf.at[k * owned + h * 64 : k * owned + (h + 1) * 64]

        return view

    units_out = RowGather(here, copies, row_view(units))
    units_out.start()
    in_first.wait()
    route(1, units)
    gates[0:owned, :] = r_gate[1]
    gates_out = RowGather(here, copies, row_view(gates))
    dall_out = RowGather(here, copies, row_view(dall))
    gates_out.start()
    dall_out.start()

    def first_low(n):
        return go[pl.ds(pl.multiple_of(n % 2 * 512, 512), 512), part(n // 2, 256)]

    def first_tile(i):
        go[part(i % 8, 128), part(i // 8, 256)] = first_buf[part(i, 128), :].astype(low)

    tiles(16, first_tile)
    in_first = copies.local(first.at[0], first_buf)
    g_d[0].first()
    units_out.forward()
    gates_out.forward()
    dall_out.forward()
    units_out.finish()
    gates_out.finish()
    dall_out.finish()
    g_d[0].second()
    g_d[1].start_late()
    g_d[1].first()
    g_d[1].second()
    wait_all([c.wait for c in cot_rows.own])
    cot_rows.complete()
    wait_all([c.wait_recv for c in cot_rows.core + cot_rows.last])

    def live_cot(at):
        return jnp.where(fact(at, 4) > 0.5, cot[at, :].astype(wide), 0.0)

    for copy in tok_in.last + cot_rows.last + [tok_in.over, cot_rows.over]:
        copy.wait_send()
        done.append(copy)

    def keep_tile(at, rows):
        top[rows, :] = live_cot(rows).astype(low)

    row_tiles(keep_tile)

    def scale_tile(i):
        at = part(i, 64)
        cot[at, :] = (gates[at, 0:1] * live_cot(at)).astype(low)

    tiles(16, scale_tile)

    first_unit = (side * SHARE + share) * unit_width

    def used_units(at, base, rows, columns):
        lane = lax.broadcasted_iota(jnp.int32, (rows, columns), 1) + base
        return lane.astype(wide) < (FF // NB) * (fact(at, 3) + 1.0)

    save_wq.wait()
    for one in g_q:
        one.drain()

    def up_tile(m, n):
        at, c = part(m, 512), slice(n * 512, (n + 1) * 512)
        made = nn(units[at, :], wu[:, c])
        acc[:, part(m * 2 + n, 512)] = made
        relu = jnp.maximum(made, 0.0)
        used = used_units(at, first_unit + n * 512, 512, 512)
        act[at, c] = jnp.where(used, relu * relu, 0.0).astype(low)

    def deliver(piece_of, dst):
        for d in range(SHARE):
            src = piece_of(here.shares[d])
            if d == 0:
                outs.append(copies.local(src, dst))
            else:
                sent.append(copies.push(src, dst, here.members[d]))
                owed.append(sent[-1])

    owed = []

    gd, gu, gq = toks, hid, wd
    blocks = [here.place, here.near_place, here.two_place, here.far_place]
    z_d = ZReduce(here, copies, gd, lambda k: (0, k * block), unit_width, block, l_d)
    z_u = ZReduce(
        here, copies, gu, lambda k: (k % 2 * block, k // 2 * unit_width), block, unit_width, l_u
    )
    z_o = ZReduce(here, copies, go, lambda k: (k * head_width, 0), head_width, block, l_o)
    z_q = ZReduce(
        here, copies, gq, lambda k: (k % 2 * block, k // 2 * 1024), block, 3 * head_width, l_q
    )

    def down_block(k, h):
        m = slice(h * 512, (h + 1) * 512)
        gd[m, k * block : (k + 1) * block] = tn(
            act[:, m], cot[:, part(blocks[k], block)]
        ).astype(low)

    for h in range(2):
        g_u[h].arrive()
        tiles(2, lambda m, h=h: up_tile(m, h))
        for k in (3, 2, 1, 0):
            down_block(k, h)
            if k:
                z_d.outward(k, rows=(h * 512, 512))

    def gup_tile(m, n):
        at, c = part(m, 512), slice(n * 512, (n + 1) * 512)
        made = nt(cot[at, :], wd[c, :])
        used = used_units(at, first_unit + n * 512, 512, 512)
        relu = jnp.maximum(acc[:, part(m * 2 + n, 512)], 0.0)
        gup[at, c] = jnp.where(used, 2.0 * relu * made, 0.0).astype(low)
        dots = jnp.sum(act[at, c].astype(wide) * made, axis=-1, keepdims=True)
        if n:
            dots = dots + gates[at, 0:1]
            r_rows[at, 256:512] = (dots * dall[at, :].astype(wide)).astype(low)
        gates[at, :] = jnp.broadcast_to(dots, (512, HD))

    def up_block(k, h):
        r, c = k % 2 * block, k // 2 * unit_width + h * 512
        gu[r : r + block, c : c + 512] = tn(
            units[:, part(blocks[k], block)], gup[:, h * 512 : (h + 1) * 512]
        ).astype(low)
        if k > 1:
            z_u.outward_half(k, h, 512)
        elif k:
            z_u.outward(k, lanes=(h * 512, 512))

    gates_out.drain()
    save_hid.wait()
    g_d[0].arrive()
    tiles(2, lambda m: gup_tile(m, 0))
    for k in (3, 2, 1, 0):
        up_block(k, 0)
    z_d.inward(0, stage)
    z_d.inward(1, stage)
    g_d[1].arrive()
    tiles(2, lambda m: gup_tile(m, 1))

    reduce.await_release()
    partial_sums(
        lambda at, n: nt(gup[at, :], wu[part(n, 512), :])
        + nt(r_rows[at, 256:512], first_low(n)),
        gates,
    )
    up_block(3, 1)
    up_block(2, 1)
    reduce.diagonal()
    up_block(1, 1)
    z_d.inward(2, stage)
    reduce.sides()
    up_block(0, 1)
    z_u.inward_half(0, 0, 512, stage)

    column = share * 2 + side
    ucol = dall
    dall_out.drain()

    def ucol_tile(i):
        ucol[part(i, 256), :] = units[part(i, 256), part(column, 256)]

    tiles(4, ucol_tile)
    units_out.drain()
    in_hid = copies.local(s_hid, units)
    for one in g_u:
        one.drain()
    in_wq = copies.local(s_wq, wu.at[:, 0 : 3 * head_width])

    r_rows_out = RowGather(here, copies, row_view(r_rows))

    def keep_gate(index, rows, weight):
        c = slice(index * 256, (index + 1) * 256)
        r_rows[rows, c] = (weight * r_dpre[index, rows, :]).astype(low)
        r_slope[index, rows, :] = weight * r_slope[index, rows, :]

    places = [here.place, here.near_place, here.two_place, here.far_place]
    planes = [None, here.near, here.two, here.far]

    def first_rows(k, h):
        target = here.shares[k // 4 + k // 2 % 2 * 2] * 2 + (side if k % 2 == 0 else 1 - side)
        base = target * 256
        if h is None:
            return o_first.at[:, pl.ds(pl.multiple_of(base, 256), 256), :]
        return o_first.at[:, pl.ds(pl.multiple_of(base + h * 128, 128), 128), :]

    first_out = RowGather(here, copies, first_rows, True)

    class FirstSum:
        def __init__(self):
            zpart[0] = tn(units[:, part(column, 256)], r_rows[:, 0:256]).astype(low)
            zpart[1] = tn(ucol[...], r_rows[:, 256:512]).astype(low)
            self.got = []
            for k in range(4):
                src, dst = zpart.at[:, part(places[k], 64), :], zland.at[here.place]
                self.got.append(
                    copies.local(src, dst) if k == 0 else to_peer(src, dst, planes[k])
                )

        def add(self):
            landed(self.got)
            for copy in self.got[1:]:
                copy.wait_send()
                done.append(copy)
            total = zland[0].astype(wide)
            for k in range(1, 4):
                total = total + zland[k].astype(wide)
            zpart[:, 0:64, :] = total.astype(low)
            at = pl.ds(pl.multiple_of(column * 256 + here.place * 64, 64), 64)
            src, dst = zpart.at[:, 0:64, :], o_first.at[:, at, :]
            self.got = [
                copies.local(src, dst) if k == 0 else to_peer(src, dst, planes[k])
                for k in range(4)
            ]

        def show(self):
            landed(self.got)
            first_out.start()

    reduce.arrive()
    gproj = cot
    gain_buf[...] = jnp.zeros_like(gain_buf)

    def grad_tile(at, rows):
        total = reduce.total(at, 64)
        grad = total[:, 0:width]
        keep_gate(1, rows, total[:, width : width + 1])
        back, gain_terms = norm_back(mid_buf[rows, :], grad, gains[1:2, :])
        grad_middle = top[rows, :].astype(wide) + back
        gproj[rows, :] = (r_gate[0, rows, 0:1] * grad_middle).astype(low)
        grad_gate = jnp.sum(grad_middle * proj[rows, :], axis=-1, keepdims=True)
        keep_gate(0, rows, grad_gate)
        r_gate[0, rows, :] = jnp.broadcast_to(grad_gate, (64, HD))
        proj[rows, :] = grad_middle
        gain_buf[1:2, :] = gain_buf[1:2, :] + jnp.sum(gain_terms, axis=0, keepdims=True)

    row_tiles(grad_tile)
    reduce.release()
    gproj_out = RowGather(here, copies, row_view(gproj))
    gproj_out.start()
    r_rows_out.start()
    in_first.wait()
    slope_tiles(0)
    z_u.inward_half(1, 0, 512, stage)
    gproj_out.forward()
    r_rows_out.forward()

    reduce.await_release()
    partial_sums(lambda at, n: nn(act[at, :], wd[:, part(n, 512)]))
    gproj_out.finish()
    reduce.diagonal()
    r_rows_out.finish()
    in_hid.wait()
    sum_first = FirstSum()
    z_u.inward_half(0, 1, 512, stage)

    def out_block(k):
        go[k * head_width : (k + 1) * head_width, :] = tn(
            att[...], gproj[:, part(blocks[k], block)]
        ).astype(low)

    gatt, gqkv = gup, act

    def gatt_tile(i):
        at = part(i, 512)
        made = nt(gproj[at, :], wo[...]).astype(low)
        for h in range(heads):
            used = 4.0 * fact(at, 2) + 4.0 > (first_head + h).astype(wide)
            gatt[at, h * HD : (h + 1) * HD] = jnp.where(
                used, made[:, h * HD : (h + 1) * HD].astype(wide), 0.0
            ).astype(low)

    tiles(2, gatt_tile)

    for h in range(heads):

        def back_group(g, h=h):
            at = part(g, 256)
            lanes = [pl.ds(j * head_width + h * HD, HD) for j in range(3)]
            query, keyed, value = (qkvb[at, lane] for lane in lanes)
            grad = gatt[at, h * HD : (h + 1) * HD]
            p = probs[part(g * heads + h, 256), :]
            grad_p = nt(grad, value)
            row_dot = jnp.sum(p * grad_p, axis=-1, keepdims=True)
            grad_s = (p * (grad_p - row_dot)).astype(low)
            cosine = cols[at, 0:HD]
            sine = cols[at, HD : 2 * HD]
            for lane, turned in (
                (lanes[0], nn(grad_s, keyed) * scale),
                (lanes[1], tn(grad_s, query) * scale),
            ):
                gqkv[at, lane] = (
                    turned * cosine - pltpu.roll(turned, HD // 2, 1) * sine
                ).astype(low)
            gqkv[at, lanes[2]] = tn(p.astype(low), grad).astype(low)

        tiles(SHARE, back_group)

    def qkv_block(k):
        r, c = k % 2 * block, k // 2 * 1024
        for j in range(3):
            gq[r : r + block, c + j * head_width : c + (j + 1) * head_width] = tn(
                units[:, part(blocks[k], block)], gqkv[:, j * head_width : (j + 1) * head_width]
            ).astype(low)

    for one in g_d:
        one.drain()
    reduce.sides()
    qkv_block(3)
    z_q.outward(3)
    out_block(3)
    z_o.outward(3)
    z_u.inward_half(1, 1, 512, stage)
    sum_first.add()
    qkv_block(2)
    z_q.outward(2)
    for k in (2, 1):
        out_block(k)
        z_o.outward(k)
    qkv_block(1)
    for j in range(3):
        z_q.outward_piece(j, head_width)
    qkv_block(0)
    out_block(0)
    z_d.finish(stage)
    deliver(lambda t: gd.at[:, part(t, owned)], o_gd.at[part(share, unit_width), :])

    z_u.inward(2, stage)
    reduce.arrive()

    def block_tile(at, rows):
        own_out[rows, :] = jnp.where(
            fact(rows, 4) > 0.5,
            mid_buf[rows, :] + r_gate[1, rows, 0:1] * reduce.total(at, 64),
            0.0,
        ).astype(low)

    row_tiles(block_tile)
    reduce.release()
    shown = copies.local(own_out, o_block.at[mine])
    shown_far = to_peer(own_out, o_block.at[mine], here.across)

    in_wq.wait()
    reduce.await_release()
    partial_sums(
        lambda at, n: nt(gqkv[at, 0 : 3 * head_width], wu[part(n, 512), 0 : 3 * head_width])
    )
    reduce.diagonal()
    z_q.inward(0, stage)
    z_o.inward(0, stage)
    reduce.sides()
    z_u.finish(stage)
    deliver(lambda t: gu.at[part(t, owned), 0:unit_width], o_gu.at[:, part(share, unit_width)])
    sum_first.show()
    z_q.inward(2, stage)
    z_q.inward(1, stage)
    z_o.inward(1, stage)
    z_o.inward(2, stage)
    shown.wait()
    shown_far.wait()
    done.append(shown_far)
    reduce.arrive()

    def input_tile(at, rows):
        grad = reduce.total(at, 64) + r_gate[0, rows, 0:1] * slope[rows, :]
        back, gain_terms = norm_back(own_tok[rows, :].astype(wide), grad, gains[0:1, :])
        own_out[rows, :] = (proj[rows, :] + back).astype(low)
        gain_buf[0:1, :] = gain_buf[0:1, :] + jnp.sum(gain_terms, axis=0, keepdims=True)

    row_tiles(input_tile)
    outs.append(copies.local(own_out, o_input.at[mine]))
    input_far = copies.push(own_out, o_input.at[mine], here.across)
    first_out.forward()

    def finish_q(j):
        z_q.finish_piece(j, head_width, stage)
        deliver(
            lambda t: gq.at[part(t, owned), j * head_width : (j + 1) * head_width],
            o_gq.at[j, :, part(share, head_width)],
        )

    for index in range(2):
        for j in range(8):
            pack[index * 8 + j : index * 8 + j + 1, :] = gain_buf[
                index : index + 1, j * 256 : (j + 1) * 256
            ]
        made = exact(r_slope[index], r_inner[index], ((0,), (0,)))
        pack[16 + index * 8 : 24 + index * 8, :] = made[0:8, :]
        lane = lax.broadcasted_iota(jnp.int32, (owned, 256), 1)
        own = pl.ds(0, owned)
        hot = (lane.astype(wide) == fact(own, 2 + index)) & (fact(own, 4) > 0.5)
        count = jnp.sum(jnp.where(hot, 1.0, 0.0), axis=0, keepdims=True)
        pack[32 + index * 8 : 40 + index * 8, :] = jnp.broadcast_to(count, (8, 256))

    def sum_slots(buf, count):
        total = buf[0]
        for k in range(1, count):
            total = total + buf[k]
        return total

    got = [
        copies.local(pack, pack_plane.at[share])
        if d == 0
        else to_peer(pack, pack_plane.at[share], here.members[d])
        for d in range(SHARE)
    ]
    z_o.finish(stage)
    deliver(
        lambda t: go.at[0:head_width, part(t, owned)], o_go.at[part(share, head_width), :]
    )
    finish_q(0)
    landed(got)
    for copy in got[1:]:
        copy.wait_send()
        done.append(copy)
    pack[...] = sum_slots(pack_plane, SHARE)
    got = [
        copies.local(pack, pack_side.at[side]),
        to_peer(pack, pack_side.at[side], here.across),
    ]
    finish_q(1)
    landed(got)
    got[1].wait_send()
    done.append(got[1])
    pack[...] = pack_side[0] + pack_side[1]
    got = [
        copies.local(pack, pack_ring.at[here.place])
        if k == 0
        else to_peer(pack, pack_ring.at[here.place], planes[k])
        for k in range(4)
    ]

    finish_q(2)
    first_out.finish()
    landed(got)
    for copy in got[1:]:
        copy.wait_send()
        done.append(copy)
    pack[...] = sum_slots(pack_ring, 4)
    outs.append(copies.local(pack, o_pack))

    drains = [g_o] + g_q + g_u + g_d + [z_d, z_u, z_o, z_q, reduce, units_out, gates_out, dall_out]
    for one in drains + [gproj_out, r_rows_out, first_out]:
        one.drain()
    input_far.wait()
    for copy in owed:
        copy.wait_recv()
    for copy in outs:
        copy.wait()
    for copy in sent:
        if not any(copy is one for one in done):
            copy.wait_send()
    copies.check()


def finish_kernel(
    block, inp, gq, go, gu, gd, gf, sums,
    o_block, o_inp, o_gains, o_gq, o_go, o_gu, o_gd, o_first, o_second, o_usage,
    b_block, b_inp, b_q, b_o, b_u, b_d, b_f, w_q, w_o, w_u, w_d, w_f, in_sems, out_sems,
):
    narrow = [(gu, b_u), (gd, b_d), (gq, b_q), (gf, b_f), (go, b_o)]
    narrow += [(block, b_block), (inp, b_inp)]
    loads = [
        pltpu.make_async_copy(src, dst, in_sems.at[i]) for i, (src, dst) in enumerate(narrow)
    ]
    for load in loads:
        load.start()
    stores = []

    def store(src, dst):
        copy = pltpu.make_async_copy(src, dst, out_sems.at[len(stores)])
        copy.start()
        stores.append(copy)

    for index in range(2):
        for j in range(8):
            o_gains[index : index + 1, j * 256 : (j + 1) * 256] = sums[
                index * 8 + j : index * 8 + j + 1, :
            ]
        o_second[index] = sums[16 + index * 8 : 16 + index * 8 + NB, :]
        o_usage[index : index + 1, :] = sums[32 + index * 8 : 33 + index * 8, 0:NB]
    wides = [(b_u, w_u, o_gu), (b_d, w_d, o_gd), (b_q, w_q, o_gq)]
    wides += [(b_f, w_f, o_first), (b_o, w_o, o_go)]
    for i, (src, dst, out) in enumerate(wides):
        loads[i].wait()
        lead = src.shape[0] if len(src.shape) == 3 else None
        step = 128
        rows = src.shape[-2]
        for n in range(lead or 1):

            def widen(k, src=src, dst=dst, n=n, lead=lead):
                at = part(k, step)
                if lead is None:
                    dst[at, :] = src[at, :].astype(wide)
                else:
                    dst[n, at, :] = src[n, at, :].astype(wide)

            tiles(rows // step, widen)
        store(dst, out)
    for i, (src, out) in enumerate(((b_block, o_block), (b_inp, o_inp))):
        loads[5 + i].wait()
        store(src, out)
    for copy in stores:
        copy.wait()


def plane(mesh):
    fsdp = mesh.shape["fsdp"]
    ring_size = fsdp // SHARE

    def shards(
        tokens,
        head_bucket,
        ffn_bucket,
        lengths,
        norm_gains,
        qkv_weight,
        out_weight,
        up_weight,
        down_weight,
        router_first,
        router_second,
        cotangent,
    ):
        rows, width = tokens.shape
        half = rows // 2
        local_units = up_weight.shape[1]
        units = local_units // SHARE
        local_width = out_weight.shape[0]
        head_width = local_width // SHARE
        heads = head_width // HD
        owned = width // fsdp
        block = width // ring_size
        plane_rows = SHARE * rows

        turns = np.float32(theta_base) ** np.float32(-2.0 * np.arange(HD // 2) / HD)
        turns = np.tile(np.concatenate([turns, turns])[None, :], (8, 1)).astype(np.float32)
        b16, f32 = low, wide
        hidden = router_first.shape[2]
        small = 48

        def shape(*dims):
            return jax.ShapeDtypeStruct(dims[1:], dims[0])

        def buffer(*dims):
            return pltpu.VMEM(dims[1:], dims[0])

        anywhere = pl.BlockSpec(memory_space=pl.ANY)
        vmem = pl.BlockSpec(memory_space=pltpu.VMEM)
        (
            block_out,
            input_grad,
            raw_qkv,
            raw_out,
            raw_up,
            raw_down,
            raw_first,
            sums,
            *_,
        ) = pl.pallas_call(
            layer_kernel,
            out_shape=[
                shape(b16, rows, width),
                shape(b16, rows, width),
                shape(b16, 3, owned, local_width),
                shape(b16, local_width, owned),
                shape(b16, owned, local_units),
                shape(b16, local_units, owned),
                shape(b16, *router_first.shape),
                shape(f32, small, 256),
                shape(b16, plane_rows, width),
                shape(b16, width, 3 * head_width),
                shape(b16, 5, block, 3 * head_width),
                shape(b16, 5, head_width, block),
                shape(b16, 5, block, units),
                shape(b16, 5, units, block),
            ],
            in_specs=[anywhere] * 7 + [vmem] * 5 + [pl.BlockSpec(memory_space=pltpu.SMEM)],
            out_specs=[anywhere] * 14,
            scratch_shapes=[
                buffer(b16, plane_rows, width),
                buffer(b16, plane_rows, width),
                buffer(b16, plane_rows, width),
                buffer(b16, plane_rows, width),
                buffer(b16, 2 * plane_rows, units),
                buffer(b16, head_width, width),
                buffer(b16, width, units),
                buffer(b16, units, width),
                buffer(f32, plane_rows, 3 * HD),
                buffer(f32, SHARE, 8, rows),
                buffer(b16, plane_rows, 3 * head_width),
                buffer(f32, SHARE * heads * rows, rows),
                buffer(b16, plane_rows, head_width),
                buffer(f32, plane_rows // 2, width + HD),
                buffer(b16, plane_rows // 2, width + HD),
                buffer(b16, plane_rows // 2, width + HD),
                buffer(b16, 3 * half, width + HD),
                buffer(b16, 3 * half, width + HD),
                buffer(f32, half, width),
                buffer(f32, half, width),
                buffer(b16, 4 * head_width, block),
                buffer(b16, 2, block, units),
                buffer(b16, half, width),
                buffer(b16, half, width),
                buffer(b16, half, width),
                buffer(f32, width, hidden),
                buffer(f32, half, width),
                buffer(f32, plane_rows, HD),
                buffer(b16, plane_rows, hidden),
                buffer(f32, 2, HD, hidden),
                buffer(f32, rows, 3 * HD),
                buffer(f32, 8, rows),
                buffer(f32, HD, HD),
                buffer(f32, 2, half, HD),
                buffer(f32, 2, half, hidden),
                buffer(f32, 2, half, HD),
                buffer(f32, 2, half, hidden),
                buffer(b16, plane_rows, 2 * hidden),
                buffer(b16, 2, 256, hidden),
                buffer(b16, 4, 2, 64, hidden),
                buffer(f32, 8, width),
                buffer(f32, small, 256),
                buffer(f32, SHARE, small, 256),
                buffer(f32, 2, small, 256),
                buffer(f32, 4, small, 256),
                pltpu.SemaphoreType.DMA((80,)),
                pltpu.SemaphoreType.DMA((240,)),
                pltpu.SemaphoreType.DMA((220,)),
                pltpu.SemaphoreType.REGULAR((3,)),
            ],
            compiler_params=pltpu.CompilerParams(
                collective_id=0, has_side_effects=True, vmem_limit_bytes=127 * 2**19
            ),
        )(
            tokens,
            cotangent,
            jnp.transpose(qkv_weight, (1, 0, 2)),
            out_weight,
            up_weight,
            down_weight,
            router_first,
            norm_gains,
            jnp.transpose(router_second, (0, 2, 1)),
            head_bucket.reshape(2, half),
            ffn_bucket.reshape(2, half),
            jnp.asarray(turns),
            lengths,
        )
        wides = [
            (3, owned, local_width),
            (local_width, owned),
            (owned, local_units),
            (local_units, owned),
            router_first.shape,
        ]
        (
            block_out,
            input_grad,
            grad_gains,
            grad_qkv,
            grad_out,
            grad_up,
            grad_down,
            grad_first,
            grad_second,
            usage,
        ) = pl.pallas_call(
            finish_kernel,
            out_shape=[shape(b16, rows, width), shape(b16, rows, width), shape(f32, 2, width)]
            + [shape(f32, *dims) for dims in wides]
            + [shape(f32, 2, NB, hidden), shape(f32, 2, NB)],
            in_specs=[anywhere] * 7 + [vmem],
            out_specs=[anywhere] * 2 + [vmem] + [anywhere] * 5 + [vmem] * 2,
            scratch_shapes=[buffer(b16, rows, width)] * 2
            + [buffer(b16, *dims) for dims in wides]
            + [buffer(f32, *dims) for dims in wides]
            + [pltpu.SemaphoreType.DMA((8,)), pltpu.SemaphoreType.DMA((8,))],
            compiler_params=pltpu.CompilerParams(vmem_limit_bytes=60 * 2**20),
        )(block_out, input_grad, raw_qkv, raw_out, raw_up, raw_down, raw_first, sums)
        grad_qkv = jnp.transpose(grad_qkv, (1, 0, 2))
        grad_second = jnp.transpose(grad_second, (0, 2, 1))
        return (
            block_out,
            input_grad,
            grad_gains,
            grad_qkv,
            grad_out,
            grad_up,
            grad_down,
            grad_first,
            grad_second,
            usage,
        )

    return shards


def solution(mesh):
    shards = plane(mesh) if mesh.shape["fsdp"] == 4 * SHARE else general(mesh)
    in_specs = (
        P("fsdp", None),
        P("fsdp"),
        P("fsdp"),
        P("fsdp", None),
        P(),
        P("fsdp", None, "tensor"),
        P("tensor", "fsdp"),
        P("fsdp", "tensor"),
        P("tensor", "fsdp"),
        P(),
        P(),
        P("fsdp", None),
    )
    out_specs = (
        P("fsdp", None),
        P("fsdp", None),
        P(),
        P("fsdp", None, "tensor"),
        P("tensor", "fsdp"),
        P("fsdp", "tensor"),
        P("tensor", "fsdp"),
        P(),
        P(),
        P(),
    )
    return jax.shard_map(
        shards, mesh=mesh, in_specs=in_specs, out_specs=out_specs, check_vma=False
    )
```

```python
from functools import partial

import jax
import jax.numpy as jnp
import numpy as np
from jax import lax
from jax.experimental import pallas as pl
from jax.experimental.pallas import tpu as pltpu
from jax.sharding import PartitionSpec as P

HEADS = 16
HD = 128
FF = 8192
NB = 4
SHARE = 4

epsilon = 1e-05
theta_base = 10000.0
highest = lax.Precision.HIGHEST
low = jnp.bfloat16
wide = jnp.float32
MESH = pl.DeviceIdType.MESH


def norm_piece(values_in, gain_row):
    return (
        values_in
        * lax.rsqrt(jnp.mean(values_in * values_in, axis=-1, keepdims=True) + epsilon)
        * gain_row
    )


def route_piece(hidden_in, router_in, router_out, bucket):
    inner = jax.nn.silu(jnp.dot(hidden_in, router_in, precision=highest))
    logits = jnp.dot(inner, router_out, precision=highest)
    probs_all = jax.nn.softmax(logits, axis=-1)
    onehot = (bucket[:, None] == jnp.arange(NB, dtype=jnp.int32)[None, :]).astype(wide)
    return NB * jnp.sum(probs_all * onehot, axis=-1)


def dot(left_in, right_in):
    return jnp.dot(left_in, right_in, preferred_element_type=wide)


def dot_rows(left_in, right_in):
    return lax.dot_general(
        left_in, right_in, (((0,), (0,)), ((), ())), preferred_element_type=wide
    )


def dot_cols(left_in, right_in):
    return lax.dot_general(
        left_in, right_in, (((1,), (1,)), ((), ())), preferred_element_type=wide
    )


def rotate(operand, cosine, sine_table):
    half_dim = operand.shape[-1] // 2
    lead_half = operand[..., :half_dim]
    tail_half = operand[..., half_dim:]
    return jnp.concatenate(
        [lead_half * cosine - tail_half * sine_table, tail_half * cosine + lead_half * sine_table],
        axis=-1,
    )


def layout(length_rows, slot_ids):
    seq_count = length_rows.shape[1]
    order = jnp.arange(seq_count, dtype=jnp.int32)
    seq_ends = jnp.sum(
        jnp.where(order[None, None, :] <= order[None, :, None], length_rows[:, None, :], 0), axis=2
    )
    seq_starts = seq_ends - length_rows
    slots = slot_ids[None, :, None]
    member = (slots >= seq_starts[:, None, :]) & (slots < seq_ends[:, None, :])
    seq_of = jnp.sum(jnp.where(member, jnp.arange(seq_count, dtype=jnp.int32), 0), axis=2)
    live_rows = jnp.any(member, axis=2)
    seq_begin = jnp.sum(jnp.where(member, seq_starts[:, None, :], 0), axis=2)
    segment = jnp.where(live_rows, seq_of, seq_count + slot_ids[None, :])
    position = slot_ids[None, :] - seq_begin
    return segment, position, live_rows


def general(mesh):
    fsdp = mesh.shape["fsdp"]
    ring_size = fsdp // SHARE

    def hop(moved, bits):
        return lax.ppermute(moved, "fsdp", [(i, i ^ bits) for i in range(fsdp)])

    def cross(moved):
        return lax.ppermute(moved, "tensor", [(0, 1), (1, 0)])

    def shards(
        tokens,
        head_bucket,
        ffn_bucket,
        lengths,
        norm_gains,
        qkv_weight,
        out_weight,
        up_weight,
        down_weight,
        router_first,
        router_second,
        cotangent,
    ):
        rows, width = tokens.shape
        half = rows // 2
        rank = lax.axis_index("fsdp")
        side = lax.axis_index("tensor")
        share = rank % SHARE
        place = rank // SHARE
        local_units = up_weight.shape[1]
        units = local_units // SHARE
        local_width = out_weight.shape[0]
        head_width = local_width // SHARE
        heads = head_width // HD
        owned = width // fsdp
        block = width // ring_size

        chain = [None, None]

        def ring(moved, stream):
            if chain[stream] is not None:
                moved, _ = lax.optimization_barrier((moved, chain[stream]))
            got = lax.ppermute(
                moved, "fsdp", [(i, (i + SHARE) % fsdp) for i in range(fsdp)]
            )
            chain[stream] = got
            return got

        def place_at(step):
            return (place - step) % ring_size

        def own_half(arr):
            return lax.dynamic_slice_in_dim(arr, side * half, half, 0)

        def relative(arr):
            return jnp.concatenate(
                [own_half(arr), lax.dynamic_slice_in_dim(arr, (1 - side) * half, half, 0)], axis=0
            )

        def gather_rows(arr):
            other = hop(arr, 2)
            plane = jnp.concatenate([arr[:half], other[:half], arr[half:], other[half:]], axis=0)
            return jnp.concatenate([plane, hop(plane, 1)], axis=0)

        def gather_halves(arr):
            pair = jnp.concatenate([arr, hop(arr, 2)], axis=0)
            plane = jnp.concatenate([pair, cross(pair)], axis=0)
            return jnp.concatenate([plane, hop(plane, 1)], axis=0)

        def reduce_rows(keep, send):
            total = keep + hop(send.astype(low), 1).astype(wide)
            total = total[: 2 * half] + cross(total[2 * half :].astype(low)).astype(wide)
            return total[:half] + hop(total[half:].astype(low), 2).astype(wide)

        def whole_rows(arr):
            other = cross(arr)
            return jnp.where(
                side == 0,
                jnp.concatenate([arr, other], axis=0),
                jnp.concatenate([other, arr], axis=0),
            )

        def spread(pieces_for, axis):
            out = None
            for bits in range(SHARE):
                piece = pieces_for(share ^ bits)
                got = piece if bits == 0 else hop(piece, bits)
                if out is None:
                    dims = list(got.shape)
                    dims[axis] *= SHARE
                    out = jnp.zeros(dims, got.dtype)
                out = lax.dynamic_update_slice_in_dim(
                    out, got, (share ^ bits) * got.shape[axis], axis
                )
            return out

        def ring_gather(own, axis):
            dims = list(own.shape)
            dims[axis] = width
            out = jnp.zeros(dims, own.dtype)
            mid = own.shape[0] // 2
            moving = [own[:mid], own[mid:]]
            for step in range(ring_size):
                if step:
                    moving = [ring(moving[s], s) for s in range(2)]
                base = place_at(step) * block
                for s in range(2):
                    if axis == 0:
                        at = (base + s * mid, 0)
                    else:
                        at = (s * mid, base)
                    out = lax.dynamic_update_slice(out, moving[s], at)
            return out

        def ring_reduce(term):
            moving = [None, None]
            for step in range(1, ring_size):
                for s in range(2):
                    part = term(place_at(step), s)
                    if moving[s] is not None:
                        part = part + moving[s].astype(wide)
                    moving[s] = part.astype(low)
                for s in range(2):
                    moving[s] = ring(moving[s], s)
            return [term(place, s) + moving[s].astype(wide) for s in range(2)]

        def scatter_back(parts, axis):
            joined = jnp.concatenate(parts, axis=0)
            other = 1 - axis
            out_dims = list(joined.shape)
            out_dims[axis] = owned
            stride = out_dims[other]
            out_dims[other] *= SHARE
            out = jnp.zeros(out_dims, wide)
            for bits in range(SHARE):
                piece = lax.dynamic_slice_in_dim(joined, (share ^ bits) * owned, owned, axis)
                if bits:
                    piece = hop(piece.astype(low), bits).astype(wide)
                out = lax.dynamic_update_slice_in_dim(out, piece, (share ^ bits) * stride, other)
            return out

        def qkv_piece(target):
            return lax.dynamic_slice_in_dim(
                qkv_weight, target * head_width, head_width, 2
            ).reshape(owned, 3 * head_width)

        qkv_block = spread(qkv_piece, 0)
        rel_tokens = relative(tokens)
        rel_cot = relative(cotangent)
        ints = relative(jnp.stack([head_bucket, ffn_bucket], axis=1))
        qkv_full = ring_gather(qkv_block, 0)
        all_tokens = gather_rows(rel_tokens)
        buckets = gather_rows(ints)
        pair_lengths = jnp.concatenate([lengths, hop(lengths, 2)], axis=0)
        group_lengths = jnp.concatenate([pair_lengths, hop(pair_lengths, 1)], axis=0)

        out_block = spread(
            lambda t: lax.dynamic_slice_in_dim(out_weight, t * head_width, head_width, 0), 1
        )
        out_full = ring_gather(out_block, 1)
        up_block = spread(lambda t: lax.dynamic_slice_in_dim(up_weight, t * units, units, 1), 0)
        up_full = ring_gather(up_block, 0)
        down_block = spread(
            lambda t: lax.dynamic_slice_in_dim(down_weight, t * units, units, 0), 1
        )
        down_full = ring_gather(down_block, 1)
        all_cot = gather_rows(rel_cot)

        slot_ids = jnp.concatenate(
            [
                side * half + jnp.arange(half, dtype=jnp.int32),
                (1 - side) * half + jnp.arange(half, dtype=jnp.int32),
            ]
        )
        segment, position, live_groups = layout(group_lengths, slot_ids)

        def to_groups(arr):
            tail = arr.shape[1:]
            arr = arr.reshape((2, 2, 2, half) + tail)
            return jnp.swapaxes(arr, 1, 2).reshape((SHARE, rows) + tail)

        def from_groups(arr):
            tail = arr.shape[2:]
            arr = arr.reshape((2, 2, 2, half) + tail)
            return jnp.swapaxes(arr, 1, 2).reshape((8 * half,) + tail)

        live_all = from_groups(live_groups)
        all_heads = buckets[:, 0]
        all_widths = buckets[:, 1]

        own_tokens = rel_tokens[:half].astype(wide)
        own_heads = all_heads[:half]
        own_widths = all_widths[:half]
        own_live = live_all[:half]

        block_in = all_tokens.astype(wide)
        hidden_heads = norm_piece(block_in, norm_gains[0]).astype(low)
        own_normed, norm_heads_back = jax.vjp(norm_piece, own_tokens, norm_gains[0])
        gate_heads, route_heads_back = jax.vjp(
            partial(route_piece, bucket=own_heads),
            own_normed.astype(low).astype(wide),
            router_first[0],
            router_second[0],
        )
        head_ids = side * (local_width // HD) + share * heads + jnp.arange(heads, dtype=jnp.int32)
        head_used = head_ids[None, :] < HEADS // NB * (all_heads[:, None] + 1)
        unit_ids = side * local_units + share * units + jnp.arange(units, dtype=jnp.int32)
        unit_used = unit_ids[None, :] < FF // NB * (all_widths[:, None] + 1)

        half_dim = HD // 2
        frequency = theta_base ** (-2.0 * jnp.arange(half_dim, dtype=wide) / HD)
        angles = position.astype(wide)[:, :, None] * frequency
        cosine = jnp.cos(angles)[:, :, None, :]
        sine_table = jnp.sin(angles)[:, :, None, :]
        qkv_all = to_groups(dot(hidden_heads, qkv_full).reshape(8 * half, 3, heads, HD))
        query = rotate(qkv_all[:, :, 0], cosine, sine_table).astype(low)
        keyed = rotate(qkv_all[:, :, 1], cosine, sine_table).astype(low)
        value = qkv_all[:, :, 2].astype(low)
        group_used = to_groups(head_used)
        same_seq = segment[:, :, None] == segment[:, None, :]
        causal = slot_ids[None, :] <= slot_ids[:, None]
        diagonal = slot_ids[None, :] == slot_ids[:, None]
        key_used = jnp.swapaxes(group_used, 1, 2)
        allowed = (same_seq & causal)[:, None] & (key_used[:, :, None, :] | diagonal)
        scale = HD ** (-0.5)
        scores = jnp.einsum("gqhe,gkhe->ghqk", query, keyed, preferred_element_type=wide) * scale
        scores = jnp.where(allowed, scores, -1e30)
        row_top = jnp.max(scores, axis=-1, keepdims=True)
        weights = jnp.exp(scores - row_top)
        probs = weights / jnp.sum(weights, axis=-1, keepdims=True)
        probs_low = probs.astype(low)
        mixed = jnp.einsum("ghqk,gkhe->gqhe", probs_low, value, preferred_element_type=wide)
        mixed = jnp.where(group_used[..., None], mixed, 0.0).astype(low)
        attended = from_groups(mixed).reshape(8 * half, head_width)

        def partial_rows(left_in, matrix, product):
            keep = product(left_in[: 4 * half], matrix)
            send = product(left_in[4 * half :], matrix)
            return reduce_rows(keep, send)

        projected = partial_rows(attended, out_full, dot)

        middle = own_tokens + gate_heads[:, None] * projected
        normed_units, norm_units_back = jax.vjp(norm_piece, middle, norm_gains[1])
        own_units = normed_units.astype(low)
        hidden_units = gather_halves(own_units)
        gate_units, route_units_back = jax.vjp(
            partial(route_piece, bucket=own_widths),
            own_units.astype(wide),
            router_first[1],
            router_second[1],
        )
        all_gates = gather_halves(gate_units[:, None])
        upward = dot(hidden_units, up_full)
        activated = jnp.where(unit_used, jnp.square(jax.nn.relu(upward)), 0.0).astype(low)
        grad_top_all = jnp.where(live_all[:, None], all_cot.astype(wide), 0.0)
        grad_down_in = (all_gates * grad_top_all).astype(low)

        def down_term(at, s):
            mid = units // 2
            return dot_rows(
                activated[:, s * mid : (s + 1) * mid],
                lax.dynamic_slice_in_dim(grad_down_in, at * block, block, 1),
            )

        grad_down = scatter_back(ring_reduce(down_term), 1)

        downward = partial_rows(activated, down_full, dot)
        own_out = jnp.where(
            own_live[:, None], middle + gate_units[:, None] * downward, 0.0
        ).astype(low)
        block_out = whole_rows(own_out)
        grad_top = jnp.where(own_live[:, None], rel_cot[:half].astype(wide), 0.0)
        grad_gate_units = jnp.sum(grad_top * downward, axis=1)

        grad_act = dot_cols(grad_down_in, down_full)
        grad_up_in = jnp.where(unit_used, 2.0 * jax.nn.relu(upward) * grad_act, 0.0).astype(low)

        def up_term(at, s):
            mid = block // 2
            return dot_rows(
                lax.dynamic_slice_in_dim(hidden_units, at * block + s * mid, mid, 1), grad_up_in
            )

        grad_up = scatter_back(ring_reduce(up_term), 0)
        route_units_grads = route_units_back(grad_gate_units)
        grad_hidden_units = partial_rows(grad_up_in, up_full, dot_cols) + route_units_grads[0]
        norm_units_grads = norm_units_back(grad_hidden_units)
        grad_middle = grad_top + norm_units_grads[0]
        grad_gate_heads = jnp.sum(grad_middle * projected, axis=1)
        grad_projected = gather_halves((gate_heads[:, None] * grad_middle).astype(low))

        def out_term(at, s):
            mid = head_width // 2
            return dot_rows(
                attended[:, s * mid : (s + 1) * mid],
                lax.dynamic_slice_in_dim(grad_projected, at * block, block, 1),
            )

        grad_out = scatter_back(ring_reduce(out_term), 1)
        grad_attended = to_groups(
            dot_cols(grad_projected, out_full).astype(low).reshape(8 * half, heads, HD)
        )
        grad_attended = jnp.where(group_used[..., None], grad_attended, jnp.zeros((), low))
        grad_value = jnp.einsum(
            "ghqk,gqhe->gkhe", probs_low, grad_attended, preferred_element_type=wide
        )
        grad_probs = jnp.einsum(
            "gqhe,gkhe->ghqk", grad_attended, value, preferred_element_type=wide
        )
        row_dot = jnp.sum(probs * grad_probs, axis=-1, keepdims=True)
        grad_scores = (probs * (grad_probs - row_dot)).astype(low)
        grad_query = (
            jnp.einsum("ghqk,gkhe->gqhe", grad_scores, keyed, preferred_element_type=wide) * scale
        )
        grad_keyed = (
            jnp.einsum("ghqk,gqhe->gkhe", grad_scores, query, preferred_element_type=wide) * scale
        )
        grad_qkv_in = jnp.stack(
            [
                rotate(grad_query, cosine, -sine_table),
                rotate(grad_keyed, cosine, -sine_table),
                grad_value,
            ],
            axis=2,
        ).astype(low)
        grad_qkv_in = from_groups(grad_qkv_in).reshape(8 * half, 3 * head_width)

        def qkv_term(at, s):
            mid = block // 2
            return dot_rows(
                lax.dynamic_slice_in_dim(hidden_heads, at * block + s * mid, mid, 1), grad_qkv_in
            )

        qkv_parts = ring_reduce(qkv_term)
        joined = jnp.concatenate(qkv_parts, axis=0)
        grad_qkv = jnp.zeros((owned, 3, local_width), wide)
        for bits in range(SHARE):
            piece = lax.dynamic_slice_in_dim(joined, (share ^ bits) * owned, owned, 0)
            if bits:
                piece = hop(piece.astype(low), bits).astype(wide)
            grad_qkv = lax.dynamic_update_slice_in_dim(
                grad_qkv, piece.reshape(owned, 3, head_width), (share ^ bits) * head_width, 2
            )

        route_heads_grads = route_heads_back(grad_gate_heads)
        grad_hidden_heads = partial_rows(grad_qkv_in, qkv_full, dot_cols) + route_heads_grads[0]
        norm_heads_grads = norm_heads_back(grad_hidden_heads)
        input_grad = whole_rows((grad_middle + norm_heads_grads[0]).astype(low))

        def total_small(arr):
            arr = arr + cross(arr)
            bits = 1
            while bits < fsdp:
                arr = arr + hop(arr, bits)
                bits *= 2
            return arr

        def total_large(arr):
            steps = [1, "tensor"] + [2**i for i in range(1, fsdp.bit_length() - 1)]
            for bits in steps:
                mid = arr.shape[0] // 2
                me = side if bits == "tensor" else (rank // bits) % 2
                send = lax.dynamic_slice_in_dim(arr, (1 - me) * mid, mid, 0)
                keep = lax.dynamic_slice_in_dim(arr, me * mid, mid, 0)
                arr = keep + (cross(send) if bits == "tensor" else hop(send, bits))
            for bits in reversed(steps):
                me = side if bits == "tensor" else (rank // bits) % 2
                other = cross(arr) if bits == "tensor" else hop(arr, bits)
                arr = jnp.where(
                    me == 0,
                    jnp.concatenate([arr, other], axis=0),
                    jnp.concatenate([other, arr], axis=0),
                )
            return arr

        bucket_ids = jnp.arange(NB, dtype=jnp.int32)[None, :]
        head_counts = jnp.sum(
            jnp.where(own_live[:, None] & (own_heads[:, None] == bucket_ids), 1.0, 0.0), axis=0
        )
        width_counts = jnp.sum(
            jnp.where(own_live[:, None] & (own_widths[:, None] == bucket_ids), 1.0, 0.0), axis=0
        )
        units_small = total_small(
            jnp.concatenate(
                [norm_units_grads[1], route_units_grads[2].reshape(-1), head_counts, width_counts]
            )
        )
        heads_small = total_small(
            jnp.concatenate([norm_heads_grads[1], route_heads_grads[2].reshape(-1)])
        )
        first_units = total_large(route_units_grads[1])
        first_heads = total_large(route_heads_grads[1])
        second_shape = router_second.shape[1:]
        second_size = second_shape[0] * second_shape[1]
        grad_gains = jnp.stack([heads_small[:width], units_small[:width]])
        grad_second = jnp.stack(
            [
                heads_small[width : width + second_size].reshape(second_shape),
                units_small[width : width + second_size].reshape(second_shape),
            ]
        )
        usage = units_small[width + second_size :].reshape(2, NB)
        grad_first = jnp.stack([first_heads, first_units])
        return (
            block_out,
            input_grad,
            grad_gains,
            grad_qkv,
            grad_out,
            grad_up,
            grad_down,
            grad_first,
            grad_second,
            usage,
        )

    return shards


def xor_one(index):
    return index + 1 - 2 * (index % 2)


class Plane:
    def __init__(self):
        self.rank = lax.axis_index("fsdp")
        self.side = lax.axis_index("tensor")
        self.share = self.rank % SHARE
        self.place = self.rank // SHARE
        core = xor_one(self.share)
        mid = (self.share + 2) % SHARE
        self.shares = [self.share, core, mid, SHARE - 1 - self.share]
        self.core = {"fsdp": self.place * SHARE + core}
        self.mid = {"fsdp": self.place * SHARE + mid}
        self.both = {"fsdp": self.place * SHARE + self.shares[3]}
        self.members = [None, self.core, self.mid, self.both]
        self.across = {"tensor": 1 - self.side}
        self.near_place = xor_one(self.place)
        self.two_place = (self.place + 2) % 4
        self.far_place = 3 - self.place
        self.near = {"fsdp": self.near_place * SHARE + self.share}
        self.two = {"fsdp": self.two_place * SHARE + self.share}
        self.far = {"fsdp": self.far_place * SHARE + self.share}
        self.inner = (self.place == 1) | (self.place == 2)
        self.outer = (self.place == 0) | (self.place == 3)

    def greet(self):
        barrier = pltpu.get_barrier_semaphore()
        peers = [self.core, self.mid, self.both, self.across, self.near, self.two, self.far]
        for peer in peers:
            pl.semaphore_signal(barrier, inc=1, device_id=peer, device_id_type=MESH)
        pl.semaphore_wait(barrier, len(peers))


class Copies:
    def __init__(self, local_sems, send_sems, recv_sems):
        self.local_sems, self.send_sems, self.recv_sems = local_sems, send_sems, recv_sems
        self.locals, self.sends, self.recvs = 0, 0, 0

    def check(self):
        assert self.locals <= self.local_sems.shape[0]
        assert self.sends <= self.send_sems.shape[0]
        assert self.recvs <= self.recv_sems.shape[0]

    def local(self, src, dst):
        copy = pltpu.make_async_copy(src, dst, self.local_sems.at[self.locals])
        self.locals += 1
        copy.start()
        return copy

    def slot(self):
        self.recvs += 1
        return self.recvs - 1

    def remote(self, src, dst, peer, slot=None):
        if slot is None:
            slot = self.slot()
        copy = pltpu.make_async_remote_copy(
            src_ref=src,
            dst_ref=dst,
            send_sem=self.send_sems.at[self.sends],
            recv_sem=self.recv_sems.at[slot],
            device_id=peer,
            device_id_type=MESH,
        )
        self.sends += 1
        return copy

    def push(self, src, dst, peer):
        copy = self.remote(src, dst, peer)
        copy.start()
        return copy


class ZGather:
    def __init__(self, here, copies, view):
        self.here, self.copies, self.view, self.drained = here, copies, view, False
        self.slots = [copies.slot() for _ in range(3)]

    def copy(self, place, peer, slot):
        block = self.view(place)
        return self.copies.remote(block, block, peer, self.slots[slot])

    def start(self, whole=True):
        here = self.here
        self.near = self.copy(here.place, here.near, 0)
        if whole:
            self.near.start()
        else:
            pl.when(here.outer)(self.near.start)
        self.far = self.copy(here.place, here.far, 1)
        self.on_far = self.copy(here.near_place, here.far, 2)
        self.on_near = self.copy(here.far_place, here.near, 1)
        self.last = self.copy(here.two_place, here.near, 2)
        pl.when(here.inner)(self.far.start)

    def start_late(self):
        pl.when(self.here.inner)(self.near.start)

    def first(self):
        @pl.when(self.here.inner)
        def _():
            self.near.wait_recv()
            self.on_far.start()
            self.far.wait_recv()
            self.on_near.start()

    def second(self):
        @pl.when(self.here.inner)
        def _():
            self.on_far.wait_recv()
            self.last.start()

    def arrive(self):
        @pl.when(self.here.outer)
        def _():
            self.near.wait_recv()
            self.on_near.wait_recv()
            self.last.wait_recv()

    def drain(self):
        if self.drained:
            return
        self.drained = True
        self.near.wait_send()

        @pl.when(self.here.inner)
        def _():
            for copy in (self.far, self.on_far, self.on_near, self.last):
                copy.wait_send()


def tiles(count, body):
    def step(i, carry):
        body(i)
        return carry

    lax.fori_loop(0, count, step, 0)


def part(index, size):
    return pl.ds(pl.multiple_of(index * size, size), size)


class RowReduce:
    def __init__(self, here, copies, bufs, acks=None):
        self.here, self.copies, self.acks = here, copies, acks
        (self.snd, self.rcv, self.acc, self.out, self.into) = bufs
        self.sent = []

    def begin(self, width):
        self.lanes = pl.ds(0, width)
        for copy in self.sent:
            copy.wait_send()
        self.sent, self.core = [], []

    def core_send(self, index):
        rows = pl.ds(index * 256, 256)
        self.core.append(self.copies.push(
                self.snd.at[rows, self.lanes], self.rcv.at[rows, self.lanes], self.here.core
            ))

    def add_core(self, first, count):
        acc, rcv, lanes = self.acc, self.rcv, self.lanes

        def body(i):
            at = pl.ds(pl.multiple_of(first + i * 32, 32), 32)
            acc[at, lanes] = acc[at, lanes] + rcv[at, lanes].astype(wide)

        tiles(count // 32, body)

    def round_out(self, first, count, extra=None):
        acc, out, into, lanes = self.acc, self.out, self.into, self.lanes

        def body(i):
            at = pl.ds(pl.multiple_of(first + i * 32, 32), 32)
            value = acc[at, lanes]
            if extra is not None:
                value = value + into[pl.ds(pl.multiple_of(extra + i * 32, 32), 32), lanes].astype(wide)
            out[pl.ds(pl.multiple_of(first - 128 + i * 32, 32), 32), lanes] = value.astype(low)

        tiles(count // 32, body)

    def hand(self, first, end, peer):
        rows = pl.ds(first, end - first)
        return self.copies.push(
            self.out.at[rows, self.lanes], self.into.at[rows, self.lanes], peer
        )

    def diagonal(self):
        for copy in self.core:
            copy.wait_recv()
        self.add_core(384, 128)
        self.round_out(384, 128)
        self.diag_x = self.hand(256, 320, self.here.across)
        self.diag_y = self.hand(320, 384, self.here.mid)
        self.add_core(128, 256)
        self.round_out(128, 64)
        self.round_out(320, 64)
        self.add_core(0, 128)

    def sides(self):
        self.diag_y.wait_recv()
        self.round_out(192, 64, 320)
        self.over_x = self.hand(0, 128, self.here.across)
        self.diag_x.wait_recv()
        self.round_out(256, 64, 256)
        self.over_y = self.hand(128, 256, self.here.mid)
        self.sent = self.core + [self.diag_x, self.diag_y, self.over_x, self.over_y]

    def arrive(self):
        self.over_x.wait_recv()
        self.over_y.wait_recv()

    def total(self, at, size):
        acc, into, lanes = self.acc, self.into, self.lanes
        return (
            acc[pl.ds(at, size), lanes]
            + into[pl.ds(at, size), lanes].astype(wide)
            + into[pl.ds(at + 128, size), lanes].astype(wide)
        )

    def release(self):
        for index, peer in enumerate((self.here.core, self.here.across, self.here.mid)):
            pl.semaphore_signal(
                self.acks.at[index], inc=1, device_id=peer, device_id_type=MESH
            )

    def await_release(self):
        for index in range(3):
            pl.semaphore_wait(self.acks.at[index], 1)

    def drain(self):
        for copy in self.sent:
            copy.wait_send()


class RowGather:
    def __init__(self, here, copies, view, fixed=False):
        self.here, self.copies, self.view, self.fixed = here, copies, view, fixed
        self.sent, self.drained = [], False

    def start(self):
        here = self.here
        self.over_x = self.pair(0, 1, here.across)
        self.over_y = self.pair(0, 2, here.mid)
        self.cores = [self.pair(0, 4, here.core)]

    def pair(self, source, target, peer, half=None):
        src = self.view(source, half)
        dst = src if self.fixed else self.view(target, half)
        copy = self.copies.push(src, dst, peer)
        self.sent.append(copy)
        return copy

    def forward(self):
        here = self.here
        self.over_y.wait_recv()
        self.diag_x = self.pair(2, 3, here.across, 0)
        self.cores.append(self.pair(2, 6, here.core))
        self.over_x.wait_recv()
        self.diag_y = self.pair(1, 3, here.mid, 1)
        self.cores.append(self.pair(1, 5, here.core))

    def finish(self):
        self.diag_x.wait_recv()
        self.diag_y.wait_recv()
        self.cores.append(self.pair(3, 7, self.here.core))
        for copy in self.cores:
            copy.wait_recv()

    def drain(self):
        if not self.drained:
            for copy in self.sent:
                copy.wait_send()
        self.drained = True


def nn(left_in, right_in):
    return lax.dot_general(
        left_in, right_in, (((1,), (0,)), ((), ())), preferred_element_type=wide
    )


def nt(left_in, right_in):
    return lax.dot_general(
        left_in, right_in, (((1,), (1,)), ((), ())), preferred_element_type=wide
    )


def tn(left_in, right_in):
    return lax.dot_general(
        left_in, right_in, (((0,), (0,)), ((), ())), preferred_element_type=wide
    )


class ZReduce:
    def __init__(self, here, copies, base, spot, rows, columns, landing):
        self.here, self.copies, self.base, self.spot = here, copies, base, spot
        self.rows, self.columns, self.landing = rows, columns, landing
        self.slots = [copies.slot() for _ in range(5)]
        self.handed, self.passed, self.halves = [], [], {}

    def copy(self, k, peer, slot, rows=None, lanes=None, own_slot=None):
        r, c = self.spot(k)
        r0, rn = rows or (0, self.rows)
        c0, cn = lanes or (0, self.columns)
        block = self.base.at[pl.ds(r + r0, rn), pl.ds(c + c0, cn)]
        dst = self.landing.at[slot, pl.ds(r0, rn), pl.ds(c0, cn)]
        return self.copies.remote(
            block, dst, peer, self.slots[slot] if own_slot is None else own_slot
        )

    def outward_half(self, k, h, size):
        slot = {3: 1, 2: 2}[k]
        lanes = (h * size, size)
        copy = self.copy(k, self.here.near, slot, lanes=lanes, own_slot=self.copies.slot())
        self.halves[k, h] = copy
        self.handed.append(copy)
        pl.when(self.here.outer)(copy.start)

    def inward_half(self, step, h, size, stage):
        here = self.here
        k, source, slot = ((2, 1, 4), (3, 2, 3))[step]
        if h == 0:
            setattr(self, f"in{k}", self.copy(k, here.far, slot))
        push = self.copy(k, here.far, slot, lanes=(h * size, size))
        self.passed.append(push)
        lanes = pl.ds(h * size, size)

        @pl.when(here.inner)
        def _():
            self.halves[5 - k, h].wait_recv()
            self.copies.local(
                self.landing.at[source, :, lanes], stage.at[0, pl.ds(0, self.rows), lanes]
            ).wait()
            self.add(k, stage, [0], h * size, size)
            push.start()

    def outward(self, k, rows=None, lanes=None):
        slot = {3: 1, 2: 2, 1: 0}[k]
        if not hasattr(self, f"out{k}"):
            setattr(self, f"out{k}", self.copy(k, self.here.near, slot))
        copy = self.copy(k, self.here.near, slot, rows, lanes)
        self.handed.append(copy)
        pl.when(self.here.outer)(copy.start)

    def outward_piece(self, n, size):
        r, c = self.spot(1)
        if n == 0:
            self.out1 = self.copy(1, self.here.near, 0)
            self.pieces = []
        lanes = pl.ds(n * size, size)
        copy = self.copies.remote(
            self.base.at[pl.ds(r, self.rows), pl.ds(c + n * size, size)],
            self.landing.at[0, :, lanes],
            self.here.near,
        )
        self.pieces.append(copy)
        self.handed.append(copy)
        pl.when(self.here.outer)(copy.start)

    def finish_piece(self, n, size, stage):
        here = self.here

        @pl.when(here.inner)
        def _():
            lanes = pl.ds(n * size, size)
            if n == 0:
                self.in3.wait_recv()
                for load in self.load(3, stage, 1):
                    load.wait()
            self.pieces[n].wait_recv()
            self.copies.local(
                self.landing.at[0, :, lanes], stage.at[0, pl.ds(0, self.rows), lanes]
            ).wait()
            self.add(0, stage, [0, 1], n * size, size)

        if n == 0:

            @pl.when(here.outer)
            def _():
                self.out1.wait_recv()
                for load in self.load(0, stage, 0):
                    load.wait()
                self.add(0, stage, [0])

    def load(self, index, stage, slot):
        size = min(self.rows, 512)
        return [
            self.copies.local(
                self.landing.at[index, pl.ds(n * size, size), :],
                stage.at[slot, pl.ds(0, size), pl.ds(n * self.columns, self.columns)],
            )
            for n in range(self.rows // size)
        ]

    def add(self, target, stage, slots, first=0, columns=None):
        size = min(self.rows, 512)
        columns = self.columns if columns is None else columns
        r, c = self.spot(target)
        for n in range(self.rows // size):

            def body(i, n=n):
                at = pl.ds(pl.multiple_of(i * 32, 32), 32)
                mine = pl.ds(pl.multiple_of(r + n * size + i * 32, 32), 32)
                lanes = pl.ds(c + first, columns)
                value = self.base[mine, lanes].astype(wide)
                for slot in slots:
                    value = value + stage[
                        slot, at, pl.ds(n * self.columns + first, columns)
                    ].astype(wide)
                self.base[mine, lanes] = value.astype(low)

            tiles(size // 32, body)

    def pass_on(self, k, wait, index, stage, copy):
        wait.wait_recv()
        for load in self.load(index, stage, 0):
            load.wait()
        self.add(k, stage, [0])
        copy.start()

    def inward(self, step, stage):
        here = self.here
        if step == 0:
            self.in2 = self.copy(2, here.far, 4)
            args = (2, self.out3, 1, stage, self.in2)
        elif step == 1:
            self.in3 = self.copy(3, here.far, 3)
            args = (3, self.out2, 2, stage, self.in3)
        else:
            self.in1 = self.copy(1, here.near, 0)
            args = (1, self.in2, 4, stage, self.in1)

        @pl.when(here.inner)
        def _():
            self.pass_on(*args)

    def finish(self, stage):
        here = self.here
        self.out1.wait_recv()
        loads = self.load(0, stage, 0)

        @pl.when(here.inner)
        def _():
            self.in3.wait_recv()
            for load in self.load(3, stage, 1) + loads:
                load.wait()
            self.add(0, stage, [0, 1])

        @pl.when(here.outer)
        def _():
            for load in loads:
                load.wait()
            self.add(0, stage, [0])

    def drain(self):
        @pl.when(self.here.inner)
        def _():
            for copy in [self.in1] + (self.passed or [self.in2, self.in3]):
                copy.wait_send()

        @pl.when(self.here.outer)
        def _():
            for copy in self.handed:
                copy.wait_send()


def norm_back(value, grad, gain):
    r = lax.rsqrt(jnp.mean(value * value, axis=-1, keepdims=True) + epsilon)
    u = gain * grad
    lean = jnp.mean(u * value, axis=-1, keepdims=True)
    return r * u - value * (r * r * r * lean), grad * value * r


def exact(left_in, right_in, contract):
    return lax.dot_general(
        left_in, right_in, (contract, ((), ())), precision=highest, preferred_element_type=wide
    )


def layer_kernel(
    tok, cot_in, qkvw, outw, upw, downw, first, gains, second_in, heads_in, widths_in, turns,
    lengths,
    o_block, o_input, o_gq, o_go, o_gu, o_gd, o_first, o_pack, s_hid, s_wq, l_q, l_o, l_u, l_d,
    toks, hid, units, cot, early, wo, wu, wd, cols, rows_info, qkvb, probs, att, acc,
    snd, rcv, out_buf, in_buf, proj, mid_buf, go, stage, top, own_tok, own_out,
    first_buf, slope, gates, dall, second, col, row, square, r_gate, r_inner, r_slope, r_dpre, r_rows, zpart, zland, gain_buf,
    pack, pack_plane, pack_side, pack_ring,
    local_sems, send_sems, recv_sems, acks,
):
    here = Plane()
    copies = Copies(local_sems, send_sems, recv_sems)
    here.greet()
    rank, share, side = here.rank, here.share, here.side
    owned = 128
    width = toks.shape[1]
    block = owned * SHARE
    head_width = wo.shape[0]
    unit_width = wu.shape[1]
    heads = head_width // HD
    own_rows = part(rank, owned)
    wq = early.at[:, 0 : 3 * head_width]
    act, gup = early.at[0:1024], early.at[1024:2048]
    sent, outs, done = [], [], []

    def to_peer(src, dst, peer):
        copy = copies.push(src, dst, peer)
        sent.append(copy)
        return copy

    def spread(src_of, dst):
        return [
            copies.local(src_of(here.shares[d]), dst)
            if d == 0
            else to_peer(src_of(here.shares[d]), dst, here.members[d])
            for d in range(SHARE)
        ]

    def landed(got):
        for i, copy in enumerate(got):
            if i % SHARE:
                copy.wait_recv()
            else:
                copy.wait()

    got_q = [
        spread(
            lambda t, j=j: qkvw.at[j, :, part(t, head_width)],
            wq.at[own_rows, j * head_width : (j + 1) * head_width],
        )
        for j in range(3)
    ]
    mine, other = part(side, owned), part(1 - side, owned)

    class Halves:
        def __init__(self, src, dst):
            self.dst = dst
            pairs = ((mine, 0), (other, owned))
            self.own = [copies.local(src(rows), dst(at)) for rows, at in pairs]
            self.mid = to_peer(src(mine), dst(256), here.mid)
            self.core = [to_peer(src(rows), dst(at + 512), here.core) for rows, at in pairs]

        def pass_on(self):
            self.mid.wait_recv()
            self.over = to_peer(self.dst(256), self.dst(384), here.across)
            self.last = [to_peer(self.dst(256), self.dst(768), here.core)]

        def complete(self):
            self.over.wait_recv()
            self.last.append(to_peer(self.dst(384), self.dst(896), here.core))

    tok_in = Halves(lambda r: tok.at[r, :], lambda at: toks.at[at : at + owned])

    row[...] = jnp.zeros_like(row)
    for h in range(2):
        slot = lax.broadcasted_iota(jnp.int32, (1, owned), 1) + h * owned
        segment = slot * 0 + (lengths.shape[1] + slot)
        position = slot
        live = slot * 0
        begin = 0
        for n in range(lengths.shape[1]):
            end = begin + lengths[0, n]
            member = (slot >= begin) & (slot < end)
            segment = jnp.where(member, n, segment)
            position = jnp.where(member, slot - begin, position)
            live = jnp.where(member, 1, live)
            begin = end
        lanes = slice(h * owned, (h + 1) * owned)
        held = (segment, slot, heads_in[h : h + 1, :], widths_in[h : h + 1, :], live, position)
        for n, value in enumerate(held):
            row[n : n + 1, lanes] = value.astype(wide)
        square[...] = jnp.zeros_like(square)
        square[0:8, :] = row[:, lanes]
        turned = jnp.transpose(square[...])
        angles = turned[:, 5:6] * turns[0:1, :]
        col[lanes, 0:HD] = jnp.cos(angles)
        sines = jnp.sin(angles)
        lane = lax.broadcasted_iota(jnp.int32, (owned, HD), 1)
        col[lanes, HD : 2 * HD] = jnp.where(lane < HD // 2, -sines, sines)
        col[lanes, 2 * HD : 3 * HD] = turned
    second[...] = jnp.zeros_like(second)
    for index in range(2):
        second[index, 0:NB, :] = second_in[index]
    col_in = Halves(lambda r: col.at[r, :], lambda at: cols.at[at : at + owned])
    row_in = Halves(
        lambda r: row.at[:, r],
        lambda at: rows_info.at[at // 256, :, at % 256 : at % 256 + owned],
    )
    got_o = spread(lambda t: outw.at[part(t, head_width), :], wo.at[:, own_rows])
    got_u = spread(lambda t: upw.at[:, part(t, unit_width)], wu.at[own_rows, :])
    got_d = spread(lambda t: downw.at[part(t, unit_width), :], wd.at[:, own_rows])
    cot_rows = Halves(lambda r: cot_in.at[r, :], lambda at: cot.at[at : at + owned])
    in_first = copies.local(first.at[0], first_buf)
    in_tok = copies.local(tok.at[mine, :], own_tok)

    g_q = [
        ZGather(here, copies, lambda k, d=d: wq.at[part(k * SHARE + here.shares[d], owned), :])
        for d in range(SHARE)
    ]
    g_o = ZGather(here, copies, lambda k: wo.at[:, part(k, block)])
    g_u = [
        ZGather(
            here,
            copies,
            lambda k, h=h: wu.at[part(k, block), h * 512 : (h + 1) * 512],
        )
        for h in range(2)
    ]
    g_d = [
        ZGather(here, copies, lambda k, h=h: wd.at[h * 512 : (h + 1) * 512, part(k, block)])
        for h in range(2)
    ]

    def fact(at, index):
        return cols[at, 2 * HD + index : 2 * HD + index + 1]

    def start_q(d):
        for got in got_q:
            if d:
                got[d].wait_recv()
            else:
                got[d].wait()
        g_q[d].start()

    start_q(0)
    start_q(1)

    def normalise(base):
        def body(i):
            at = pl.ds(pl.multiple_of(base + i * 64, 64), 64)
            x = toks[at, :].astype(wide)
            r = lax.rsqrt(jnp.mean(x * x, axis=-1, keepdims=True) + epsilon)
            hid[at, :] = (x * r * gains[0:1, :]).astype(low)

        tiles(4, body)

    def wait_all(waits):
        for wait in waits:
            wait()

    wait_all([c.wait for c in tok_in.own + col_in.own + row_in.own])
    normalise(0)

    def route(index, rows_of):
        made = exact(rows_of[0:owned, :].astype(wide), first_buf[...], ((1,), (0,)))
        sig = 1.0 / (1.0 + jnp.exp(-made))
        inner = made * sig
        logits = exact(inner, second[index], ((1,), (1,)))
        lane = lax.broadcasted_iota(jnp.int32, (owned, HD), 1)
        logits = jnp.where(lane < NB, logits, -1e30)
        raised = jnp.where(
            lane < NB, jnp.exp(logits - jnp.max(logits, axis=-1, keepdims=True)), 0.0
        )
        shares = raised / jnp.sum(raised, axis=-1, keepdims=True)
        hot = jnp.where(lane.astype(wide) == fact(pl.ds(0, owned), 2 + index), 1.0, 0.0)
        gate = NB * jnp.sum(shares * hot, axis=-1, keepdims=True)
        lean = hot - shares
        bare = exact(lean, second[index], ((1,), (0,))) * (sig * (1.0 + made * (1.0 - sig)))
        r_gate[index] = jnp.broadcast_to(gate, (owned, HD))
        r_inner[index] = inner
        r_slope[index] = lean if index else gate * lean
        r_dpre[index] = bare if index else gate * bare
        if index == 1:
            dall[0:owned, :] = bare.astype(low)

    def slope_tiles(index):
        def body(i):
            c = part(i, 256)
            slope[:, c] = exact(r_dpre[index], first_buf[c, :], ((1,), (1,)))

        tiles(8, body)

    in_first.wait()
    route(0, hid)
    in_first = copies.local(first.at[1], first_buf)
    start_q(2)
    start_q(3)
    g_q[0].first()
    g_q[1].first()
    tok_in.pass_on()
    wait_all([c.wait_recv for c in tok_in.core])
    normalise(512)
    g_q[0].second()
    g_q[1].second()
    g_q[2].first()
    g_q[3].first()
    tok_in.complete()
    normalise(256)
    g_q[2].second()
    g_q[3].second()
    wait_all([c.wait_recv for c in tok_in.last])
    normalise(768)
    save_hid = copies.local(hid, s_hid)
    col_in.pass_on()
    row_in.pass_on()
    landed(got_o)
    g_o.start()
    col_in.complete()
    row_in.complete()
    wait_all([c.wait_recv for c in col_in.core + row_in.core + col_in.last + row_in.last])
    g_o.first()
    landed(got_u)
    g_o.second()
    g_u[0].start()
    for one in g_q:
        one.arrive()
    save_wq = copies.local(wq, s_wq)

    for j in range(3):

        def qkv_tile(i, j=j):
            at = part(i, 512)
            made = nn(hid[at, :], wq[:, j * head_width : (j + 1) * head_width])
            if j < 2:
                cosine = cols[at, 0:HD]
                sine = cols[at, HD : 2 * HD]
                for h in range(heads):
                    one = made[:, h * HD : (h + 1) * HD]
                    turned = one * cosine + pltpu.roll(one, HD // 2, 1) * sine
                    qkvb[at, j * head_width + h * HD : j * head_width + (h + 1) * HD] = (
                        turned.astype(low)
                    )
            else:
                qkvb[at, j * head_width : (j + 1) * head_width] = made.astype(low)

        tiles(2, qkv_tile)

    g_u[0].first()
    g_u[1].start()

    first_head = (side * SHARE + share) * heads
    scale = HD ** (-0.5)
    for h in range(heads):
        head = (first_head + h).astype(wide)

        def attend_group(g, h=h, head=head):
            at = part(g, 256)
            query, keyed, value = (
                qkvb[at, pl.ds(j * head_width + h * HD, HD)] for j in range(3)
            )
            info = rows_info[g]
            seg_k, slot_k, bucket_k = info[0:1, :], info[1:2, :], info[2:3, :]
            reach_k = jnp.where(4.0 * bucket_k + 4.0 > head, 1.0, 0.0)
            slot_q = fact(at, 1)
            usable = (reach_k > 0.5) | (slot_k == slot_q)
            allowed = (fact(at, 0) == seg_k) & (slot_k <= slot_q) & usable
            scores = jnp.where(allowed, nt(query, keyed) * scale, -1e30)
            weights = jnp.exp(scores - jnp.max(scores, axis=-1, keepdims=True))
            p = weights / jnp.sum(weights, axis=-1, keepdims=True)
            probs[part(g * heads + h, 256), :] = p
            mixed = nn(p.astype(low), value)
            att[at, h * HD : (h + 1) * HD] = jnp.where(
                4.0 * fact(at, 2) + 4.0 > head, mixed, 0.0
            ).astype(low)

        tiles(SHARE, attend_group)

    reduce = RowReduce(here, copies, (snd, rcv, acc, out_buf, in_buf), acks)

    def partial_sums(term, extra=None):
        lanes = acc.shape[1] if extra is not None else width
        reduce.begin(lanes)
        for i in range(2):

            def send_tile(n, i=i):
                snd[i * 256 : (i + 1) * 256, part(n, 512)] = term(
                    pl.ds(512 + i * 256, 256), n
                ).astype(low)

            tiles(4, send_tile)
            if extra is not None:
                snd[i * 256 : (i + 1) * 256, width:lanes] = extra[
                    pl.ds(512 + i * 256, 256), :
                ].astype(low)
            reduce.core_send(i)

        def own_tile(n):
            acc[:, part(n, 512)] = term(pl.ds(0, 512), n)

        tiles(4, own_tile)
        if extra is not None:
            acc[:, width:lanes] = extra[0:512, :]

    cot_rows.pass_on()
    g_o.arrive()
    partial_sums(lambda at, n: nn(att[at, :], wo[:, part(n, 512)]))
    g_u[0].second()
    reduce.diagonal()
    g_u[1].first()
    reduce.sides()
    g_u[1].second()
    landed(got_d)
    g_d[0].start()
    g_d[1].start(False)
    in_tok.wait()
    reduce.arrive()

    def row_tiles(body):
        def step(i):
            at = pl.multiple_of(i * 64, 64)
            body(at, pl.ds(at, 64))

        tiles(owned // 64, step)

    def middle_tile(at, rows):
        projected = reduce.total(at, 64)
        proj[rows, :] = projected
        middle = own_tok[rows, :].astype(wide) + r_gate[0, rows, 0:1] * projected
        mid_buf[rows, :] = middle
        r = lax.rsqrt(jnp.mean(middle * middle, axis=-1, keepdims=True) + epsilon)
        units[rows, :] = (middle * r * gains[1:2, :]).astype(low)

    row_tiles(middle_tile)
    reduce.release()

    def row_view(buf):
        def view(k, h):
            if h is None:
                return buf.at[k * owned : (k + 1) * owned]
            return buf.at[k * owned + h * 64 : k * owned + (h + 1) * 64]

        return view

    units_out = RowGather(here, copies, row_view(units))
    units_out.start()
    in_first.wait()
    route(1, units)
    gates[0:owned, :] = r_gate[1]
    gates_out = RowGather(here, copies, row_view(gates))
    dall_out = RowGather(here, copies, row_view(dall))
    gates_out.start()
    dall_out.start()

    def first_low(n):
        return go[pl.ds(pl.multiple_of(n % 2 * 512, 512), 512), part(n // 2, 256)]

    def first_tile(i):
        go[part(i % 8, 128), part(i // 8, 256)] = first_buf[part(i, 128), :].astype(low)

    tiles(16, first_tile)
    in_first = copies.local(first.at[0], first_buf)
    g_d[0].first()
    units_out.forward()
    gates_out.forward()
    dall_out.forward()
    units_out.finish()
    gates_out.finish()
    dall_out.finish()
    g_d[0].second()
    g_d[1].start_late()
    g_d[1].first()
    g_d[1].second()
    wait_all([c.wait for c in cot_rows.own])
    cot_rows.complete()
    wait_all([c.wait_recv for c in cot_rows.core + cot_rows.last])

    def live_cot(at):
        return jnp.where(fact(at, 4) > 0.5, cot[at, :].astype(wide), 0.0)

    for copy in tok_in.last + cot_rows.last + [tok_in.over, cot_rows.over]:
        copy.wait_send()
        done.append(copy)

    def keep_tile(at, rows):
        top[rows, :] = live_cot(rows).astype(low)

    row_tiles(keep_tile)

    def scale_tile(i):
        at = part(i, 64)
        cot[at, :] = (gates[at, 0:1] * live_cot(at)).astype(low)

    tiles(16, scale_tile)

    first_unit = (side * SHARE + share) * unit_width

    def used_units(at, base, rows, columns):
        lane = lax.broadcasted_iota(jnp.int32, (rows, columns), 1) + base
        return lane.astype(wide) < (FF // NB) * (fact(at, 3) + 1.0)

    save_wq.wait()
    for one in g_q:
        one.drain()

    def up_tile(m, n):
        at, c = part(m, 512), slice(n * 512, (n + 1) * 512)
        made = nn(units[at, :], wu[:, c])
        acc[:, part(m * 2 + n, 512)] = made
        relu = jnp.maximum(made, 0.0)
        used = used_units(at, first_unit + n * 512, 512, 512)
        act[at, c] = jnp.where(used, relu * relu, 0.0).astype(low)

    def deliver(piece_of, dst):
        for d in range(SHARE):
            src = piece_of(here.shares[d])
            if d == 0:
                outs.append(copies.local(src, dst))
            else:
                sent.append(copies.push(src, dst, here.members[d]))
                owed.append(sent[-1])

    owed = []

    gd, gu, gq = toks, hid, wd
    blocks = [here.place, here.near_place, here.two_place, here.far_place]
    z_d = ZReduce(here, copies, gd, lambda k: (0, k * block), unit_width, block, l_d)
    z_u = ZReduce(
        here, copies, gu, lambda k: (k % 2 * block, k // 2 * unit_width), block, unit_width, l_u
    )
    z_o = ZReduce(here, copies, go, lambda k: (k * head_width, 0), head_width, block, l_o)
    z_q = ZReduce(
        here, copies, gq, lambda k: (k % 2 * block, k // 2 * 1024), block, 3 * head_width, l_q
    )

    def down_block(k, h):
        m = slice(h * 512, (h + 1) * 512)

        def body(i):
            lanes = pl.ds(pl.multiple_of(k * block + i * 256, 256), 256)
            gd[m, lanes] = tn(act[:, m], cot[:, part(2 * blocks[k] + i, 256)]).astype(low)

        tiles(2, body)

    for h in range(2):
        g_u[h].arrive()
        tiles(2, lambda m, h=h: up_tile(m, h))
        for k in (3, 2, 1, 0):
            down_block(k, h)
            if k:
                z_d.outward(k, rows=(h * 512, 512))

    def gup_tile(m, n):
        at, c = part(m, 512), slice(n * 512, (n + 1) * 512)
        made = nt(cot[at, :], wd[c, :])
        used = used_units(at, first_unit + n * 512, 512, 512)
        relu = jnp.maximum(acc[:, part(m * 2 + n, 512)], 0.0)
        gup[at, c] = jnp.where(used, 2.0 * relu * made, 0.0).astype(low)
        dots = jnp.sum(act[at, c].astype(wide) * made, axis=-1, keepdims=True)
        if n:
            dots = dots + gates[at, 0:1]
            r_rows[at, 256:512] = (dots * dall[at, :].astype(wide)).astype(low)
        gates[at, :] = jnp.broadcast_to(dots, (512, HD))

    def up_block(k, h):
        r, c = k % 2 * block, k // 2 * unit_width + h * 512

        def body(i):
            gu[r : r + block, pl.ds(pl.multiple_of(c + i * 256, 256), 256)] = tn(
                units[:, part(blocks[k], block)], gup[:, part(2 * h + i, 256)]
            ).astype(low)

        tiles(2, body)
        if k > 1:
            z_u.outward_half(k, h, 512)
        elif k:
            z_u.outward(k, lanes=(h * 512, 512))

    gates_out.drain()
    save_hid.wait()
    g_d[0].arrive()
    tiles(2, lambda m: gup_tile(m, 0))
    for k in (3, 2, 1, 0):
        up_block(k, 0)
    z_d.inward(0, stage)
    z_d.inward(1, stage)
    g_d[1].arrive()
    tiles(2, lambda m: gup_tile(m, 1))

    reduce.await_release()
    partial_sums(
        lambda at, n: nt(gup[at, :], wu[part(n, 512), :])
        + nt(r_rows[at, 256:512], first_low(n)),
        gates,
    )
    up_block(3, 1)
    up_block(2, 1)
    reduce.diagonal()
    up_block(1, 1)
    z_d.inward(2, stage)
    reduce.sides()
    up_block(0, 1)
    z_u.inward_half(0, 0, 512, stage)

    column = share * 2 + side
    ucol = dall
    dall_out.drain()

    def ucol_tile(i):
        ucol[part(i, 256), :] = units[part(i, 256), part(column, 256)]

    tiles(4, ucol_tile)
    units_out.drain()
    in_hid = copies.local(s_hid, units)
    for one in g_u:
        one.drain()
    in_wq = copies.local(s_wq, wu.at[:, 0 : 3 * head_width])

    r_rows_out = RowGather(here, copies, row_view(r_rows))

    def keep_gate(index, rows, weight):
        c = slice(index * 256, (index + 1) * 256)
        r_rows[rows, c] = (weight * r_dpre[index, rows, :]).astype(low)
        r_slope[index, rows, :] = weight * r_slope[index, rows, :]

    places = [here.place, here.near_place, here.two_place, here.far_place]
    planes = [None, here.near, here.two, here.far]

    def first_rows(k, h):
        target = here.shares[k // 4 + k // 2 % 2 * 2] * 2 + (side if k % 2 == 0 else 1 - side)
        base = target * 256
        if h is None:
            return o_first.at[:, pl.ds(pl.multiple_of(base, 256), 256), :]
        return o_first.at[:, pl.ds(pl.multiple_of(base + h * 128, 128), 128), :]

    first_out = RowGather(here, copies, first_rows, True)

    class FirstSum:
        def __init__(self):
            zpart[0] = tn(units[:, part(column, 256)], r_rows[:, 0:256]).astype(low)
            zpart[1] = tn(ucol[...], r_rows[:, 256:512]).astype(low)
            self.got = []
            for k in range(4):
                src, dst = zpart.at[:, part(places[k], 64), :], zland.at[here.place]
                self.got.append(
                    copies.local(src, dst) if k == 0 else to_peer(src, dst, planes[k])
                )

        def add(self):
            landed(self.got)
            for copy in self.got[1:]:
                copy.wait_send()
                done.append(copy)
            total = zland[0].astype(wide)
            for k in range(1, 4):
                total = total + zland[k].astype(wide)
            zpart[:, 0:64, :] = total.astype(low)
            at = pl.ds(pl.multiple_of(column * 256 + here.place * 64, 64), 64)
            src, dst = zpart.at[:, 0:64, :], o_first.at[:, at, :]
            self.got = [
                copies.local(src, dst) if k == 0 else to_peer(src, dst, planes[k])
                for k in range(4)
            ]

        def show(self):
            landed(self.got)
            first_out.start()

    reduce.arrive()
    gproj = cot
    gain_buf[...] = jnp.zeros_like(gain_buf)

    def grad_tile(at, rows):
        total = reduce.total(at, 64)
        grad = total[:, 0:width]
        keep_gate(1, rows, total[:, width : width + 1])
        back, gain_terms = norm_back(mid_buf[rows, :], grad, gains[1:2, :])
        grad_middle = top[rows, :].astype(wide) + back
        gproj[rows, :] = (r_gate[0, rows, 0:1] * grad_middle).astype(low)
        grad_gate = jnp.sum(grad_middle * proj[rows, :], axis=-1, keepdims=True)
        keep_gate(0, rows, grad_gate)
        r_gate[0, rows, :] = jnp.broadcast_to(grad_gate, (64, HD))
        proj[rows, :] = grad_middle
        gain_buf[1:2, :] = gain_buf[1:2, :] + jnp.sum(gain_terms, axis=0, keepdims=True)

    row_tiles(grad_tile)
    reduce.release()
    gproj_out = RowGather(here, copies, row_view(gproj))
    gproj_out.start()
    r_rows_out.start()
    in_first.wait()
    slope_tiles(0)
    z_u.inward_half(1, 0, 512, stage)
    gproj_out.forward()
    r_rows_out.forward()

    reduce.await_release()
    partial_sums(lambda at, n: nn(act[at, :], wd[:, part(n, 512)]))
    gproj_out.finish()
    reduce.diagonal()
    r_rows_out.finish()
    in_hid.wait()
    sum_first = FirstSum()
    z_u.inward_half(0, 1, 512, stage)

    def out_block(k):
        def body(i):
            go[k * head_width : (k + 1) * head_width, part(i, 256)] = tn(
                att[...], gproj[:, part(2 * blocks[k] + i, 256)]
            ).astype(low)

        tiles(2, body)

    gatt, gqkv = gup, act

    def gatt_tile(i):
        at = part(i, 512)
        made = nt(gproj[at, :], wo[...]).astype(low)
        for h in range(heads):
            used = 4.0 * fact(at, 2) + 4.0 > (first_head + h).astype(wide)
            gatt[at, h * HD : (h + 1) * HD] = jnp.where(
                used, made[:, h * HD : (h + 1) * HD].astype(wide), 0.0
            ).astype(low)

    tiles(2, gatt_tile)

    for h in range(heads):

        def back_group(g, h=h):
            at = part(g, 256)
            lanes = [pl.ds(j * head_width + h * HD, HD) for j in range(3)]
            query, keyed, value = (qkvb[at, lane] for lane in lanes)
            grad = gatt[at, h * HD : (h + 1) * HD]
            p = probs[part(g * heads + h, 256), :]
            grad_p = nt(grad, value)
            row_dot = jnp.sum(p * grad_p, axis=-1, keepdims=True)
            grad_s = (p * (grad_p - row_dot)).astype(low)
            cosine = cols[at, 0:HD]
            sine = cols[at, HD : 2 * HD]
            for lane, turned in (
                (lanes[0], nn(grad_s, keyed) * scale),
                (lanes[1], tn(grad_s, query) * scale),
            ):
                gqkv[at, lane] = (
                    turned * cosine - pltpu.roll(turned, HD // 2, 1) * sine
                ).astype(low)
            gqkv[at, lanes[2]] = tn(p.astype(low), grad).astype(low)

        tiles(SHARE, back_group)

    def qkv_block(k):
        r, c = k % 2 * block, k // 2 * 1024

        def body(j):
            lanes = pl.ds(pl.multiple_of(c + j * head_width, head_width), head_width)
            gq[r : r + block, lanes] = tn(
                units[:, part(blocks[k], block)], gqkv[:, part(j, head_width)]
            ).astype(low)

        tiles(3, body)

    for one in g_d:
        one.drain()
    reduce.sides()
    qkv_block(3)
    z_q.outward(3)
    out_block(3)
    z_o.outward(3)
    z_u.inward_half(1, 1, 512, stage)
    sum_first.add()
    qkv_block(2)
    z_q.outward(2)
    for k in (2, 1):
        out_block(k)
        z_o.outward(k)
    qkv_block(1)
    for j in range(3):
        z_q.outward_piece(j, head_width)
    qkv_block(0)
    out_block(0)
    z_d.finish(stage)
    deliver(lambda t: gd.at[:, part(t, owned)], o_gd.at[part(share, unit_width), :])

    z_u.inward(2, stage)
    reduce.arrive()

    def block_tile(at, rows):
        own_out[rows, :] = jnp.where(
            fact(rows, 4) > 0.5,
            mid_buf[rows, :] + r_gate[1, rows, 0:1] * reduce.total(at, 64),
            0.0,
        ).astype(low)

    row_tiles(block_tile)
    reduce.release()
    shown = copies.local(own_out, o_block.at[mine])
    shown_far = to_peer(own_out, o_block.at[mine], here.across)

    in_wq.wait()
    reduce.await_release()
    partial_sums(
        lambda at, n: nt(gqkv[at, 0 : 3 * head_width], wu[part(n, 512), 0 : 3 * head_width])
    )
    reduce.diagonal()
    z_q.inward(0, stage)
    z_o.inward(0, stage)
    reduce.sides()
    z_u.finish(stage)
    deliver(lambda t: gu.at[part(t, owned), 0:unit_width], o_gu.at[:, part(share, unit_width)])
    sum_first.show()
    z_q.inward(2, stage)
    z_q.inward(1, stage)
    z_o.inward(1, stage)
    z_o.inward(2, stage)
    shown.wait()
    shown_far.wait()
    done.append(shown_far)
    reduce.arrive()

    def input_tile(at, rows):
        grad = reduce.total(at, 64) + r_gate[0, rows, 0:1] * slope[rows, :]
        back, gain_terms = norm_back(own_tok[rows, :].astype(wide), grad, gains[0:1, :])
        own_out[rows, :] = (proj[rows, :] + back).astype(low)
        gain_buf[0:1, :] = gain_buf[0:1, :] + jnp.sum(gain_terms, axis=0, keepdims=True)

    row_tiles(input_tile)
    outs.append(copies.local(own_out, o_input.at[mine]))
    input_far = copies.push(own_out, o_input.at[mine], here.across)
    first_out.forward()

    def finish_q(j):
        z_q.finish_piece(j, head_width, stage)
        deliver(
            lambda t: gq.at[part(t, owned), j * head_width : (j + 1) * head_width],
            o_gq.at[j, :, part(share, head_width)],
        )

    for index in range(2):
        for j in range(8):
            pack[index * 8 + j : index * 8 + j + 1, :] = gain_buf[
                index : index + 1, j * 256 : (j + 1) * 256
            ]
        made = exact(r_slope[index], r_inner[index], ((0,), (0,)))
        pack[16 + index * 8 : 24 + index * 8, :] = made[0:8, :]
        lane = lax.broadcasted_iota(jnp.int32, (owned, 256), 1)
        own = pl.ds(0, owned)
        hot = (lane.astype(wide) == fact(own, 2 + index)) & (fact(own, 4) > 0.5)
        count = jnp.sum(jnp.where(hot, 1.0, 0.0), axis=0, keepdims=True)
        pack[32 + index * 8 : 40 + index * 8, :] = jnp.broadcast_to(count, (8, 256))

    def sum_slots(buf, count):
        total = buf[0]
        for k in range(1, count):
            total = total + buf[k]
        return total

    got = [
        copies.local(pack, pack_plane.at[share])
        if d == 0
        else to_peer(pack, pack_plane.at[share], here.members[d])
        for d in range(SHARE)
    ]
    z_o.finish(stage)
    deliver(
        lambda t: go.at[0:head_width, part(t, owned)], o_go.at[part(share, head_width), :]
    )
    finish_q(0)
    landed(got)
    for copy in got[1:]:
        copy.wait_send()
        done.append(copy)
    pack[...] = sum_slots(pack_plane, SHARE)
    got = [
        copies.local(pack, pack_side.at[side]),
        to_peer(pack, pack_side.at[side], here.across),
    ]
    finish_q(1)
    landed(got)
    got[1].wait_send()
    done.append(got[1])
    pack[...] = pack_side[0] + pack_side[1]
    got = [
        copies.local(pack, pack_ring.at[here.place])
        if k == 0
        else to_peer(pack, pack_ring.at[here.place], planes[k])
        for k in range(4)
    ]

    finish_q(2)
    first_out.finish()
    landed(got)
    for copy in got[1:]:
        copy.wait_send()
        done.append(copy)
    pack[...] = sum_slots(pack_ring, 4)
    outs.append(copies.local(pack, o_pack))

    drains = [g_o] + g_q + g_u + g_d + [z_d, z_u, z_o, z_q, reduce, units_out, gates_out, dall_out]
    for one in drains + [gproj_out, r_rows_out, first_out]:
        one.drain()
    input_far.wait()
    for copy in owed:
        copy.wait_recv()
    for copy in outs:
        copy.wait()
    for copy in sent:
        if not any(copy is one for one in done):
            copy.wait_send()
    copies.check()


def finish_kernel(
    block, inp, gq, go, gu, gd, gf, sums,
    o_block, o_inp, o_gains, o_gq, o_go, o_gu, o_gd, o_first, o_second, o_usage,
    b_block, b_inp, b_q, b_o, b_u, b_d, b_f, w_q, w_o, w_u, w_d, w_f, in_sems, out_sems,
):
    narrow = [(gu, b_u), (gd, b_d), (gq, b_q), (gf, b_f), (go, b_o)]
    narrow += [(block, b_block), (inp, b_inp)]
    loads = [
        pltpu.make_async_copy(src, dst, in_sems.at[i]) for i, (src, dst) in enumerate(narrow)
    ]
    for load in loads:
        load.start()
    stores = []

    def store(src, dst):
        copy = pltpu.make_async_copy(src, dst, out_sems.at[len(stores)])
        copy.start()
        stores.append(copy)

    for index in range(2):
        for j in range(8):
            o_gains[index : index + 1, j * 256 : (j + 1) * 256] = sums[
                index * 8 + j : index * 8 + j + 1, :
            ]
        o_second[index] = sums[16 + index * 8 : 16 + index * 8 + NB, :]
        o_usage[index : index + 1, :] = sums[32 + index * 8 : 33 + index * 8, 0:NB]
    wides = [(b_u, w_u, o_gu), (b_d, w_d, o_gd), (b_q, w_q, o_gq)]
    wides += [(b_f, w_f, o_first), (b_o, w_o, o_go)]
    for i, (src, dst, out) in enumerate(wides):
        loads[i].wait()
        lead = src.shape[0] if len(src.shape) == 3 else None
        step = 128 if src.shape[-1] < 1024 else 32
        rows = src.shape[-2]
        for n in range(lead or 1):

            def widen(k, src=src, dst=dst, n=n, lead=lead):
                at = part(k, step)
                if lead is None:
                    dst[at, :] = src[at, :].astype(wide)
                else:
                    dst[n, at, :] = src[n, at, :].astype(wide)

            tiles(rows // step, widen)
        store(dst, out)
    for i, (src, out) in enumerate(((b_block, o_block), (b_inp, o_inp))):
        loads[5 + i].wait()
        store(src, out)
    for copy in stores:
        copy.wait()


def plane(mesh):
    fsdp = mesh.shape["fsdp"]
    ring_size = fsdp // SHARE

    def shards(
        tokens,
        head_bucket,
        ffn_bucket,
        lengths,
        norm_gains,
        qkv_weight,
        out_weight,
        up_weight,
        down_weight,
        router_first,
        router_second,
        cotangent,
    ):
        rows, width = tokens.shape
        half = rows // 2
        local_units = up_weight.shape[1]
        units = local_units // SHARE
        local_width = out_weight.shape[0]
        head_width = local_width // SHARE
        heads = head_width // HD
        owned = width // fsdp
        block = width // ring_size
        plane_rows = SHARE * rows

        turns = np.float32(theta_base) ** np.float32(-2.0 * np.arange(HD // 2) / HD)
        turns = np.tile(np.concatenate([turns, turns])[None, :], (8, 1)).astype(np.float32)
        b16, f32 = low, wide
        hidden = router_first.shape[2]
        small = 48

        def shape(*dims):
            return jax.ShapeDtypeStruct(dims[1:], dims[0])

        def buffer(*dims):
            return pltpu.VMEM(dims[1:], dims[0])

        anywhere = pl.BlockSpec(memory_space=pl.ANY)
        vmem = pl.BlockSpec(memory_space=pltpu.VMEM)
        (
            block_out,
            input_grad,
            raw_qkv,
            raw_out,
            raw_up,
            raw_down,
            raw_first,
            sums,
            *_,
        ) = pl.pallas_call(
            layer_kernel,
            out_shape=[
                shape(b16, rows, width),
                shape(b16, rows, width),
                shape(b16, 3, owned, local_width),
                shape(b16, local_width, owned),
                shape(b16, owned, local_units),
                shape(b16, local_units, owned),
                shape(b16, *router_first.shape),
                shape(f32, small, 256),
                shape(b16, plane_rows, width),
                shape(b16, width, 3 * head_width),
                shape(b16, 5, block, 3 * head_width),
                shape(b16, 5, head_width, block),
                shape(b16, 5, block, units),
                shape(b16, 5, units, block),
            ],
            in_specs=[anywhere] * 7 + [vmem] * 5 + [pl.BlockSpec(memory_space=pltpu.SMEM)],
            out_specs=[anywhere] * 14,
            scratch_shapes=[
                buffer(b16, plane_rows, width),
                buffer(b16, plane_rows, width),
                buffer(b16, plane_rows, width),
                buffer(b16, plane_rows, width),
                buffer(b16, 2 * plane_rows, units),
                buffer(b16, head_width, width),
                buffer(b16, width, units),
                buffer(b16, units, width),
                buffer(f32, plane_rows, 3 * HD),
                buffer(f32, SHARE, 8, rows),
                buffer(b16, plane_rows, 3 * head_width),
                buffer(f32, SHARE * heads * rows, rows),
                buffer(b16, plane_rows, head_width),
                buffer(f32, plane_rows // 2, width + HD),
                buffer(b16, plane_rows // 2, width + HD),
                buffer(b16, plane_rows // 2, width + HD),
                buffer(b16, 3 * half, width + HD),
                buffer(b16, 3 * half, width + HD),
                buffer(f32, half, width),
                buffer(f32, half, width),
                buffer(b16, 4 * head_width, block),
                buffer(b16, 2, block, units),
                buffer(b16, half, width),
                buffer(b16, half, width),
                buffer(b16, half, width),
                buffer(f32, width, hidden),
                buffer(f32, half, width),
                buffer(f32, plane_rows, HD),
                buffer(b16, plane_rows, hidden),
                buffer(f32, 2, HD, hidden),
                buffer(f32, rows, 3 * HD),
                buffer(f32, 8, rows),
                buffer(f32, HD, HD),
                buffer(f32, 2, half, HD),
                buffer(f32, 2, half, hidden),
                buffer(f32, 2, half, HD),
                buffer(f32, 2, half, hidden),
                buffer(b16, plane_rows, 2 * hidden),
                buffer(b16, 2, 256, hidden),
                buffer(b16, 4, 2, 64, hidden),
                buffer(f32, 8, width),
                buffer(f32, small, 256),
                buffer(f32, SHARE, small, 256),
                buffer(f32, 2, small, 256),
                buffer(f32, 4, small, 256),
                pltpu.SemaphoreType.DMA((80,)),
                pltpu.SemaphoreType.DMA((240,)),
                pltpu.SemaphoreType.DMA((220,)),
                pltpu.SemaphoreType.REGULAR((3,)),
            ],
            compiler_params=pltpu.CompilerParams(
                collective_id=0, has_side_effects=True, vmem_limit_bytes=127 * 2**19
            ),
        )(
            tokens,
            cotangent,
            jnp.transpose(qkv_weight, (1, 0, 2)),
            out_weight,
            up_weight,
            down_weight,
            router_first,
            norm_gains,
            jnp.transpose(router_second, (0, 2, 1)),
            head_bucket.reshape(2, half),
            ffn_bucket.reshape(2, half),
            jnp.asarray(turns),
            lengths,
        )
        wides = [
            (3, owned, local_width),
            (local_width, owned),
            (owned, local_units),
            (local_units, owned),
            router_first.shape,
        ]
        (
            block_out,
            input_grad,
            grad_gains,
            grad_qkv,
            grad_out,
            grad_up,
            grad_down,
            grad_first,
            grad_second,
            usage,
        ) = pl.pallas_call(
            finish_kernel,
            out_shape=[shape(b16, rows, width), shape(b16, rows, width), shape(f32, 2, width)]
            + [shape(f32, *dims) for dims in wides]
            + [shape(f32, 2, NB, hidden), shape(f32, 2, NB)],
            in_specs=[anywhere] * 7 + [vmem],
            out_specs=[anywhere] * 2 + [vmem] + [anywhere] * 5 + [vmem] * 2,
            scratch_shapes=[buffer(b16, rows, width)] * 2
            + [buffer(b16, *dims) for dims in wides]
            + [buffer(f32, *dims) for dims in wides]
            + [pltpu.SemaphoreType.DMA((8,)), pltpu.SemaphoreType.DMA((8,))],
            compiler_params=pltpu.CompilerParams(vmem_limit_bytes=60 * 2**20),
        )(block_out, input_grad, raw_qkv, raw_out, raw_up, raw_down, raw_first, sums)
        grad_qkv = jnp.transpose(grad_qkv, (1, 0, 2))
        grad_second = jnp.transpose(grad_second, (0, 2, 1))
        return (
            block_out,
            input_grad,
            grad_gains,
            grad_qkv,
            grad_out,
            grad_up,
            grad_down,
            grad_first,
            grad_second,
            usage,
        )

    return shards


def solution(mesh):
    shards = plane(mesh) if mesh.shape["fsdp"] == 4 * SHARE else general(mesh)
    in_specs = (
        P("fsdp", None),
        P("fsdp"),
        P("fsdp"),
        P("fsdp", None),
        P(),
        P("fsdp", None, "tensor"),
        P("tensor", "fsdp"),
        P("fsdp", "tensor"),
        P("tensor", "fsdp"),
        P(),
        P(),
        P("fsdp", None),
    )
    out_specs = (
        P("fsdp", None),
        P("fsdp", None),
        P(),
        P("fsdp", None, "tensor"),
        P("tensor", "fsdp"),
        P("fsdp", "tensor"),
        P("tensor", "fsdp"),
        P(),
        P(),
        P(),
    )
    return jax.shard_map(
        shards, mesh=mesh, in_specs=in_specs, out_specs=out_specs, check_vma=False
    )
```
